32 devices in a mesh: section: 2 (over x), dp: 16 (over z, y, core).
Axes of the slice: x: 2, y: 2, z: 4, core: 2. Of those that a mesh axis runs over, the one named last changes fastest.
Arguments:
- inputs: bfloat16 [2, 32, 256, 512], P('section', 'dp'), may hold values from -6 to 6
- lengths: int32 [2, 32, 8], P(None, 'dp'), may hold values from 8 to 32, as said below
- cotangent: bfloat16 [32, 256, 512], P('dp'), may hold values from -6 to 6
- matrices: bfloat16 [2, 7168, 512], P('section')
- vectors: bfloat16 [2, 5632], P('section')
- master_matrices: float32 [2, 7168, 512], P('section', 'dp'), may hold values from -0.005859375 to 0.005859375
- master_vectors: float32 [2, 5632], P('section', 'dp'), may hold values from -0.005859375 to 0.005859375
- matrix_mean: float32 [2, 7168, 512], P('section', 'dp'), may hold values from -128 to 128
- matrix_square: float32 [2, 7168, 512], P('section', 'dp'), may hold values from 2 to 200
- vector_mean: float32 [2, 5632], P('section', 'dp'), may hold values from -128 to 128
- vector_square: float32 [2, 5632], P('section', 'dp'), may hold values from 2 to 200
- adam_step: int32 [1], replicated, may hold values from 3000 to 5000
Outputs:
- layer_outputs: bfloat16 [2, 32, 256, 512], P('section', 'dp')
- input_grads: float32 [2, 32, 256, 512], P('section', 'dp')
- matrix_grads: float32 [2, 7168, 512], P('section', 'dp')
- vector_grads: float32 [2, 5632], P('section', 'dp')
- matrix_change: float32 [2, 7168, 512], P('section', 'dp')
- vector_change: float32 [2, 5632], P('section', 'dp')
- matrix_mean_new: float32 [2, 7168, 512], P('section', 'dp')
- matrix_square_new: float32 [2, 7168, 512], P('section', 'dp')
- vector_mean_new: float32 [2, 5632], P('section', 'dp')
- vector_square_new: float32 [2, 5632], P('section', 'dp')
- matrices_new: bfloat16 [2, 7168, 512], P('section')
- vectors_new: bfloat16 [2, 5632], P('section')
The draws below stay inside these ranges and needn't reach their ends.
Inputs may be any that keep to these rules, and one draw needn't show every extreme that they name: lengths[s, r, :] are the lengths of the 8 sentences packed in row r of the source (s = 0) and of the target (s = 1), sentence j of a target row translating sentence j of the source row; a row's total is at most 256, the rest is padding, and every row has one sentence of exactly 32 tokens.
All inputs are finite; a program needn't handle non-finite values.
Results may differ from the reference program's by a relative error of at most 0.025.
Values may be sent and summed in bfloat16 or wider, within the bound.
No kernel may reach another device: no remote copies, remote signals or barrier semaphores. Data moves between devices by JAX's collectives and lax.ppermute only.
A program may use at most 256 MiB of HBM per device.

```python
import math
import jax
import jax.numpy as jnp
from jax import lax

D = 512
HEADS = 8
FF = 2048
LEN = 256
SENTS = 8
SENT_MOST = 32
SENT_LEAST = 8
ROWS = 32
PROWS = 7168
VEC = 5632
N_DP = 16


def draw_lengths(key, part):
    key = jax.random.fold_in(key, 17)
    key_base, key_pick = jax.random.split(key)
    base_lens = jax.random.randint(key_base, (2, ROWS, SENTS), SENT_LEAST, SENT_MOST + 1)
    picked = jax.random.randint(key_pick, (2, ROWS, 1), 0, SENTS)
    position = jnp.arange(SENTS)[None, None, :]
    return jnp.where(position == picked, SENT_MOST, base_lens).astype(jnp.int32)


def draw_matrices(key, part):
    key = jax.random.fold_in(key, 11)
    total_rows = 6 * D + 2 * FF
    normals = jax.random.truncated_normal(key, -4.0, 4.0, (2, total_rows, D), jnp.float32)
    position = jnp.arange(total_rows)[None, :, None]
    section_pos = jnp.arange(2)[:, None, None]
    boost_out = math.sqrt(max(1, 5 * SENT_MOST // 8))
    base_scale = D ** (-0.5)
    cross_scale = jnp.where((section_pos == 1) & ((position - 4 * D) % 2 == 1), base_scale * boost_out, base_scale)
    scale_map = jnp.where(position < 3 * D, base_scale, jnp.where(position < 4 * D, base_scale * boost_out, jnp.where(position < 6 * D, cross_scale, jnp.where(position < 6 * D + FF, base_scale, 1.5 * FF ** (-0.5)))))
    return (normals * scale_map).astype(jnp.bfloat16)


def draw_vectors(key, part):
    key = jax.random.fold_in(key, 13)
    key_normal, key_gain = jax.random.split(key)
    total_len = FF + 7 * D
    normals = jax.random.truncated_normal(key_normal, -4.0, 4.0, (2, total_len), jnp.float32)
    gains = jax.random.uniform(key_gain, (2, total_len), jnp.float32, 0.5, 1.5)
    position = jnp.arange(total_len)[None, :]
    slot_index = (position - FF) // D
    is_gain = (position >= FF) & (slot_index % 2 == 1)
    values = jnp.where(position < FF, 0.5 * normals, jnp.where(is_gain, gains, 0.3 * normals))
    return values.astype(jnp.bfloat16)


def strengthened(values, rng, source, target, blocks, factor):
    owner, partner = [(jnp.arange(values.shape[dim]) // (values.shape[dim] // blocks)).reshape([-1 if axis == dim else 1 for axis in range(values.ndim)]) for dim in (source, target)]
    chosen = jax.random.permutation(rng, blocks)[partner]
    strong = (owner == chosen) | (owner == (partner + blocks // 2) % blocks)
    return jnp.where(strong, factor * values, values)


def shard_levels(own_key, shape, cuts, least, largest):
    def one(axis_at, parts):
        steps = jax.random.uniform(jax.random.fold_in(jax.random.fold_in(own_key, 6), axis_at), (parts,), jnp.float32, least / len(cuts), largest / len(cuts))
        return jnp.repeat(jnp.exp(steps), shape[axis_at] // parts).reshape((-1,) + (1,) * (len(shape) - axis_at - 1))

    factor_of = one(*cuts[0])
    for cut in cuts[1:]:
        factor_of = factor_of * one(*cut)
    return factor_of


def bell_draw(own_key, dims, scale, most, cuts=(), kind=jnp.bfloat16):
    drawn = jax.random.normal(own_key, dims, jnp.float32) * scale
    if len(cuts) > 0:
        drawn = shard_levels(own_key, dims, cuts, -0.22, 0.18) * drawn
    return jnp.clip(drawn, min=-most, max=most).astype(kind)


def gaussian_with(own_key, shape, scale, reach, cuts, heavy, held_as=jnp.bfloat16):
    array = scale * jax.random.normal(own_key, shape, jnp.float32)
    if cuts:
        array = array * shard_levels(own_key, shape, cuts, -0.22, 0.18)
    return jnp.clip(strengthened(array, jax.random.fold_in(own_key, 3), *heavy), -reach, reach).astype(held_as)


def setup_inputs(seed: int = 0) -> dict:
    seeds = jax.random.split(jax.random.key(seed), 13)
    return {
        "inputs": bell_draw(seeds[0], (2, ROWS, LEN, D), 1.0, 6.0, ((0, 2), (1, 16))),
        "lengths": draw_lengths(jax.random.fold_in(seeds[12], 71), 0),
        "cotangent": gaussian_with(seeds[2], (ROWS, LEN, D), 1.0, 6.0, ((0, 16),), (0, 2, 16, 2.0)),
        "matrices": draw_matrices(jax.random.fold_in(seeds[12], 71), 0),
        "vectors": draw_vectors(jax.random.fold_in(seeds[12], 71), 0),
        "master_matrices": bell_draw(seeds[5], (2, PROWS, D), 0.001, 0.005859375, ((0, 2), (1, 16)), jnp.float32),
        "master_vectors": bell_draw(seeds[6], (2, VEC), 0.001, 0.005859375, ((0, 2), (1, 16)), jnp.float32),
        "matrix_mean": bell_draw(seeds[7], (2, PROWS, D), 20.0, 128.0, ((0, 2), (1, 16)), jnp.float32),
        "matrix_square": jnp.clip(jnp.exp(math.log(200.0) - 4.6051702 * jax.random.uniform(seeds[8], (2, PROWS, D), jnp.float32) ** shard_levels(seeds[8], (2, PROWS, D), ((0, 2), (1, 16)), -0.2, 0.2)), 2.0, 200.0),
        "vector_mean": bell_draw(seeds[9], (2, VEC), 20.0, 128.0, ((0, 2), (1, 16)), jnp.float32),
        "vector_square": jnp.clip(jnp.exp(math.log(200.0) - 4.6051702 * jax.random.uniform(seeds[10], (2, VEC), jnp.float32) ** shard_levels(seeds[10], (2, VEC), ((0, 2), (1, 16)), -0.2, 0.2)), 2.0, 200.0),
        "adam_step": jax.random.randint(seeds[11], (1,), 3000, 5001).astype(jnp.int32),
    }


@jax.custom_vjp
def low(v):
    return lax.optimization_barrier(v.astype(jnp.bfloat16)).astype(jnp.float32)

@jax.custom_vjp
def low_back(v):
    return v

def low_keep(v):
    return (low(v), None)

def low_pass(kept, grad):
    return (grad,)

def back_keep(v):
    return (v, None)

def back_low(kept, grad):
    return (low(grad),)
low.defvjp(low_keep, low_pass)
low_back.defvjp(back_keep, back_low)
MASK_FILL = -1e+30
NORM_EPS = 1e-05
ADAM_EPS = 1e-09
WARMUP_STEPS = 4000.0
HIGH = lax.Precision.HIGHEST

def rounded_both(values):
    return low(low_back(values))

def linear(first_op, second_op):
    return jnp.dot(first_op, second_op, precision=HIGH)

def norm_rows(hidden, norm_gain, norm_shift):
    centre = hidden - lax.optimization_barrier(jnp.mean(hidden, axis=-1, keepdims=True))
    spread = lax.optimization_barrier(jnp.mean(centre * centre, axis=-1, keepdims=True))
    return centre * lax.rsqrt(spread + NORM_EPS) * norm_gain + norm_shift

def segment_ids(sent_lens, seq_len):
    sent_ends = jnp.cumsum(sent_lens, axis=-1)
    position = jnp.arange(seq_len, dtype=jnp.int32)
    return lax.optimization_barrier(jnp.sum((position[None, :, None] >= sent_ends[:, None, :]).astype(jnp.int32), axis=-1))

def mask_of(query_ids, key_ids, pad_id, causal):
    same_sent = query_ids[:, :, None] == key_ids[:, None, :]
    if causal:
        position = jnp.arange(query_ids.shape[1], dtype=jnp.int32)
        same_sent = same_sent & (position[None, :, None] >= position[None, None, :])
    return same_sent | (query_ids == pad_id)[:, :, None]

def attend(queries, key_vecs, values, allowed):
    score_scale = queries.shape[-1] ** (-0.5)
    scores = low_back(jnp.einsum('rqhd,rkhd->rhqk', queries, key_vecs, precision=HIGH) * score_scale)
    scores = jnp.where(allowed[:, None], scores, MASK_FILL)
    attn_probs = low(jax.nn.softmax(scores, axis=-1))
    return jnp.einsum('rhqk,rkhd->rqhd', attn_probs, values, precision=HIGH)

def unpack(weights, small_vecs):
    model_width = weights.shape[1]
    ffn_width = (weights.shape[0] - 6 * model_width) // 2
    attn_in = weights[:3 * model_width].reshape(model_width, 3 * model_width)
    attn_out = weights[3 * model_width:4 * model_width]
    cross_w = weights[4 * model_width:6 * model_width].reshape(model_width, 2 * model_width)
    ffn_in = weights[6 * model_width:6 * model_width + ffn_width].reshape(model_width, ffn_width)
    ffn_out = weights[6 * model_width + ffn_width:]
    bias_in = small_vecs[:ffn_width]
    row_params = small_vecs[ffn_width:].reshape(7, model_width)
    return (attn_in, attn_out, cross_w, ffn_in, ffn_out, bias_in, row_params)

def self_branch(hidden, attn_in, attn_out, allowed, head_count):
    row_count, seq_len, model_width = hidden.shape
    packed = rounded_both(linear(hidden, attn_in)).reshape(row_count, seq_len, 3, head_count, model_width // head_count)
    mixed = attend(packed[:, :, 0], packed[:, :, 1], packed[:, :, 2], allowed)
    mixed = rounded_both(mixed.reshape(row_count, seq_len, model_width))
    return low_back(linear(mixed, attn_out))

def feed_forward(normed, ffn_in, bias_in, ffn_out, bias_out):
    pre_act = low_back(linear(low(normed), ffn_in) + bias_in)
    activated = low(jax.nn.gelu(pre_act, approximate=False))
    return low_back(linear(activated, ffn_out) + bias_out)

def encoder(source, params, src_ids, pad_id, head_count):
    attn_in, attn_out, cross_w, ffn_in, ffn_out, bias_in, row_params = params
    allowed = mask_of(src_ids, src_ids, pad_id, False)
    normed_one = norm_rows(source + self_branch(source, attn_in, attn_out, allowed, head_count), row_params[1], row_params[2])
    normed_two = norm_rows(normed_one + feed_forward(normed_one, ffn_in, bias_in, ffn_out, row_params[0]), row_params[3], row_params[4])
    memory = norm_rows(normed_two, row_params[5], row_params[6])
    return (memory, rounded_both(linear(low(memory), cross_w)))

def decoder(target, mem_pairs, params, tgt_ids, src_ids, pad_id, head_count):
    attn_in, attn_out, cross_w, ffn_in, ffn_out, bias_in, row_params = params
    row_count, seq_len, model_width = target.shape
    head_dim = model_width // head_count
    allowed = mask_of(tgt_ids, tgt_ids, pad_id, True)
    cross_allowed = mask_of(tgt_ids, src_ids, pad_id, False)
    normed_one = norm_rows(target + self_branch(target, attn_in, attn_out, allowed, head_count), row_params[1], row_params[2])
    queries = rounded_both(linear(low(normed_one), cross_w[:, :model_width])).reshape(row_count, seq_len, head_count, head_dim)
    memory_heads = mem_pairs.reshape(row_count, seq_len, 2, head_count, head_dim)
    mixed = attend(queries, memory_heads[:, :, 0], memory_heads[:, :, 1], cross_allowed)
    mixed = rounded_both(mixed.reshape(row_count, seq_len, model_width))
    normed_two = norm_rows(normed_one + low_back(linear(mixed, cross_w[:, model_width:])), row_params[3], row_params[4])
    return norm_rows(normed_two + feed_forward(normed_two, ffn_in, bias_in, ffn_out, row_params[0]), row_params[5], row_params[6])

def adam_update(grad, master, mean_old, square_old, step_now):
    mean_new = 0.9 * mean_old + 0.1 * grad
    square_new = 0.98 * square_old + 0.02 * grad * grad
    rate = D ** (-0.5) * jnp.minimum(lax.rsqrt(step_now), step_now * WARMUP_STEPS ** (-1.5))
    fixed_mean = mean_new / (1.0 - jnp.power(0.9, step_now))
    fixed_square = square_new / (1.0 - jnp.power(0.98, step_now))
    change = -rate * fixed_mean / (jnp.sqrt(fixed_square) + ADAM_EPS)
    return (change, mean_new, square_new, master + change)

def reference(inputs, lengths, cotangent, matrices, vectors, master_matrices, master_vectors, matrix_mean, matrix_square, vector_mean, vector_square, adam_step):
    rows_dev = ROWS // N_DP
    pad_id = SENTS
    weights = matrices.astype(jnp.float32)
    small_vecs = vectors.astype(jnp.float32)
    acts = inputs.astype(jnp.float32)
    src_ids = segment_ids(lengths[0], LEN)
    tgt_ids = segment_ids(lengths[1], LEN)

    def pair_group(wts, vcs, source, target, group_src, group_tgt):
        memory, mem_pairs = encoder(source, unpack(wts[0], vcs[0]), group_src, pad_id, HEADS)
        top = decoder(target, mem_pairs, unpack(wts[1], vcs[1]), group_tgt, group_src, pad_id, HEADS)
        return (top, memory)
    group_fn = jax.checkpoint(pair_group)

    def whole(wts, vcs, all_acts):

        def scan_turn(carried, item_group):
            source, target, group_src, group_tgt = item_group
            return (carried, group_fn(wts, vcs, source, target, group_src, group_tgt))
        item_groups = (all_acts[0].reshape(N_DP, rows_dev, LEN, D), all_acts[1].reshape(N_DP, rows_dev, LEN, D), src_ids.reshape(N_DP, rows_dev, LEN), tgt_ids.reshape(N_DP, rows_dev, LEN))
        _, (tops, memories) = lax.scan(scan_turn, jnp.zeros((), jnp.float32), item_groups)
        return (tops.reshape(ROWS, LEN, D), memories.reshape(ROWS, LEN, D))
    top, pullback, memory = jax.vjp(whole, weights, small_vecs, acts, has_aux=True)
    valid = (tgt_ids < pad_id).astype(jnp.float32)
    grad_weights, grad_vecs, grad_acts = pullback(cotangent.astype(jnp.float32) * valid[:, :, None])
    step_now = adam_step[0].astype(jnp.float32)
    change_m, mean_m, square_m, master_m = adam_update(grad_weights, master_matrices, matrix_mean, matrix_square, step_now)
    change_v, mean_v, square_v, master_v = adam_update(grad_vecs, master_vectors, vector_mean, vector_square, step_now)
    layer_outputs = jnp.stack([memory.astype(jnp.bfloat16), top.astype(jnp.bfloat16)])
    return (layer_outputs, grad_acts, grad_weights, grad_vecs, change_m, change_v, mean_m, square_m, mean_v, square_v, master_m.astype(jnp.bfloat16), master_v.astype(jnp.bfloat16))
```

```python
import jax
import jax.numpy as jnp
from jax import lax
from jax.sharding import PartitionSpec as P

HEADS = 8
MICRO = 1


MASK_FILL = -1e30
NORM_EPS = 1e-05
ADAM_EPS = 1e-09
WARMUP_STEPS = 4000.0


def passed_along(array, axis, by):
    devices = lax.axis_size(axis)
    pairs = [(i, i + by) for i in range(devices) if 0 <= i + by < devices]
    return lax.ppermute(array, axis, pairs)


def layer_norm(hidden, norm_gain, norm_shift):
    centre = hidden - jnp.mean(hidden, axis=-1, keepdims=True)
    spread = jnp.mean(centre * centre, axis=-1, keepdims=True)
    return centre * lax.rsqrt(spread + NORM_EPS) * norm_gain + norm_shift


def smooth_act(values):
    return jax.nn.gelu(values, approximate=False)


def matmul(first_op, second_op):
    return jnp.dot(first_op, second_op, preferred_element_type=jnp.float32)


def matmul_tn(first_op, second_op):
    return lax.dot_general(
        first_op, second_op, (((0,), (0,)), ((), ())), preferred_element_type=jnp.float32
    )


def matmul_nt(first_op, second_op):
    return lax.dot_general(
        first_op, second_op, (((1,), (1,)), ((), ())), preferred_element_type=jnp.float32
    )


def segment_ids(sent_lens, seq_len):
    sent_ends = jnp.cumsum(sent_lens, axis=-1)
    position = jnp.arange(seq_len, dtype=jnp.int32)
    return jnp.sum((position[None, :, None] >= sent_ends[:, None, :]).astype(jnp.int32), axis=-1)


def mask_of(query_ids, key_ids, pad_id, causal):
    same_sent = query_ids[:, :, None] == key_ids[:, None, :]
    if causal:
        position = jnp.arange(query_ids.shape[1], dtype=jnp.int32)
        same_sent = same_sent & (position[None, :, None] >= position[None, None, :])
    return same_sent | (query_ids == pad_id)[:, :, None]


def attend_forward(queries, key_vecs, values, allowed):
    score_scale = queries.shape[-1] ** (-0.5)
    scores = (
        jnp.einsum("rqhd,rkhd->rhqk", queries, key_vecs, preferred_element_type=jnp.float32)
        * score_scale
    )
    scores = jnp.where(allowed[:, None], scores, MASK_FILL)
    row_max = jnp.max(scores, axis=-1, keepdims=True)
    exp_scores = jnp.exp(scores - row_max)
    row_total = jnp.sum(exp_scores, axis=-1, keepdims=True)
    attn_probs = (exp_scores / row_total).astype(jnp.bfloat16)
    result = jnp.einsum("rhqk,rkhd->rqhd", attn_probs, values, preferred_element_type=jnp.float32)
    return (result, row_max + jnp.log(row_total))


def attend_backward(queries, key_vecs, values, allowed, logsum, grad_out):
    score_scale = queries.shape[-1] ** (-0.5)
    scores = (
        jnp.einsum("rqhd,rkhd->rhqk", queries, key_vecs, preferred_element_type=jnp.float32)
        * score_scale
    )
    scores = jnp.where(allowed[:, None], scores, MASK_FILL)
    attn_probs = jnp.exp(scores - logsum)
    grad_values = jnp.einsum(
        "rhqk,rqhd->rkhd",
        attn_probs.astype(jnp.bfloat16),
        grad_out,
        preferred_element_type=jnp.float32,
    )
    grad_probs = jnp.einsum("rqhd,rkhd->rhqk", grad_out, values, preferred_element_type=jnp.float32)
    inner = jnp.sum(attn_probs * grad_probs, axis=-1, keepdims=True)
    grad_scores = (attn_probs * (grad_probs - inner)).astype(jnp.bfloat16)
    grad_queries = (
        jnp.einsum("rhqk,rkhd->rqhd", grad_scores, key_vecs, preferred_element_type=jnp.float32)
        * score_scale
    )
    grad_keys = (
        jnp.einsum("rhqk,rqhd->rkhd", grad_scores, queries, preferred_element_type=jnp.float32)
        * score_scale
    )
    return (grad_queries, grad_keys, grad_values)


def unpack(weights, small_vecs):
    model_width = weights.shape[1]
    ffn_width = (weights.shape[0] - 6 * model_width) // 2
    attn_in = weights[: 3 * model_width].reshape(model_width, 3 * model_width)
    attn_out = weights[3 * model_width : 4 * model_width]
    cross_w = weights[4 * model_width : 6 * model_width].reshape(model_width, 2 * model_width)
    ffn_in = weights[6 * model_width : 6 * model_width + ffn_width].reshape(model_width, ffn_width)
    ffn_out = weights[6 * model_width + ffn_width :]
    bias_in = small_vecs[:ffn_width]
    row_params = small_vecs[ffn_width:].reshape(7, model_width)
    return (attn_in, attn_out, cross_w, ffn_in, ffn_out, bias_in, row_params)


def pack_grads(mat_list, vec_list):
    model_width = mat_list[1].shape[0]
    grad_mat = jnp.concatenate(
        [
            mat_list[0].reshape(-1, model_width),
            mat_list[1],
            mat_list[2].reshape(-1, model_width),
            mat_list[3].reshape(-1, model_width),
            mat_list[4],
        ],
        axis=0,
    )
    return (grad_mat, jnp.concatenate(vec_list, axis=0))


def self_forward(source, attn_in, attn_out, allowed, head_count):
    row_count, seq_len, model_width = source.shape
    flat_low = source.reshape(row_count * seq_len, model_width)
    packed = (
        matmul(flat_low, attn_in)
        .astype(jnp.bfloat16)
        .reshape(row_count, seq_len, 3, head_count, model_width // head_count)
    )
    queries, key_vecs, values = (packed[:, :, 0], packed[:, :, 1], packed[:, :, 2])
    mixed, logsum = attend_forward(queries, key_vecs, values, allowed)
    mixed_low = mixed.astype(jnp.bfloat16).reshape(row_count * seq_len, model_width)
    return (matmul(mixed_low, attn_out), (queries, key_vecs, values, logsum, mixed_low))


def self_backward(source, attn_in, attn_out, allowed, kept_att, grad_branch):
    queries, key_vecs, values, logsum, mixed_low = kept_att
    row_count, seq_len, model_width = source.shape
    grad_low = grad_branch.astype(jnp.bfloat16)
    grad_attn_out = matmul_tn(mixed_low, grad_low)
    grad_mixed = matmul_nt(grad_low, attn_out).astype(jnp.bfloat16).reshape(queries.shape)
    grad_q, grad_k, grad_v = attend_backward(queries, key_vecs, values, allowed, logsum, grad_mixed)
    grad_packed = (
        jnp.stack([grad_q, grad_k, grad_v], axis=2)
        .reshape(row_count * seq_len, 3 * model_width)
        .astype(jnp.bfloat16)
    )
    flat_low = source.reshape(row_count * seq_len, model_width)
    return (matmul_tn(flat_low, grad_packed), grad_attn_out, matmul_nt(grad_packed, attn_in))


def ffn_forward(normed, ffn_in, bias_in, ffn_out, bias_out):
    normed_low = normed.astype(jnp.bfloat16)
    pre_act = matmul(normed_low, ffn_in) + bias_in
    activated, act_back = jax.vjp(smooth_act, pre_act)
    act_low = activated.astype(jnp.bfloat16)
    return (matmul(act_low, ffn_out) + bias_out, (normed_low, act_back, act_low))


def ffn_backward(ffn_in, ffn_out, kept_ffn, grad_branch):
    normed_low, act_back, act_low = kept_ffn
    grad_low = grad_branch.astype(jnp.bfloat16)
    grad_ffn_out = matmul_tn(act_low, grad_low)
    grad_bias_out = jnp.sum(grad_low.astype(jnp.float32), axis=0)
    grad_pre = act_back(matmul_nt(grad_low, ffn_out))[0].astype(jnp.bfloat16)
    grad_bias_in = jnp.sum(grad_pre.astype(jnp.float32), axis=0)
    return (
        matmul_tn(normed_low, grad_pre),
        grad_bias_in,
        grad_ffn_out,
        grad_bias_out,
        matmul_nt(grad_pre, ffn_in),
    )


def encoder_run(params, source, src_ids, pad_id, head_count, grad_pairs):
    attn_in, attn_out, cross_w, ffn_in, ffn_out, bias_in, row_params = params
    row_count, seq_len, model_width = source.shape
    allowed = mask_of(src_ids, src_ids, pad_id, False)
    branch, kept_att = self_forward(source, attn_in, attn_out, allowed, head_count)
    flat_in = source.reshape(row_count * seq_len, model_width).astype(jnp.float32)
    normed_one, back_one = jax.vjp(layer_norm, flat_in + branch, row_params[1], row_params[2])
    branch_two, kept_ffn = ffn_forward(normed_one, ffn_in, bias_in, ffn_out, row_params[0])
    normed_two, back_two = jax.vjp(
        layer_norm, normed_one + branch_two, row_params[3], row_params[4]
    )
    memory, back_three = jax.vjp(layer_norm, normed_two, row_params[5], row_params[6])
    memory_low = memory.astype(jnp.bfloat16)
    if grad_pairs is None:
        mem_pairs = matmul(memory_low, cross_w).astype(jnp.bfloat16)
        return (
            mem_pairs.reshape(row_count, seq_len, 2 * model_width),
            memory_low.reshape(row_count, seq_len, model_width),
        )
    grad_low = grad_pairs.reshape(row_count * seq_len, 2 * model_width)
    grad_cross = matmul_tn(memory_low, grad_low)
    grad_two, gain_three, shift_three = back_three(matmul_nt(grad_low, cross_w))
    grad_sum_two, gain_two, shift_two = back_two(grad_two)
    grad_ffn_in, grad_bias_in, grad_ffn_out, grad_bias_out, grad_normed = ffn_backward(
        ffn_in, ffn_out, kept_ffn, grad_sum_two
    )
    grad_sum_one, gain_one, shift_one = back_one(grad_sum_two + grad_normed)
    grad_attn_in, grad_attn_out, grad_source = self_backward(
        source, attn_in, attn_out, allowed, kept_att, grad_sum_one
    )
    packed_grads = pack_grads(
        [grad_attn_in, grad_attn_out, grad_cross, grad_ffn_in, grad_ffn_out],
        [
            grad_bias_in,
            grad_bias_out,
            gain_one,
            shift_one,
            gain_two,
            shift_two,
            gain_three,
            shift_three,
        ],
    )
    return (packed_grads, (grad_sum_one + grad_source).reshape(row_count, seq_len, model_width))


def decoder_run(params, target, tgt_ids, src_ids, pad_id, head_count, mem_pairs, grad_top):
    attn_in, attn_out, cross_w, ffn_in, ffn_out, bias_in, row_params = params
    row_count, seq_len, model_width = target.shape
    head_dim = model_width // head_count
    allowed = mask_of(tgt_ids, tgt_ids, pad_id, True)
    cross_allowed = mask_of(tgt_ids, src_ids, pad_id, False)
    branch, kept_att = self_forward(target, attn_in, attn_out, allowed, head_count)
    flat_in = target.reshape(row_count * seq_len, model_width).astype(jnp.float32)
    normed_one, back_one = jax.vjp(layer_norm, flat_in + branch, row_params[1], row_params[2])
    normed_low = normed_one.astype(jnp.bfloat16)
    cross_query, cross_out = (cross_w[:, :model_width], cross_w[:, model_width:])
    queries = (
        matmul(normed_low, cross_query)
        .astype(jnp.bfloat16)
        .reshape(row_count, seq_len, head_count, head_dim)
    )
    memory_heads = mem_pairs.reshape(row_count, seq_len, 2, head_count, head_dim)
    key_vecs, values = (memory_heads[:, :, 0], memory_heads[:, :, 1])
    mixed, logsum = attend_forward(queries, key_vecs, values, cross_allowed)
    mixed_low = mixed.astype(jnp.bfloat16).reshape(row_count * seq_len, model_width)
    normed_two, back_two = jax.vjp(
        layer_norm, normed_one + matmul(mixed_low, cross_out), row_params[3], row_params[4]
    )
    branch_three, kept_ffn = ffn_forward(normed_two, ffn_in, bias_in, ffn_out, row_params[0])
    result_top, back_three = jax.vjp(
        layer_norm, normed_two + branch_three, row_params[5], row_params[6]
    )
    grad_sum_three, gain_three, shift_three = back_three(
        grad_top.reshape(row_count * seq_len, model_width)
    )
    grad_ffn_in, grad_bias_in, grad_ffn_out, grad_bias_out, grad_normed = ffn_backward(
        ffn_in, ffn_out, kept_ffn, grad_sum_three
    )
    grad_sum_two, gain_two, shift_two = back_two(grad_sum_three + grad_normed)
    grad_mix_low = grad_sum_two.astype(jnp.bfloat16)
    grad_cross_out = matmul_tn(mixed_low, grad_mix_low)
    grad_mixed = matmul_nt(grad_mix_low, cross_out).astype(jnp.bfloat16).reshape(queries.shape)
    grad_q, grad_k, grad_v = attend_backward(
        queries, key_vecs, values, cross_allowed, logsum, grad_mixed
    )
    grad_pairs = (
        jnp.stack([grad_k, grad_v], axis=2)
        .reshape(row_count, seq_len, 2 * model_width)
        .astype(jnp.bfloat16)
    )
    grad_q_low = grad_q.reshape(row_count * seq_len, model_width).astype(jnp.bfloat16)
    grad_cross_query = matmul_tn(normed_low, grad_q_low)
    grad_sum_one, gain_one, shift_one = back_one(grad_sum_two + matmul_nt(grad_q_low, cross_query))
    grad_attn_in, grad_attn_out, grad_target = self_backward(
        target, attn_in, attn_out, allowed, kept_att, grad_sum_one
    )
    grad_cross = jnp.concatenate([grad_cross_query, grad_cross_out], axis=1)
    packed_grads = pack_grads(
        [grad_attn_in, grad_attn_out, grad_cross, grad_ffn_in, grad_ffn_out],
        [
            grad_bias_in,
            grad_bias_out,
            gain_one,
            shift_one,
            gain_two,
            shift_two,
            gain_three,
            shift_three,
        ],
    )
    result_low = result_top.astype(jnp.bfloat16).reshape(row_count, seq_len, model_width)
    grad_input = (grad_sum_one + grad_target).reshape(row_count, seq_len, model_width)
    return (result_low, packed_grads, grad_input, grad_pairs)


def adam_update(grad, master, mean_old, square_old, step_now, model_width):
    mean_new = 0.9 * mean_old + 0.1 * grad
    square_new = 0.98 * square_old + 0.02 * grad * grad
    rate = model_width ** (-0.5) * jnp.minimum(
        lax.rsqrt(step_now), step_now * WARMUP_STEPS ** (-1.5)
    )
    fixed_mean = mean_new / (1.0 - jnp.power(0.9, step_now))
    fixed_square = square_new / (1.0 - jnp.power(0.98, step_now))
    change = -rate * fixed_mean / (jnp.sqrt(fixed_square) + ADAM_EPS)
    return (change, mean_new, square_new, master + change)


def body(
    inputs,
    lengths,
    cotangent,
    matrices,
    vectors,
    master_matrices,
    master_vectors,
    matrix_mean,
    matrix_square,
    vector_mean,
    vector_square,
    adam_step,
):
    section_id = lax.axis_index("section")
    row_count, seq_len, model_width = (inputs.shape[1], inputs.shape[2], inputs.shape[3])
    rows_mb = row_count // MICRO
    pad_id = lengths.shape[2]
    head_count = HEADS
    src_ids = segment_ids(lengths[0], seq_len)
    tgt_ids = segment_ids(lengths[1], seq_len)
    params = unpack(matrices[0], vectors[0].astype(jnp.float32))
    local_in = inputs[0]
    grad_top_all = (
        cotangent.astype(jnp.float32) * (tgt_ids < pad_id).astype(jnp.float32)[:, :, None]
    )
    zero_pairs = jnp.zeros((rows_mb, seq_len, 2 * model_width), jnp.bfloat16)
    zero_mat = jnp.zeros(matrices.shape[1:], jnp.float32)
    zero_vec = jnp.zeros(vectors.shape[1:], jnp.float32)
    recv_fwd = zero_pairs
    recv_back = zero_pairs
    outs_buf = jnp.zeros(inputs.shape[1:], jnp.bfloat16)
    dins_buf = jnp.zeros(inputs.shape[1:], jnp.float32)
    total_mat, total_vec = (zero_mat, zero_vec)
    for step_index in range(MICRO + 2):

        def encoder_turn(carried, step_index=step_index):
            outs_now, dins_now, from_next = (carried[0], carried[1], carried[3])
            send_pairs, grad_mat, grad_vec = (zero_pairs, zero_mat, zero_vec)
            if step_index < MICRO:
                picked = slice(step_index * rows_mb, (step_index + 1) * rows_mb)
                send_pairs, memory_low = encoder_run(
                    params, local_in[picked], src_ids[picked], pad_id, head_count, None
                )
                outs_now = outs_now.at[picked].set(memory_low)
            if step_index >= 2:
                picked = slice((step_index - 2) * rows_mb, (step_index - 1) * rows_mb)
                (grad_mat, grad_vec), grad_input = encoder_run(
                    params, local_in[picked], src_ids[picked], pad_id, head_count, from_next
                )
                dins_now = dins_now.at[picked].set(grad_input)
            return (send_pairs, zero_pairs, grad_mat, grad_vec, outs_now, dins_now)

        def decoder_turn(carried, step_index=step_index):
            outs_now, dins_now, from_prev = (carried[0], carried[1], carried[2])
            grad_pairs, grad_mat, grad_vec = (zero_pairs, zero_mat, zero_vec)
            if 1 <= step_index <= MICRO:
                picked = slice((step_index - 1) * rows_mb, step_index * rows_mb)
                result_low, (grad_mat, grad_vec), grad_input, grad_pairs = decoder_run(
                    params,
                    local_in[picked],
                    tgt_ids[picked],
                    src_ids[picked],
                    pad_id,
                    head_count,
                    from_prev,
                    grad_top_all[picked],
                )
                outs_now = outs_now.at[picked].set(result_low)
                dins_now = dins_now.at[picked].set(grad_input)
            return (zero_pairs, grad_pairs, grad_mat, grad_vec, outs_now, dins_now)

        send_pairs, send_grads, grad_mat, grad_vec, outs_buf, dins_buf = lax.cond(
            section_id == 0, encoder_turn, decoder_turn, (outs_buf, dins_buf, recv_fwd, recv_back)
        )
        if step_index < MICRO:
            recv_fwd = passed_along(send_pairs, "section", 1)
        if 1 <= step_index <= MICRO:
            recv_back = passed_along(send_grads, "section", -1)
        total_mat = total_mat + grad_mat
        total_vec = total_vec + grad_vec
    ranks = lax.axis_size("dp")
    mat_share, vec_share = total_mat.shape[0] // ranks, total_vec.shape[0] // ranks
    vec_rows = 16 * (-(-vec_share // (16 * model_width)))
    vec_block = jnp.pad(
        total_vec.reshape(ranks, vec_share), ((0, 0), (0, vec_rows * model_width - vec_share))
    ).reshape(ranks, vec_rows, model_width)
    blocks = jnp.concatenate(
        [total_mat.reshape(ranks, mat_share, model_width), vec_block], axis=1
    ).astype(jnp.bfloat16)
    summed = lax.psum_scatter(
        blocks.reshape(-1, model_width), "dp", scatter_dimension=0, tiled=True
    ).astype(jnp.float32)
    shard_mat = summed[:mat_share]
    shard_vec = summed[mat_share:].reshape(-1)[:vec_share]
    step_now = adam_step[0].astype(jnp.float32)
    change_m, mean_m, square_m, master_m = adam_update(
        shard_mat, master_matrices[0], matrix_mean[0], matrix_square[0], step_now, model_width
    )
    change_v, mean_v, square_v, master_v = adam_update(
        shard_vec, master_vectors[0], vector_mean[0], vector_square[0], step_now, model_width
    )
    vec_tail = jnp.pad(master_v, (0, vec_rows * model_width - vec_share))
    low_block = jnp.concatenate(
        [master_m, vec_tail.reshape(vec_rows, model_width)], axis=0
    ).astype(jnp.bfloat16)
    gathered = lax.all_gather(low_block, "dp", axis=0, tiled=False)
    new_mat = gathered[:, :mat_share].reshape(1, -1, model_width)
    new_vec = gathered[:, mat_share:].reshape(ranks, -1)[:, :vec_share].reshape(1, -1)
    return (
        outs_buf[None],
        dins_buf[None],
        shard_mat[None],
        shard_vec[None],
        change_m[None],
        change_v[None],
        mean_m[None],
        square_m[None],
        mean_v[None],
        square_v[None],
        new_mat,
        new_vec,
    )


def solution(mesh):
    return jax.shard_map(
        body,
        mesh=mesh,
        in_specs=(
            P("section", "dp", None, None),
            P(None, "dp", None),
            P("dp", None, None),
            P("section", None, None),
            P("section", None),
            P("section", "dp", None),
            P("section", "dp"),
            P("section", "dp", None),
            P("section", "dp", None),
            P("section", "dp"),
            P("section", "dp"),
            P(),
        ),
        out_specs=(
            P("section", "dp", None, None),
            P("section", "dp", None, None),
            P("section", "dp", None),
            P("section", "dp"),
            P("section", "dp", None),
            P("section", "dp"),
            P("section", "dp", None),
            P("section", "dp", None),
            P("section", "dp"),
            P("section", "dp"),
            P("section", None, None),
            P("section", None),
        ),
        check_vma=False,
    )
```

```python
import functools

import jax
import jax.numpy as jnp
from jax import lax
from jax.experimental import pallas as pl
from jax.experimental.pallas import tpu as pltpu
from jax.sharding import PartitionSpec as P

HEADS = 8
HEAD_DIM = 64
PAIR = 2 * HEAD_DIM
LANES = 128

MASK_FILL = -1e30
NORM_EPS = 1e-05
ADAM_EPS = 1e-09
WARMUP_STEPS = 4000.0
VMEM_BYTES = 56 * 1024 * 1024

F32 = jnp.float32
BF16 = jnp.bfloat16

BIAS_OUT, GAIN1, SHIFT1, GAIN2, SHIFT2, GAIN3, SHIFT3 = range(4, 11)


def dot(left, right):
    return jnp.dot(left, right, preferred_element_type=F32)


def dot_nt(left, right):
    return lax.dot_general(left, right, (((1,), (1,)), ((), ())), preferred_element_type=F32)


def dot_tn(left, right):
    return lax.dot_general(left, right, (((0,), (0,)), ((), ())), preferred_element_type=F32)


def norm_parts(hidden):
    centre = hidden - jnp.mean(hidden, axis=-1, keepdims=True)
    rstd = lax.rsqrt(jnp.mean(centre * centre, axis=-1, keepdims=True) + NORM_EPS)
    return centre * rstd, rstd


def norm_forward(hidden, gain, shift):
    return norm_parts(hidden)[0] * gain + shift


def norm_backward(hidden, gain, grad):
    normal, rstd = norm_parts(hidden)
    scaled = grad * gain
    inner = jnp.mean(scaled * normal, axis=-1, keepdims=True)
    grad_in = rstd * (scaled - jnp.mean(scaled, axis=-1, keepdims=True) - normal * inner)
    grad_gain = jnp.sum(grad * normal, axis=0, keepdims=True)
    grad_shift = jnp.sum(grad, axis=0, keepdims=True)
    return grad_in, grad_gain, grad_shift


def act_parts(pre):
    cdf = 0.5 * (1.0 + lax.erf(pre * (0.5**0.5)))
    pdf = jnp.exp(-0.5 * pre * pre) * 0.3989422804014327
    return pre * cdf, cdf + pre * pdf


def split_rows(raw, wide, parts, out, base):
    width = raw.shape[1]
    for c in range(width // LANES):
        cut = slice(c * LANES, (c + 1) * LANES)
        wide[c, : parts * width] = raw[: parts * width, cut].astype(F32)
        for j in range(parts):
            out[(base + j) * width : (base + j + 1) * width, cut] = wide[
                c, pl.ds(j, width, stride=parts), :
            ].astype(BF16)


def put_part(wide, j, parts, values):
    rows, width = values.shape
    for c in range(width // LANES):
        wide[c, pl.ds(j, rows, stride=parts), :] = values[:, c * LANES : (c + 1) * LANES]


def take_parts(wide, rows, out, base):
    for c in range(wide.shape[0]):
        out[base : base + rows, c * LANES : (c + 1) * LANES] = wide[c, :rows].astype(BF16)


def sentence_ends(lens, side, row, row_count, sents):
    ends, total = [], 0
    for j in range(sents):
        total = total + lens[(side * row_count + row) * sents + j]
        ends.append(total)
    return ends


def sentence_of(ends, position):
    found = jnp.zeros(position.shape, jnp.int32)
    for end in ends:
        found = found + (position >= end).astype(jnp.int32)
    return found


def fill_mask(mask, lens, query_side, key_side, row_count, sents, causal):
    seq_len = mask.shape[1]
    q_pos = lax.broadcasted_iota(jnp.int32, (seq_len, seq_len), 0)
    k_pos = lax.broadcasted_iota(jnp.int32, (seq_len, seq_len), 1)
    for r in range(row_count):
        q_ids = sentence_of(sentence_ends(lens, query_side, r, row_count, sents), q_pos)
        k_ids = sentence_of(sentence_ends(lens, key_side, r, row_count, sents), k_pos)
        same = jnp.where(q_ids == k_ids, 1, 0)
        if causal is not None:
            same = jnp.where(q_pos >= k_pos, same, jnp.where(causal, 0, same))
        allowed = jnp.where(q_ids == sents, 1, same)
        mask[r * seq_len : (r + 1) * seq_len] = allowed.astype(F32)


def both_heads(block, lane):
    even = (lane < HEAD_DIM).astype(BF16)
    return jnp.concatenate([block * even, block * (1 - even)], axis=0)


def one_of(stacked, lane):
    keys = stacked.shape[0] // 2
    return jnp.where(lane < HEAD_DIM, stacked[:keys], stacked[keys:])


def attend_forward(query, keys, values, mask, out, lse, row_count):
    seq_len = mask.shape[1]
    lane = lax.broadcasted_iota(jnp.int32, (1, PAIR), 1)
    (q_ref, q_at), (k_ref, k_at), (v_ref, v_at) = query, keys, values
    for r in range(row_count):
        rows = slice(r * seq_len, (r + 1) * seq_len)
        for p in range(HEADS // 2):
            q = q_ref[rows, q_at + p * PAIR : q_at + (p + 1) * PAIR]
            k2 = both_heads(k_ref[rows, k_at + p * PAIR : k_at + (p + 1) * PAIR], lane)
            v2 = both_heads(v_ref[rows, v_at + p * PAIR : v_at + (p + 1) * PAIR], lane)
            scores = dot_nt(q, k2) * HEAD_DIM ** (-0.5)
            probs = []
            for half in range(2):
                part = scores[:, half * seq_len : (half + 1) * seq_len]
                part = jnp.where(mask[rows] > 0.0, part, MASK_FILL)
                top = jnp.max(part, axis=-1, keepdims=True)
                raised = jnp.exp(part - top)
                total = jnp.sum(raised, axis=-1, keepdims=True)
                probs.append((raised * (1.0 / total)).astype(BF16))
                head = 2 * p + half
                lse[rows, head : head + 1] = top + jnp.log(total)
            mixed = dot(jnp.concatenate(probs, axis=1), v2)
            out[rows, p * PAIR : (p + 1) * PAIR] = mixed.astype(BF16)


def attend_backward(query, keys, values, mask, lse, grad_out, grad_q, grad_k, grad_v, row_count):
    seq_len = mask.shape[1]
    lane = lax.broadcasted_iota(jnp.int32, (1, PAIR), 1)
    scale = HEAD_DIM ** (-0.5)

    def lanes(pair, p):
        ref, at = pair
        return ref, slice(at + p * PAIR, at + (p + 1) * PAIR)

    for r in range(row_count):
        rows = slice(r * seq_len, (r + 1) * seq_len)
        for p in range(HEADS // 2):
            q_ref, q_l = lanes(query, p)
            k_ref, k_l = lanes(keys, p)
            v_ref, v_l = lanes(values, p)
            q = q_ref[rows, q_l]
            k2 = both_heads(k_ref[rows, k_l], lane)
            v2 = both_heads(v_ref[rows, v_l], lane)
            go = grad_out[rows, p * PAIR : (p + 1) * PAIR]
            scores = dot_nt(q, k2) * scale
            grad_probs = dot_nt(go, v2)
            probs, grad_scores = [], []
            for half in range(2):
                cut = slice(half * seq_len, (half + 1) * seq_len)
                head = 2 * p + half
                part = jnp.where(mask[rows] > 0.0, scores[:, cut], MASK_FILL)
                prob = jnp.exp(part - lse[rows, head : head + 1])
                gp = grad_probs[:, cut]
                inner = jnp.sum(prob * gp, axis=-1, keepdims=True)
                probs.append(prob.astype(BF16))
                grad_scores.append((prob * (gp - inner)).astype(BF16))
            probs = jnp.concatenate(probs, axis=1)
            grad_scores = jnp.concatenate(grad_scores, axis=1)
            ref, l = lanes(grad_v, p)
            ref[rows, l] = one_of(dot_tn(probs, go), lane).astype(BF16)
            ref, l = lanes(grad_q, p)
            ref[rows, l] = (dot(grad_scores, k2) * scale).astype(BF16)
            ref, l = lanes(grad_k, p)
            ref[rows, l] = (one_of(dot_tn(grad_scores, q), lane) * scale).astype(BF16)


def self_forward_kernel(
    info, lens, x, mats, vecs, qkv, lse, mixed, pre1, h1, qc, w_attn, w_cross,
    raw, wide, w_out, mask, sems, *, row_count, sents,
):
    width = x.shape[1]
    sec = info[0]
    get_in = pltpu.make_async_copy(mats.at[: 3 * width], raw.at[: 3 * width], sems.at[0])
    get_out = pltpu.make_async_copy(mats.at[3 * width : 4 * width], w_out, sems.at[1])
    get_cross = pltpu.make_async_copy(
        mats.at[4 * width : 6 * width], raw.at[3 * width : 5 * width], sems.at[2]
    )
    get_in.start()
    get_out.start()
    get_cross.start()
    fill_mask(mask, lens, sec, sec, row_count, sents, sec == 1)
    get_in.wait()
    split_rows(raw, wide, 3, w_attn, 0)
    for j in range(3):
        part = dot(x[...], w_attn[j * width : (j + 1) * width])
        qkv[:, j * width : (j + 1) * width] = part.astype(BF16)
    attend_forward((qkv, 0), (qkv, width), (qkv, 2 * width), mask, mixed, lse, row_count)
    get_out.wait()
    get_cross.wait()
    hidden = x[...].astype(F32) + dot(mixed[...], w_out[...])
    pre1[...] = hidden
    normed = norm_forward(hidden, vecs[GAIN1 : GAIN1 + 1], vecs[SHIFT1 : SHIFT1 + 1])
    h1[...] = normed

    @pl.when(sec == 1)
    def _():
        split_rows(raw.at[3 * width : 5 * width], wide, 2, w_cross, 0)
        qc[...] = dot(normed.astype(BF16), w_cross[:width]).astype(BF16)


def ffn_forward(normed, w_in, w_out, vecs, act, slope, chunks):
    width = normed.shape[1]
    low = normed.astype(BF16)
    total = None
    for j in range(chunks):
        cut = slice(j * width, (j + 1) * width)
        pre = dot(low, w_in[cut]) + vecs[j : j + 1]
        value, derivative = act_parts(pre)
        value = value.astype(BF16)
        act[:, cut] = value
        slope[:, cut] = derivative.astype(slope.dtype)
        term = dot(value, w_out[cut])
        total = term if total is None else total + term
    return total + vecs[BIAS_OUT : BIAS_OUT + 1]


def memory_kernel(
    info, h1, mats, vecs, cross_mine, cross_other, memory, act, slope, pre2, h2, w_in, w_pairs,
    raw, wide, w_out, sems,
):
    width = h1.shape[1]
    ffn = w_in.shape[0]
    sec, core = info[0], info[1]
    get_in = pltpu.make_async_copy(
        mats.at[6 * width : 6 * width + ffn], raw.at[:ffn], sems.at[0]
    )
    get_out = pltpu.make_async_copy(mats.at[6 * width + ffn :], w_out, sems.at[1])
    get_in.start()
    get_out.start()
    get_in.wait()
    split_rows(raw, wide, ffn // width, w_in, 0)
    get_out.wait()

    @pl.when(sec == 0)
    def _():
        normed = h1[...]
        hidden = normed + ffn_forward(normed, w_in, w_out, vecs, act, slope, ffn // width)
        pre2[...] = hidden
        second = norm_forward(hidden, vecs[GAIN2 : GAIN2 + 1], vecs[SHIFT2 : SHIFT2 + 1])
        h2[...] = second
        third = norm_forward(second, vecs[GAIN3 : GAIN3 + 1], vecs[SHIFT3 : SHIFT3 + 1])
        memory[...] = third.astype(BF16)

    @pl.when(sec == 1)
    def _():
        mine = pltpu.make_async_copy(
            cross_mine, raw.at[pl.ds(pl.multiple_of(core * width, width), width)], sems.at[2]
        )
        other = pltpu.make_async_copy(
            cross_other, raw.at[pl.ds(pl.multiple_of((1 - core) * width, width), width)], sems.at[3]
        )
        mine.start()
        other.start()
        mine.wait()
        other.wait()
        split_rows(raw, wide, 2, w_pairs, 0)


def decoder_kernel(
    info, lens, memory, w_pairs, w_cross, qc, h1, w_in, mats, vecs, cot,
    top, grad_memory, grad_pairs, act, grad_pre, grad_ffn, low2, mixed, grad_branch, grad_qc,
    grad_sum2, vec_grads,
    w_out, pairs, slope, lse, mask, grad_mixed, sems, *, row_count, sents,
):
    width = h1.shape[1]
    ffn = w_in.shape[0]
    chunks = ffn // width
    seq_len = mask.shape[1]

    @pl.when(info[0] == 1)
    def _():
        get_out = pltpu.make_async_copy(mats.at[6 * width + ffn :], w_out, sems.at[0])
        get_out.start()
        fill_mask(mask, lens, 1, 0, row_count, sents, None)
        for j in range(2):
            part = dot(memory[...], w_pairs[j * width : (j + 1) * width])
            pairs[:, j * width : (j + 1) * width] = part.astype(BF16)
        attend_forward((qc, 0), (pairs, 0), (pairs, width), mask, mixed, lse, row_count)
        hidden2 = h1[...] + dot(mixed[...], w_cross[width:])
        gain2, shift2 = vecs[GAIN2 : GAIN2 + 1], vecs[SHIFT2 : SHIFT2 + 1]
        normed2 = norm_forward(hidden2, gain2, shift2)
        low2[...] = normed2.astype(BF16)
        get_out.wait()
        hidden3 = normed2 + ffn_forward(normed2, w_in, w_out, vecs, act, slope, chunks)
        gain3, shift3 = vecs[GAIN3 : GAIN3 + 1], vecs[SHIFT3 : SHIFT3 + 1]
        top[...] = norm_forward(hidden3, gain3, shift3).astype(BF16)
        grads = []
        position = lax.broadcasted_iota(jnp.int32, (seq_len, 1), 0)
        for r in range(row_count):
            used = sentence_ends(lens, 1, r, row_count, sents)[-1]
            block = cot[r * seq_len : (r + 1) * seq_len].astype(F32)
            grads.append(jnp.where(position < used, block, 0.0))
        grad_sum3, d_gain, d_shift = norm_backward(hidden3, gain3, jnp.concatenate(grads, axis=0))
        vec_grads[GAIN3 : GAIN3 + 1] = d_gain
        vec_grads[SHIFT3 : SHIFT3 + 1] = d_shift
        grad_low = grad_sum3.astype(BF16)
        grad_ffn[...] = grad_low
        vec_grads[BIAS_OUT : BIAS_OUT + 1] = jnp.sum(grad_low.astype(F32), axis=0, keepdims=True)
        total = grad_sum3
        for j in range(chunks):
            cut = slice(j * width, (j + 1) * width)
            grad = (dot_nt(grad_low, w_out[cut]) * slope[:, cut]).astype(BF16)
            grad_pre[:, cut] = grad
            vec_grads[j : j + 1] = jnp.sum(grad.astype(F32), axis=0, keepdims=True)
            total = total + dot_nt(grad, w_in[cut])
        grad_hidden2, d_gain, d_shift = norm_backward(hidden2, gain2, total)
        vec_grads[GAIN2 : GAIN2 + 1] = d_gain
        vec_grads[SHIFT2 : SHIFT2 + 1] = d_shift
        grad_sum2[...] = grad_hidden2
        low = grad_hidden2.astype(BF16)
        grad_branch[...] = low
        grad_mixed[...] = dot_nt(low, w_cross[width:]).astype(BF16)
        attend_backward(
            (qc, 0), (pairs, 0), (pairs, width), mask, lse, grad_mixed,
            (grad_qc, 0), (grad_pairs, 0), (grad_pairs, width), row_count,
        )
        back = dot_nt(grad_pairs[:, :width], w_pairs[:width])
        back = back + dot_nt(grad_pairs[:, width:], w_pairs[width:])
        grad_memory[...] = back.astype(BF16)


def ffn_grad_kernel(
    info, grad_memory, enc_act, enc_slope, pre2, h2, h1, w_in, mats, vecs,
    dec_act, dec_grad_pre, dec_grad_ffn, low2, w_cross, grad_qc, grad_sum2, dec_vec_grads,
    grad_h1, vec_grads, grads,
    act, slope, w_out, grad_pre, grad_ffn, low, wide, sems,
):
    width = h1.shape[1]
    ffn = w_in.shape[0]
    chunks = ffn // width

    @pl.when(info[0] == 0)
    def _():
        get_out = pltpu.make_async_copy(mats.at[6 * width + ffn :], w_out, sems.at[0])
        get_act = pltpu.make_async_copy(enc_act, act, sems.at[1])
        get_slope = pltpu.make_async_copy(enc_slope, slope, sems.at[2])
        get_out.start()
        get_slope.start()
        get_act.start()
        low[...] = h1[...].astype(BF16)
        grad, d_gain, d_shift = norm_backward(
            h2[...], vecs[GAIN3 : GAIN3 + 1], grad_memory[...].astype(F32)
        )
        vec_grads[GAIN3 : GAIN3 + 1] = d_gain
        vec_grads[SHIFT3 : SHIFT3 + 1] = d_shift
        total, d_gain, d_shift = norm_backward(pre2[...], vecs[GAIN2 : GAIN2 + 1], grad)
        vec_grads[GAIN2 : GAIN2 + 1] = d_gain
        vec_grads[SHIFT2 : SHIFT2 + 1] = d_shift
        grad_low = total.astype(BF16)
        grad_ffn[...] = grad_low
        vec_grads[BIAS_OUT : BIAS_OUT + 1] = jnp.sum(grad_low.astype(F32), axis=0, keepdims=True)
        get_out.wait()
        get_slope.wait()
        for j in range(chunks):
            cut = slice(j * width, (j + 1) * width)
            grad = (dot_nt(grad_low, w_out[cut]) * slope[:, cut].astype(F32)).astype(BF16)
            grad_pre[:, cut] = grad
            vec_grads[j : j + 1] = jnp.sum(grad.astype(F32), axis=0, keepdims=True)
            total = total + dot_nt(grad, w_in[cut])
        grad_h1[...] = total
        get_act.wait()

    @pl.when(info[0] == 1)
    def _():
        copies = [
            pltpu.make_async_copy(dec_act, act, sems.at[0]),
            pltpu.make_async_copy(dec_grad_pre, grad_pre, sems.at[1]),
            pltpu.make_async_copy(dec_grad_ffn, grad_ffn, sems.at[2]),
            pltpu.make_async_copy(low2, low, sems.at[3]),
        ]
        for copy in copies:
            copy.start()
        vec_grads[...] = dec_vec_grads[...]
        grad_h1[...] = grad_sum2[...] + dot_nt(grad_qc[...], w_cross[:width])
        for copy in copies:
            copy.wait()

    for j in range(chunks):
        cut = slice(j * width, (j + 1) * width)
        grads[ffn + j * width : ffn + (j + 1) * width] = dot_tn(act[:, cut], grad_ffn[...]).astype(
            BF16
        )
        put_part(wide, j, chunks, dot_tn(low[...], grad_pre[:, cut]))
    take_parts(wide, ffn, grads, 0)


def self_grad_kernel(
    info, lens, grad_h1, pre1, qkv, lse, mixed, x, w_attn, mats, vecs, vec_in,
    memory, grad_pairs, h1, grad_qc, cross_mixed, grad_branch,
    grad_x, vec_grads, grads,
    w_out, mask, grad_mixed, grad_qkv, wide, sems, *, row_count, sents,
):
    width = x.shape[1]
    sec = info[0]
    get_out = pltpu.make_async_copy(mats.at[3 * width : 4 * width], w_out, sems.at[0])
    get_out.start()
    fill_mask(mask, lens, sec, sec, row_count, sents, sec == 1)
    grad, d_gain, d_shift = norm_backward(pre1[...], vecs[GAIN1 : GAIN1 + 1], grad_h1[...])
    vec_grads[...] = vec_in[...]
    vec_grads[GAIN1 : GAIN1 + 1] = d_gain
    vec_grads[SHIFT1 : SHIFT1 + 1] = d_shift
    low = grad.astype(BF16)
    get_out.wait()
    grad_mixed[...] = dot_nt(low, w_out[...]).astype(BF16)
    grads[3 * width : 4 * width] = dot_tn(mixed[...], low).astype(BF16)
    attend_backward(
        (qkv, 0), (qkv, width), (qkv, 2 * width), mask, lse, grad_mixed,
        (grad_qkv, 0), (grad_qkv, width), (grad_qkv, 2 * width), row_count,
    )
    for j in range(3):
        cut = slice(j * width, (j + 1) * width)
        grad = grad + dot_nt(grad_qkv[:, cut], w_attn[cut])
        put_part(wide, j, 3, dot_tn(x[...], grad_qkv[:, cut]))
    grad_x[...] = grad
    take_parts(wide, 3 * width, grads, 0)

    @pl.when(sec == 0)
    def _():
        for j in range(2):
            cut = slice(j * width, (j + 1) * width)
            put_part(wide, j, 2, dot_tn(memory[...], grad_pairs[:, cut]))

    @pl.when(sec == 1)
    def _():
        put_part(wide, 0, 2, dot_tn(h1[...].astype(BF16), grad_qc[...]))
        put_part(wide, 1, 2, dot_tn(cross_mixed[...], grad_branch[...]))

    take_parts(wide, 2 * width, grads, 4 * width)


SMEM = pl.BlockSpec(memory_space=pltpu.SMEM)
VMEM = pl.BlockSpec(memory_space=pltpu.VMEM)
ANY = pl.BlockSpec(memory_space=pl.ANY)


def run_kernel(kernel, name, args, places, outs, scratch, flops):
    return pl.pallas_call(
        kernel,
        name=name,
        in_specs=places,
        out_specs=[VMEM] * len(outs),
        out_shape=[jax.ShapeDtypeStruct(shape, dtype) for shape, dtype in outs],
        scratch_shapes=scratch,
        compiler_params=pltpu.CompilerParams(vmem_limit_bytes=VMEM_BYTES),
        cost_estimate=pl.CostEstimate(
            flops=flops, bytes_accessed=8 * 1024 * 1024, transcendentals=0
        ),
    )(*args)


def adam_update(grad, master, mean_old, square_old, step_now, model_width):
    mean_new = 0.9 * mean_old + 0.1 * grad
    square_new = 0.98 * square_old + 0.02 * grad * grad
    rate = model_width ** (-0.5) * jnp.minimum(
        lax.rsqrt(step_now), step_now * WARMUP_STEPS ** (-1.5)
    )
    fixed_mean = mean_new / (1.0 - jnp.power(0.9, step_now))
    fixed_square = square_new / (1.0 - jnp.power(0.98, step_now))
    change = -rate * fixed_mean / (jnp.sqrt(fixed_square) + ADAM_EPS)
    return (change, mean_new, square_new, master + change)


def swapped(array, axis, bit):
    devices = lax.axis_size(axis)
    return lax.ppermute(array, axis, [(i, i ^ bit) for i in range(devices)])


def body(
    inputs,
    lengths,
    cotangent,
    matrices,
    vectors,
    master_matrices,
    master_vectors,
    matrix_mean,
    matrix_square,
    vector_mean,
    vector_square,
    adam_step,
):
    row_count, seq_len, width = inputs.shape[1:]
    sents = lengths.shape[2]
    tokens = row_count * seq_len
    rows_all = matrices.shape[1]
    ffn = (rows_all - 6 * width) // 2
    core = lax.axis_index("dp") % 2
    info = jnp.stack([lax.axis_index("section"), core]).astype(jnp.int32)
    lens = lengths.reshape(-1)
    x = inputs.reshape(tokens, width)
    cot = cotangent.reshape(tokens, width)
    mats = matrices.reshape(rows_all, width)
    vecs = vectors.reshape(-1, width).astype(F32)
    vec_rows = vecs.shape[0]
    sizes = {"row_count": row_count, "sents": sents}
    mask_scratch = pltpu.VMEM((tokens, seq_len), F32)

    cross_half = lax.dynamic_slice(mats, (4 * width + core * width, 0), (width, width))
    cross_mine = swapped(cross_half, "section", 1)

    full, low, one = ((tokens, width), F32), ((tokens, width), BF16), (width, width)
    qkv, lse, mixed, pre1, h1, qc, w_attn, w_cross = run_kernel(
        functools.partial(self_forward_kernel, **sizes),
        "self_forward",
        (info, lens, x, mats, vecs),
        [SMEM, SMEM, VMEM, ANY, VMEM],
        [
            ((tokens, 3 * width), BF16),
            ((tokens, 128), F32),
            low,
            full,
            full,
            low,
            ((3 * width, width), BF16),
            ((2 * width, width), BF16),
        ],
        [
            pltpu.VMEM((5 * width, width), BF16),
            pltpu.VMEM((width // LANES, 3 * width, LANES), F32),
            pltpu.VMEM(one, BF16),
            mask_scratch,
            pltpu.SemaphoreType.DMA((3,)),
        ],
        4 * 10**9,
    )
    cross_other = swapped(cross_mine, "dp", 1)
    memory, enc_act, enc_slope, pre2, h2, w_in, w_pairs = run_kernel(
        memory_kernel,
        "memory",
        (info, h1, mats, vecs, cross_mine, cross_other),
        [SMEM, VMEM, ANY, VMEM, ANY, ANY],
        [
            low,
            ((tokens, ffn), BF16),
            ((tokens, ffn), BF16),
            full,
            full,
            ((ffn, width), BF16),
            ((2 * width, width), BF16),
        ],
        [
            pltpu.VMEM((ffn, width), BF16),
            pltpu.VMEM((width // LANES, ffn, LANES), F32),
            pltpu.VMEM((ffn, width), BF16),
            pltpu.SemaphoreType.DMA((4,)),
        ],
        4 * 10**9,
    )
    memory_far = swapped(memory, "section", 1)
    (
        top, grad_memory, grad_pairs, dec_act, dec_grad_pre, dec_grad_ffn, low2, cross_mixed,
        grad_branch, grad_qc, grad_sum2, dec_vec_grads,
    ) = run_kernel(
        functools.partial(decoder_kernel, **sizes),
        "decoder",
        (info, lens, memory_far, w_pairs, w_cross, qc, h1, w_in, mats, vecs, cot),
        [SMEM, SMEM, VMEM, VMEM, VMEM, VMEM, VMEM, VMEM, ANY, VMEM, VMEM],
        [
            low, low, ((tokens, 2 * width), BF16), ((tokens, ffn), BF16), ((tokens, ffn), BF16),
            low, low, low, low, low, full, ((vec_rows, width), F32),
        ],
        [
            pltpu.VMEM((ffn, width), BF16),
            pltpu.VMEM((tokens, 2 * width), BF16),
            pltpu.VMEM((tokens, ffn), F32),
            pltpu.VMEM((tokens, 128), F32),
            mask_scratch,
            pltpu.VMEM((tokens, width), BF16),
            pltpu.SemaphoreType.DMA((1,)),
        ],
        8 * 10**9,
    )
    grad_memory_far = swapped(grad_memory, "section", 1)
    grad_pairs_far = swapped(grad_pairs, "section", 1)
    grad_h1, vec_part, grads_ffn = run_kernel(
        ffn_grad_kernel,
        "ffn_grad",
        (
            info, grad_memory_far, enc_act, enc_slope, pre2, h2, h1, w_in, mats, vecs,
            dec_act, dec_grad_pre, dec_grad_ffn, low2, w_cross, grad_qc, grad_sum2, dec_vec_grads,
        ),
        [SMEM, VMEM, ANY, ANY, VMEM, VMEM, VMEM, VMEM, ANY, VMEM]
        + [ANY, ANY, ANY, ANY, VMEM, VMEM, VMEM, VMEM],
        [full, ((vec_rows, width), F32), ((2 * ffn, width), BF16)],
        [
            pltpu.VMEM((tokens, ffn), BF16),
            pltpu.VMEM((tokens, ffn), BF16),
            pltpu.VMEM((ffn, width), BF16),
            pltpu.VMEM((tokens, ffn), BF16),
            pltpu.VMEM((tokens, width), BF16),
            pltpu.VMEM((tokens, width), BF16),
            pltpu.VMEM((width // LANES, ffn, LANES), F32),
            pltpu.SemaphoreType.DMA((4,)),
        ],
        8 * 10**9,
    )
    grad_x, vec_grads, grads_attn = run_kernel(
        functools.partial(self_grad_kernel, **sizes),
        "self_grad",
        (
            info, lens, grad_h1, pre1, qkv, lse, mixed, x, w_attn, mats, vecs, vec_part,
            memory, grad_pairs_far, h1, grad_qc, cross_mixed, grad_branch,
        ),
        [SMEM, SMEM] + [VMEM] * 7 + [ANY] + [VMEM] * 8,
        [full, ((vec_rows, width), F32), ((6 * width, width), BF16)],
        [
            pltpu.VMEM(one, BF16),
            mask_scratch,
            pltpu.VMEM((tokens, width), BF16),
            pltpu.VMEM((tokens, 3 * width), BF16),
            pltpu.VMEM((width // LANES, 3 * width, LANES), F32),
            pltpu.SemaphoreType.DMA((1,)),
        ],
        8 * 10**9,
    )

    ranks = lax.axis_size("dp")
    mat_share, vec_share = rows_all // ranks, vectors.shape[1] // ranks
    tail_rows = 16 * (-(-vec_share // (16 * width)))
    tail = jnp.pad(
        vec_grads.astype(BF16).reshape(ranks, vec_share),
        ((0, 0), (0, tail_rows * width - vec_share)),
    ).reshape(ranks, tail_rows, width)
    blocks = jnp.concatenate(
        [jnp.concatenate([grads_attn, grads_ffn], axis=0).reshape(ranks, mat_share, width), tail],
        axis=1,
    )
    summed = lax.psum_scatter(
        blocks.reshape(-1, width), "dp", scatter_dimension=0, tiled=True
    ).astype(F32)
    shard_mat = summed[:mat_share]
    shard_vec = summed[mat_share:].reshape(-1)[:vec_share]
    step_now = adam_step[0].astype(F32)
    change_m, mean_m, square_m, master_m = adam_update(
        shard_mat, master_matrices[0], matrix_mean[0], matrix_square[0], step_now, width
    )
    change_v, mean_v, square_v, master_v = adam_update(
        shard_vec, master_vectors[0], vector_mean[0], vector_square[0], step_now, width
    )
    vec_tail = jnp.pad(master_v, (0, tail_rows * width - vec_share))
    low_block = jnp.concatenate(
        [master_m, vec_tail.reshape(tail_rows, width)], axis=0
    ).astype(BF16)
    gathered = lax.all_gather(low_block, "dp", axis=0, tiled=False)
    new_mat = gathered[:, :mat_share].reshape(1, -1, width)
    new_vec = gathered[:, mat_share:].reshape(ranks, -1)[:, :vec_share].reshape(1, -1)
    outs = jnp.where(info[0] == 0, memory, top)
    return (
        outs.reshape(1, row_count, seq_len, width),
        grad_x.reshape(1, row_count, seq_len, width),
        shard_mat[None],
        shard_vec[None],
        change_m[None],
        change_v[None],
        mean_m[None],
        square_m[None],
        mean_v[None],
        square_v[None],
        new_mat,
        new_vec,
    )


def solution(mesh):
    return jax.shard_map(
        body,
        mesh=mesh,
        in_specs=(
            P("section", "dp", None, None),
            P(None, "dp", None),
            P("dp", None, None),
            P("section", None, None),
            P("section", None),
            P("section", "dp", None),
            P("section", "dp"),
            P("section", "dp", None),
            P("section", "dp", None),
            P("section", "dp"),
            P("section", "dp"),
            P(),
        ),
        out_specs=(
            P("section", "dp", None, None),
            P("section", "dp", None, None),
            P("section", "dp", None),
            P("section", "dp"),
            P("section", "dp", None),
            P("section", "dp"),
            P("section", "dp", None),
            P("section", "dp", None),
            P("section", "dp"),
            P("section", "dp"),
            P("section", None, None),
            P("section", None),
        ),
        check_vma=False,
    )
```

```python
import math
import types

import jax
import jax.numpy as jnp
from jax import lax
from jax.experimental import pallas as pl
from jax.experimental.pallas import tpu as pltpu
from jax.sharding import PartitionSpec as P

HEADS = 8
HEAD_DIM = 64
PAIR = 2 * HEAD_DIM
LANES = 128
TAIL = 16

MASK_FILL = -1e30
NORM_EPS = 1e-05
ADAM_EPS = 1e-09
WARMUP_STEPS = 4000.0

F32 = jnp.float32
BF16 = jnp.bfloat16

BIAS_OUT, GAIN1, SHIFT1, GAIN2, SHIFT2, GAIN3, SHIFT3 = range(-7, 0)


def dot(left, right):
    return jnp.dot(left, right, preferred_element_type=F32)


def dot_nt(left, right):
    return lax.dot_general(left, right, (((1,), (1,)), ((), ())), preferred_element_type=F32)


def dot_tn(left, right):
    return lax.dot_general(left, right, (((0,), (0,)), ((), ())), preferred_element_type=F32)


def norm_parts(hidden):
    centre = hidden - jnp.mean(hidden, axis=-1, keepdims=True)
    rstd = lax.rsqrt(jnp.mean(centre * centre, axis=-1, keepdims=True) + NORM_EPS)
    return centre * rstd, rstd


def norm_forward(hidden, gain, shift):
    return norm_parts(hidden)[0] * gain + shift


def norm_backward(hidden, gain, grad):
    normal, rstd = norm_parts(hidden)
    scaled = grad * gain
    inner = jnp.mean(scaled * normal, axis=-1, keepdims=True)
    grad_in = rstd * (scaled - jnp.mean(scaled, axis=-1, keepdims=True) - normal * inner)
    grad_gain = jnp.sum(grad * normal, axis=0, keepdims=True)
    grad_shift = jnp.sum(grad, axis=0, keepdims=True)
    return grad_in, grad_gain, grad_shift


def act_parts(pre):
    cdf = 0.5 * (1.0 + lax.erf(pre * (0.5**0.5)))
    pdf = jnp.exp(-0.5 * pre * pre) * 0.3989422804014327
    return pre * cdf, cdf + pre * pdf


def split_rows(raw, wide, parts, out, base):
    width = raw.shape[1]
    for c in range(width // LANES):
        cut = slice(c * LANES, (c + 1) * LANES)
        wide[c, : parts * width] = raw[: parts * width, cut].astype(F32)
        for j in range(parts):
            out[(base + j) * width : (base + j + 1) * width, cut] = wide[
                c, pl.ds(j, width, stride=parts), :
            ].astype(BF16)


def put_part(wide, j, parts, values):
    rows, width = values.shape
    for c in range(width // LANES):
        wide[c, pl.ds(j, rows, stride=parts), :] = values[:, c * LANES : (c + 1) * LANES]


def block_cuts(out, first, rows, core):
    sides, _, share, _ = out.shape
    share -= TAIL if sides == 2 else 0
    at = first
    while at < first + rows:
        block, offset = divmod(at, share)
        count = min(share - offset, first + rows - at)
        side = 0 if sides == 1 else (core if block % 2 == 0 else 1 - core)
        yield side, block // sides, slice(offset, offset + count), slice(at - first, at - first + count)
        at += count


def put_rows(out, first, values, core):
    for side, block, there, here in block_cuts(out, first, values.shape[0], core):
        out[side, block, there] = values[here].astype(BF16)


def take_parts(wide, skip, rows, out, first, core):
    for side, block, there, here in block_cuts(out, first, rows, core):
        for c in range(wide.shape[0]):
            got = wide[c, skip + here.start : skip + here.stop]
            out[side, block, there, c * LANES : (c + 1) * LANES] = got.astype(BF16)


def sentence_ends(lens, side, row):
    ends, total = [], 0
    for j in range(lens.shape[2]):
        total = total + lens[side, row, j]
        ends.append(total)
    return ends


def sentence_of(ends, position):
    found = jnp.zeros(position.shape, jnp.int32)
    for end in ends:
        found = found + (position >= end).astype(jnp.int32)
    return found


def fill_mask(mask, lens, query_side, key_side, causal):
    seq_len = mask.shape[1]
    row_count, sents = lens.shape[1:]
    q_pos = lax.broadcasted_iota(jnp.int32, (seq_len, seq_len), 0)
    k_pos = lax.broadcasted_iota(jnp.int32, (seq_len, seq_len), 1)
    for r in range(row_count):
        q_ids = sentence_of(sentence_ends(lens, query_side, r), q_pos)
        k_ids = sentence_of(sentence_ends(lens, key_side, r), k_pos)
        same = jnp.where(q_ids == k_ids, 1, 0)
        if causal is not None:
            same = jnp.where(q_pos >= k_pos, same, jnp.where(causal, 0, same))
        allowed = jnp.where(q_ids == sents, 1, same)
        mask[r * seq_len : (r + 1) * seq_len] = allowed.astype(F32)


def both_heads(block, lane):
    even = (lane < HEAD_DIM).astype(BF16)
    return jnp.concatenate([block * even, block * (1 - even)], axis=0)


def one_of(stacked, lane):
    keys = stacked.shape[0] // 2
    return jnp.where(lane < HEAD_DIM, stacked[:keys], stacked[keys:])


def attend_forward(query, keys, values, mask, out, lse):
    seq_len = mask.shape[1]
    row_count = mask.shape[0] // seq_len
    lane = lax.broadcasted_iota(jnp.int32, (1, PAIR), 1)
    (q_ref, q_at), (k_ref, k_at), (v_ref, v_at) = query, keys, values
    for r in range(row_count):
        rows = slice(r * seq_len, (r + 1) * seq_len)
        for p in range(HEADS // 2):
            q = q_ref[rows, q_at + p * PAIR : q_at + (p + 1) * PAIR]
            k2 = both_heads(k_ref[rows, k_at + p * PAIR : k_at + (p + 1) * PAIR], lane)
            v2 = both_heads(v_ref[rows, v_at + p * PAIR : v_at + (p + 1) * PAIR], lane)
            scores = dot_nt(q, k2) * HEAD_DIM ** (-0.5)
            probs = []
            for half in range(2):
                part = scores[:, half * seq_len : (half + 1) * seq_len]
                part = jnp.where(mask[rows] > 0.0, part, MASK_FILL)
                top = jnp.max(part, axis=-1, keepdims=True)
                raised = jnp.exp(part - top)
                total = jnp.sum(raised, axis=-1, keepdims=True)
                probs.append((raised * (1.0 / total)).astype(BF16))
                head = 2 * p + half
                lse[rows, head : head + 1] = top + jnp.log(total)
            mixed = dot(jnp.concatenate(probs, axis=1), v2)
            out[rows, p * PAIR : (p + 1) * PAIR] = mixed.astype(BF16)


def attend_backward(query, keys, values, mask, lse, grad_out, grad_q, grad_k, grad_v):
    seq_len = mask.shape[1]
    row_count = mask.shape[0] // seq_len
    lane = lax.broadcasted_iota(jnp.int32, (1, PAIR), 1)
    scale = HEAD_DIM ** (-0.5)

    def lanes(pair, p):
        ref, at = pair
        return ref, slice(at + p * PAIR, at + (p + 1) * PAIR)

    for r in range(row_count):
        rows = slice(r * seq_len, (r + 1) * seq_len)
        for p in range(HEADS // 2):
            q_ref, q_l = lanes(query, p)
            k_ref, k_l = lanes(keys, p)
            v_ref, v_l = lanes(values, p)
            q = q_ref[rows, q_l]
            k2 = both_heads(k_ref[rows, k_l], lane)
            v2 = both_heads(v_ref[rows, v_l], lane)
            go = grad_out[rows, p * PAIR : (p + 1) * PAIR]
            scores = dot_nt(q, k2) * scale
            grad_probs = dot_nt(go, v2)
            probs, grad_scores = [], []
            for half in range(2):
                cut = slice(half * seq_len, (half + 1) * seq_len)
                head = 2 * p + half
                part = jnp.where(mask[rows] > 0.0, scores[:, cut], MASK_FILL)
                prob = jnp.exp(part - lse[rows, head : head + 1])
                gp = grad_probs[:, cut]
                inner = jnp.sum(prob * gp, axis=-1, keepdims=True)
                probs.append(prob.astype(BF16))
                grad_scores.append((prob * (gp - inner)).astype(BF16))
            probs = jnp.concatenate(probs, axis=1)
            grad_scores = jnp.concatenate(grad_scores, axis=1)
            ref, l = lanes(grad_v, p)
            ref[rows, l] = one_of(dot_tn(probs, go), lane).astype(BF16)
            ref, l = lanes(grad_q, p)
            ref[rows, l] = (dot(grad_scores, k2) * scale).astype(BF16)
            ref, l = lanes(grad_k, p)
            ref[rows, l] = (one_of(dot_tn(grad_scores, q), lane) * scale).astype(BF16)


def small(vecs, which, width):
    pieces = vecs.shape[1] // width
    at = (which if which >= 0 else pieces + which) * width
    return vecs[:, at : at + width].astype(F32)


def set_small(vecs, which, width, value):
    pieces = vecs.shape[1] // width
    at = (which if which >= 0 else pieces + which) * width
    vecs[:, at : at + width] = value


def where_am_i():
    return lax.axis_index("section"), lax.rem(lax.axis_index("dp"), 2)


def ffn_forward(normed, w_in, w_out, vecs, act, slope):
    width = normed.shape[1]
    low = normed.astype(BF16)
    total = None
    for j in range(w_in.shape[0] // width):
        cut = slice(j * width, (j + 1) * width)
        pre = dot(low, w_in[cut]) + small(vecs, j, width)
        value, derivative = act_parts(pre)
        value = value.astype(BF16)
        act[:, cut] = value
        slope[:, cut] = derivative.astype(slope.dtype)
        term = dot(value, w_out[cut])
        total = term if total is None else total + term
    return total + small(vecs, BIAS_OUT, width)


def load(source, target, sem):
    copy = pltpu.make_async_copy(source, target, sem)
    copy.start()
    return copy


def forward_kernel(k):
    width = k.h1.shape[1]
    ffn = k.w_in.shape[0]
    sec, _ = where_am_i()
    get_lens = load(k.lengths, k.lens, k.sems.at[7])
    get_in = load(k.mats.at[: 3 * width], k.raw_attn, k.sems.at[0])
    get_x = load(k.x, k.x_here, k.sems.at[1])
    get_vecs = load(k.vectors, k.raw_vecs, k.sems.at[2])
    get_attn_out = load(k.mats.at[3 * width : 4 * width], k.w_attn_out, k.sems.at[3])
    get_ffn = load(k.mats.at[6 * width : 6 * width + ffn], k.raw_ffn, k.sems.at[4])
    get_out = load(k.mats.at[6 * width + ffn :], k.w_out, k.sems.at[5])
    get_cross = pltpu.make_async_copy(k.mats.at[4 * width : 6 * width], k.raw_cross, k.sems.at[6])

    @pl.when(sec == 1)
    def _():
        get_cross.start()

    get_lens.wait()
    fill_mask(k.mask, k.lens, sec, sec, sec == 1)
    k.leave("mask")
    get_in.wait()
    split_rows(k.raw_attn, k.wide, 3, k.w_attn, 0)
    k.leave("w_attn")
    get_x.wait()
    for j in range(3):
        part = dot(k.x_here[...], k.w_attn[j * width : (j + 1) * width])
        k.qkv[:, j * width : (j + 1) * width] = part.astype(BF16)
    k.leave("qkv")
    attend_forward((k.qkv, 0), (k.qkv, width), (k.qkv, 2 * width), k.mask, k.mixed, k.lse)
    k.leave("mixed", "lse")
    get_vecs.wait()
    k.vecs[...] = k.raw_vecs[...].astype(F32)
    vecs = k.vecs
    get_attn_out.wait()
    k.leave("w_attn_out")
    hidden = k.x_here[...].astype(F32) + dot(k.mixed[...], k.w_attn_out[...])
    k.pre1[...] = hidden
    k.leave("pre1")
    k.h1[...] = norm_forward(hidden, small(vecs, GAIN1, width), small(vecs, SHIFT1, width))
    get_ffn.wait()
    split_rows(k.raw_ffn, k.wide, ffn // width, k.w_in, 0)
    get_out.wait()

    @pl.when(sec == 0)
    def _():
        hidden = k.h1[...] + ffn_forward(k.h1[...], k.w_in, k.w_out, vecs, k.act, k.slope)
        k.pre2[...] = hidden
        second = norm_forward(hidden, small(vecs, GAIN2, width), small(vecs, SHIFT2, width))
        k.h2[...] = second
        third = norm_forward(second, small(vecs, GAIN3, width), small(vecs, SHIFT3, width))
        k.memory[...] = third.astype(BF16)
        k.low[...] = third.astype(BF16)
        k.leave("low")

    @pl.when(sec == 1)
    def _():
        k.low[...] = k.h1[...].astype(BF16)
        k.leave("low")
        get_cross.wait()
        split_rows(k.raw_cross, k.wide, 2, k.w_cross, 0)
        k.qc[...] = dot(k.low[...], k.w_cross[:width]).astype(BF16)

    k.left("mask", "w_attn", "qkv", "mixed", "lse", "w_attn_out", "pre1", "low")


def prepare_kernel(k):
    width = k.raw.shape[1]
    seq_len = k.mask.shape[1]
    sec, core = where_am_i()

    @pl.when(sec == 1)
    def _():
        get_cot = load(k.cot_all, k.raw_cot, k.sems.at[0])
        get_lens = load(k.lengths, k.lens, k.sems.at[1])
        k.raw[pl.ds(pl.multiple_of(core * width, width), width)] = k.cross_mine[...]
        k.raw[pl.ds(pl.multiple_of((1 - core) * width, width), width)] = k.cross_other[...]
        split_rows(k.raw, k.wide, 2, k.w_pairs, 0)
        get_lens.wait()
        fill_mask(k.mask, k.lens, 1, 0, None)
        get_cot.wait()
        position = lax.broadcasted_iota(jnp.int32, (seq_len, 1), 0)
        for r in range(k.lens.shape[1]):
            used = sentence_ends(k.lens, 1, r)[-1]
            rows = slice(r * seq_len, (r + 1) * seq_len)
            k.cot[rows] = jnp.where(position < used, k.raw_cot[rows].astype(F32), 0.0).astype(BF16)


def decoder_kernel(k):
    width = k.h1.shape[1]
    ffn = k.w_in.shape[0]
    vecs = k.vecs
    sec, _ = where_am_i()

    @pl.when(sec == 0)
    def _():
        k.layer_out[...] = k.near_memory[...]
        k.leave("layer_out")

    @pl.when(sec == 1)
    def _():
        for j in range(2):
            part = dot(k.memory[...], k.w_pairs[j * width : (j + 1) * width])
            k.pairs[:, j * width : (j + 1) * width] = part.astype(BF16)
        attend_forward((k.qc, 0), (k.pairs, 0), (k.pairs, width), k.mask, k.mixed, k.lse)
        k.leave("mixed")
        hidden2 = k.h1[...] + dot(k.mixed[...], k.w_cross[width:])
        gain2, shift2 = small(vecs, GAIN2, width), small(vecs, SHIFT2, width)
        normed2 = norm_forward(hidden2, gain2, shift2)
        k.low2[...] = normed2.astype(BF16)
        hidden3 = normed2 + ffn_forward(normed2, k.w_in, k.w_out, vecs, k.act, k.slope)
        gain3, shift3 = small(vecs, GAIN3, width), small(vecs, SHIFT3, width)
        k.layer_out[...] = norm_forward(hidden3, gain3, shift3).astype(BF16)
        k.leave("layer_out")
        grad_sum3, d_gain, d_shift = norm_backward(hidden3, gain3, k.cot[...].astype(F32))
        set_small(k.vec_grads, GAIN3, width, d_gain)
        set_small(k.vec_grads, SHIFT3, width, d_shift)
        grad_low = grad_sum3.astype(BF16)
        k.grad_ffn[...] = grad_low
        set_small(
            k.vec_grads, BIAS_OUT, width, jnp.sum(grad_low.astype(F32), axis=0, keepdims=True)
        )
        total = grad_sum3
        for j in range(ffn // width):
            cut = slice(j * width, (j + 1) * width)
            grad = (dot_nt(grad_low, k.w_out[cut]) * k.slope[:, cut]).astype(BF16)
            k.side[:, cut] = grad
            set_small(k.vec_grads, j, width, jnp.sum(grad.astype(F32), axis=0, keepdims=True))
            total = total + dot_nt(grad, k.w_in[cut])
        grad_hidden2, d_gain, d_shift = norm_backward(hidden2, gain2, total)
        set_small(k.vec_grads, GAIN2, width, d_gain)
        set_small(k.vec_grads, SHIFT2, width, d_shift)
        k.grad_sum2[...] = grad_hidden2
        low = grad_hidden2.astype(BF16)
        k.right[:, width:] = low
        k.grad_mixed[...] = dot_nt(low, k.w_cross[width:]).astype(BF16)
        attend_backward(
            (k.qc, 0), (k.pairs, 0), (k.pairs, width), k.mask, k.lse, k.grad_mixed,
            (k.right, 0), (k.grad_pairs, 0), (k.grad_pairs, width),
        )
        k.leave("right")
        k.grad_qc[...] = k.right[:, :width]
        back = dot_nt(k.grad_pairs[:, :width], k.w_pairs[:width])
        back = back + dot_nt(k.grad_pairs[:, width:], k.w_pairs[width:])
        k.grad_memory[...] = back.astype(BF16)
        k.left("mixed", "right")

    k.left("layer_out")


def ffn_weight_grads(k, act, low, grad_pre, grad_ffn, core):
    width = k.h1.shape[1]
    ffn = k.w_in.shape[0]
    chunks = ffn // width
    early = k.early.shape[0]
    for j in range(chunks):
        cut = slice(j * width, (j + 1) * width)
        put_part(k.wide, j, chunks, dot_tn(low[...], grad_pre[:, cut]))
        put_rows(k.blocks, ffn - early + j * width, dot_tn(act[:, cut], grad_ffn[...]), core)


def put_given(k, vec_grads, first_owner, core):
    sides, count, rows, width = k.blocks.shape
    if sides == 1:
        return
    share = vec_grads.shape[1] // (2 * sides * count)
    for n in range(sides * count):
        owner = first_owner + n
        row = vec_grads[:, owner * share : (owner + 1) * share]
        row = jnp.concatenate([row, jnp.zeros((1, width - share), F32)], axis=1)
        side = core if n % 2 == 0 else 1 - core
        k.blocks[side, n // 2, rows - TAIL :] = jnp.broadcast_to(row, (TAIL, width)).astype(BF16)
    k.give[...] = k.blocks[1]


def backward_kernel(k):
    width = k.h1.shape[1]
    ffn = k.w_in.shape[0]
    vecs = k.vecs
    sec, core = where_am_i()
    wanted = ("pre1", "w_attn_out", "mask", "lse", "qkv", "w_attn")
    wanted_next = ("x", "mixed", "low", "right", "cross_mixed")
    coming = [
        load(getattr(k, "far_" + name), getattr(k, name), k.sems.at[at])
        for at, name in enumerate(wanted + wanted_next)
    ]

    @pl.when(sec == 0)
    def _():
        grad, d_gain, d_shift = norm_backward(
            k.h2[...], small(vecs, GAIN3, width), k.grad_memory[...].astype(F32)
        )
        set_small(k.vec_grads, GAIN3, width, d_gain)
        set_small(k.vec_grads, SHIFT3, width, d_shift)
        total, d_gain, d_shift = norm_backward(k.pre2[...], small(vecs, GAIN2, width), grad)
        set_small(k.vec_grads, GAIN2, width, d_gain)
        set_small(k.vec_grads, SHIFT2, width, d_shift)
        grad_low = total.astype(BF16)
        k.grad_ffn[...] = grad_low
        set_small(
            k.vec_grads, BIAS_OUT, width, jnp.sum(grad_low.astype(F32), axis=0, keepdims=True)
        )
        k.low1[...] = k.h1[...].astype(BF16)
        for j in range(ffn // width):
            cut = slice(j * width, (j + 1) * width)
            grad = (dot_nt(grad_low, k.w_out[cut]) * k.side[:, cut].astype(F32)).astype(BF16)
            k.grad_pre[:, cut] = grad
            set_small(k.vec_grads, j, width, jnp.sum(grad.astype(F32), axis=0, keepdims=True))
            total = total + dot_nt(grad, k.w_in[cut])
        k.grad_h1[...] = total
        ffn_weight_grads(k, k.act, k.low1, k.grad_pre, k.grad_ffn, core)

    @pl.when(sec == 1)
    def _():
        k.vec_grads[...] = k.dec_vec_grads[...]
        k.grad_h1[...] = k.grad_sum2[...] + dot_nt(k.grad_qc[...], k.w_cross[:width])
        ffn_weight_grads(k, k.act, k.low2, k.side, k.dec_grad_ffn, core)

    early = k.early.shape[0]
    for c in range(width // LANES):
        k.early[:, c * LANES : (c + 1) * LANES] = k.wide[c, :early].astype(BF16)
    take_parts(k.wide, early, ffn - early, k.blocks, 0, core)
    for copy in coming:
        copy.wait()
    grad, d_gain, d_shift = norm_backward(k.pre1[...], small(vecs, GAIN1, width), k.grad_h1[...])
    set_small(k.vec_grads, GAIN1, width, d_gain)
    set_small(k.vec_grads, SHIFT1, width, d_shift)
    put_given(k, k.vec_grads, 2 * k.blocks.shape[1], core)
    low = grad.astype(BF16)
    k.grad_attn[...] = low
    k.grad_mixed[...] = dot_nt(low, k.w_attn_out[...]).astype(BF16)
    attend_backward(
        (k.qkv, 0), (k.qkv, width), (k.qkv, 2 * width), k.mask, k.lse, k.grad_mixed,
        (k.grad_qkv, 0), (k.grad_qkv, width), (k.grad_qkv, 2 * width),
    )
    for j in range(3):
        cut = slice(j * width, (j + 1) * width)
        grad = grad + dot_nt(k.grad_qkv[:, cut], k.w_attn[cut])
    k.grad_x[...] = grad
    k.leave("grad_x")
    k.left("grad_x")


def attn_grad_kernel(k):
    width = k.x.shape[1]
    sec, core = where_am_i()
    for j in range(3):
        put_part(k.wide, j, 3, dot_tn(k.x[...], k.grad_qkv[:, j * width : (j + 1) * width]))
    take_parts(k.wide, 0, 3 * width, k.blocks, 0, core)
    put_rows(k.blocks, 3 * width, dot_tn(k.mixed[...], k.grad_attn[...]), core)

    @pl.when(sec == 0)
    def _():
        for j in range(2):
            cut = slice(j * width, (j + 1) * width)
            put_part(k.wide, j, 2, dot_tn(k.low[...], k.grad_pairs[:, cut]))

    @pl.when(sec == 1)
    def _():
        put_part(k.wide, 0, 2, dot_tn(k.low[...], k.right[:, :width]))
        put_part(k.wide, 1, 2, dot_tn(k.cross_mixed[...], k.right[:, width:]))

    take_parts(k.wide, 0, 2 * width, k.blocks, 4 * width, core)
    put_rows(k.blocks, 6 * width, k.early[...], core)
    put_given(k, k.vec_grads, 0, core)


class Refs(types.SimpleNamespace):
    def leave(self, *names):
        for name in names:
            self.leaving[name].start()

    def left(self, *names):
        for name in names:
            self.leaving[name].wait()


def run_kernel(kernel, name, hbm, vmem, outs, far_outs, scratch, loads, spare, reuse=(), work=10**10, smem=None):
    smem = smem or {}
    ins = {**smem, **hbm, **vmem}
    near = {n: pltpu.VMEM(*spec) for n, spec in far_outs.items()}
    near.update({n: pltpu.VMEM(*spec) if isinstance(spec, tuple) else spec for n, spec in scratch.items()})
    names = [*ins, *outs, *far_outs, *near, "sems", "leave_sems"]

    def run(*refs):
        k = Refs(**dict(zip(names, refs)))
        first = len(ins) + len(outs)
        k.leaving = {
            n: pltpu.make_async_copy(getattr(k, n), refs[first + at], k.leave_sems.at[at])
            for at, n in enumerate(far_outs)
        }
        kernel(k)

    results = pl.pallas_call(
        run,
        name=name,
        in_specs=[SMEM] * len(smem) + [HBM] * len(hbm) + [VMEM] * len(vmem),
        out_specs=[VMEM] * len(outs) + [HBM] * len(far_outs),
        out_shape=[pltpu.VMEM(*spec) for spec in outs.values()]
        + [pltpu.HBM(*spec) for spec in far_outs.values()],
        scratch_shapes=[
            *near.values(),
            pltpu.SemaphoreType.DMA((max(loads, 1),)),
            pltpu.SemaphoreType.DMA((max(len(far_outs), 1),)),
        ],
        compiler_params=pltpu.CompilerParams(
            vmem_limit_bytes=int(spare * 2**20)
            + sum(math.prod(b.shape) * jnp.dtype(b.dtype).itemsize for b in near.values())
        ),
        input_output_aliases={[*ins].index(old): [*outs].index(new) for old, new in reuse},
        cost_estimate=pl.CostEstimate(flops=work, bytes_accessed=1, transcendentals=0),
    )(
        *smem.values(),
        *[pltpu.with_memory_space_constraint(array, pltpu.HBM) for array in hbm.values()],
        *[pltpu.with_memory_space_constraint(array, pltpu.VMEM) for array in vmem.values()],
    )
    return dict(zip([*outs, *far_outs], results))


SMEM = pl.BlockSpec(memory_space=pltpu.SMEM)
HBM = pl.BlockSpec(memory_space=pltpu.HBM)
VMEM = pl.BlockSpec(memory_space=pltpu.VMEM)
ANY = pl.BlockSpec(memory_space=pl.ANY)


def swapped(array, axis, bit):
    devices = lax.axis_size(axis)
    return lax.ppermute(array, axis, [(i, i ^ bit) for i in range(devices)])


def held_until(array, *others):
    return lax.optimization_barrier((array, *others))[0]


def own_bit(bit):
    return (lax.axis_index("dp") >> bit) & 1


def core_sum(k, z, y, cut):
    return k.blocks[0, 2 * z + y, cut].astype(F32) + k.from_core[2 * z + y, cut].astype(F32)


class Phase:
    def __init__(self, blocks, from_core, cuts):
        self.blocks, self.from_core, self.cuts = blocks, from_core, cuts
        self.width = blocks.shape[3]

    def for_y(self):
        def kernel(k):
            y = own_bit(1)
            for at, cut in enumerate(self.cuts):
                for z in range(2):
                    getattr(k, f"out{at}")[z] = core_sum(k, z, 1 - y, cut).astype(BF16)

        outs = {
            f"out{at}": ((2, cut.stop - cut.start, self.width), BF16)
            for at, cut in enumerate(self.cuts)
        }
        ins = {"blocks": self.blocks, "from_core": self.from_core}
        return [*run_kernel(kernel, "for_y", {}, ins, outs, {}, {}, 0, 4, work=10**8).values()]

    def for_z(self, at, from_y):
        cut = self.cuts[at]

        def kernel(k):
            y, z = own_bit(1), own_bit(2)
            k.give[...] = (core_sum(k, 1 - z, y, cut) + k.from_y[1 - z].astype(F32)).astype(BF16)
            k.mine[...] = core_sum(k, z, y, cut) + k.from_y[z].astype(F32)

        shape = (cut.stop - cut.start, self.width)
        outs = {"give": (shape, BF16), "mine": (shape, F32)}
        ins = {"blocks": self.blocks, "from_core": self.from_core, "from_y": from_y}
        return [*run_kernel(kernel, "for_z", {}, ins, outs, {}, {}, 0, 4, work=10**8).values()]


def for_far_z(high, from_high, low, from_low):
    def kernel(k):
        upper = k.high[...] + k.from_high[...].astype(F32)
        lower = k.low[...] + k.from_low[...].astype(F32)

        @pl.when(own_bit(3) == 0)
        def _():
            k.give[...] = upper.astype(BF16)
            k.mine[...] = lower

        @pl.when(own_bit(3) == 1)
        def _():
            k.give[...] = lower.astype(BF16)
            k.mine[...] = upper

    ins = {"high": high, "from_high": from_high, "low": low, "from_low": from_low}
    outs = {"give": (high.shape, BF16), "mine": (high.shape, F32)}
    return [*run_kernel(kernel, "for_far_z", {}, ins, outs, {}, {}, 0, 4, work=10**8).values()]


def sum_over_dp(blocks_high, core_high, blocks_low, core_low, cuts):
    high, low = Phase(blocks_high, core_high, cuts), Phase(blocks_low, core_low, cuts)
    y_high, y_low = high.for_y(), low.for_y()
    pairs = []
    for at in range(len(cuts)):
        z_high, mine_high = high.for_z(at, swapped(y_high[at], "dp", 2))
        z_low, mine_low = low.for_z(at, swapped(y_low[at], "dp", 2))
        give, mine = for_far_z(
            mine_high, swapped(z_high, "dp", 4), mine_low, swapped(z_low, "dp", 4)
        )
        pairs.append((mine, swapped(give, "dp", 8)))
    return pairs


def adam_of(grad, master, mean_old, square_old, step):
    mean_new = 0.9 * mean_old + 0.1 * grad
    square_new = 0.98 * square_old + 0.02 * grad * grad
    rate = step.shape[1] ** (-0.5) * jnp.minimum(lax.rsqrt(step), step * WARMUP_STEPS ** (-1.5))
    mean_share = 1.0 - jnp.exp(step * math.log(0.9))
    square_share = 1.0 - jnp.exp(step * math.log(0.98))
    fixed_mean = mean_new * (1.0 / mean_share)
    fixed_square = square_new * (1.0 / square_share)
    change = -rate * fixed_mean / (jnp.sqrt(fixed_square) + ADAM_EPS)
    return change, mean_new, square_new, master + change


def adam_kernel(k, full):
    width = k.master.shape[1]
    share = k.vec_master.shape[1]
    step = jnp.full((1, width), k.step[0], jnp.int32).astype(F32)
    first = 0
    vec_grad = None
    count = len([name for name in vars(k) if name.startswith("mine")])
    for at in range(count):
        rows = getattr(k, f"mine{at}").shape[0]
        grad = getattr(k, f"mine{at}")[...] + getattr(k, f"got{at}")[...].astype(F32)
        if at == count - 1:
            rows -= TAIL
            vec_grad, grad = grad[rows : rows + 1], grad[:rows]
        here = slice(first, first + rows)
        parts = adam_of(grad, k.master[here], k.mean[here], k.square[here], step)
        if full:
            k.grad[here] = grad
            k.change[here], k.mean_new[here], k.square_new[here] = parts[:3]
        else:
            k.own[here] = parts[3].astype(BF16)
        first += rows
    pad = jnp.zeros((1, width - share), F32)

    def padded(ref):
        return jnp.concatenate([ref[...], pad], axis=1)

    parts = adam_of(
        vec_grad, padded(k.vec_master), padded(k.vec_mean), padded(k.vec_square), step
    )
    if full:
        k.vec_grad[...] = vec_grad[:, :share]
        k.vec_change[...] = parts[0][:, :share]
        k.vec_mean_new[...] = parts[1][:, :share]
        k.vec_square_new[...] = parts[2][:, :share]
        names = [*k.leaving]
        k.leave(*names)
        k.left(*names)
    else:
        k.own[first:] = jnp.broadcast_to(parts[3], (TAIL, width)).astype(BF16)


def adam(pairs, state, step, full):
    shape, vec_shape = state["master"].shape, state["vec_master"].shape
    ins = {f"mine{at}": mine for at, (mine, _) in enumerate(pairs)}
    ins.update({f"got{at}": got for at, (_, got) in enumerate(pairs)})
    outs, far = {}, {}
    if full:
        far = dict.fromkeys(("grad", "change", "mean_new", "square_new"), (shape, F32))
        far.update({"vec_" + name: (vec_shape, F32) for name in far})
    else:
        outs = {"own": ((shape[0] + TAIL, shape[1]), BF16)}
    return run_kernel(
        lambda k: adam_kernel(k, full), "adam_outputs" if full else "adam", {},
        {**ins, **state}, outs, far, {}, 0, 6, work=10**9, smem={"step": step},
    )


def place_blocks(pieces, share, rows_all, before=None):
    masks = [mask for mask, _ in pieces]
    arrays = [array for _, array in pieces]
    width = arrays[0].shape[1]
    extra = [] if before is None else [*before]

    def kernel(*refs):
        ins, (target, tails, sems) = refs[: len(arrays)], refs[-3:]
        me = lax.axis_index("dp")
        copies = []
        for at, (mask, ref) in enumerate(zip(masks, ins)):
            owner = me ^ mask
            there = pl.ds(pl.multiple_of(owner * share, share), share)
            copies.append(load(ref.at[:share], target.at[there], sems.at[at]))
        if extra:
            tails[...] = refs[len(arrays) + 1][...]
        for mask, ref in zip(masks, ins):
            tails[me ^ mask] = ref[share:]
        for copy in copies:
            copy.wait()

    return pl.pallas_call(
        kernel,
        name="place_blocks",
        in_specs=[VMEM] * len(arrays) + [HBM, VMEM][: len(extra)],
        out_specs=[HBM, VMEM],
        out_shape=[
            pltpu.HBM((rows_all, width), BF16),
            pltpu.VMEM((rows_all // share, TAIL, width), BF16),
        ],
        scratch_shapes=[pltpu.SemaphoreType.DMA((len(arrays),))],
        input_output_aliases={len(arrays): 0} if extra else {},
        compiler_params=pltpu.CompilerParams(vmem_limit_bytes=4 * 2**20),
        cost_estimate=pl.CostEstimate(flops=10**9, bytes_accessed=1, transcendentals=0),
    )(*[pltpu.with_memory_space_constraint(array, pltpu.VMEM) for array in arrays], *extra)


def gather_blocks(own, share, rows_all):
    def go(array, bit):
        return swapped(array, "dp", bit)

    got = {0: own}
    got[2], got[4], got[8] = go(own, 2), go(own, 4), go(own, 8)
    got[2], got[4] = lax.optimization_barrier((got[2], got[4]))
    got[6] = go(got[4], 2)
    got[6], got[8] = lax.optimization_barrier((got[6], got[8]))
    got[12], got[10] = go(got[8], 4), go(got[8], 2)
    got[12], got[10] = lax.optimization_barrier((got[12], got[10]))
    got[14] = go(got[12], 2)
    early, late = [0, 2, 4, 6, 8], [12, 10, 14]
    for mask in early + late:
        got[mask | 1] = go(got[mask], 1)
    first = place_blocks([(m | c, got[m | c]) for m in early for c in (0, 1)], share, rows_all)
    return place_blocks([(m | c, got[m | c]) for m in late for c in (0, 1)], share, rows_all, first)


def body(
    inputs,
    lengths,
    cotangent,
    matrices,
    vectors,
    master_matrices,
    master_vectors,
    matrix_mean,
    matrix_square,
    vector_mean,
    vector_square,
    adam_step,
):
    row_count, seq_len, width = inputs.shape[1:]
    tokens = row_count * seq_len
    rows_all, vec_all = matrices.shape[1], vectors.shape[1]
    ffn = (rows_all - 6 * width) // 2
    half = rows_all // 2
    ranks = lax.axis_size("dp")
    share, vec_share = rows_all // ranks, vec_all // ranks
    by_swaps = ranks == 16 and share % 32 == 0
    blocks = (2, ranks // 4, share + TAIL, width) if by_swaps else (1, 1, half, width)
    me = lax.axis_index("dp")

    x = inputs.reshape(tokens, width)
    cot = cotangent.reshape(tokens, width)
    mats = matrices.reshape(rows_all, width)
    lens_here = pltpu.SMEM(lengths.shape, jnp.int32)

    def spec(columns, dtype):
        return ((tokens, columns), dtype)

    full, low, deep = spec(width, F32), spec(width, BF16), spec(ffn, BF16)
    square, mask = ((width, width), BF16), spec(seq_len, F32)
    double, lse, w_ffn = ((2 * width, width), BF16), spec(LANES, F32), ((ffn, width), BF16)
    all_vecs, triple = ((1, vec_all), F32), spec(3 * width, BF16)
    sided = {"blocks": (blocks, BF16)}
    if by_swaps:
        sided["give"] = (blocks[1:], BF16)
    early = ((half - 6 * width, width), BF16)

    def wide(rows):
        return ((width // LANES, rows, LANES), F32)

    def pick(arrays, *names):
        return {name: arrays[name] for name in names}

    cross_half = lax.dynamic_slice(mats, ((4 + (me & 1)) * width, 0), (width, width), allow_negative_indices=False)
    cross_mine = swapped(cross_half, "section", 1)
    f = run_kernel(
        forward_kernel, "forward", {"mats": mats, "x": x, "vectors": vectors, "lengths": lengths}, {},
        {
            "h1": full, "w_in": w_ffn, "act": deep, "slope": deep, "pre2": full, "h2": full,
            "memory": low, "w_cross": double, "qc": low, "w_out": w_ffn, "vecs": all_vecs,
        },
        {
            "qkv": triple, "lse": lse, "mixed": low, "pre1": full, "mask": mask, "w_attn_out": square,
            "w_attn": ((3 * width, width), BF16), "low": low,
        },
        {
            "raw_attn": ((3 * width, width), BF16), "raw_cross": double, "raw_ffn": w_ffn,
            "x_here": low, "wide": wide(ffn), "raw_vecs": ((1, vec_all), BF16), "lens": lens_here,
        },
        8, 10,
    )
    memory_far = swapped(f["memory"], "section", 1)
    cross_mine = held_until(cross_mine, f["memory"])
    cross_other = swapped(cross_mine, "dp", 1)
    p = run_kernel(
        prepare_kernel, "prepare", {"cot_all": cot, "lengths": lengths},
        {"cross_mine": cross_mine, "cross_other": cross_other},
        {"w_pairs": double, "mask": mask, "cot": low}, {},
        {"raw": double, "wide": wide(2 * width), "raw_cot": low, "lens": lens_here},
        2, 4,
    )
    d = run_kernel(
        decoder_kernel, "decoder", {},
        {
            "memory": memory_far, "near_memory": f["memory"], **p, "enc_act": f["act"],
            "enc_slope": f["slope"],
            **pick(f, "w_cross", "qc", "h1", "w_in", "w_out", "vecs"),
        },
        {
            "grad_memory": low, "grad_pairs": spec(2 * width, BF16), "act": deep,
            "side": deep, "grad_ffn": low, "low2": low, "grad_qc": low, "grad_sum2": full,
            "vec_grads": all_vecs,
        },
        {"layer_out": low, "mixed": low, "right": spec(2 * width, BF16)},
        {"pairs": spec(2 * width, BF16), "slope": spec(ffn, F32), "lse": lse, "grad_mixed": low},
        0, 11, (("enc_act", "act"), ("enc_slope", "side")),
    )
    grad_memory_far = swapped(d["grad_memory"], "section", 1)
    grad_pairs_far = swapped(d["grad_pairs"], "section", 1)
    ahead = {
        "pre1": full, "w_attn_out": square, "mask": mask, "lse": lse, "qkv": triple,
        "w_attn": ((3 * width, width), BF16),
    }
    s = run_kernel(
        backward_kernel, "backward",
        {
            **{"far_" + name: f[name] for name in ahead},
            "far_x": x, "far_mixed": f["mixed"], "far_low": f["low"], "far_right": d["right"],
            "far_cross_mixed": d["mixed"],
        },
        {
            "dec_grad_ffn": d["grad_ffn"], "dec_vec_grads": d["vec_grads"],
            "grad_memory": grad_memory_far, **pick(d, "act", "side", "low2", "grad_qc", "grad_sum2"),
            **pick(f, "pre2", "h2", "h1", "w_in", "w_out", "w_cross", "vecs"),
        },
        {
            "vec_grads": all_vecs, "early": early, **sided, "grad_attn": low, "grad_qkv": triple,
            "x": low, "mixed": low, "low": low, "right": spec(2 * width, BF16), "cross_mixed": low,
        },
        {"grad_x": full},
        {
            "grad_pre": deep, "grad_ffn": low, "low1": low, "wide": wide(ffn), "grad_h1": full,
            "grad_mixed": low, **ahead,
        },
        11, 9, work=4 * 10**10,
    )
    from_core = swapped(s["give"], "dp", 1) if by_swaps else None
    a = run_kernel(
        attn_grad_kernel, "attn_grad", {},
        {
            "grad_qkv": s["grad_qkv"], "vec_grads": s["vec_grads"], "early": s["early"], "grad_pairs": grad_pairs_far,
            **pick(s, "x", "grad_attn", "mixed", "low", "right", "cross_mixed"),
        },
        sided, {}, {"wide": wide(3 * width)}, 0, 4,
    )

    state = {"master": master_matrices[0], "mean": matrix_mean[0], "square": matrix_square[0]}
    state.update(vec_master=master_vectors, vec_mean=vector_mean, vec_square=vector_square)
    if by_swaps:
        first_rows = (share + TAIL) // 2 // 16 * 16
        cuts = [slice(0, first_rows), slice(first_rows, share + TAIL)]
        pairs = sum_over_dp(
            s["blocks"], from_core, a["blocks"], swapped(a["give"], "dp", 1), cuts
        )
        own = adam(pairs, state, adam_step, False)["own"]
        new_mat, tails = gather_blocks(own, share, rows_all)
        new_vec = tails[:, 0, :vec_share].reshape(1, vec_all)
        result = adam(pairs, state, adam_step, True)
    else:
        whole = jnp.concatenate([a["blocks"][0, 0], s["blocks"][0, 0]], axis=0)
        grad = lax.psum_scatter(whole, "dp", scatter_dimension=0, tiled=True).astype(F32)
        vec_grad = lax.dynamic_slice(
            lax.psum(s["vec_grads"], "dp"), (0, me * vec_share), (1, vec_share)
        )
        step = jnp.full((1, width), adam_step[0].astype(F32))
        parts = adam_of(grad, state["master"], state["mean"], state["square"], step)
        vec_step = jnp.full((1, width), adam_step[0].astype(F32))
        pad = ((0, 0), (0, width - vec_share))
        vec_parts = [
            part[:, :vec_share]
            for part in adam_of(
                *[jnp.pad(v, pad) for v in (vec_grad, master_vectors, vector_mean, vector_square)],
                vec_step,
            )
        ]
        names = ("change", "mean_new", "square_new")
        result = {"grad": grad, "vec_grad": vec_grad, **dict(zip(names, parts))}
        result.update({"vec_" + name: part for name, part in zip(names, vec_parts)})
        new_mat = lax.all_gather(parts[3].astype(BF16), "dp", axis=0, tiled=True)
        new_vec = lax.all_gather(vec_parts[3].astype(BF16), "dp", axis=1, tiled=True)
    return (
        d["layer_out"].reshape(1, row_count, seq_len, width),
        s["grad_x"].reshape(1, row_count, seq_len, width),
        result["grad"][None],
        result["vec_grad"],
        result["change"][None],
        result["vec_change"],
        result["mean_new"][None],
        result["square_new"][None],
        result["vec_mean_new"],
        result["vec_square_new"],
        new_mat[None],
        new_vec,
    )


def solution(mesh):
    return jax.shard_map(
        body,
        mesh=mesh,
        in_specs=(
            P("section", "dp", None, None),
            P(None, "dp", None),
            P("dp", None, None),
            P("section", None, None),
            P("section", None),
            P("section", "dp", None),
            P("section", "dp"),
            P("section", "dp", None),
            P("section", "dp", None),
            P("section", "dp"),
            P("section", "dp"),
            P(),
        ),
        out_specs=(
            P("section", "dp", None, None),
            P("section", "dp", None, None),
            P("section", "dp", None),
            P("section", "dp"),
            P("section", "dp", None),
            P("section", "dp"),
            P("section", "dp", None),
            P("section", "dp", None),
            P("section", "dp"),
            P("section", "dp"),
            P("section", None, None),
            P("section", None),
        ),
        check_vma=False,
    )
```

```python
import math
import types

import jax
import jax.numpy as jnp
from jax import lax
from jax.experimental import pallas as pl
from jax.experimental.pallas import tpu as pltpu
from jax.sharding import PartitionSpec as P

HEADS = 8
HEAD_DIM = 64
PAIR = 2 * HEAD_DIM
LANES = 128
TAIL = 16
UNROLL_PAIRS = 4
UNROLL_CHUNKS = True

MASK_FILL = -1e30
NORM_EPS = 1e-05
ADAM_EPS = 1e-09
WARMUP_STEPS = 4000.0

F32 = jnp.float32
BF16 = jnp.bfloat16

BIAS_OUT, GAIN1, SHIFT1, GAIN2, SHIFT2, GAIN3, SHIFT3 = range(-7, 0)


def dot(left, right):
    return jnp.dot(left, right, preferred_element_type=F32)


def dot_nt(left, right):
    return lax.dot_general(left, right, (((1,), (1,)), ((), ())), preferred_element_type=F32)


def dot_tn(left, right):
    return lax.dot_general(left, right, (((0,), (0,)), ((), ())), preferred_element_type=F32)


def norm_parts(hidden):
    centre = hidden - jnp.mean(hidden, axis=-1, keepdims=True)
    rstd = lax.rsqrt(jnp.mean(centre * centre, axis=-1, keepdims=True) + NORM_EPS)
    return centre * rstd, rstd


def norm_forward(hidden, gain, shift):
    return norm_parts(hidden)[0] * gain + shift


def norm_backward(hidden, gain, grad):
    normal, rstd = norm_parts(hidden)
    scaled = grad * gain
    inner = jnp.mean(scaled * normal, axis=-1, keepdims=True)
    grad_in = rstd * (scaled - jnp.mean(scaled, axis=-1, keepdims=True) - normal * inner)
    grad_gain = jnp.sum(grad * normal, axis=0, keepdims=True)
    grad_shift = jnp.sum(grad, axis=0, keepdims=True)
    return grad_in, grad_gain, grad_shift


def act_parts(pre):
    cdf = 0.5 * (1.0 + lax.erf(pre * (0.5**0.5)))
    pdf = jnp.exp(-0.5 * pre * pre) * 0.3989422804014327
    return pre * cdf, cdf + pre * pdf


def split_rows(raw, wide, parts, out, base):
    width = raw.shape[1]
    for c in range(width // LANES):
        cut = slice(c * LANES, (c + 1) * LANES)
        wide[c, : parts * width] = raw[: parts * width, cut].astype(F32)
        for j in range(parts):
            out[(base + j) * width : (base + j + 1) * width, cut] = wide[
                c, pl.ds(j, width, stride=parts), :
            ].astype(BF16)


def put_part(wide, j, parts, values):
    rows, width = values.shape
    for c in range(width // LANES):
        wide[c, pl.ds(j, rows, stride=parts), :] = values[:, c * LANES : (c + 1) * LANES]


def take_parts(wide, rows, out, first):
    for c in range(wide.shape[0]):
        out[first : first + rows, c * LANES : (c + 1) * LANES] = wide[c, :rows].astype(BF16)


def sentence_ends(lens, side, row):
    ends, total = [], 0
    for j in range(lens.shape[2]):
        total = total + lens[side, row, j]
        ends.append(total)
    return ends


def sentence_of(ends, position):
    found = jnp.zeros(position.shape, jnp.int32)
    for end in ends:
        found = found + (position >= end).astype(jnp.int32)
    return found


def fill_mask(mask, lens, query_side, key_side, causal):
    seq_len = mask.shape[1]
    row_count, sents = lens.shape[1:]
    q_pos = lax.broadcasted_iota(jnp.int32, (seq_len, seq_len), 0)
    k_pos = lax.broadcasted_iota(jnp.int32, (seq_len, seq_len), 1)
    for r in range(row_count):
        q_ids = sentence_of(sentence_ends(lens, query_side, r), q_pos)
        k_ids = sentence_of(sentence_ends(lens, key_side, r), k_pos)
        same = jnp.where(q_ids == k_ids, 1, 0)
        if causal is not None:
            same = jnp.where(q_pos >= k_pos, same, jnp.where(causal, 0, same))
        allowed = jnp.where(q_ids == sents, 1, same)
        mask[r * seq_len : (r + 1) * seq_len] = allowed.astype(F32)


def both_heads(block, lane):
    even = (lane < HEAD_DIM).astype(BF16)
    return jnp.concatenate([block * even, block * (1 - even)], axis=0)


def one_of(stacked, lane):
    keys = stacked.shape[0] // 2
    return jnp.where(lane < HEAD_DIM, stacked[:keys], stacked[keys:])


def for_pairs(mask, step):
    seq_len = mask.shape[1]
    pairs = HEADS // 2

    def turn(i, carried):
        row, pair = i // pairs, lax.rem(i, pairs)
        rows = pl.ds(pl.multiple_of(row * seq_len, seq_len), seq_len)
        step(rows, lambda first: pl.ds(pl.multiple_of(first + pair * PAIR, PAIR), PAIR))
        return carried

    lax.fori_loop(0, mask.shape[0] // seq_len * pairs, turn, 0, unroll=UNROLL_PAIRS)


def attend_forward(query, keys, values, mask, out, lse):
    seq_len = mask.shape[1]
    lane = lax.broadcasted_iota(jnp.int32, (1, PAIR), 1)
    (q_ref, q_at), (k_ref, k_at), (v_ref, v_at) = query, keys, values

    def step(rows, lanes):
        q = q_ref[rows, lanes(q_at)]
        k2 = both_heads(k_ref[rows, lanes(k_at)], lane)
        v2 = both_heads(v_ref[rows, lanes(v_at)], lane)
        scores = dot_nt(q, k2) * HEAD_DIM ** (-0.5)
        probs, logs = [], []
        for half in range(2):
            part = scores[:, half * seq_len : (half + 1) * seq_len]
            part = jnp.where(mask[rows] > 0.0, part, MASK_FILL)
            top = jnp.max(part, axis=-1, keepdims=True)
            raised = jnp.exp(part - top)
            total = jnp.sum(raised, axis=-1, keepdims=True)
            probs.append((raised * (1.0 / total)).astype(BF16))
            logs.append(top + jnp.log(total))
        lse[rows, lanes(0)] = jnp.where(lane < HEAD_DIM, logs[0], logs[1])
        out[rows, lanes(0)] = dot(jnp.concatenate(probs, axis=1), v2).astype(BF16)

    for_pairs(mask, step)


def attend_backward(query, keys, values, mask, lse, grad_out, grad_q, grad_k, grad_v):
    seq_len = mask.shape[1]
    lane = lax.broadcasted_iota(jnp.int32, (1, PAIR), 1)
    scale = HEAD_DIM ** (-0.5)
    (q_ref, q_at), (k_ref, k_at), (v_ref, v_at) = query, keys, values
    (gq_ref, gq_at), (gk_ref, gk_at), (gv_ref, gv_at) = grad_q, grad_k, grad_v

    def step(rows, lanes):
        q = q_ref[rows, lanes(q_at)]
        k2 = both_heads(k_ref[rows, lanes(k_at)], lane)
        v2 = both_heads(v_ref[rows, lanes(v_at)], lane)
        go = grad_out[rows, lanes(0)]
        logs = lse[rows, lanes(0)]
        scores = dot_nt(q, k2) * scale
        grad_probs = dot_nt(go, v2)
        probs, grad_scores = [], []
        for half in range(2):
            cut = slice(half * seq_len, (half + 1) * seq_len)
            part = jnp.where(mask[rows] > 0.0, scores[:, cut], MASK_FILL)
            prob = jnp.exp(part - logs[:, half * HEAD_DIM : half * HEAD_DIM + 1])
            gp = grad_probs[:, cut]
            inner = jnp.sum(prob * gp, axis=-1, keepdims=True)
            probs.append(prob.astype(BF16))
            grad_scores.append((prob * (gp - inner)).astype(BF16))
        probs = jnp.concatenate(probs, axis=1)
        grad_scores = jnp.concatenate(grad_scores, axis=1)
        gv_ref[rows, lanes(gv_at)] = one_of(dot_tn(probs, go), lane).astype(BF16)
        gq_ref[rows, lanes(gq_at)] = (dot(grad_scores, k2) * scale).astype(BF16)
        gk_ref[rows, lanes(gk_at)] = (one_of(dot_tn(grad_scores, q), lane) * scale).astype(BF16)

    for_pairs(mask, step)


def small(vecs, which, width):
    pieces = vecs.shape[1] // width
    at = (which if which >= 0 else pieces + which) * width
    return vecs[:, at : at + width].astype(F32)


def set_small(vecs, which, width, value):
    pieces = vecs.shape[1] // width
    at = (which if which >= 0 else pieces + which) * width
    vecs[:, at : at + width] = value


def where_am_i():
    return lax.axis_index("section"), lax.rem(lax.axis_index("dp"), 2)


def for_chunks(count, width, step):
    def turn(j, carried):
        step(j, pl.ds(pl.multiple_of(j * width, width), width))
        return carried

    lax.fori_loop(0, count, turn, 0, unroll=UNROLL_CHUNKS)


def ffn_forward(normed, w_in, w_out, vecs, act, slope, total):
    width = normed.shape[1]
    low = normed.astype(BF16)
    total[...] = normed + small(vecs, BIAS_OUT, width)

    def step(j, cut):
        pre = dot(low, w_in[cut]) + vecs[:, cut]
        value, derivative = act_parts(pre)
        value = value.astype(BF16)
        act[:, cut] = value
        slope[:, cut] = derivative.astype(slope.dtype)
        total[...] += dot(value, w_out[cut])

    for_chunks(w_in.shape[0] // width, width, step)


def ffn_backward(grad_low, w_in, w_out, slope, grad_pre, vec_grads, total):
    width = grad_low.shape[1]

    def step(j, cut):
        grad = (dot_nt(grad_low, w_out[cut]) * slope[:, cut].astype(F32)).astype(BF16)
        grad_pre[:, cut] = grad
        vec_grads[:, cut] = jnp.sum(grad.astype(F32), axis=0, keepdims=True)
        total[...] += dot_nt(grad, w_in[cut])

    for_chunks(w_in.shape[0] // width, width, step)


def load(source, target, sem):
    copy = pltpu.make_async_copy(source, target, sem)
    copy.start()
    return copy


def forward_kernel(k):
    width = k.h1.shape[1]
    ffn = k.w_in.shape[0]
    sec, _ = where_am_i()
    get_lens = load(k.lengths, k.lens, k.sems.at[7])
    get_in = load(k.mats.at[: 3 * width], k.raw_attn, k.sems.at[0])
    get_x = load(k.x, k.x_here, k.sems.at[1])
    get_vecs = load(k.vectors, k.raw_vecs, k.sems.at[2])
    get_attn_out = load(k.mats.at[3 * width : 4 * width], k.w_attn_out, k.sems.at[3])
    get_ffn = load(k.mats.at[6 * width : 6 * width + ffn], k.raw_ffn, k.sems.at[4])
    get_out = load(k.mats.at[6 * width + ffn :], k.w_out, k.sems.at[5])
    get_cross = pltpu.make_async_copy(k.mats.at[4 * width : 6 * width], k.raw_cross, k.sems.at[6])

    @pl.when(sec == 1)
    def _():
        get_cross.start()

    get_lens.wait()
    fill_mask(k.mask, k.lens, sec, sec, sec == 1)
    k.go.mask.start()
    get_in.wait()
    split_rows(k.raw_attn, k.wide, 3, k.w_attn, 0)
    k.go.w_attn.start()
    get_x.wait()
    for j in range(3):
        part = dot(k.x_here[...], k.w_attn[j * width : (j + 1) * width])
        k.qkv[:, j * width : (j + 1) * width] = part.astype(BF16)
    k.go.qkv.start()
    attend_forward((k.qkv, 0), (k.qkv, width), (k.qkv, 2 * width), k.mask, k.mixed, k.lse)
    k.go.mixed.start()
    k.go.lse.start()
    get_vecs.wait()
    k.vecs[...] = k.raw_vecs[...].astype(F32)
    vecs = k.vecs
    get_attn_out.wait()
    k.go.w_attn_out.start()
    hidden = k.x_here[...].astype(F32) + dot(k.mixed[...], k.w_attn_out[...])
    k.pre1[...] = hidden
    k.go.pre1.start()
    k.h1[...] = norm_forward(hidden, small(vecs, GAIN1, width), small(vecs, SHIFT1, width))
    get_ffn.wait()
    split_rows(k.raw_ffn, k.wide, ffn // width, k.w_in, 0)
    get_out.wait()

    @pl.when(sec == 0)
    def _():
        ffn_forward(k.h1[...], k.w_in, k.w_out, vecs, k.act, k.slope, k.pre2)
        hidden = k.pre2[...]
        second = norm_forward(hidden, small(vecs, GAIN2, width), small(vecs, SHIFT2, width))
        k.h2[...] = second
        third = norm_forward(second, small(vecs, GAIN3, width), small(vecs, SHIFT3, width))
        k.memory[...] = third.astype(BF16)
        k.low[...] = third.astype(BF16)
        k.go.low.start()

    @pl.when(sec == 1)
    def _():
        k.low[...] = k.h1[...].astype(BF16)
        k.go.low.start()
        get_cross.wait()
        split_rows(k.raw_cross, k.wide, 2, k.w_cross, 0)
        k.qc[...] = dot(k.low[...], k.w_cross[:width]).astype(BF16)

    k.go.mask.wait()
    k.go.w_attn.wait()
    k.go.qkv.wait()
    k.go.mixed.wait()
    k.go.lse.wait()
    k.go.w_attn_out.wait()
    k.go.pre1.wait()
    k.go.low.wait()


def prepare_kernel(k):
    width = k.raw.shape[1]
    seq_len = k.mask.shape[1]
    sec, core = where_am_i()

    @pl.when(sec == 1)
    def _():
        get_cot = load(k.cot_all, k.raw_cot, k.sems.at[0])
        get_lens = load(k.lengths, k.lens, k.sems.at[1])
        k.raw[pl.ds(pl.multiple_of(core * width, width), width)] = k.cross_mine[...]
        k.raw[pl.ds(pl.multiple_of((1 - core) * width, width), width)] = k.cross_other[...]
        split_rows(k.raw, k.wide, 2, k.w_pairs, 0)
        get_lens.wait()
        fill_mask(k.mask, k.lens, 1, 0, None)
        get_cot.wait()
        position = lax.broadcasted_iota(jnp.int32, (seq_len, 1), 0)
        for r in range(k.lens.shape[1]):
            used = sentence_ends(k.lens, 1, r)[-1]
            rows = slice(r * seq_len, (r + 1) * seq_len)
            k.cot[rows] = jnp.where(position < used, k.raw_cot[rows].astype(F32), 0.0).astype(BF16)


def decoder_kernel(k):
    width = k.h1.shape[1]
    ffn = k.w_in.shape[0]
    vecs = k.vecs
    sec, _ = where_am_i()

    @pl.when(sec == 0)
    def _():
        k.layer_out[...] = k.near_memory[...]
        k.go.layer_out.start()

    @pl.when(sec == 1)
    def _():
        for j in range(2):
            part = dot(k.memory[...], k.w_pairs[j * width : (j + 1) * width])
            k.pairs[:, j * width : (j + 1) * width] = part.astype(BF16)
        attend_forward((k.qc, 0), (k.pairs, 0), (k.pairs, width), k.mask, k.mixed, k.lse)
        k.go.mixed.start()
        hidden2 = k.h1[...] + dot(k.mixed[...], k.w_cross[width:])
        gain2, shift2 = small(vecs, GAIN2, width), small(vecs, SHIFT2, width)
        normed2 = norm_forward(hidden2, gain2, shift2)
        k.low2[...] = normed2.astype(BF16)
        k.hidden2[...] = hidden2
        ffn_forward(normed2, k.w_in, k.w_out, vecs, k.act, k.slope, k.total)
        hidden3 = k.total[...]
        gain3, shift3 = small(vecs, GAIN3, width), small(vecs, SHIFT3, width)
        k.layer_out[...] = norm_forward(hidden3, gain3, shift3).astype(BF16)
        k.go.layer_out.start()
        grad_sum3, d_gain, d_shift = norm_backward(hidden3, gain3, k.cot[...].astype(F32))
        set_small(k.vec_grads, GAIN3, width, d_gain)
        set_small(k.vec_grads, SHIFT3, width, d_shift)
        grad_low = grad_sum3.astype(BF16)
        k.grad_ffn[...] = grad_low
        set_small(
            k.vec_grads, BIAS_OUT, width, jnp.sum(grad_low.astype(F32), axis=0, keepdims=True)
        )
        k.total[...] = grad_sum3
        ffn_backward(grad_low, k.w_in, k.w_out, k.slope, k.side, k.vec_grads, k.total)
        grad_hidden2, d_gain, d_shift = norm_backward(k.hidden2[...], gain2, k.total[...])
        set_small(k.vec_grads, GAIN2, width, d_gain)
        set_small(k.vec_grads, SHIFT2, width, d_shift)
        k.grad_sum2[...] = grad_hidden2
        low = grad_hidden2.astype(BF16)
        k.right[:, width:] = low
        k.grad_mixed[...] = dot_nt(low, k.w_cross[width:]).astype(BF16)
        attend_backward(
            (k.qc, 0), (k.pairs, 0), (k.pairs, width), k.mask, k.lse, k.grad_mixed,
            (k.right, 0), (k.grad_pairs, 0), (k.grad_pairs, width),
        )
        k.go.right.start()
        k.grad_qc[...] = k.right[:, :width]
        back = dot_nt(k.grad_pairs[:, :width], k.w_pairs[:width])
        back = back + dot_nt(k.grad_pairs[:, width:], k.w_pairs[width:])
        k.grad_memory[...] = back.astype(BF16)
        k.go.mixed.wait()
        k.go.right.wait()

    k.go.layer_out.wait()


def ffn_weight_grads(k, act, low, grad_pre, grad_ffn):
    width = k.h1.shape[1]
    ffn = k.w_in.shape[0]
    chunks = ffn // width

    def step(j, cut):
        put_part(k.wide, j, chunks, dot_tn(low[...], grad_pre[:, cut]))
        there = pl.ds(pl.multiple_of(ffn + j * width, width), width)
        k.flat[there] = dot_tn(act[:, cut], grad_ffn[...]).astype(BF16)

    for_chunks(chunks, width, step)


def put_sides(k, first, vec_grads, first_owner, core):
    width = k.flat.shape[1]
    if len(k.keep.shape) == 2:
        k.keep[...] = k.flat[first : first + k.keep.shape[0]]
        return
    count, rows, _ = k.keep.shape
    rows -= TAIL
    share = vec_grads.shape[1] // (4 * count)

    def tail(at):
        owner = first_owner + at
        row = vec_grads[:, owner * share : (owner + 1) * share]
        row = jnp.concatenate([row, jnp.zeros((1, width - share), F32)], axis=1)
        return jnp.broadcast_to(row, (TAIL, width)).astype(BF16)

    for at in range(count):
        mine = first + (2 * at + core) * rows
        other = first + (2 * at + 1 - core) * rows
        k.keep[at, :rows] = k.flat[pl.ds(pl.multiple_of(mine, TAIL), rows)]
        k.give[at, :rows] = k.flat[pl.ds(pl.multiple_of(other, TAIL), rows)]

        @pl.when(core == 0)
        def _(at=at):
            k.keep[at, rows:] = tail(2 * at)
            k.give[at, rows:] = tail(2 * at + 1)

        @pl.when(core == 1)
        def _(at=at):
            k.keep[at, rows:] = tail(2 * at + 1)
            k.give[at, rows:] = tail(2 * at)


def backward_kernel(k):
    width = k.h1.shape[1]
    ffn = k.w_in.shape[0]
    vecs = k.vecs
    sec, core = where_am_i()
    wanted = ("pre1", "w_attn_out", "mask", "lse", "qkv", "w_attn")
    wanted_next = ("x", "mixed", "low", "right", "cross_mixed")
    coming = [
        load(getattr(k, "far_" + name), getattr(k, name), k.sems.at[at])
        for at, name in enumerate(wanted + wanted_next)
    ]

    @pl.when(sec == 0)
    def _():
        grad, d_gain, d_shift = norm_backward(
            k.h2[...], small(vecs, GAIN3, width), k.grad_memory[...].astype(F32)
        )
        set_small(k.vec_grads, GAIN3, width, d_gain)
        set_small(k.vec_grads, SHIFT3, width, d_shift)
        total, d_gain, d_shift = norm_backward(k.pre2[...], small(vecs, GAIN2, width), grad)
        set_small(k.vec_grads, GAIN2, width, d_gain)
        set_small(k.vec_grads, SHIFT2, width, d_shift)
        grad_low = total.astype(BF16)
        k.grad_ffn[...] = grad_low
        set_small(
            k.vec_grads, BIAS_OUT, width, jnp.sum(grad_low.astype(F32), axis=0, keepdims=True)
        )
        k.low1[...] = k.h1[...].astype(BF16)
        k.grad_h1[...] = total
        ffn_backward(grad_low, k.w_in, k.w_out, k.side, k.grad_pre, k.vec_grads, k.grad_h1)
        ffn_weight_grads(k, k.act, k.low1, k.grad_pre, k.grad_ffn)

    @pl.when(sec == 1)
    def _():
        k.vec_grads[...] = k.dec_vec_grads[...]
        k.grad_h1[...] = k.grad_sum2[...] + dot_nt(k.grad_qc[...], k.w_cross[:width])
        ffn_weight_grads(k, k.act, k.low2, k.side, k.dec_grad_ffn)

    take_parts(k.wide, ffn, k.flat, 0)
    early = k.early.shape[0]
    k.early[...] = k.flat[:early]
    for copy in coming:
        copy.wait()
    grad, d_gain, d_shift = norm_backward(k.pre1[...], small(vecs, GAIN1, width), k.grad_h1[...])
    set_small(k.vec_grads, GAIN1, width, d_gain)
    set_small(k.vec_grads, SHIFT1, width, d_shift)
    put_sides(k, early, k.vec_grads, 2 * k.keep.shape[0], core)
    low = grad.astype(BF16)
    k.grad_attn[...] = low
    k.grad_mixed[...] = dot_nt(low, k.w_attn_out[...]).astype(BF16)
    attend_backward(
        (k.qkv, 0), (k.qkv, width), (k.qkv, 2 * width), k.mask, k.lse, k.grad_mixed,
        (k.grad_qkv, 0), (k.grad_qkv, width), (k.grad_qkv, 2 * width),
    )
    for j in range(3):
        cut = slice(j * width, (j + 1) * width)
        grad = grad + dot_nt(k.grad_qkv[:, cut], k.w_attn[cut])
    k.grad_x[...] = grad
    k.go.grad_x.start()
    k.go.grad_x.wait()


def attn_grad_kernel(k):
    width = k.x.shape[1]
    sec, core = where_am_i()

    def step(j, cut):
        put_part(k.wide, j, 3, dot_tn(k.x[...], k.grad_qkv[:, cut]))

    for_chunks(3, width, step)
    take_parts(k.wide, 3 * width, k.flat, 0)
    k.flat[3 * width : 4 * width] = dot_tn(k.mixed[...], k.grad_attn[...]).astype(BF16)

    @pl.when(sec == 0)
    def _():
        for j in range(2):
            cut = slice(j * width, (j + 1) * width)
            put_part(k.wide, j, 2, dot_tn(k.low[...], k.grad_pairs[:, cut]))

    @pl.when(sec == 1)
    def _():
        put_part(k.wide, 0, 2, dot_tn(k.low[...], k.right[:, :width]))
        put_part(k.wide, 1, 2, dot_tn(k.cross_mixed[...], k.right[:, width:]))

    take_parts(k.wide, 2 * width, k.flat, 4 * width)
    k.flat[6 * width :] = k.early[...]
    put_sides(k, 0, k.vec_grads, 0, core)


class Refs(types.SimpleNamespace):
    pass


def run_kernel(kernel, name, hbm, vmem, outs, far_outs, scratch, loads, spare, reuse=(), work=10**10, smem=None):
    smem = smem or {}
    ins = {**smem, **hbm, **vmem}
    near = {n: pltpu.VMEM(*spec) for n, spec in far_outs.items()}
    near.update({n: pltpu.VMEM(*spec) if isinstance(spec, tuple) else spec for n, spec in scratch.items()})
    names = [*ins, *outs, *far_outs, *near, "sems", "leave_sems"]

    def run(*refs):
        k = Refs(**dict(zip(names, refs)))
        first = len(ins) + len(outs)
        k.go = Refs()
        for at, n in enumerate(far_outs):
            copy = pltpu.make_async_copy(getattr(k, n), refs[first + at], k.leave_sems.at[at])
            setattr(k.go, n, copy)
        kernel(k)

    results = pl.pallas_call(
        run,
        name=name,
        in_specs=[SMEM] * len(smem) + [HBM] * len(hbm) + [VMEM] * len(vmem),
        out_specs=[VMEM] * len(outs) + [HBM] * len(far_outs),
        out_shape=[pltpu.VMEM(*spec) for spec in outs.values()]
        + [pltpu.HBM(*spec) for spec in far_outs.values()],
        scratch_shapes=[
            *near.values(),
            pltpu.SemaphoreType.DMA((max(loads, 1),)),
            pltpu.SemaphoreType.DMA((max(len(far_outs), 1),)),
        ],
        compiler_params=pltpu.CompilerParams(
            vmem_limit_bytes=int(spare * 2**20)
            + sum(math.prod(b.shape) * jnp.dtype(b.dtype).itemsize for b in near.values())
        ),
        input_output_aliases={[*ins].index(old): [*outs].index(new) for old, new in reuse},
        cost_estimate=pl.CostEstimate(flops=work, bytes_accessed=1, transcendentals=0),
    )(
        *smem.values(),
        *[pltpu.with_memory_space_constraint(array, pltpu.HBM) for array in hbm.values()],
        *[pltpu.with_memory_space_constraint(array, pltpu.VMEM) for array in vmem.values()],
    )
    return Refs(**dict(zip([*outs, *far_outs], results)))


SMEM = pl.BlockSpec(memory_space=pltpu.SMEM)
HBM = pl.BlockSpec(memory_space=pltpu.HBM)
VMEM = pl.BlockSpec(memory_space=pltpu.VMEM)
ANY = pl.BlockSpec(memory_space=pl.ANY)


def swapped(array, axis, bit):
    devices = lax.axis_size(axis)
    return lax.ppermute(array, axis, [(i, i ^ bit) for i in range(devices)])


def held_until(array, *others):
    return lax.optimization_barrier((array, *others))[0]


def own_bit(bit):
    return (lax.axis_index("dp") >> bit) & 1


def core_sum(k, z, y, cut):
    return k.keep[2 * z + y, cut].astype(F32) + k.from_core[2 * z + y, cut].astype(F32)


class Phase:
    def __init__(self, keep, from_core, cuts):
        self.keep, self.from_core, self.cuts = keep, from_core, cuts
        self.width = keep.shape[2]

    def for_y(self):
        def kernel(k):
            y = own_bit(1)
            for at, cut in enumerate(self.cuts):
                for z in range(2):
                    getattr(k, f"out{at}")[z] = core_sum(k, z, 1 - y, cut).astype(BF16)

        outs = {
            f"out{at}": ((2, cut.stop - cut.start, self.width), BF16)
            for at, cut in enumerate(self.cuts)
        }
        ins = dict(keep=self.keep, from_core=self.from_core)
        return [*vars(run_kernel(kernel, "for_y", {}, ins, outs, {}, {}, 0, 4, work=10**8)).values()]

    def for_z(self, at, from_y):
        cut = self.cuts[at]

        def kernel(k):
            y, z = own_bit(1), own_bit(2)
            k.give[...] = (core_sum(k, 1 - z, y, cut) + k.from_y[1 - z].astype(F32)).astype(BF16)
            k.mine[...] = core_sum(k, z, y, cut) + k.from_y[z].astype(F32)

        shape = (cut.stop - cut.start, self.width)
        outs = dict(give=(shape, BF16), mine=(shape, F32))
        ins = dict(keep=self.keep, from_core=self.from_core, from_y=from_y)
        return [*vars(run_kernel(kernel, "for_z", {}, ins, outs, {}, {}, 0, 4, work=10**8)).values()]


def for_far_z(high, from_high, low, from_low):
    def kernel(k):
        upper = k.high[...] + k.from_high[...].astype(F32)
        lower = k.low[...] + k.from_low[...].astype(F32)

        @pl.when(own_bit(3) == 0)
        def _():
            k.give[...] = upper.astype(BF16)
            k.mine[...] = lower

        @pl.when(own_bit(3) == 1)
        def _():
            k.give[...] = lower.astype(BF16)
            k.mine[...] = upper

    ins = dict(high=high, from_high=from_high, low=low, from_low=from_low)
    outs = dict(give=(high.shape, BF16), mine=(high.shape, F32))
    return [*vars(run_kernel(kernel, "for_far_z", {}, ins, outs, {}, {}, 0, 4, work=10**8)).values()]


def sum_over_dp(high, y_high, low, y_low):
    pairs = []
    for at in range(len(high.cuts)):
        z_high, mine_high = high.for_z(at, swapped(y_high[at], "dp", 2))
        z_low, mine_low = low.for_z(at, swapped(y_low[at], "dp", 2))
        give, mine = for_far_z(
            mine_high, swapped(z_high, "dp", 4), mine_low, swapped(z_low, "dp", 4)
        )
        pairs.append((mine, swapped(give, "dp", 8)))
    return pairs


def adam_of(grad, master, mean_old, square_old, step):
    mean_new = 0.9 * mean_old + 0.1 * grad
    square_new = 0.98 * square_old + 0.02 * grad * grad
    rate = step.shape[1] ** (-0.5) * jnp.minimum(lax.rsqrt(step), step * WARMUP_STEPS ** (-1.5))
    mean_share = 1.0 - jnp.exp(step * math.log(0.9))
    square_share = 1.0 - jnp.exp(step * math.log(0.98))
    fixed_mean = mean_new * (1.0 / mean_share)
    fixed_square = square_new * (1.0 / square_share)
    change = -rate * fixed_mean / (jnp.sqrt(fixed_square) + ADAM_EPS)
    return change, mean_new, square_new, master + change


def adam_kernel(k, full):
    width = k.master.shape[1]
    share = k.vec_master.shape[1]
    step = jnp.full((1, width), k.step[0], jnp.int32).astype(F32)
    first = 0
    vec_grad = None
    count = len([name for name in vars(k) if name.startswith("mine")])
    for at in range(count):
        rows = getattr(k, f"mine{at}").shape[0]
        grad = getattr(k, f"mine{at}")[...] + getattr(k, f"got{at}")[...].astype(F32)
        if at == count - 1:
            rows -= TAIL
            vec_grad, grad = grad[rows : rows + 1], grad[:rows]
        here = slice(first, first + rows)
        parts = adam_of(grad, k.master[here], k.mean[here], k.square[here], step)
        if full:
            k.grad[here] = grad
            k.change[here], k.mean_new[here], k.square_new[here] = parts[:3]
        else:
            k.own[here] = parts[3].astype(BF16)
        first += rows
    pad = jnp.zeros((1, width - share), F32)

    def padded(ref):
        return jnp.concatenate([ref[...], pad], axis=1)

    parts = adam_of(
        vec_grad, padded(k.vec_master), padded(k.vec_mean), padded(k.vec_square), step
    )
    if full:
        k.vec_grad[...] = vec_grad[:, :share]
        k.vec_change[...] = parts[0][:, :share]
        k.vec_mean_new[...] = parts[1][:, :share]
        k.vec_square_new[...] = parts[2][:, :share]
        for copy in vars(k.go).values():
            copy.start()
        for copy in vars(k.go).values():
            copy.wait()
    else:
        k.own[first:] = jnp.broadcast_to(parts[3], (TAIL, width)).astype(BF16)


def adam(pairs, state, step, full):
    shape, vec_shape = state.master.shape, state.vec_master.shape
    ins = {f"mine{at}": mine for at, (mine, _) in enumerate(pairs)}
    ins.update({f"got{at}": got for at, (_, got) in enumerate(pairs)})
    outs, far = {}, {}
    if full:
        far = dict.fromkeys(("grad", "change", "mean_new", "square_new"), (shape, F32))
        far.update({"vec_" + name: (vec_shape, F32) for name in far})
    else:
        outs = {"own": ((shape[0] + TAIL, shape[1]), BF16)}
    return run_kernel(
        lambda k: adam_kernel(k, full), "adam_outputs" if full else "adam", {},
        {**ins, **vars(state)}, outs, far, {}, 0, 6, work=10**9, smem={"step": step},
    )


def place_blocks(pieces, share, rows_all, before=None):
    masks = [mask for mask, _ in pieces]
    arrays = [array for _, array in pieces]
    width = arrays[0].shape[1]
    extra = [] if before is None else [*before]

    def kernel(*refs):
        ins, (target, tails, sems) = refs[: len(arrays)], refs[-3:]
        me = lax.axis_index("dp")
        copies = []
        for at, (mask, ref) in enumerate(zip(masks, ins)):
            owner = me ^ mask
            there = pl.ds(pl.multiple_of(owner * share, share), share)
            copies.append(load(ref.at[:share], target.at[there], sems.at[at]))
        if extra:
            tails[...] = refs[len(arrays) + 1][...]
        for mask, ref in zip(masks, ins):
            tails[me ^ mask] = ref[share:]
        for copy in copies:
            copy.wait()

    return pl.pallas_call(
        kernel,
        name="place_blocks",
        in_specs=[VMEM] * len(arrays) + [HBM, VMEM][: len(extra)],
        out_specs=[HBM, VMEM],
        out_shape=[
            pltpu.HBM((rows_all, width), BF16),
            pltpu.VMEM((rows_all // share, TAIL, width), BF16),
        ],
        scratch_shapes=[pltpu.SemaphoreType.DMA((len(arrays),))],
        input_output_aliases={len(arrays): 0} if extra else {},
        compiler_params=pltpu.CompilerParams(vmem_limit_bytes=4 * 2**20),
        cost_estimate=pl.CostEstimate(flops=10**9, bytes_accessed=1, transcendentals=0),
    )(*[pltpu.with_memory_space_constraint(array, pltpu.VMEM) for array in arrays], *extra)


def gather_blocks(own, share, rows_all, meanwhile):
    def go(array, bit):
        return swapped(array, "dp", bit)

    got = {0: own}
    got[2], got[4], got[8] = go(own, 2), go(own, 4), go(own, 8)
    got[2], got[4] = lax.optimization_barrier((got[2], got[4]))
    got[6] = go(got[4], 2)
    got[6], got[8] = lax.optimization_barrier((got[6], got[8]))
    got[12], got[10] = go(got[8], 4), go(got[8], 2)
    got[12], got[10] = lax.optimization_barrier((got[12], got[10]))
    got[14] = go(got[12], 2)
    early, late = [0, 2, 4, 6, 8], [12, 10, 14]
    for mask in early:
        got[mask | 1] = go(got[mask], 1)
    first = place_blocks([(m | c, got[m | c]) for m in early for c in (0, 1)], share, rows_all)
    got[14] = held_until(got[14], *first, meanwhile)
    for mask in late:
        got[mask | 1] = go(got[mask], 1)
    return place_blocks([(m | c, got[m | c]) for m in late for c in (0, 1)], share, rows_all, first)


def body(
    inputs,
    lengths,
    cotangent,
    matrices,
    vectors,
    master_matrices,
    master_vectors,
    matrix_mean,
    matrix_square,
    vector_mean,
    vector_square,
    adam_step,
):
    row_count, seq_len, width = inputs.shape[1:]
    tokens = row_count * seq_len
    rows_all, vec_all = matrices.shape[1], vectors.shape[1]
    ffn = (rows_all - 6 * width) // 2
    half = rows_all // 2
    ranks = lax.axis_size("dp")
    share, vec_share = rows_all // ranks, vec_all // ranks
    by_swaps = ranks == 16 and share % 32 == 0
    block = (ranks // 4, share + TAIL, width) if by_swaps else (half, width)
    me = lax.axis_index("dp")

    x = inputs.reshape(tokens, width)
    cot = cotangent.reshape(tokens, width)
    mats = matrices.reshape(rows_all, width)
    lens_here = pltpu.SMEM(lengths.shape, jnp.int32)

    def spec(columns, dtype):
        return ((tokens, columns), dtype)

    full, low, deep = spec(width, F32), spec(width, BF16), spec(ffn, BF16)
    square, mask = ((width, width), BF16), spec(seq_len, F32)
    double, lse, w_ffn = ((2 * width, width), BF16), spec(HEADS // 2 * PAIR, F32), ((ffn, width), BF16)
    all_vecs, triple = ((1, vec_all), F32), spec(3 * width, BF16)
    sided = dict(keep=(block, BF16))
    if by_swaps:
        sided["give"] = (block, BF16)
    early = ((half - 6 * width, width), BF16)

    def wide(rows):
        return ((width // LANES, rows, LANES), F32)

    cross_half = lax.dynamic_slice(mats, ((4 + (me & 1)) * width, 0), (width, width), allow_negative_indices=False)
    cross_mine = swapped(cross_half, "section", 1)
    f = run_kernel(
        forward_kernel, "forward", dict(mats=mats, x=x, vectors=vectors, lengths=lengths), {},
        dict(
            h1=full, w_in=w_ffn, act=deep, slope=deep, pre2=full, h2=full,
            memory=low, w_cross=double, qc=low, w_out=w_ffn, vecs=all_vecs,
        ),
        dict(
            qkv=triple, lse=lse, mixed=low, pre1=full, mask=mask, w_attn_out=square,
            w_attn=((3 * width, width), BF16), low=low,
        ),
        dict(
            raw_attn=((3 * width, width), BF16), raw_cross=double, raw_ffn=w_ffn,
            x_here=low, wide=wide(ffn), raw_vecs=((1, vec_all), BF16), lens=lens_here,
        ),
        8, 10,
    )
    memory_far = swapped(f.memory, "section", 1)
    cross_mine = held_until(cross_mine, f.memory)
    cross_other = swapped(cross_mine, "dp", 1)
    p = run_kernel(
        prepare_kernel, "prepare", dict(cot_all=cot, lengths=lengths),
        dict(cross_mine=cross_mine, cross_other=cross_other),
        dict(w_pairs=double, mask=mask, cot=low), {},
        dict(raw=double, wide=wide(2 * width), raw_cot=low, lens=lens_here),
        2, 4,
    )
    d = run_kernel(
        decoder_kernel, "decoder", {},
        dict(
            memory=memory_far, near_memory=f.memory, **vars(p), enc_act=f.act,
            enc_slope=f.slope,
            w_cross=f.w_cross, qc=f.qc, h1=f.h1, w_in=f.w_in, w_out=f.w_out, vecs=f.vecs,
        ),
        dict(
            grad_memory=low, grad_pairs=spec(2 * width, BF16), act=deep,
            side=deep, grad_ffn=low, low2=low, grad_qc=low, grad_sum2=full,
            vec_grads=all_vecs,
        ),
        dict(layer_out=low, mixed=low, right=spec(2 * width, BF16)),
        dict(pairs=spec(2 * width, BF16), slope=spec(ffn, F32), lse=lse, grad_mixed=low, total=full, hidden2=full),
        0, 11, (("enc_act", "act"), ("enc_slope", "side")),
    )
    grad_memory_far = swapped(d.grad_memory, "section", 1)
    grad_pairs_far = swapped(d.grad_pairs, "section", 1)
    ahead = dict(
        pre1=full, w_attn_out=square, mask=mask, lse=lse, qkv=triple,
        w_attn=((3 * width, width), BF16),
    )
    s = run_kernel(
        backward_kernel, "backward",
        dict(
            **{"far_" + name: getattr(f, name) for name in ahead},
            far_x=x, far_mixed=f.mixed, far_low=f.low, far_right=d.right,
            far_cross_mixed=d.mixed,
        ),
        dict(
            dec_grad_ffn=d.grad_ffn, dec_vec_grads=d.vec_grads,
            grad_memory=grad_memory_far, act=d.act, side=d.side, low2=d.low2, grad_qc=d.grad_qc, grad_sum2=d.grad_sum2,
            pre2=f.pre2, h2=f.h2, h1=f.h1, w_in=f.w_in, w_out=f.w_out, w_cross=f.w_cross, vecs=f.vecs,
        ),
        dict(
            vec_grads=all_vecs, early=early, **sided, grad_attn=low, grad_qkv=triple,
            x=low, mixed=low, low=low, right=spec(2 * width, BF16), cross_mixed=low,
        ),
        dict(grad_x=full),
        dict(
            grad_pre=deep, grad_ffn=low, low1=low, wide=wide(ffn), grad_h1=full,
            flat=((2 * ffn, width), BF16), grad_mixed=low, **ahead,
        ),
        11, 9, work=4 * 10**10,
    )
    grad_qkv = s.grad_qkv
    if by_swaps:
        first_rows = (share + TAIL) // 2 // 16 * 16
        cuts = [slice(0, first_rows), slice(first_rows, share + TAIL)]
        high = Phase(s.keep, swapped(s.give, "dp", 1), cuts)
    a = run_kernel(
        attn_grad_kernel, "attn_grad", {},
        dict(
            grad_qkv=grad_qkv, vec_grads=s.vec_grads, early=s.early, grad_pairs=grad_pairs_far,
            x=s.x, grad_attn=s.grad_attn, mixed=s.mixed, low=s.low, right=s.right, cross_mixed=s.cross_mixed,
        ),
        sided, {}, dict(wide=wide(3 * width), flat=((half, width), BF16)), 0, 4,
    )

    state = Refs(master=master_matrices[0], mean=matrix_mean[0], square=matrix_square[0])
    state = Refs(**vars(state), vec_master=master_vectors, vec_mean=vector_mean, vec_square=vector_square)
    if by_swaps:
        low_half = Phase(a.keep, swapped(a.give, "dp", 1), cuts)
        pairs = sum_over_dp(high, high.for_y(), low_half, low_half.for_y())
        own = adam(pairs, state, adam_step, False).own
        result = adam(pairs, state, adam_step, True)
        new_mat, tails = gather_blocks(own, share, rows_all, result.change)
        new_vec = tails[:, 0, :vec_share].reshape(1, vec_all)
    else:
        whole = jnp.concatenate([a.keep, s.keep], axis=0)
        grad = lax.psum_scatter(whole, "dp", scatter_dimension=0, tiled=True).astype(F32)
        vec_grad = lax.dynamic_slice(
            lax.psum(s.vec_grads, "dp"), (0, me * vec_share), (1, vec_share)
        )
        step = jnp.full((1, width), adam_step[0].astype(F32))
        parts = adam_of(grad, state.master, state.mean, state.square, step)
        vec_step = jnp.full((1, width), adam_step[0].astype(F32))
        pad = ((0, 0), (0, width - vec_share))
        vec_parts = [
            part[:, :vec_share]
            for part in adam_of(
                *[jnp.pad(v, pad) for v in (vec_grad, master_vectors, vector_mean, vector_square)],
                vec_step,
            )
        ]
        names = ("change", "mean_new", "square_new")
        result = dict(grad=grad, vec_grad=vec_grad, **dict(zip(names, parts)))
        result.update({"vec_" + name: part for name, part in zip(names, vec_parts)})
        result = Refs(**result)
        new_mat = lax.all_gather(parts[3].astype(BF16), "dp", axis=0, tiled=True)
        new_vec = lax.all_gather(vec_parts[3].astype(BF16), "dp", axis=1, tiled=True)
    return (
        d.layer_out.reshape(1, row_count, seq_len, width),
        s.grad_x.reshape(1, row_count, seq_len, width),
        result.grad[None],
        result.vec_grad,
        result.change[None],
        result.vec_change,
        result.mean_new[None],
        result.square_new[None],
        result.vec_mean_new,
        result.vec_square_new,
        new_mat[None],
        new_vec,
    )


def solution(mesh):
    return jax.shard_map(
        body,
        mesh=mesh,
        in_specs=(
            P("section", "dp", None, None),
            P(None, "dp", None),
            P("dp", None, None),
            P("section", None, None),
            P("section", None),
            P("section", "dp", None),
            P("section", "dp"),
            P("section", "dp", None),
            P("section", "dp", None),
            P("section", "dp"),
            P("section", "dp"),
            P(),
        ),
        out_specs=(
            P("section", "dp", None, None),
            P("section", "dp", None, None),
            P("section", "dp", None),
            P("section", "dp"),
            P("section", "dp", None),
            P("section", "dp"),
            P("section", "dp", None),
            P("section", "dp", None),
            P("section", "dp"),
            P("section", "dp"),
            P("section", None, None),
            P("section", None),
        ),
        check_vma=False,
    )
```

```python
import math
import types

import jax
import jax.numpy as jnp
from jax import lax
from jax.experimental import pallas as pl
from jax.experimental.pallas import tpu as pltpu
from jax.sharding import PartitionSpec as P

HEADS = 8
HEAD_DIM = 64
PAIR = 2 * HEAD_DIM
LANES = 128
TAIL = 16
UNROLL_PAIRS = 4
UNROLL_CHUNKS = True

MASK_FILL = -1e30
NORM_EPS = 1e-05
ADAM_EPS = 1e-09
WARMUP_STEPS = 4000.0

F32 = jnp.float32
BF16 = jnp.bfloat16

BIAS_OUT, GAIN1, SHIFT1, GAIN2, SHIFT2, GAIN3, SHIFT3 = range(-7, 0)


def dot(left, right):
    return jnp.dot(left, right, preferred_element_type=F32)


def dot_nt(left, right):
    return lax.dot_general(left, right, (((1,), (1,)), ((), ())), preferred_element_type=F32)


def dot_tn(left, right):
    return lax.dot_general(left, right, (((0,), (0,)), ((), ())), preferred_element_type=F32)


def norm_parts(hidden):
    centre = hidden - jnp.mean(hidden, axis=-1, keepdims=True)
    rstd = lax.rsqrt(jnp.mean(centre * centre, axis=-1, keepdims=True) + NORM_EPS)
    return centre * rstd, rstd


def norm_forward(hidden, gain, shift):
    return norm_parts(hidden)[0] * gain + shift


def norm_backward(hidden, gain, grad):
    normal, rstd = norm_parts(hidden)
    scaled = grad * gain
    inner = jnp.mean(scaled * normal, axis=-1, keepdims=True)
    grad_in = rstd * (scaled - jnp.mean(scaled, axis=-1, keepdims=True) - normal * inner)
    grad_gain = jnp.sum(grad * normal, axis=0, keepdims=True)
    grad_shift = jnp.sum(grad, axis=0, keepdims=True)
    return grad_in, grad_gain, grad_shift


def act_parts(pre):
    cdf = 0.5 * (1.0 + lax.erf(pre * (0.5**0.5)))
    pdf = jnp.exp(-0.5 * pre * pre) * 0.3989422804014327
    return pre * cdf, cdf + pre * pdf


def split_rows(raw, wide, parts, out, base):
    width = raw.shape[1]
    for c in range(width // LANES):
        cut = slice(c * LANES, (c + 1) * LANES)
        wide[c, : parts * width] = raw[: parts * width, cut].astype(F32)
        for j in range(parts):
            out[(base + j) * width : (base + j + 1) * width, cut] = wide[
                c, pl.ds(j, width, stride=parts), :
            ].astype(BF16)


def put_part(wide, j, parts, values):
    rows, width = values.shape
    for c in range(width // LANES):
        wide[c, pl.ds(j, rows, stride=parts), :] = values[:, c * LANES : (c + 1) * LANES]


def take_parts(wide, rows, out, first):
    for c in range(wide.shape[0]):
        out[first : first + rows, c * LANES : (c + 1) * LANES] = wide[c, :rows].astype(BF16)


def sentence_ends(lens, side, row):
    ends, total = [], 0
    for j in range(lens.shape[2]):
        total = total + lens[side, row, j]
        ends.append(total)
    return ends


def sentence_of(ends, position):
    found = jnp.zeros(position.shape, jnp.int32)
    for end in ends:
        found = found + (position >= end).astype(jnp.int32)
    return found


def fill_mask(mask, lens, query_side, key_side, causal):
    seq_len = mask.shape[1]
    row_count, sents = lens.shape[1:]
    q_pos = lax.broadcasted_iota(jnp.int32, (seq_len, seq_len), 0)
    k_pos = lax.broadcasted_iota(jnp.int32, (seq_len, seq_len), 1)
    for r in range(row_count):
        q_ids = sentence_of(sentence_ends(lens, query_side, r), q_pos)
        k_ids = sentence_of(sentence_ends(lens, key_side, r), k_pos)
        same = jnp.where(q_ids == k_ids, 1, 0)
        if causal is not None:
            same = jnp.where(q_pos >= k_pos, same, jnp.where(causal, 0, same))
        allowed = jnp.where(q_ids == sents, 1, same)
        mask[r * seq_len : (r + 1) * seq_len] = allowed.astype(F32)


def both_heads(block, lane):
    even = (lane < HEAD_DIM).astype(BF16)
    return jnp.concatenate([block * even, block * (1 - even)], axis=0)


def one_of(stacked, lane):
    keys = stacked.shape[0] // 2
    return jnp.where(lane < HEAD_DIM, stacked[:keys], stacked[keys:])


def for_pairs(mask, step):
    seq_len = mask.shape[1]
    pairs = HEADS // 2

    def turn(i, carried):
        row, pair = i // pairs, lax.rem(i, pairs)
        rows = pl.ds(pl.multiple_of(row * seq_len, seq_len), seq_len)
        step(rows, lambda first: pl.ds(pl.multiple_of(first + pair * PAIR, PAIR), PAIR))
        return carried

    lax.fori_loop(0, mask.shape[0] // seq_len * pairs, turn, 0, unroll=UNROLL_PAIRS)


def attend_forward(query, keys, values, mask, out, lse):
    seq_len = mask.shape[1]
    lane = lax.broadcasted_iota(jnp.int32, (1, PAIR), 1)
    (q_ref, q_at), (k_ref, k_at), (v_ref, v_at) = query, keys, values

    def step(rows, lanes):
        q = q_ref[rows, lanes(q_at)]
        k2 = both_heads(k_ref[rows, lanes(k_at)], lane)
        v2 = both_heads(v_ref[rows, lanes(v_at)], lane)
        scores = dot_nt(q, k2) * HEAD_DIM ** (-0.5)
        probs, logs = [], []
        for half in range(2):
            part = scores[:, half * seq_len : (half + 1) * seq_len]
            part = jnp.where(mask[rows] > 0.0, part, MASK_FILL)
            top = jnp.max(part, axis=-1, keepdims=True)
            raised = jnp.exp(part - top)
            total = jnp.sum(raised, axis=-1, keepdims=True)
            probs.append((raised * (1.0 / total)).astype(BF16))
            logs.append(top + jnp.log(total))
        lse[rows, lanes(0)] = jnp.where(lane < HEAD_DIM, logs[0], logs[1])
        out[rows, lanes(0)] = dot(jnp.concatenate(probs, axis=1), v2).astype(BF16)

    for_pairs(mask, step)


def attend_backward(query, keys, values, mask, lse, grad_out, grad_q, grad_k, grad_v):
    seq_len = mask.shape[1]
    lane = lax.broadcasted_iota(jnp.int32, (1, PAIR), 1)
    scale = HEAD_DIM ** (-0.5)
    (q_ref, q_at), (k_ref, k_at), (v_ref, v_at) = query, keys, values
    (gq_ref, gq_at), (gk_ref, gk_at), (gv_ref, gv_at) = grad_q, grad_k, grad_v

    def step(rows, lanes):
        q = q_ref[rows, lanes(q_at)]
        k2 = both_heads(k_ref[rows, lanes(k_at)], lane)
        v2 = both_heads(v_ref[rows, lanes(v_at)], lane)
        go = grad_out[rows, lanes(0)]
        logs = lse[rows, lanes(0)]
        scores = dot_nt(q, k2) * scale
        grad_probs = dot_nt(go, v2)
        probs, grad_scores = [], []
        for half in range(2):
            cut = slice(half * seq_len, (half + 1) * seq_len)
            part = jnp.where(mask[rows] > 0.0, scores[:, cut], MASK_FILL)
            prob = jnp.exp(part - logs[:, half * HEAD_DIM : half * HEAD_DIM + 1])
            gp = grad_probs[:, cut]
            inner = jnp.sum(prob * gp, axis=-1, keepdims=True)
            probs.append(prob.astype(BF16))
            grad_scores.append((prob * (gp - inner)).astype(BF16))
        probs = jnp.concatenate(probs, axis=1)
        grad_scores = jnp.concatenate(grad_scores, axis=1)
        gv_ref[rows, lanes(gv_at)] = one_of(dot_tn(probs, go), lane).astype(BF16)
        gq_ref[rows, lanes(gq_at)] = (dot(grad_scores, k2) * scale).astype(BF16)
        gk_ref[rows, lanes(gk_at)] = (one_of(dot_tn(grad_scores, q), lane) * scale).astype(BF16)

    for_pairs(mask, step)


def small(vecs, which, width):
    pieces = vecs.shape[1] // width
    at = (which if which >= 0 else pieces + which) * width
    return vecs[:, at : at + width].astype(F32)


def set_small(vecs, which, width, value):
    pieces = vecs.shape[1] // width
    at = (which if which >= 0 else pieces + which) * width
    vecs[:, at : at + width] = value


def where_am_i():
    return lax.axis_index("section"), lax.rem(lax.axis_index("dp"), 2)


def for_chunks(count, width, step):
    def turn(j, carried):
        step(j, pl.ds(pl.multiple_of(j * width, width), width))
        return carried

    lax.fori_loop(0, count, turn, 0, unroll=UNROLL_CHUNKS)


def ffn_forward(normed, w_in, w_out, vecs, act, slope, total):
    width = normed.shape[1]
    low = normed.astype(BF16)
    total[...] = normed + small(vecs, BIAS_OUT, width)

    def step(j, cut):
        pre = dot(low, w_in[cut]) + vecs[:, cut]
        value, derivative = act_parts(pre)
        value = value.astype(BF16)
        act[:, cut] = value
        slope[:, cut] = derivative.astype(slope.dtype)
        total[...] += dot(value, w_out[cut])

    for_chunks(w_in.shape[0] // width, width, step)


def ffn_backward(grad_low, w_in, w_out, slope, grad_pre, vec_grads, total):
    width = grad_low.shape[1]

    def step(j, cut):
        grad = (dot_nt(grad_low, w_out[cut]) * slope[:, cut].astype(F32)).astype(BF16)
        grad_pre[:, cut] = grad
        vec_grads[:, cut] = jnp.sum(grad.astype(F32), axis=0, keepdims=True)
        total[...] += dot_nt(grad, w_in[cut])

    for_chunks(w_in.shape[0] // width, width, step)


def load(source, target, sem):
    copy = pltpu.make_async_copy(source, target, sem)
    copy.start()
    return copy


def forward_kernel(k):
    width = k.h1.shape[1]
    ffn = k.w_in.shape[0]
    sec, _ = where_am_i()
    get_lens = load(k.lengths, k.lens, k.sems.at[7])
    get_in = load(k.mats.at[: 3 * width], k.raw_attn, k.sems.at[0])
    get_x = load(k.x, k.x_here, k.sems.at[1])
    get_vecs = load(k.vectors, k.raw_vecs, k.sems.at[2])
    get_attn_out = load(k.mats.at[3 * width : 4 * width], k.w_attn_out, k.sems.at[3])
    get_ffn = load(k.mats.at[6 * width : 6 * width + ffn], k.raw_ffn, k.sems.at[4])
    get_out = load(k.mats.at[6 * width + ffn :], k.w_out, k.sems.at[5])
    get_cross = pltpu.make_async_copy(k.mats.at[4 * width : 6 * width], k.raw_cross, k.sems.at[6])

    @pl.when(sec == 1)
    def _():
        get_cross.start()

    get_lens.wait()
    fill_mask(k.mask, k.lens, sec, sec, sec == 1)
    k.go.mask.start()
    get_in.wait()
    split_rows(k.raw_attn, k.wide, 3, k.w_attn, 0)
    k.go.w_attn.start()
    get_x.wait()
    for j in range(3):
        part = dot(k.x_here[...], k.w_attn[j * width : (j + 1) * width])
        k.qkv[:, j * width : (j + 1) * width] = part.astype(BF16)
    k.go.qkv.start()
    attend_forward((k.qkv, 0), (k.qkv, width), (k.qkv, 2 * width), k.mask, k.mixed, k.lse)
    k.go.mixed.start()
    k.go.lse.start()
    get_vecs.wait()
    k.vecs[...] = k.raw_vecs[...].astype(F32)
    vecs = k.vecs
    get_attn_out.wait()
    k.go.w_attn_out.start()
    hidden = k.x_here[...].astype(F32) + dot(k.mixed[...], k.w_attn_out[...])
    k.pre1[...] = hidden
    k.go.pre1.start()
    k.h1[...] = norm_forward(hidden, small(vecs, GAIN1, width), small(vecs, SHIFT1, width))
    get_ffn.wait()
    split_rows(k.raw_ffn, k.wide, ffn // width, k.w_in, 0)
    get_out.wait()

    @pl.when(sec == 0)
    def _():
        ffn_forward(k.h1[...], k.w_in, k.w_out, vecs, k.act, k.slope, k.pre2)
        hidden = k.pre2[...]
        second = norm_forward(hidden, small(vecs, GAIN2, width), small(vecs, SHIFT2, width))
        k.h2[...] = second
        third = norm_forward(second, small(vecs, GAIN3, width), small(vecs, SHIFT3, width))
        k.memory[...] = third.astype(BF16)
        k.low[...] = third.astype(BF16)
        k.go.low.start()

    @pl.when(sec == 1)
    def _():
        k.low[...] = k.h1[...].astype(BF16)
        k.go.low.start()
        get_cross.wait()
        split_rows(k.raw_cross, k.wide, 2, k.w_cross, 0)
        k.qc[...] = dot(k.low[...], k.w_cross[:width]).astype(BF16)

    k.go.mask.wait()
    k.go.w_attn.wait()
    k.go.qkv.wait()
    k.go.mixed.wait()
    k.go.lse.wait()
    k.go.w_attn_out.wait()
    k.go.pre1.wait()
    k.go.low.wait()


def prepare_kernel(k):
    width = k.raw.shape[1]
    seq_len = k.mask.shape[1]
    sec, core = where_am_i()

    @pl.when(sec == 1)
    def _():
        get_cot = load(k.cot_all, k.raw_cot, k.sems.at[0])
        get_lens = load(k.lengths, k.lens, k.sems.at[1])
        k.raw[pl.ds(pl.multiple_of(core * width, width), width)] = k.cross_mine[...]
        k.raw[pl.ds(pl.multiple_of((1 - core) * width, width), width)] = k.cross_other[...]
        split_rows(k.raw, k.wide, 2, k.w_pairs, 0)
        get_lens.wait()
        fill_mask(k.mask, k.lens, 1, 0, None)
        get_cot.wait()
        position = lax.broadcasted_iota(jnp.int32, (seq_len, 1), 0)
        for r in range(k.lens.shape[1]):
            used = sentence_ends(k.lens, 1, r)[-1]
            rows = slice(r * seq_len, (r + 1) * seq_len)
            k.cot[rows] = jnp.where(position < used, k.raw_cot[rows].astype(F32), 0.0).astype(BF16)


def decoder_kernel(k):
    width = k.h1.shape[1]
    ffn = k.w_in.shape[0]
    vecs = k.vecs
    sec, _ = where_am_i()

    @pl.when(sec == 0)
    def _():
        k.layer_out[...] = k.near_memory[...]
        k.go.layer_out.start()

    @pl.when(sec == 1)
    def _():
        for j in range(2):
            part = dot(k.memory[...], k.w_pairs[j * width : (j + 1) * width])
            k.pairs[:, j * width : (j + 1) * width] = part.astype(BF16)
        attend_forward((k.qc, 0), (k.pairs, 0), (k.pairs, width), k.mask, k.mixed, k.lse)
        k.go.mixed.start()
        hidden2 = k.h1[...] + dot(k.mixed[...], k.w_cross[width:])
        gain2, shift2 = small(vecs, GAIN2, width), small(vecs, SHIFT2, width)
        normed2 = norm_forward(hidden2, gain2, shift2)
        k.low2[...] = normed2.astype(BF16)
        k.hidden2[...] = hidden2
        ffn_forward(normed2, k.w_in, k.w_out, vecs, k.act, k.slope, k.total)
        hidden3 = k.total[...]
        gain3, shift3 = small(vecs, GAIN3, width), small(vecs, SHIFT3, width)
        k.layer_out[...] = norm_forward(hidden3, gain3, shift3).astype(BF16)
        k.go.layer_out.start()
        grad_sum3, d_gain, d_shift = norm_backward(hidden3, gain3, k.cot[...].astype(F32))
        set_small(k.vec_grads, GAIN3, width, d_gain)
        set_small(k.vec_grads, SHIFT3, width, d_shift)
        grad_low = grad_sum3.astype(BF16)
        k.grad_ffn[...] = grad_low
        set_small(
            k.vec_grads, BIAS_OUT, width, jnp.sum(grad_low.astype(F32), axis=0, keepdims=True)
        )
        k.total[...] = grad_sum3
        ffn_backward(grad_low, k.w_in, k.w_out, k.slope, k.side, k.vec_grads, k.total)
        grad_hidden2, d_gain, d_shift = norm_backward(k.hidden2[...], gain2, k.total[...])
        set_small(k.vec_grads, GAIN2, width, d_gain)
        set_small(k.vec_grads, SHIFT2, width, d_shift)
        k.grad_sum2[...] = grad_hidden2
        low = grad_hidden2.astype(BF16)
        k.right[:, width:] = low
        k.grad_mixed[...] = dot_nt(low, k.w_cross[width:]).astype(BF16)
        attend_backward(
            (k.qc, 0), (k.pairs, 0), (k.pairs, width), k.mask, k.lse, k.grad_mixed,
            (k.right, 0), (k.grad_pairs, 0), (k.grad_pairs, width),
        )
        k.go.right.start()
        k.grad_qc[...] = k.right[:, :width]
        back = dot_nt(k.grad_pairs[:, :width], k.w_pairs[:width])
        back = back + dot_nt(k.grad_pairs[:, width:], k.w_pairs[width:])
        k.grad_memory[...] = back.astype(BF16)
        k.go.mixed.wait()
        k.go.right.wait()

    k.go.layer_out.wait()


def ffn_weight_grads(k, act, low, grad_pre, grad_ffn):
    width = k.h1.shape[1]
    ffn = k.w_in.shape[0]
    chunks = ffn // width

    def step(j, cut):
        put_part(k.wide, j, chunks, dot_tn(low[...], grad_pre[:, cut]))
        there = pl.ds(pl.multiple_of(ffn + j * width, width), width)
        k.flat[there] = dot_tn(act[:, cut], grad_ffn[...]).astype(BF16)

    for_chunks(chunks, width, step)


def put_sides(k, first, vec_grads, first_owner, core):
    width = k.flat.shape[1]
    if len(k.keep.shape) == 2:
        k.keep[...] = k.flat[first : first + k.keep.shape[0]]
        return
    count, rows, _ = k.keep.shape
    rows -= TAIL
    share = vec_grads.shape[1] // (4 * count)

    def tail(at):
        owner = first_owner + at
        row = vec_grads[:, owner * share : (owner + 1) * share]
        row = jnp.concatenate([row, jnp.zeros((1, width - share), F32)], axis=1)
        return jnp.broadcast_to(row, (TAIL, width)).astype(BF16)

    for at in range(count):
        mine = first + (2 * at + core) * rows
        other = first + (2 * at + 1 - core) * rows
        k.keep[at, :rows] = k.flat[pl.ds(pl.multiple_of(mine, TAIL), rows)]
        k.give[at, :rows] = k.flat[pl.ds(pl.multiple_of(other, TAIL), rows)]

        @pl.when(core == 0)
        def _(at=at):
            k.keep[at, rows:] = tail(2 * at)
            k.give[at, rows:] = tail(2 * at + 1)

        @pl.when(core == 1)
        def _(at=at):
            k.keep[at, rows:] = tail(2 * at + 1)
            k.give[at, rows:] = tail(2 * at)


def backward_kernel(k):
    width = k.h1.shape[1]
    ffn = k.w_in.shape[0]
    vecs = k.vecs
    sec, core = where_am_i()
    wanted = ("pre1", "w_attn_out", "mask", "lse", "qkv", "w_attn")
    wanted_next = ("x", "mixed", "low", "right", "cross_mixed")
    coming = [
        load(getattr(k, "far_" + name), getattr(k, name), k.sems.at[at])
        for at, name in enumerate(wanted + wanted_next)
    ]

    @pl.when(sec == 0)
    def _():
        grad, d_gain, d_shift = norm_backward(
            k.h2[...], small(vecs, GAIN3, width), k.grad_memory[...].astype(F32)
        )
        set_small(k.vec_grads, GAIN3, width, d_gain)
        set_small(k.vec_grads, SHIFT3, width, d_shift)
        total, d_gain, d_shift = norm_backward(k.pre2[...], small(vecs, GAIN2, width), grad)
        set_small(k.vec_grads, GAIN2, width, d_gain)
        set_small(k.vec_grads, SHIFT2, width, d_shift)
        grad_low = total.astype(BF16)
        k.grad_ffn[...] = grad_low
        set_small(
            k.vec_grads, BIAS_OUT, width, jnp.sum(grad_low.astype(F32), axis=0, keepdims=True)
        )
        k.low1[...] = k.h1[...].astype(BF16)
        k.grad_h1[...] = total
        ffn_backward(grad_low, k.w_in, k.w_out, k.side, k.grad_pre, k.vec_grads, k.grad_h1)
        ffn_weight_grads(k, k.act, k.low1, k.grad_pre, k.grad_ffn)

    @pl.when(sec == 1)
    def _():
        k.vec_grads[...] = k.dec_vec_grads[...]
        k.grad_h1[...] = k.grad_sum2[...] + dot_nt(k.grad_qc[...], k.w_cross[:width])
        ffn_weight_grads(k, k.act, k.low2, k.side, k.dec_grad_ffn)

    take_parts(k.wide, ffn, k.flat, 0)
    early = k.early.shape[0]
    k.early[...] = k.flat[:early]
    for copy in coming:
        copy.wait()
    grad, d_gain, d_shift = norm_backward(k.pre1[...], small(vecs, GAIN1, width), k.grad_h1[...])
    set_small(k.vec_grads, GAIN1, width, d_gain)
    set_small(k.vec_grads, SHIFT1, width, d_shift)
    put_sides(k, early, k.vec_grads, 2 * k.keep.shape[0], core)
    low = grad.astype(BF16)
    k.grad_attn[...] = low
    k.grad_mixed[...] = dot_nt(low, k.w_attn_out[...]).astype(BF16)
    attend_backward(
        (k.qkv, 0), (k.qkv, width), (k.qkv, 2 * width), k.mask, k.lse, k.grad_mixed,
        (k.grad_qkv, 0), (k.grad_qkv, width), (k.grad_qkv, 2 * width),
    )
    for j in range(3):
        cut = slice(j * width, (j + 1) * width)
        grad = grad + dot_nt(k.grad_qkv[:, cut], k.w_attn[cut])
    k.grad_x[...] = grad
    k.go.grad_x.start()
    k.go.grad_x.wait()


def attn_grad_kernel(k):
    width = k.x.shape[1]
    sec, core = where_am_i()

    def step(j, cut):
        put_part(k.wide, j, 3, dot_tn(k.x[...], k.grad_qkv[:, cut]))

    for_chunks(3, width, step)
    take_parts(k.wide, 3 * width, k.flat, 0)
    k.flat[3 * width : 4 * width] = dot_tn(k.mixed[...], k.grad_attn[...]).astype(BF16)

    @pl.when(sec == 0)
    def _():
        for j in range(2):
            cut = slice(j * width, (j + 1) * width)
            put_part(k.wide, j, 2, dot_tn(k.low[...], k.grad_pairs[:, cut]))

    @pl.when(sec == 1)
    def _():
        put_part(k.wide, 0, 2, dot_tn(k.low[...], k.right[:, :width]))
        put_part(k.wide, 1, 2, dot_tn(k.cross_mixed[...], k.right[:, width:]))

    take_parts(k.wide, 2 * width, k.flat, 4 * width)
    k.flat[6 * width :] = k.early[...]
    put_sides(k, 0, k.vec_grads, 0, core)


class Refs(types.SimpleNamespace):
    pass


def run_kernel(kernel, name, hbm, vmem, outs, far_outs, scratch, loads, spare, reuse=(), work=10**10, smem=None):
    smem = smem or {}
    ins = {**smem, **hbm, **vmem}
    near = {n: pltpu.VMEM(*spec) for n, spec in far_outs.items()}
    near.update({n: pltpu.VMEM(*spec) if isinstance(spec, tuple) else spec for n, spec in scratch.items()})
    names = [*ins, *outs, *far_outs, *near, "sems", "leave_sems"]

    def run(*refs):
        k = Refs(**dict(zip(names, refs)))
        first = len(ins) + len(outs)
        k.go = Refs()
        for at, n in enumerate(far_outs):
            copy = pltpu.make_async_copy(getattr(k, n), refs[first + at], k.leave_sems.at[at])
            setattr(k.go, n, copy)
        kernel(k)

    results = pl.pallas_call(
        run,
        name=name,
        in_specs=[SMEM] * len(smem) + [HBM] * len(hbm) + [VMEM] * len(vmem),
        out_specs=[VMEM] * len(outs) + [HBM] * len(far_outs),
        out_shape=[pltpu.VMEM(*spec) for spec in outs.values()]
        + [pltpu.HBM(*spec) for spec in far_outs.values()],
        scratch_shapes=[
            *near.values(),
            pltpu.SemaphoreType.DMA((max(loads, 1),)),
            pltpu.SemaphoreType.DMA((max(len(far_outs), 1),)),
        ],
        compiler_params=pltpu.CompilerParams(
            vmem_limit_bytes=int(spare * 2**20)
            + sum(math.prod(b.shape) * jnp.dtype(b.dtype).itemsize for b in near.values())
        ),
        input_output_aliases={[*ins].index(old): [*outs].index(new) for old, new in reuse},
        cost_estimate=pl.CostEstimate(flops=work, bytes_accessed=1, transcendentals=0),
    )(
        *smem.values(),
        *[pltpu.with_memory_space_constraint(array, pltpu.HBM) for array in hbm.values()],
        *[pltpu.with_memory_space_constraint(array, pltpu.VMEM) for array in vmem.values()],
    )
    return Refs(**dict(zip([*outs, *far_outs], results)))


SMEM = pl.BlockSpec(memory_space=pltpu.SMEM)
HBM = pl.BlockSpec(memory_space=pltpu.HBM)
VMEM = pl.BlockSpec(memory_space=pltpu.VMEM)
ANY = pl.BlockSpec(memory_space=pl.ANY)


def swapped(array, axis, bit):
    devices = lax.axis_size(axis)
    return lax.ppermute(array, axis, [(i, i ^ bit) for i in range(devices)])


def held_until(array, *others):
    return lax.optimization_barrier((array, *others))[0]


def own_bit(bit):
    return (lax.axis_index("dp") >> bit) & 1


def swapped_middle(array):
    ranks = lax.axis_size("dp")
    quarter = ranks // 4
    pairs = [(i, i + quarter) for i in range(quarter, 2 * quarter)]
    pairs += [(j, i) for i, j in pairs]
    outer = [*range(quarter), *range(ranks - quarter, ranks)]
    return lax.ppermute(array, "dp", pairs + [(i, i ^ 1) for i in outer])


def at_middle():
    return own_bit(2) != own_bit(3)


def quick_kernel(kernel, name, ins, outs):
    return run_kernel(kernel, name, {}, ins, outs, {}, {}, 0, 4, work=10**8)


def sum_of_cores(far, low, core_low, high, core_high):
    shape = low.shape[1:]

    def kernel(k):
        y, z = own_bit(1), own_bit(2)

        def fill(keep, core, at, give, mine):
            give[...] = (
                keep[2 * at + 1 - y].astype(F32) + core[2 * at + 1 - y].astype(F32)
            ).astype(BF16)
            mine[...] = keep[2 * at + y].astype(F32) + core[2 * at + y].astype(F32)

        @pl.when(own_bit(3) == 0)
        def _():
            side = (k.high, k.core_high) if far else (k.low, k.core_low)
            fill(*side, 1 if far else 1 - z, k.give0, k.mine0)
            fill(*side, 0 if far else z, k.give1, k.mine1)

        @pl.when(own_bit(3) == 1)
        def _():
            side = (k.low, k.core_low) if far else (k.high, k.core_high)
            fill(*side, 0 if far else 1 - z, k.give0, k.mine0)
            fill(*side, 1 if far else z, k.give1, k.mine1)

    ins = dict(low=low, core_low=core_low, high=high, core_high=core_high)
    outs = dict(give0=(shape, BF16), mine0=(shape, F32), give1=(shape, BF16), mine1=(shape, F32))
    return quick_kernel(kernel, "sum_of_cores", ins, outs)


def added(wide, part, middle=None):
    def kernel(k):
        total = k.wide[...] + k.part[...].astype(F32)
        if middle is not None:
            total = total + jnp.where(at_middle(), k.middle[...].astype(F32), 0.0)
        k.low[...] = total.astype(BF16)
        k.full[...] = total

    ins = dict(wide=wide, part=part)
    if middle is not None:
        ins = dict(wide=wide, part=part, middle=middle)
    return quick_kernel(
        kernel, "added", ins, dict(low=(wide.shape, BF16), full=(wide.shape, F32))
    )


def sum_over_dp(low, core_low, high, core_high):
    far = sum_of_cores(True, low, core_low, high, core_high)
    near = sum_of_cores(False, low, core_low, high, core_high)
    from_y3, from_y2 = swapped(far.give0, "dp", 2), swapped(far.give1, "dp", 2)
    from_y1, from_y0 = swapped(near.give0, "dp", 2), swapped(near.give1, "dp", 2)
    third = added(far.mine0, from_y3)
    from_end3 = swapped(third.low, "dp", 4)
    second = added(far.mine1, from_y2)
    from_end2 = swapped(second.low, "dp", 4)
    from_middle3 = swapped_middle(added(third.full, from_end3).low)
    from_middle2 = swapped_middle(added(second.full, from_end2).low)
    from_end1 = swapped(added(near.mine0, from_y1, from_middle3).low, "dp", 4)
    return dict(mine=near.mine1, from_y=from_y0, from_middle=from_middle2, from_end=from_end1)


def adam_of(grad, master, mean_old, square_old, step):
    mean_new = 0.9 * mean_old + 0.1 * grad
    square_new = 0.98 * square_old + 0.02 * grad * grad
    rate = step.shape[1] ** (-0.5) * jnp.minimum(lax.rsqrt(step), step * WARMUP_STEPS ** (-1.5))
    mean_share = 1.0 - jnp.exp(step * math.log(0.9))
    square_share = 1.0 - jnp.exp(step * math.log(0.98))
    fixed_mean = mean_new * (1.0 / mean_share)
    fixed_square = square_new * (1.0 / square_share)
    change = -rate * fixed_mean / (jnp.sqrt(fixed_square) + ADAM_EPS)
    return change, mean_new, square_new, master + change


def adam_kernel(k, full):
    width = k.master.shape[1]
    share = k.vec_master.shape[1]
    step = jnp.full((1, width), k.step[0], jnp.int32).astype(F32)
    rows = k.master.shape[0]
    total = k.mine[...] + k.from_y[...].astype(F32) + k.from_end[...].astype(F32)
    total = total + jnp.where(at_middle(), k.from_middle[...].astype(F32), 0.0)
    grad, vec_grad = total[:rows], total[rows : rows + 1]
    parts = adam_of(grad, k.master[...], k.mean[...], k.square[...], step)
    if full:
        k.grad[...] = grad
        k.change[...], k.mean_new[...], k.square_new[...] = parts[:3]
    else:
        k.own[:rows] = parts[3].astype(BF16)
    pad = jnp.zeros((1, width - share), F32)

    def padded(ref):
        return jnp.concatenate([ref[...], pad], axis=1)

    parts = adam_of(
        vec_grad, padded(k.vec_master), padded(k.vec_mean), padded(k.vec_square), step
    )
    if full:
        k.vec_grad[...] = vec_grad[:, :share]
        k.vec_change[...] = parts[0][:, :share]
        k.vec_mean_new[...] = parts[1][:, :share]
        k.vec_square_new[...] = parts[2][:, :share]
        for copy in vars(k.go).values():
            copy.start()
        for copy in vars(k.go).values():
            copy.wait()
    else:
        k.own[rows:] = jnp.broadcast_to(parts[3], (TAIL, width)).astype(BF16)


def adam(summands, state, step, full):
    shape, vec_shape = state.master.shape, state.vec_master.shape
    outs, far = {}, {}
    if full:
        far = dict.fromkeys(("grad", "change", "mean_new", "square_new"), (shape, F32))
        far.update({"vec_" + name: (vec_shape, F32) for name in far})
    else:
        outs = {"own": ((shape[0] + TAIL, shape[1]), BF16)}
    return run_kernel(
        lambda k: adam_kernel(k, full), "adam_outputs" if full else "adam", {},
        {**summands, **vars(state)}, outs, far, {}, 0, 6, work=10**9, smem={"step": step},
    )


def place_blocks(pieces, share, rows_all, before=None):
    arrays = [piece[-1] for piece in pieces]
    width = arrays[0].shape[1]
    extra = [] if before is None else [*before]

    def kernel(*refs):
        ins, (target, tails, sems) = refs[: len(arrays)], refs[-3:]
        me = lax.axis_index("dp")
        owners = [z(me >> 2) * 4 + ((me & 3) ^ (2 * y + core)) for z, y, core, _ in pieces]
        copies = []
        for at, (owner, ref) in enumerate(zip(owners, ins)):
            there = pl.ds(pl.multiple_of(owner * share, share), share)
            copies.append(load(ref.at[:share], target.at[there], sems.at[at]))
        if extra:
            tails[...] = refs[len(arrays) + 1][...]
        for owner, ref in zip(owners, ins):
            tails[owner] = ref[share:]
        for copy in copies:
            copy.wait()

    return pl.pallas_call(
        kernel,
        name="place_blocks",
        in_specs=[VMEM] * len(arrays) + [HBM, VMEM][: len(extra)],
        out_specs=[HBM, VMEM],
        out_shape=[
            pltpu.HBM((rows_all, width), BF16),
            pltpu.VMEM((rows_all // share, TAIL, width), BF16),
        ],
        scratch_shapes=[pltpu.SemaphoreType.DMA((len(arrays),))],
        input_output_aliases={len(arrays): 0} if extra else {},
        compiler_params=pltpu.CompilerParams(vmem_limit_bytes=4 * 2**20),
        cost_estimate=pl.CostEstimate(flops=10**9, bytes_accessed=1, transcendentals=0),
    )(*[pltpu.with_memory_space_constraint(array, pltpu.VMEM) for array in arrays], *extra)


def either(middle, end):
    def kernel(k):
        @pl.when(at_middle())
        def _():
            k.out[...] = k.middle[...]

        @pl.when(jnp.logical_not(at_middle()))
        def _():
            k.out[...] = k.end[...]

    outs = dict(out=(end.shape, BF16))
    return quick_kernel(kernel, "either", dict(middle=middle, end=end), outs).out


def gather_blocks(own, share, rows_all, meanwhile):
    end1, middle1 = swapped(own, "dp", 4), swapped_middle(own)
    end1, from_y0 = lax.optimization_barrier((end1, swapped(own, "dp", 2)))
    end2, middle2 = swapped(middle1, "dp", 4), swapped_middle(end1)
    from_y1 = swapped(end1, "dp", 2)
    end3 = swapped(middle2, "dp", 4)
    second = either(middle1, end2)
    from_y2 = swapped(second, "dp", 2)
    third = either(middle2, end3)
    from_y3 = swapped(third, "dp", 2)

    def both(z, y, array):
        return [(z, y, 0, array), (z, y, 1, swapped(array, "dp", 1))]

    def same(z):
        return z

    def next_to(z):
        return z ^ 1

    def nearer(z):
        return 2 - (z >> 1)

    def farther(z):
        return 3 - 3 * (z >> 1)

    early = both(same, 0, own) + both(same, 1, from_y0) + both(next_to, 0, end1)
    early += both(next_to, 1, from_y1) + both(nearer, 0, second)
    first = place_blocks(early, share, rows_all)
    from_y3 = held_until(from_y3, *first, meanwhile)
    late = both(nearer, 1, from_y2) + both(farther, 0, third) + both(farther, 1, from_y3)
    return place_blocks(late, share, rows_all, first)


def body(
    inputs,
    lengths,
    cotangent,
    matrices,
    vectors,
    master_matrices,
    master_vectors,
    matrix_mean,
    matrix_square,
    vector_mean,
    vector_square,
    adam_step,
):
    row_count, seq_len, width = inputs.shape[1:]
    tokens = row_count * seq_len
    rows_all, vec_all = matrices.shape[1], vectors.shape[1]
    ffn = (rows_all - 6 * width) // 2
    half = rows_all // 2
    ranks = lax.axis_size("dp")
    share, vec_share = rows_all // ranks, vec_all // ranks
    by_swaps = ranks == 16 and share % 32 == 0
    block = (ranks // 4, share + TAIL, width) if by_swaps else (half, width)
    me = lax.axis_index("dp")

    x = inputs.reshape(tokens, width)
    cot = cotangent.reshape(tokens, width)
    mats = matrices.reshape(rows_all, width)
    lens_here = pltpu.SMEM(lengths.shape, jnp.int32)

    def spec(columns, dtype):
        return ((tokens, columns), dtype)

    full, low, deep = spec(width, F32), spec(width, BF16), spec(ffn, BF16)
    square, mask = ((width, width), BF16), spec(seq_len, F32)
    double, lse, w_ffn = ((2 * width, width), BF16), spec(HEADS // 2 * PAIR, F32), ((ffn, width), BF16)
    all_vecs, triple = ((1, vec_all), F32), spec(3 * width, BF16)
    sided = dict(keep=(block, BF16))
    if by_swaps:
        sided["give"] = (block, BF16)
    early = ((half - 6 * width, width), BF16)

    def wide(rows):
        return ((width // LANES, rows, LANES), F32)

    cross_half = lax.dynamic_slice(mats, ((4 + (me & 1)) * width, 0), (width, width), allow_negative_indices=False)
    cross_mine = swapped(cross_half, "section", 1)
    f = run_kernel(
        forward_kernel, "forward", dict(mats=mats, x=x, vectors=vectors, lengths=lengths), {},
        dict(
            h1=full, w_in=w_ffn, act=deep, slope=deep, pre2=full, h2=full,
            memory=low, w_cross=double, qc=low, w_out=w_ffn, vecs=all_vecs,
        ),
        dict(
            qkv=triple, lse=lse, mixed=low, pre1=full, mask=mask, w_attn_out=square,
            w_attn=((3 * width, width), BF16), low=low,
        ),
        dict(
            raw_attn=((3 * width, width), BF16), raw_cross=double, raw_ffn=w_ffn,
            x_here=low, wide=wide(ffn), raw_vecs=((1, vec_all), BF16), lens=lens_here,
        ),
        8, 10,
    )
    memory_far = swapped(f.memory, "section", 1)
    cross_mine = held_until(cross_mine, f.memory)
    cross_other = swapped(cross_mine, "dp", 1)
    p = run_kernel(
        prepare_kernel, "prepare", dict(cot_all=cot, lengths=lengths),
        dict(cross_mine=cross_mine, cross_other=cross_other),
        dict(w_pairs=double, mask=mask, cot=low), {},
        dict(raw=double, wide=wide(2 * width), raw_cot=low, lens=lens_here),
        2, 4,
    )
    d = run_kernel(
        decoder_kernel, "decoder", {},
        dict(
            memory=memory_far, near_memory=f.memory, **vars(p), enc_act=f.act,
            enc_slope=f.slope,
            w_cross=f.w_cross, qc=f.qc, h1=f.h1, w_in=f.w_in, w_out=f.w_out, vecs=f.vecs,
        ),
        dict(
            grad_memory=low, grad_pairs=spec(2 * width, BF16), act=deep,
            side=deep, grad_ffn=low, low2=low, grad_qc=low, grad_sum2=full,
            vec_grads=all_vecs,
        ),
        dict(layer_out=low, mixed=low, right=spec(2 * width, BF16)),
        dict(pairs=spec(2 * width, BF16), slope=spec(ffn, F32), lse=lse, grad_mixed=low, total=full, hidden2=full),
        0, 11, (("enc_act", "act"), ("enc_slope", "side")),
    )
    grad_memory_far = swapped(d.grad_memory, "section", 1)
    grad_pairs_far = swapped(d.grad_pairs, "section", 1)
    ahead = dict(
        pre1=full, w_attn_out=square, mask=mask, lse=lse, qkv=triple,
        w_attn=((3 * width, width), BF16),
    )
    s = run_kernel(
        backward_kernel, "backward",
        dict(
            **{"far_" + name: getattr(f, name) for name in ahead},
            far_x=x, far_mixed=f.mixed, far_low=f.low, far_right=d.right,
            far_cross_mixed=d.mixed,
        ),
        dict(
            dec_grad_ffn=d.grad_ffn, dec_vec_grads=d.vec_grads,
            grad_memory=grad_memory_far, act=d.act, side=d.side, low2=d.low2, grad_qc=d.grad_qc, grad_sum2=d.grad_sum2,
            pre2=f.pre2, h2=f.h2, h1=f.h1, w_in=f.w_in, w_out=f.w_out, w_cross=f.w_cross, vecs=f.vecs,
        ),
        dict(
            vec_grads=all_vecs, early=early, **sided, grad_attn=low, grad_qkv=triple,
            x=low, mixed=low, low=low, right=spec(2 * width, BF16), cross_mixed=low,
        ),
        dict(grad_x=full),
        dict(
            grad_pre=deep, grad_ffn=low, low1=low, wide=wide(ffn), grad_h1=full,
            flat=((2 * ffn, width), BF16), grad_mixed=low, **ahead,
        ),
        11, 9, work=4 * 10**10,
    )
    if by_swaps:
        core_high = swapped(s.give, "dp", 1)
    a = run_kernel(
        attn_grad_kernel, "attn_grad", {},
        dict(
            grad_qkv=s.grad_qkv, vec_grads=s.vec_grads, early=s.early, grad_pairs=grad_pairs_far,
            x=s.x, grad_attn=s.grad_attn, mixed=s.mixed, low=s.low, right=s.right, cross_mixed=s.cross_mixed,
        ),
        sided, {}, dict(wide=wide(3 * width), flat=((half, width), BF16)), 0, 4,
    )

    state = Refs(master=master_matrices[0], mean=matrix_mean[0], square=matrix_square[0])
    state = Refs(**vars(state), vec_master=master_vectors, vec_mean=vector_mean, vec_square=vector_square)
    if by_swaps:
        summands = sum_over_dp(a.keep, swapped(a.give, "dp", 1), s.keep, core_high)
        own = adam(summands, state, adam_step, False).own
        result = adam(summands, state, adam_step, True)
        new_mat, tails = gather_blocks(own, share, rows_all, result.change)
        new_vec = tails[:, 0, :vec_share].reshape(1, vec_all)
    else:
        whole = jnp.concatenate([a.keep, s.keep], axis=0)
        grad = lax.psum_scatter(whole, "dp", scatter_dimension=0, tiled=True).astype(F32)
        vec_grad = lax.dynamic_slice(
            lax.psum(s.vec_grads, "dp"), (0, me * vec_share), (1, vec_share)
        )
        step = jnp.full((1, width), adam_step[0].astype(F32))
        parts = adam_of(grad, state.master, state.mean, state.square, step)
        vec_step = jnp.full((1, width), adam_step[0].astype(F32))
        pad = ((0, 0), (0, width - vec_share))
        vec_parts = [
            part[:, :vec_share]
            for part in adam_of(
                *[jnp.pad(v, pad) for v in (vec_grad, master_vectors, vector_mean, vector_square)],
                vec_step,
            )
        ]
        names = ("change", "mean_new", "square_new")
        result = dict(grad=grad, vec_grad=vec_grad, **dict(zip(names, parts)))
        result.update({"vec_" + name: part for name, part in zip(names, vec_parts)})
        result = Refs(**result)
        new_mat = lax.all_gather(parts[3].astype(BF16), "dp", axis=0, tiled=True)
        new_vec = lax.all_gather(vec_parts[3].astype(BF16), "dp", axis=1, tiled=True)
    return (
        d.layer_out.reshape(1, row_count, seq_len, width),
        s.grad_x.reshape(1, row_count, seq_len, width),
        result.grad[None],
        result.vec_grad,
        result.change[None],
        result.vec_change,
        result.mean_new[None],
        result.square_new[None],
        result.vec_mean_new,
        result.vec_square_new,
        new_mat[None],
        new_vec,
    )


def solution(mesh):
    return jax.shard_map(
        body,
        mesh=mesh,
        in_specs=(
            P("section", "dp", None, None),
            P(None, "dp", None),
            P("dp", None, None),
            P("section", None, None),
            P("section", None),
            P("section", "dp", None),
            P("section", "dp"),
            P("section", "dp", None),
            P("section", "dp", None),
            P("section", "dp"),
            P("section", "dp"),
            P(),
        ),
        out_specs=(
            P("section", "dp", None, None),
            P("section", "dp", None, None),
            P("section", "dp", None),
            P("section", "dp"),
            P("section", "dp", None),
            P("section", "dp"),
            P("section", "dp", None),
            P("section", "dp", None),
            P("section", "dp"),
            P("section", "dp"),
            P("section", None, None),
            P("section", None),
        ),
        check_vma=False,
    )
```

```python
import math
import types

import jax
import jax.numpy as jnp
from jax import lax
from jax.experimental import pallas as pl
from jax.experimental.pallas import tpu as pltpu
from jax.sharding import PartitionSpec as P

HEADS = 8
HEAD_DIM = 64
PAIR = 2 * HEAD_DIM
LANES = 128
TAIL = 16
UNROLL_PAIRS = 4
UNROLL_CHUNKS = True
WORK_REST = 10**10
WORK_D = 4 * 10**10
SPARE_D = 8

MASK_FILL = -1e30
NORM_EPS = 1e-05
ADAM_EPS = 1e-09
WARMUP_STEPS = 4000.0

F32 = jnp.float32
BF16 = jnp.bfloat16

BIAS_OUT, GAIN1, SHIFT1, GAIN2, SHIFT2, GAIN3, SHIFT3 = range(-7, 0)


def dot(left, right):
    return jnp.dot(left, right, preferred_element_type=F32)


def dot_nt(left, right):
    return lax.dot_general(left, right, (((1,), (1,)), ((), ())), preferred_element_type=F32)


def dot_tn(left, right):
    return lax.dot_general(left, right, (((0,), (0,)), ((), ())), preferred_element_type=F32)


def norm_parts(hidden):
    centre = hidden - jnp.mean(hidden, axis=-1, keepdims=True)
    rstd = lax.rsqrt(jnp.mean(centre * centre, axis=-1, keepdims=True) + NORM_EPS)
    return centre * rstd, rstd


def norm_forward(hidden, gain, shift):
    return norm_parts(hidden)[0] * gain + shift


def norm_backward(hidden, gain, grad):
    normal, rstd = norm_parts(hidden)
    scaled = grad * gain
    inner = jnp.mean(scaled * normal, axis=-1, keepdims=True)
    grad_in = rstd * (scaled - jnp.mean(scaled, axis=-1, keepdims=True) - normal * inner)
    grad_gain = jnp.sum(grad * normal, axis=0, keepdims=True)
    grad_shift = jnp.sum(grad, axis=0, keepdims=True)
    return grad_in, grad_gain, grad_shift


def act_parts(pre):
    cdf = 0.5 * (1.0 + lax.erf(pre * (0.5**0.5)))
    pdf = jnp.exp(-0.5 * pre * pre) * 0.3989422804014327
    return pre * cdf, cdf + pre * pdf


def split_rows(raw, wide, parts, out, base):
    width = raw.shape[1]
    for c in range(width // LANES):
        cut = slice(c * LANES, (c + 1) * LANES)
        wide[c, : parts * width] = raw[: parts * width, cut].astype(F32)
        for j in range(parts):
            out[(base + j) * width : (base + j + 1) * width, cut] = wide[
                c, pl.ds(j, width, stride=parts), :
            ].astype(BF16)


def put_part(wide, j, parts, values):
    rows, width = values.shape
    for c in range(width // LANES):
        wide[c, pl.ds(j, rows, stride=parts), :] = values[:, c * LANES : (c + 1) * LANES]


def take_parts(wide, rows, out, first):
    for c in range(wide.shape[0]):
        out[first : first + rows, c * LANES : (c + 1) * LANES] = wide[c, :rows].astype(BF16)


def sentence_ends(lens, side, row):
    ends, total = [], 0
    for j in range(lens.shape[2]):
        total = total + lens[side, row, j]
        ends.append(total)
    return ends


def sentence_of(ends, position):
    found = jnp.zeros(position.shape, jnp.int32)
    for end in ends:
        found = found + (position >= end).astype(jnp.int32)
    return found


def fill_mask(mask, lens, query_side, key_side, causal):
    seq_len = mask.shape[1]
    row_count, sents = lens.shape[1:]
    q_pos = lax.broadcasted_iota(jnp.int32, (seq_len, seq_len), 0)
    k_pos = lax.broadcasted_iota(jnp.int32, (seq_len, seq_len), 1)
    for r in range(row_count):
        q_ids = sentence_of(sentence_ends(lens, query_side, r), q_pos)
        k_ids = sentence_of(sentence_ends(lens, key_side, r), k_pos)
        same = jnp.where(q_ids == k_ids, 1, 0)
        if causal is not None:
            same = jnp.where(q_pos >= k_pos, same, jnp.where(causal, 0, same))
        allowed = jnp.where(q_ids == sents, 1, same)
        mask[r * seq_len : (r + 1) * seq_len] = allowed.astype(F32)


def both_heads(block, lane):
    even = (lane < HEAD_DIM).astype(BF16)
    return jnp.concatenate([block * even, block * (1 - even)], axis=0)


def one_of(stacked, lane):
    keys = stacked.shape[0] // 2
    return jnp.where(lane < HEAD_DIM, stacked[:keys], stacked[keys:])


def for_pairs(mask, step):
    seq_len = mask.shape[1]
    pairs = HEADS // 2

    def turn(i, carried):
        row, pair = i // pairs, lax.rem(i, pairs)
        rows = pl.ds(pl.multiple_of(row * seq_len, seq_len), seq_len)
        step(rows, lambda first: pl.ds(pl.multiple_of(first + pair * PAIR, PAIR), PAIR))
        return carried

    lax.fori_loop(0, mask.shape[0] // seq_len * pairs, turn, 0, unroll=UNROLL_PAIRS)


def attend_forward(query, keys, values, mask, out, lse):
    seq_len = mask.shape[1]
    lane = lax.broadcasted_iota(jnp.int32, (1, PAIR), 1)
    (q_ref, q_at), (k_ref, k_at), (v_ref, v_at) = query, keys, values

    def step(rows, lanes):
        q = q_ref[rows, lanes(q_at)]
        k2 = both_heads(k_ref[rows, lanes(k_at)], lane)
        v2 = both_heads(v_ref[rows, lanes(v_at)], lane)
        scores = dot_nt(q, k2) * HEAD_DIM ** (-0.5)
        probs, logs = [], []
        for half in range(2):
            part = scores[:, half * seq_len : (half + 1) * seq_len]
            part = jnp.where(mask[rows] > 0.0, part, MASK_FILL)
            top = jnp.max(part, axis=-1, keepdims=True)
            raised = jnp.exp(part - top)
            total = jnp.sum(raised, axis=-1, keepdims=True)
            probs.append((raised * (1.0 / total)).astype(BF16))
            logs.append(top + jnp.log(total))
        lse[rows, lanes(0)] = jnp.where(lane < HEAD_DIM, logs[0], logs[1])
        out[rows, lanes(0)] = dot(jnp.concatenate(probs, axis=1), v2).astype(BF16)

    for_pairs(mask, step)


def attend_backward(query, keys, values, mask, lse, grad_out, grad_q, grad_k, grad_v):
    seq_len = mask.shape[1]
    lane = lax.broadcasted_iota(jnp.int32, (1, PAIR), 1)
    scale = HEAD_DIM ** (-0.5)
    (q_ref, q_at), (k_ref, k_at), (v_ref, v_at) = query, keys, values
    (gq_ref, gq_at), (gk_ref, gk_at), (gv_ref, gv_at) = grad_q, grad_k, grad_v

    def step(rows, lanes):
        q = q_ref[rows, lanes(q_at)]
        k2 = both_heads(k_ref[rows, lanes(k_at)], lane)
        v2 = both_heads(v_ref[rows, lanes(v_at)], lane)
        go = grad_out[rows, lanes(0)]
        logs = lse[rows, lanes(0)]
        scores = dot_nt(q, k2) * scale
        grad_probs = dot_nt(go, v2)
        probs, grad_scores = [], []
        for half in range(2):
            cut = slice(half * seq_len, (half + 1) * seq_len)
            part = jnp.where(mask[rows] > 0.0, scores[:, cut], MASK_FILL)
            prob = jnp.exp(part - logs[:, half * HEAD_DIM : half * HEAD_DIM + 1])
            gp = grad_probs[:, cut]
            inner = jnp.sum(prob * gp, axis=-1, keepdims=True)
            probs.append(prob.astype(BF16))
            grad_scores.append((prob * (gp - inner)).astype(BF16))
        probs = jnp.concatenate(probs, axis=1)
        grad_scores = jnp.concatenate(grad_scores, axis=1)
        gv_ref[rows, lanes(gv_at)] = one_of(dot_tn(probs, go), lane).astype(BF16)
        gq_ref[rows, lanes(gq_at)] = (dot(grad_scores, k2) * scale).astype(BF16)
        gk_ref[rows, lanes(gk_at)] = (one_of(dot_tn(grad_scores, q), lane) * scale).astype(BF16)

    for_pairs(mask, step)


def small(vecs, which, width):
    pieces = vecs.shape[1] // width
    at = (which if which >= 0 else pieces + which) * width
    return vecs[:, at : at + width].astype(F32)


def set_small(vecs, which, width, value):
    pieces = vecs.shape[1] // width
    at = (which if which >= 0 else pieces + which) * width
    vecs[:, at : at + width] = value


def where_am_i():
    return lax.axis_index("section"), lax.rem(lax.axis_index("dp"), 2)


def for_chunks(count, width, step):
    def turn(j, carried):
        step(j, pl.ds(pl.multiple_of(j * width, width), width))
        return carried

    lax.fori_loop(0, count, turn, 0, unroll=UNROLL_CHUNKS)


def ffn_forward(normed, w_in, w_out, vecs, act, slope, total):
    width = normed.shape[1]
    low = normed.astype(BF16)
    total[...] = normed + small(vecs, BIAS_OUT, width)

    def step(j, cut):
        pre = dot(low, w_in[cut]) + vecs[:, cut]
        value, derivative = act_parts(pre)
        value = value.astype(BF16)
        act[:, cut] = value
        slope[:, cut] = derivative.astype(slope.dtype)
        total[...] += dot(value, w_out[cut])

    for_chunks(w_in.shape[0] // width, width, step)


def ffn_backward(grad_low, w_in, w_out, slope, grad_pre, vec_grads, total):
    width = grad_low.shape[1]

    def step(j, cut):
        grad = (dot_nt(grad_low, w_out[cut]) * slope[:, cut].astype(F32)).astype(BF16)
        grad_pre[:, cut] = grad
        vec_grads[:, cut] = jnp.sum(grad.astype(F32), axis=0, keepdims=True)
        total[...] += dot_nt(grad, w_in[cut])

    for_chunks(w_in.shape[0] // width, width, step)


def load(source, target, sem):
    copy = pltpu.make_async_copy(source, target, sem)
    copy.start()
    return copy


def memory_of(k, rows):
    width = k.h1.shape[1]
    vecs = k.vecs
    pre2 = k.pre2.at[rows]
    ffn_forward(k.h1[rows], k.w_in, k.w_out, vecs, k.act.at[rows], k.slope.at[rows], pre2)
    second = norm_forward(pre2[...], small(vecs, GAIN2, width), small(vecs, SHIFT2, width))
    k.h2[rows] = second
    third = norm_forward(second, small(vecs, GAIN3, width), small(vecs, SHIFT3, width))
    k.memory[...] = third.astype(BF16)


def forward_kernel(k):
    width = k.h1.shape[1]
    ffn = k.w_in.shape[0]
    sec, _ = where_am_i()
    get_lens = load(k.lengths, k.lens, k.sems.at[7])
    get_in = load(k.mats.at[: 3 * width], k.raw_attn, k.sems.at[0])
    get_x = load(k.x, k.x_here, k.sems.at[1])
    get_vecs = load(k.vectors, k.raw_vecs, k.sems.at[2])
    get_attn_out = load(k.mats.at[3 * width : 4 * width], k.w_attn_out, k.sems.at[3])
    get_ffn = load(k.mats.at[6 * width : 6 * width + ffn], k.raw_ffn, k.sems.at[4])
    get_out = load(k.mats.at[6 * width + ffn :], k.w_out, k.sems.at[5])
    get_cross = pltpu.make_async_copy(k.mats.at[4 * width : 6 * width], k.raw_cross, k.sems.at[6])

    @pl.when(sec == 1)
    def _():
        get_cross.start()

    get_lens.wait()
    fill_mask(k.mask, k.lens, sec, sec, sec == 1)
    k.go.mask.start()
    get_in.wait()
    split_rows(k.raw_attn, k.wide, 3, k.w_attn, 0)
    k.go.w_attn.start()
    get_x.wait()
    for j in range(3):
        part = dot(k.x_here[...], k.w_attn[j * width : (j + 1) * width])
        k.qkv[:, j * width : (j + 1) * width] = part.astype(BF16)
    k.go.qkv.start()
    attend_forward((k.qkv, 0), (k.qkv, width), (k.qkv, 2 * width), k.mask, k.mixed, k.lse)
    k.go.mixed.start()
    k.go.lse.start()
    get_vecs.wait()
    k.vecs[...] = k.raw_vecs[...].astype(F32)
    vecs = k.vecs
    get_attn_out.wait()
    k.go.w_attn_out.start()
    hidden = k.x_here[...].astype(F32) + dot(k.mixed[...], k.w_attn_out[...])
    k.pre1[...] = hidden
    k.go.pre1.start()
    k.h1[...] = norm_forward(hidden, small(vecs, GAIN1, width), small(vecs, SHIFT1, width))
    get_ffn.wait()
    split_rows(k.raw_ffn, k.wide, ffn // width, k.w_in, 0)
    get_out.wait()

    @pl.when(sec == 0)
    def _():
        memory_of(k, slice(0, k.memory.shape[0]))
        k.low[: k.memory.shape[0]] = k.memory[...]
        k.go.low.start()

    @pl.when(sec == 1)
    def _():
        k.low[...] = k.h1[...].astype(BF16)
        k.go.low.start()
        get_cross.wait()
        split_rows(k.raw_cross, k.wide, 2, k.w_cross, 0)
        k.qc[...] = dot(k.low[...], k.w_cross[:width]).astype(BF16)

    k.go.mask.wait()
    k.go.w_attn.wait()
    k.go.qkv.wait()
    k.go.mixed.wait()
    k.go.lse.wait()
    k.go.w_attn_out.wait()
    k.go.pre1.wait()
    k.go.low.wait()


def forward_rest_kernel(k):
    sec, _ = where_am_i()

    @pl.when(sec == 0)
    def _():
        half = k.memory.shape[0]
        memory_of(k, slice(half, 2 * half))
        k.low_rest[...] = k.memory[...]
        k.go.low_rest.start()
        k.go.low_rest.wait()


def prepare_kernel(k):
    width = k.raw.shape[1]
    seq_len = k.mask.shape[1]
    sec, core = where_am_i()

    @pl.when(sec == 1)
    def _():
        get_cot = load(k.cot_all, k.raw_cot, k.sems.at[0])
        get_lens = load(k.lengths, k.lens, k.sems.at[1])
        k.raw[pl.ds(pl.multiple_of(core * width, width), width)] = k.cross_mine[...]
        k.raw[pl.ds(pl.multiple_of((1 - core) * width, width), width)] = k.cross_other[...]
        split_rows(k.raw, k.wide, 2, k.w_pairs, 0)
        get_lens.wait()
        fill_mask(k.mask, k.lens, 1, 0, None)
        get_cot.wait()
        position = lax.broadcasted_iota(jnp.int32, (seq_len, 1), 0)
        for r in range(k.lens.shape[1]):
            used = sentence_ends(k.lens, 1, r)[-1]
            rows = slice(r * seq_len, (r + 1) * seq_len)
            k.cot[rows] = jnp.where(position < used, k.raw_cot[rows].astype(F32), 0.0).astype(BF16)


def decoder_kernel(k, part):
    half, width = k.memory.shape
    rows = slice(part * half, (part + 1) * half)
    vecs = k.vecs
    sec, _ = where_am_i()
    top = k.layer_out.at[rows] if part == 1 else k.top
    grad_keys = (k.back, width) if part == 0 else (k.rest, width)
    grad_values = (k.grad_values, 0) if part == 0 else (k.rest, 2 * width)
    if part == 1:
        k.layer_out[:half] = k.top_before[...]

    @pl.when(sec == 0)
    def _():
        top[...] = k.near_memory[...]

    @pl.when(sec == 1)
    def _():
        mask, qc, act, side = k.mask.at[rows], k.qc.at[rows], k.act.at[rows], k.side.at[rows]
        for j in range(2):
            pair = dot(k.memory[...], k.w_pairs[j * width : (j + 1) * width])
            k.pairs[:, j * width : (j + 1) * width] = pair.astype(BF16)
        attend_forward((qc, 0), (k.pairs, 0), (k.pairs, width), mask, k.mixed, k.lse)
        k.go.mixed.start()
        hidden2 = k.h1[rows] + dot(k.mixed[...], k.w_cross[width:])
        gain2, shift2 = small(vecs, GAIN2, width), small(vecs, SHIFT2, width)
        normed2 = norm_forward(hidden2, gain2, shift2)
        k.low2[rows] = normed2.astype(BF16)
        k.hidden2[...] = hidden2
        ffn_forward(normed2, k.w_in, k.w_out, vecs, act, k.slope, k.total)
        hidden3 = k.total[...]
        gain3, shift3 = small(vecs, GAIN3, width), small(vecs, SHIFT3, width)
        top[...] = norm_forward(hidden3, gain3, shift3).astype(BF16)
        grad_sum3, d_gain, d_shift = norm_backward(hidden3, gain3, k.cot[rows].astype(F32))
        set_small(k.vec_grads, GAIN3, width, d_gain)
        set_small(k.vec_grads, SHIFT3, width, d_shift)
        grad_low = grad_sum3.astype(BF16)
        k.grad_ffn[rows] = grad_low
        set_small(
            k.vec_grads, BIAS_OUT, width, jnp.sum(grad_low.astype(F32), axis=0, keepdims=True)
        )
        k.total[...] = grad_sum3
        ffn_backward(grad_low, k.w_in, k.w_out, k.slope, side, k.vec_grads, k.total)
        grad_hidden2, d_gain, d_shift = norm_backward(k.hidden2[...], gain2, k.total[...])
        set_small(k.vec_grads, GAIN2, width, d_gain)
        set_small(k.vec_grads, SHIFT2, width, d_shift)
        k.grad_sum2[rows] = grad_hidden2
        low = grad_hidden2.astype(BF16)
        k.right[:, width:] = low
        k.grad_mixed[...] = dot_nt(low, k.w_cross[width:]).astype(BF16)
        attend_backward(
            (qc, 0), (k.pairs, 0), (k.pairs, width), mask, k.lse, k.grad_mixed,
            (k.right, 0), grad_keys, grad_values,
        )
        k.go.right.start()
        k.grad_qc[rows] = k.right[:, :width]
        back = jnp.zeros((half, width), F32)
        for j, (ref, at) in enumerate((grad_keys, grad_values)):
            back = back + dot_nt(ref[:, at : at + width], k.w_pairs[j * width : (j + 1) * width])
        if part == 0:
            k.back[:, :width] = back.astype(BF16)
        else:
            k.grad_memory[...] = back.astype(BF16)
            k.rest[:, :width] = k.values_before[...]
        if part == 1:
            k.vec_grads[...] += k.vec_before[...]
        k.go.mixed.wait()
        k.go.right.wait()

    if part == 1:
        k.go.layer_out.start()
        k.go.layer_out.wait()


def ffn_weight_grads(k, act, low, grad_pre, grad_ffn):
    width = k.h1.shape[1]
    ffn = k.w_in.shape[0]
    chunks = ffn // width

    def step(j, cut):
        put_part(k.wide, j, chunks, dot_tn(low[...], grad_pre[:, cut]))
        there = pl.ds(pl.multiple_of(ffn + j * width, width), width)
        k.flat[there] = dot_tn(act[:, cut], grad_ffn[...]).astype(BF16)

    for_chunks(chunks, width, step)


def put_sides(k, first, vec_grads, first_owner, core):
    width = k.flat.shape[1]
    if len(k.keep.shape) == 2:
        k.keep[...] = k.flat[first : first + k.keep.shape[0]]
        return
    count, rows, _ = k.keep.shape
    rows -= TAIL
    share = vec_grads.shape[1] // (4 * count)

    def tail(at):
        owner = first_owner + at
        row = vec_grads[:, owner * share : (owner + 1) * share]
        row = jnp.concatenate([row, jnp.zeros((1, width - share), F32)], axis=1)
        return jnp.broadcast_to(row, (TAIL, width)).astype(BF16)

    for at in range(count):
        mine = first + (2 * at + core) * rows
        other = first + (2 * at + 1 - core) * rows
        k.keep[at, :rows] = k.flat[pl.ds(pl.multiple_of(mine, TAIL), rows)]
        k.give[at, :rows] = k.flat[pl.ds(pl.multiple_of(other, TAIL), rows)]

        @pl.when(core == 0)
        def _(at=at):
            k.keep[at, rows:] = tail(2 * at)
            k.give[at, rows:] = tail(2 * at + 1)

        @pl.when(core == 1)
        def _(at=at):
            k.keep[at, rows:] = tail(2 * at + 1)
            k.give[at, rows:] = tail(2 * at)


def backward_kernel(k):
    width = k.h1.shape[1]
    ffn = k.w_in.shape[0]
    vecs = k.vecs
    sec, core = where_am_i()
    half = k.back.shape[0]
    first, rest = slice(0, half), slice(half, 2 * half)
    wanted = ("pre1", "w_attn_out", "mask", "lse", "qkv", "w_attn", "x", "mixed")
    arriving = [(getattr(k, "far_" + name), getattr(k, name)) for name in wanted]
    arriving += [
        (k.far_low.at[first], k.low.at[first]),
        (k.far_right0, k.right.at[first]),
        (k.far_right1, k.right.at[rest]),
        (k.far_cross_mixed0, k.cross_mixed.at[first]),
        (k.far_cross_mixed1, k.cross_mixed.at[rest]),
    ]
    coming = [load(*ends, k.sems.at[at]) for at, ends in enumerate(arriving)]
    last_sem = k.sems.at[len(coming)]

    @pl.when(sec == 0)
    def _():
        load(k.far_low_rest, k.low.at[rest], last_sem)

    @pl.when(sec == 1)
    def _():
        load(k.far_low.at[rest], k.low.at[rest], last_sem)

    coming.append(pltpu.make_async_copy(k.far_low_rest, k.low.at[rest], last_sem))

    @pl.when(sec == 0)
    def _():
        grad_memory = jnp.concatenate([k.back[:, :width], k.grad_memory[...]], axis=0)
        grad, d_gain, d_shift = norm_backward(
            k.h2[...], small(vecs, GAIN3, width), grad_memory.astype(F32)
        )
        set_small(k.vec_grads, GAIN3, width, d_gain)
        set_small(k.vec_grads, SHIFT3, width, d_shift)
        total, d_gain, d_shift = norm_backward(k.pre2[...], small(vecs, GAIN2, width), grad)
        set_small(k.vec_grads, GAIN2, width, d_gain)
        set_small(k.vec_grads, SHIFT2, width, d_shift)
        grad_low = total.astype(BF16)
        k.grad_ffn[...] = grad_low
        set_small(
            k.vec_grads, BIAS_OUT, width, jnp.sum(grad_low.astype(F32), axis=0, keepdims=True)
        )
        k.low1[...] = k.h1[...].astype(BF16)
        k.grad_h1[...] = total
        ffn_backward(grad_low, k.w_in, k.w_out, k.side, k.grad_pre, k.vec_grads, k.grad_h1)
        ffn_weight_grads(k, k.act, k.low1, k.grad_pre, k.grad_ffn)

    @pl.when(sec == 1)
    def _():
        k.vec_grads[...] = k.dec_vec_grads[...]
        k.grad_h1[...] = k.grad_sum2[...] + dot_nt(k.grad_qc[...], k.w_cross[:width])
        ffn_weight_grads(k, k.act, k.low2, k.side, k.dec_grad_ffn)

    take_parts(k.wide, ffn, k.flat, 0)
    early = k.early.shape[0]
    k.early[...] = k.flat[:early]
    for copy in coming:
        copy.wait()
    grad, d_gain, d_shift = norm_backward(k.pre1[...], small(vecs, GAIN1, width), k.grad_h1[...])
    set_small(k.vec_grads, GAIN1, width, d_gain)
    set_small(k.vec_grads, SHIFT1, width, d_shift)
    put_sides(k, early, k.vec_grads, 2 * k.keep.shape[0], core)
    low = grad.astype(BF16)
    k.grad_attn[...] = low
    k.grad_mixed[...] = dot_nt(low, k.w_attn_out[...]).astype(BF16)
    attend_backward(
        (k.qkv, 0), (k.qkv, width), (k.qkv, 2 * width), k.mask, k.lse, k.grad_mixed,
        (k.grad_qkv, 0), (k.grad_qkv, width), (k.grad_qkv, 2 * width),
    )
    for j in range(3):
        cut = slice(j * width, (j + 1) * width)
        grad = grad + dot_nt(k.grad_qkv[:, cut], k.w_attn[cut])
    k.grad_x[...] = grad
    k.go.grad_x.start()
    k.go.grad_x.wait()


def attn_grad_kernel(k):
    width = k.x.shape[1]
    half = k.rest.shape[0]
    sec, core = where_am_i()

    def step(j, cut):
        put_part(k.wide, j, 3, dot_tn(k.x[...], k.grad_qkv[:, cut]))

    for_chunks(3, width, step)
    take_parts(k.wide, 3 * width, k.flat, 0)
    k.flat[3 * width : 4 * width] = dot_tn(k.mixed[...], k.grad_attn[...]).astype(BF16)

    @pl.when(sec == 0)
    def _():
        for j in range(2):
            first = k.back[:, width:] if j == 0 else k.rest[:, :width]
            second = k.rest[:, (j + 1) * width : (j + 2) * width]
            put_part(k.wide, j, 2, dot_tn(k.low[:half], first) + dot_tn(k.low[half:], second))

    @pl.when(sec == 1)
    def _():
        put_part(k.wide, 0, 2, dot_tn(k.low[...], k.right[:, :width]))
        put_part(k.wide, 1, 2, dot_tn(k.cross_mixed[...], k.right[:, width:]))

    take_parts(k.wide, 2 * width, k.flat, 4 * width)
    k.flat[6 * width :] = k.early[...]
    put_sides(k, 0, k.vec_grads, 0, core)


class Refs(types.SimpleNamespace):
    pass


def run_kernel(kernel, name, hbm, vmem, outs, far_outs, scratch, loads, spare, reuse=(), work=10**10, smem=None):
    smem = smem or {}
    ins = {**smem, **hbm, **vmem}
    near = {n: pltpu.VMEM(*spec) for n, spec in far_outs.items()}
    near.update({n: pltpu.VMEM(*spec) if isinstance(spec, tuple) else spec for n, spec in scratch.items()})
    names = [*ins, *outs, *far_outs, *near, "sems", "leave_sems"]

    def run(*refs):
        k = Refs(**dict(zip(names, refs)))
        first = len(ins) + len(outs)
        k.go = Refs()
        for at, n in enumerate(far_outs):
            copy = pltpu.make_async_copy(getattr(k, n), refs[first + at], k.leave_sems.at[at])
            setattr(k.go, n, copy)
        kernel(k)

    results = pl.pallas_call(
        run,
        name=name,
        in_specs=[SMEM] * len(smem) + [HBM] * len(hbm) + [VMEM] * len(vmem),
        out_specs=[VMEM] * len(outs) + [HBM] * len(far_outs),
        out_shape=[pltpu.VMEM(*spec) for spec in outs.values()]
        + [pltpu.HBM(*spec) for spec in far_outs.values()],
        scratch_shapes=[
            *near.values(),
            pltpu.SemaphoreType.DMA((max(loads, 1),)),
            pltpu.SemaphoreType.DMA((max(len(far_outs), 1),)),
        ],
        compiler_params=pltpu.CompilerParams(
            vmem_limit_bytes=int(spare * 2**20)
            + sum(math.prod(b.shape) * jnp.dtype(b.dtype).itemsize for b in near.values())
        ),
        input_output_aliases={[*ins].index(old): [*outs].index(new) for old, new in reuse},
        cost_estimate=pl.CostEstimate(flops=work, bytes_accessed=1, transcendentals=0),
    )(
        *smem.values(),
        *[pltpu.with_memory_space_constraint(array, pltpu.HBM) for array in hbm.values()],
        *[pltpu.with_memory_space_constraint(array, pltpu.VMEM) for array in vmem.values()],
    )
    return Refs(**dict(zip([*outs, *far_outs], results)))


SMEM = pl.BlockSpec(memory_space=pltpu.SMEM)
HBM = pl.BlockSpec(memory_space=pltpu.HBM)
VMEM = pl.BlockSpec(memory_space=pltpu.VMEM)
ANY = pl.BlockSpec(memory_space=pl.ANY)


def swapped(array, axis, bit):
    devices = lax.axis_size(axis)
    return lax.ppermute(array, axis, [(i, i ^ bit) for i in range(devices)])


def held_until(array, *others):
    return lax.optimization_barrier((array, *others))[0]


def own_bit(bit):
    return (lax.axis_index("dp") >> bit) & 1


def swapped_middle(array):
    ranks = lax.axis_size("dp")
    quarter = ranks // 4
    pairs = [(i, i + quarter) for i in range(quarter, 2 * quarter)]
    pairs += [(j, i) for i, j in pairs]
    outer = [*range(quarter), *range(ranks - quarter, ranks)]
    return lax.ppermute(array, "dp", pairs + [(i, i ^ 1) for i in outer])


def at_middle():
    return own_bit(2) != own_bit(3)


def quick_kernel(kernel, name, ins, outs):
    return run_kernel(kernel, name, {}, ins, outs, {}, {}, 0, 4, work=10**8)


def sum_of_cores(far, low, core_low, high, core_high):
    shape = low.shape[1:]

    def kernel(k):
        y, z = own_bit(1), own_bit(2)

        def fill(keep, core, at, give, mine):
            give[...] = (
                keep[2 * at + 1 - y].astype(F32) + core[2 * at + 1 - y].astype(F32)
            ).astype(BF16)
            mine[...] = keep[2 * at + y].astype(F32) + core[2 * at + y].astype(F32)

        @pl.when(own_bit(3) == 0)
        def _():
            side = (k.high, k.core_high) if far else (k.low, k.core_low)
            fill(*side, 1 if far else 1 - z, k.give0, k.mine0)
            fill(*side, 0 if far else z, k.give1, k.mine1)

        @pl.when(own_bit(3) == 1)
        def _():
            side = (k.low, k.core_low) if far else (k.high, k.core_high)
            fill(*side, 0 if far else 1 - z, k.give0, k.mine0)
            fill(*side, 1 if far else z, k.give1, k.mine1)

    ins = dict(low=low, core_low=core_low, high=high, core_high=core_high)
    outs = dict(give0=(shape, BF16), mine0=(shape, F32), give1=(shape, BF16), mine1=(shape, F32))
    return quick_kernel(kernel, "sum_of_cores", ins, outs)


def added(wide, part, middle=None):
    def kernel(k):
        total = k.wide[...] + k.part[...].astype(F32)
        if middle is not None:
            total = total + jnp.where(at_middle(), k.middle[...].astype(F32), 0.0)
        k.low[...] = total.astype(BF16)
        k.full[...] = total

    ins = dict(wide=wide, part=part)
    if middle is not None:
        ins = dict(wide=wide, part=part, middle=middle)
    return quick_kernel(
        kernel, "added", ins, dict(low=(wide.shape, BF16), full=(wide.shape, F32))
    )


def sum_over_dp(low, core_low, high, core_high):
    far = sum_of_cores(True, low, core_low, high, core_high)
    near = sum_of_cores(False, low, core_low, high, core_high)
    from_y3, from_y2 = swapped(far.give0, "dp", 2), swapped(far.give1, "dp", 2)
    from_y1, from_y0 = swapped(near.give0, "dp", 2), swapped(near.give1, "dp", 2)
    third = added(far.mine0, from_y3)
    from_end3 = swapped(third.low, "dp", 4)
    second = added(far.mine1, from_y2)
    from_end2 = swapped(second.low, "dp", 4)
    from_middle3 = swapped_middle(added(third.full, from_end3).low)
    from_middle2 = swapped_middle(added(second.full, from_end2).low)
    from_end1 = swapped(added(near.mine0, from_y1, from_middle3).low, "dp", 4)
    return dict(mine=near.mine1, from_y=from_y0, from_middle=from_middle2, from_end=from_end1)


def adam_of(grad, master, mean_old, square_old, step):
    mean_new = 0.9 * mean_old + 0.1 * grad
    square_new = 0.98 * square_old + 0.02 * grad * grad
    rate = step.shape[1] ** (-0.5) * jnp.minimum(lax.rsqrt(step), step * WARMUP_STEPS ** (-1.5))
    mean_share = 1.0 - jnp.exp(step * math.log(0.9))
    square_share = 1.0 - jnp.exp(step * math.log(0.98))
    fixed_mean = mean_new * (1.0 / mean_share)
    fixed_square = square_new * (1.0 / square_share)
    change = -rate * fixed_mean / (jnp.sqrt(fixed_square) + ADAM_EPS)
    return change, mean_new, square_new, master + change


def adam_kernel(k, full):
    width = k.master.shape[1]
    share = k.vec_master.shape[1]
    step = jnp.full((1, width), k.step[0], jnp.int32).astype(F32)
    rows = k.master.shape[0]
    total = k.mine[...] + k.from_y[...].astype(F32) + k.from_end[...].astype(F32)
    total = total + jnp.where(at_middle(), k.from_middle[...].astype(F32), 0.0)
    grad, vec_grad = total[:rows], total[rows : rows + 1]
    parts = adam_of(grad, k.master[...], k.mean[...], k.square[...], step)
    if full:
        k.grad[...] = grad
        k.change[...], k.mean_new[...], k.square_new[...] = parts[:3]
    else:
        k.own[:rows] = parts[3].astype(BF16)
    pad = jnp.zeros((1, width - share), F32)

    def padded(ref):
        return jnp.concatenate([ref[...], pad], axis=1)

    parts = adam_of(
        vec_grad, padded(k.vec_master), padded(k.vec_mean), padded(k.vec_square), step
    )
    if full:
        k.vec_grad[...] = vec_grad[:, :share]
        k.vec_change[...] = parts[0][:, :share]
        k.vec_mean_new[...] = parts[1][:, :share]
        k.vec_square_new[...] = parts[2][:, :share]
        for copy in vars(k.go).values():
            copy.start()
        for copy in vars(k.go).values():
            copy.wait()
    else:
        k.own[rows:] = jnp.broadcast_to(parts[3], (TAIL, width)).astype(BF16)


def adam(summands, state, step, full):
    shape, vec_shape = state.master.shape, state.vec_master.shape
    outs, far = {}, {}
    if full:
        far = dict.fromkeys(("grad", "change", "mean_new", "square_new"), (shape, F32))
        far.update({"vec_" + name: (vec_shape, F32) for name in far})
    else:
        outs = {"own": ((shape[0] + TAIL, shape[1]), BF16)}
    return run_kernel(
        lambda k: adam_kernel(k, full), "adam_outputs" if full else "adam", {},
        {**summands, **vars(state)}, outs, far, {}, 0, 6, work=10**9, smem={"step": step},
    )


def place_blocks(pieces, share, rows_all, before=None):
    arrays = [piece[-1] for piece in pieces]
    width = arrays[0].shape[1]
    extra = [] if before is None else [*before]

    def kernel(*refs):
        ins, (target, tails, sems) = refs[: len(arrays)], refs[-3:]
        me = lax.axis_index("dp")
        owners = [z(me >> 2) * 4 + ((me & 3) ^ (2 * y + core)) for z, y, core, _ in pieces]
        copies = []
        for at, (owner, ref) in enumerate(zip(owners, ins)):
            there = pl.ds(pl.multiple_of(owner * share, share), share)
            copies.append(load(ref.at[:share], target.at[there], sems.at[at]))
        if extra:
            tails[...] = refs[len(arrays) + 1][...]
        for owner, ref in zip(owners, ins):
            tails[owner] = ref[share:]
        for copy in copies:
            copy.wait()

    return pl.pallas_call(
        kernel,
        name="place_blocks",
        in_specs=[VMEM] * len(arrays) + [HBM, VMEM][: len(extra)],
        out_specs=[HBM, VMEM],
        out_shape=[
            pltpu.HBM((rows_all, width), BF16),
            pltpu.VMEM((rows_all // share, TAIL, width), BF16),
        ],
        scratch_shapes=[pltpu.SemaphoreType.DMA((len(arrays),))],
        input_output_aliases={len(arrays): 0} if extra else {},
        compiler_params=pltpu.CompilerParams(vmem_limit_bytes=4 * 2**20),
        cost_estimate=pl.CostEstimate(flops=10**9, bytes_accessed=1, transcendentals=0),
    )(*[pltpu.with_memory_space_constraint(array, pltpu.VMEM) for array in arrays], *extra)


def either(middle, end):
    def kernel(k):
        @pl.when(at_middle())
        def _():
            k.out[...] = k.middle[...]

        @pl.when(jnp.logical_not(at_middle()))
        def _():
            k.out[...] = k.end[...]

    outs = dict(out=(end.shape, BF16))
    return quick_kernel(kernel, "either", dict(middle=middle, end=end), outs).out


def gather_blocks(own, share, rows_all, meanwhile):
    end1, middle1 = swapped(own, "dp", 4), swapped_middle(own)
    end1, from_y0 = lax.optimization_barrier((end1, swapped(own, "dp", 2)))
    end2, middle2 = swapped(middle1, "dp", 4), swapped_middle(end1)
    from_y1 = swapped(end1, "dp", 2)
    end3 = swapped(middle2, "dp", 4)
    second = either(middle1, end2)
    from_y2 = swapped(second, "dp", 2)
    third = either(middle2, end3)
    from_y3 = swapped(third, "dp", 2)

    def both(z, y, array):
        return [(z, y, 0, array), (z, y, 1, swapped(array, "dp", 1))]

    def same(z):
        return z

    def next_to(z):
        return z ^ 1

    def nearer(z):
        return 2 - (z >> 1)

    def farther(z):
        return 3 - 3 * (z >> 1)

    early = both(same, 0, own) + both(same, 1, from_y0) + both(next_to, 0, end1)
    early += both(next_to, 1, from_y1) + both(nearer, 0, second)
    first = place_blocks(early, share, rows_all)
    from_y3 = held_until(from_y3, *first, meanwhile)
    late = both(nearer, 1, from_y2) + both(farther, 0, third) + both(farther, 1, from_y3)
    return place_blocks(late, share, rows_all, first)


def body(
    inputs,
    lengths,
    cotangent,
    matrices,
    vectors,
    master_matrices,
    master_vectors,
    matrix_mean,
    matrix_square,
    vector_mean,
    vector_square,
    adam_step,
):
    row_count, seq_len, width = inputs.shape[1:]
    tokens = row_count * seq_len
    rows_all, vec_all = matrices.shape[1], vectors.shape[1]
    ffn = (rows_all - 6 * width) // 2
    half = rows_all // 2
    ranks = lax.axis_size("dp")
    share, vec_share = rows_all // ranks, vec_all // ranks
    by_swaps = ranks == 16 and share % 32 == 0
    block = (ranks // 4, share + TAIL, width) if by_swaps else (half, width)
    me = lax.axis_index("dp")

    x = inputs.reshape(tokens, width)
    cot = cotangent.reshape(tokens, width)
    mats = matrices.reshape(rows_all, width)
    lens_here = pltpu.SMEM(lengths.shape, jnp.int32)

    def spec(columns, dtype):
        return ((tokens, columns), dtype)

    full, low, deep = spec(width, F32), spec(width, BF16), spec(ffn, BF16)
    square, mask = ((width, width), BF16), spec(seq_len, F32)
    double, lse, w_ffn = ((2 * width, width), BF16), spec(HEADS // 2 * PAIR, F32), ((ffn, width), BF16)
    half_tokens = tokens // 2
    half_low, half_full = ((half_tokens, width), BF16), ((half_tokens, width), F32)
    half_double, half_triple = ((half_tokens, 2 * width), BF16), ((half_tokens, 3 * width), BF16)
    all_vecs, triple = ((1, vec_all), F32), spec(3 * width, BF16)
    sided = dict(keep=(block, BF16))
    if by_swaps:
        sided["give"] = (block, BF16)
    early = ((half - 6 * width, width), BF16)

    def wide(rows):
        return ((width // LANES, rows, LANES), F32)

    cross_half = lax.dynamic_slice(mats, ((4 + (me & 1)) * width, 0), (width, width), allow_negative_indices=False)
    cross_mine = swapped(cross_half, "section", 1)
    f = run_kernel(
        forward_kernel, "forward", dict(mats=mats, x=x, vectors=vectors, lengths=lengths), {},
        dict(
            h1=full, w_in=w_ffn, act=deep, slope=deep, pre2=full, h2=full,
            memory=half_low, w_cross=double, qc=low, w_out=w_ffn, vecs=all_vecs,
        ),
        dict(
            qkv=triple, lse=lse, mixed=low, pre1=full, mask=mask, w_attn_out=square,
            w_attn=((3 * width, width), BF16), low=low,
        ),
        dict(
            raw_attn=((3 * width, width), BF16), raw_cross=double, raw_ffn=w_ffn,
            x_here=low, wide=wide(ffn), raw_vecs=((1, vec_all), BF16), lens=lens_here,
        ),
        8, 10,
    )
    memory_far0 = swapped(f.memory, "section", 1)
    r = run_kernel(
        forward_rest_kernel, "forward_rest", {},
        dict(
            h1=f.h1, w_in=f.w_in, w_out=f.w_out, vecs=f.vecs, old_act=f.act, old_slope=f.slope,
            old_pre2=f.pre2, old_h2=f.h2,
        ),
        dict(act=deep, slope=deep, pre2=full, h2=full, memory=half_low), dict(low_rest=half_low), {},
        0, 6,
        (("old_act", "act"), ("old_slope", "slope"), ("old_pre2", "pre2"), ("old_h2", "h2")),
        work=WORK_REST,
    )
    memory_far1 = swapped(r.memory, "section", 1)
    cross_mine = held_until(cross_mine, f.memory)
    cross_other = swapped(cross_mine, "dp", 1)
    p = run_kernel(
        prepare_kernel, "prepare", dict(cot_all=cot, lengths=lengths),
        dict(cross_mine=cross_mine, cross_other=cross_other),
        dict(w_pairs=double, mask=mask, cot=low), {},
        dict(raw=double, wide=wide(2 * width), raw_cot=low, lens=lens_here),
        2, 4,
    )
    shared = dict(
        **vars(p), w_cross=f.w_cross, qc=f.qc, h1=f.h1, w_in=f.w_in, w_out=f.w_out, vecs=f.vecs,
    )
    for_tokens = dict(act=deep, side=deep, grad_ffn=low, low2=low, grad_qc=low, grad_sum2=full)
    far_half = dict(mixed=half_low, right=half_double)
    held = dict(
        pairs=half_double, slope=((half_tokens, ffn), F32), lse=((half_tokens, HEADS // 2 * PAIR), F32),
        grad_mixed=half_low, total=half_full, hidden2=half_full,
    )
    d = run_kernel(
        lambda k: decoder_kernel(k, 0), "decoder", {},
        dict(memory=memory_far0, near_memory=f.memory, **shared, enc_act=r.act, enc_slope=r.slope),
        dict(
            back=half_double, grad_values=half_low, vec_grads=all_vecs, **for_tokens, top=half_low,
        ),
        far_half, held,
        0, SPARE_D, (("enc_act", "act"), ("enc_slope", "side")), work=WORK_D,
    )
    back_far = swapped(d.back, "section", 1)
    before = {"old_" + name: getattr(d, name) for name in for_tokens}
    e = run_kernel(
        lambda k: decoder_kernel(k, 1), "decoder_rest", {},
        dict(
            memory=memory_far1, near_memory=r.memory, **shared, **before, vec_before=d.vec_grads,
            top_before=d.top, values_before=d.grad_values,
        ),
        dict(grad_memory=half_low, rest=half_triple, vec_grads=all_vecs, **for_tokens),
        dict(layer_out=low, **far_half), held,
        0, SPARE_D, [("old_" + name, name) for name in for_tokens], work=WORK_D,
    )
    grad_memory_far = swapped(e.grad_memory, "section", 1)
    rest_far = swapped(e.rest, "section", 1)
    ahead = dict(
        pre1=full, w_attn_out=square, mask=mask, lse=lse, qkv=triple,
        w_attn=((3 * width, width), BF16),
    )
    s = run_kernel(
        backward_kernel, "backward",
        dict(
            **{"far_" + name: getattr(f, name) for name in ahead},
            far_x=x, far_mixed=f.mixed, far_low=f.low, far_low_rest=r.low_rest,
            far_right0=d.right, far_right1=e.right, far_cross_mixed0=d.mixed, far_cross_mixed1=e.mixed,
        ),
        dict(
            dec_grad_ffn=e.grad_ffn, dec_vec_grads=e.vec_grads,
            back=back_far, grad_memory=grad_memory_far, act=e.act, side=e.side,
            low2=e.low2, grad_qc=e.grad_qc, grad_sum2=e.grad_sum2, pre2=r.pre2, h2=r.h2, h1=f.h1, w_in=f.w_in, w_out=f.w_out, w_cross=f.w_cross, vecs=f.vecs,
        ),
        dict(
            vec_grads=all_vecs, early=early, **sided, grad_attn=low, grad_qkv=triple,
            x=low, mixed=low, low=low, right=spec(2 * width, BF16), cross_mixed=low,
        ),
        dict(grad_x=full),
        dict(
            grad_pre=deep, grad_ffn=low, low1=low, wide=wide(ffn), grad_h1=full,
            flat=((2 * ffn, width), BF16), grad_mixed=low, **ahead,
        ),
        14, 9, work=4 * 10**10,
    )
    if by_swaps:
        core_high = swapped(s.give, "dp", 1)
    a = run_kernel(
        attn_grad_kernel, "attn_grad", {},
        dict(
            grad_qkv=s.grad_qkv, vec_grads=s.vec_grads, early=s.early, back=back_far, rest=rest_far,
            x=s.x, grad_attn=s.grad_attn, mixed=s.mixed, low=s.low, right=s.right, cross_mixed=s.cross_mixed,
        ),
        sided, {}, dict(wide=wide(3 * width), flat=((half, width), BF16)), 0, 4,
    )

    state = Refs(master=master_matrices[0], mean=matrix_mean[0], square=matrix_square[0])
    state = Refs(**vars(state), vec_master=master_vectors, vec_mean=vector_mean, vec_square=vector_square)
    if by_swaps:
        summands = sum_over_dp(a.keep, swapped(a.give, "dp", 1), s.keep, core_high)
        own = adam(summands, state, adam_step, False).own
        result = adam(summands, state, adam_step, True)
        new_mat, tails = gather_blocks(own, share, rows_all, result.change)
        new_vec = tails[:, 0, :vec_share].reshape(1, vec_all)
    else:
        whole = jnp.concatenate([a.keep, s.keep], axis=0)
        grad = lax.psum_scatter(whole, "dp", scatter_dimension=0, tiled=True).astype(F32)
        vec_grad = lax.dynamic_slice(
            lax.psum(s.vec_grads, "dp"), (0, me * vec_share), (1, vec_share)
        )
        step = jnp.full((1, width), adam_step[0].astype(F32))
        parts = adam_of(grad, state.master, state.mean, state.square, step)
        vec_step = jnp.full((1, width), adam_step[0].astype(F32))
        pad = ((0, 0), (0, width - vec_share))
        vec_parts = [
            part[:, :vec_share]
            for part in adam_of(
                *[jnp.pad(v, pad) for v in (vec_grad, master_vectors, vector_mean, vector_square)],
                vec_step,
            )
        ]
        names = ("change", "mean_new", "square_new")
        result = dict(grad=grad, vec_grad=vec_grad, **dict(zip(names, parts)))
        result.update({"vec_" + name: part for name, part in zip(names, vec_parts)})
        result = Refs(**result)
        new_mat = lax.all_gather(parts[3].astype(BF16), "dp", axis=0, tiled=True)
        new_vec = lax.all_gather(vec_parts[3].astype(BF16), "dp", axis=1, tiled=True)
    return (
        e.layer_out.reshape(1, row_count, seq_len, width),
        s.grad_x.reshape(1, row_count, seq_len, width),
        result.grad[None],
        result.vec_grad,
        result.change[None],
        result.vec_change,
        result.mean_new[None],
        result.square_new[None],
        result.vec_mean_new,
        result.vec_square_new,
        new_mat[None],
        new_vec,
    )


def solution(mesh):
    return jax.shard_map(
        body,
        mesh=mesh,
        in_specs=(
            P("section", "dp", None, None),
            P(None, "dp", None),
            P("dp", None, None),
            P("section", None, None),
            P("section", None),
            P("section", "dp", None),
            P("section", "dp"),
            P("section", "dp", None),
            P("section", "dp", None),
            P("section", "dp"),
            P("section", "dp"),
            P(),
        ),
        out_specs=(
            P("section", "dp", None, None),
            P("section", "dp", None, None),
            P("section", "dp", None),
            P("section", "dp"),
            P("section", "dp", None),
            P("section", "dp"),
            P("section", "dp", None),
            P("section", "dp", None),
            P("section", "dp"),
            P("section", "dp"),
            P("section", None, None),
            P("section", None),
        ),
        check_vma=False,
    )
```

```python
import math
import types

import jax
import jax.numpy as jnp
from jax import lax
from jax.experimental import pallas as pl
from jax.experimental.pallas import tpu as pltpu
from jax.sharding import PartitionSpec as P

HEADS = 8
HEAD_DIM = 64
PAIR = 2 * HEAD_DIM
LANES = 128
TAIL = 16
SUMMANDS = ("mine", "from_y", "from_end", "from_middle")
UNROLL_CHUNKS = True
WORK_REST = 10**10
WORK_D = 4 * 10**10
SPARE_D = 8

MASK_FILL = -1e30
NORM_EPS = 1e-05
ADAM_EPS = 1e-09
WARMUP_STEPS = 4000.0

F32 = jnp.float32
BF16 = jnp.bfloat16

BIAS_OUT, GAIN1, SHIFT1, GAIN2, SHIFT2, GAIN3, SHIFT3 = range(-7, 0)


def dot(left, right):
    return jnp.dot(left, right, preferred_element_type=F32)


def dot_nt(left, right):
    return lax.dot_general(left, right, (((1,), (1,)), ((), ())), preferred_element_type=F32)


def dot_tn(left, right):
    return lax.dot_general(left, right, (((0,), (0,)), ((), ())), preferred_element_type=F32)


def norm_parts(hidden):
    centre = hidden - jnp.mean(hidden, axis=-1, keepdims=True)
    rstd = lax.rsqrt(jnp.mean(centre * centre, axis=-1, keepdims=True) + NORM_EPS)
    return centre * rstd, rstd


def norm_backward(normal, rstd, gain, grad):
    scaled = grad * gain
    inner = jnp.mean(scaled * normal, axis=-1, keepdims=True)
    grad_in = rstd * (scaled - jnp.mean(scaled, axis=-1, keepdims=True) - normal * inner)
    grad_gain = jnp.sum(grad * normal, axis=0, keepdims=True)
    grad_shift = jnp.sum(grad, axis=0, keepdims=True)
    return grad_in, grad_gain, grad_shift


def act_parts(pre):
    cdf = 0.5 * (1.0 + lax.erf(pre * (0.5**0.5)))
    pdf = jnp.exp(-0.5 * pre * pre) * 0.3989422804014327
    return pre * cdf, cdf + pre * pdf


def split_rows(raw, wide, parts, out, base):
    width = raw.shape[1]
    for c in range(width // LANES):
        cut = slice(c * LANES, (c + 1) * LANES)
        wide[c, : parts * width] = raw[: parts * width, cut].astype(F32)
        for j in range(parts):
            out[(base + j) * width : (base + j + 1) * width, cut] = wide[
                c, pl.ds(j, width, stride=parts), :
            ].astype(BF16)


def put_part(wide, j, parts, values):
    rows, width = values.shape
    for c in range(width // LANES):
        wide[c, pl.ds(j, rows, stride=parts), :] = values[:, c * LANES : (c + 1) * LANES]


def take_parts(wide, rows, out, first):
    for c in range(wide.shape[0]):
        out[first : first + rows, c * LANES : (c + 1) * LANES] = wide[c, :rows].astype(BF16)


def sentence_ends(lens, side, row):
    ends, total = [], 0
    for j in range(lens.shape[2]):
        total = total + lens[side, row, j]
        ends.append(total)
    return ends


def sentence_of(ends, position):
    found = jnp.zeros(position.shape, jnp.int32)
    for end in ends:
        found = found + (position >= end).astype(jnp.int32)
    return found


def fill_mask(mask, lens, query_side, key_side, causal):
    seq_len = mask.shape[1]
    row_count, sents = lens.shape[1:]
    q_pos = lax.broadcasted_iota(jnp.int32, (seq_len, seq_len), 1)
    k_pos = lax.broadcasted_iota(jnp.int32, (seq_len, seq_len), 0)
    for r in range(row_count):
        q_ids = sentence_of(sentence_ends(lens, query_side, r), q_pos)
        k_ids = sentence_of(sentence_ends(lens, key_side, r), k_pos)
        same = jnp.where(q_ids == k_ids, 1, 0)
        if causal is not None:
            same = jnp.where(q_pos >= k_pos, same, jnp.where(causal, 0, same))
        allowed = jnp.where(q_ids == sents, 1, same)
        mask[r * seq_len : (r + 1) * seq_len] = allowed.astype(F32)


def both_heads(block, lane):
    even = (lane < HEAD_DIM).astype(BF16)
    return jnp.concatenate([block * even, block * (1 - even)], axis=0)


def both_heads_across(block):
    turned = block.T
    even = (lax.broadcasted_iota(jnp.int32, (PAIR, 1), 0) < HEAD_DIM).astype(BF16)
    return jnp.concatenate([turned * even, turned * (1 - even)], axis=1)


def one_of(stacked, lane):
    keys = stacked.shape[0] // 2
    return jnp.where(lane < HEAD_DIM, stacked[:keys], stacked[keys:])


def for_rows(mask, step):
    seq_len = mask.shape[1]

    def turn(row, carried):
        step(row, pl.ds(pl.multiple_of(row * seq_len, seq_len), seq_len), range(HEADS // 2))
        return carried

    lax.fori_loop(0, mask.shape[0] // seq_len, turn, 0)


def pair_lanes(first, p):
    return slice(first + p * PAIR, first + (p + 1) * PAIR)


def attend_forward(query, keys, values, mask, out, lse):
    seq_len = mask.shape[1]
    lane = lax.broadcasted_iota(jnp.int32, (1, PAIR), 1)
    (q_ref, q_at), (k_ref, k_at), (v_ref, v_at) = query, keys, values

    def step(row, rows, pairs):
        scores = [
            dot_nt(both_heads(k_ref[rows, pair_lanes(k_at, p)], lane), q_ref[rows, pair_lanes(q_at, p)])
            for p in pairs
        ]
        mixed = []
        for p in pairs:
            probs = []
            for half in range(2):
                part = scores[p][half * seq_len : (half + 1) * seq_len] * HEAD_DIM ** (-0.5)
                part = jnp.where(mask[rows] > 0.0, part, MASK_FILL)
                top = jnp.max(part, axis=0, keepdims=True)
                raised = jnp.exp(part - top)
                total = jnp.sum(raised, axis=0, keepdims=True)
                probs.append((raised * (1.0 / total)).astype(BF16))
                lse[row, 2 * p + half : 2 * p + half + 1] = top + jnp.log(total)
            values = both_heads_across(v_ref[rows, pair_lanes(v_at, p)])
            mixed.append(dot(values, jnp.concatenate(probs, axis=0)))
        for p in pairs:
            out[rows, pair_lanes(0, p)] = mixed[p].T.astype(BF16)

    for_rows(mask, step)


def attend_backward(query, keys, values, mask, lse, grad_out, grad_q, grad_k, grad_v):
    seq_len = mask.shape[1]
    lane = lax.broadcasted_iota(jnp.int32, (1, PAIR), 1)
    scale = HEAD_DIM ** (-0.5)
    (q_ref, q_at), (k_ref, k_at), (v_ref, v_at) = query, keys, values
    (gq_ref, gq_at), (gk_ref, gk_at), (gv_ref, gv_at) = grad_q, grad_k, grad_v

    def step(row, rows, pairs):
        qs = [q_ref[rows, pair_lanes(q_at, p)] for p in pairs]
        ks = [k_ref[rows, pair_lanes(k_at, p)] for p in pairs]
        gos = [grad_out[rows, pair_lanes(0, p)] for p in pairs]
        scores = [dot_nt(both_heads(ks[p], lane), qs[p]) for p in pairs]
        grad_probs = [
            dot_nt(both_heads(v_ref[rows, pair_lanes(v_at, p)], lane), gos[p]) for p in pairs
        ]
        probs, grad_scores = [], []
        for p in pairs:
            prob_parts, score_parts = [], []
            for half in range(2):
                cut = slice(half * seq_len, (half + 1) * seq_len)
                part = jnp.where(mask[rows] > 0.0, scores[p][cut] * scale, MASK_FILL)
                prob = jnp.exp(part - lse[row, 2 * p + half : 2 * p + half + 1])
                gp = grad_probs[p][cut]
                inner = jnp.sum(prob * gp, axis=0, keepdims=True)
                prob_parts.append(prob.astype(BF16))
                score_parts.append((prob * (gp - inner)).astype(BF16))
            probs.append(jnp.concatenate(prob_parts, axis=0))
            grad_scores.append(jnp.concatenate(score_parts, axis=0))
        grad_vs = [dot(probs[p], gos[p]) for p in pairs]
        grad_ks = [dot(grad_scores[p], qs[p]) for p in pairs]
        grad_qs = [dot(both_heads_across(ks[p]), grad_scores[p]) for p in pairs]
        for p in pairs:
            gv_ref[rows, pair_lanes(gv_at, p)] = one_of(grad_vs[p], lane).astype(BF16)
            gk_ref[rows, pair_lanes(gk_at, p)] = (one_of(grad_ks[p], lane) * scale).astype(BF16)
            gq_ref[rows, pair_lanes(gq_at, p)] = (grad_qs[p].T * scale).astype(BF16)

    for_rows(mask, step)


def small(vecs, which, width):
    pieces = vecs.shape[1] // width
    at = (which if which >= 0 else pieces + which) * width
    return vecs[:, at : at + width].astype(F32)


def set_small(vecs, which, width, value):
    pieces = vecs.shape[1] // width
    at = (which if which >= 0 else pieces + which) * width
    vecs[:, at : at + width] = value


def where_am_i():
    return lax.axis_index("section"), lax.rem(lax.axis_index("dp"), 2)


def for_chunks(count, width, step):
    def turn(j, carried):
        step(j, pl.ds(pl.multiple_of(j * width, width), width))
        return carried

    lax.fori_loop(0, count, turn, 0, unroll=UNROLL_CHUNKS)


def ffn_forward(normed, w_in, w_out, vecs, act, slope, total):
    width = normed.shape[1]
    low = normed.astype(BF16)
    total[...] = normed + small(vecs, BIAS_OUT, width)

    def step(j, cut):
        pre = dot(low, w_in[cut]) + vecs[:, cut]
        value, derivative = act_parts(pre)
        value = value.astype(BF16)
        act[:, cut] = value
        slope[:, cut] = derivative.astype(slope.dtype)
        total[...] += dot(value, w_out[cut])

    for_chunks(w_in.shape[0] // width, width, step)


def ffn_backward(grad_low, w_in, w_out, slope, grad_pre, vec_grads, total):
    width = grad_low.shape[1]

    def step(j, cut):
        grad = (dot_nt(grad_low, w_out[cut]) * slope[:, cut].astype(F32)).astype(BF16)
        grad_pre[:, cut] = grad
        vec_grads[:, cut] = jnp.sum(grad.astype(F32), axis=0, keepdims=True)
        total[...] += dot_nt(grad, w_in[cut])

    for_chunks(w_in.shape[0] // width, width, step)


def load(source, target, sem):
    copy = pltpu.make_async_copy(source, target, sem)
    copy.start()
    return copy


def memory_of(k, rows):
    width = k.h1.shape[1]
    vecs = k.vecs
    ffn_forward(k.h1[rows], k.w_in, k.w_out, vecs, k.act.at[rows], k.slope.at[rows], k.total)
    normal, rstd = norm_parts(k.total[...])
    k.normal2[rows], k.rstd2[rows] = normal, jnp.broadcast_to(rstd, (rstd.shape[0], LANES))
    normal, rstd = norm_parts(normal * small(vecs, GAIN2, width) + small(vecs, SHIFT2, width))
    k.normal3[rows], k.rstd3[rows] = normal, jnp.broadcast_to(rstd, (rstd.shape[0], LANES))
    third = normal * small(vecs, GAIN3, width) + small(vecs, SHIFT3, width)
    k.memory[...] = third.astype(BF16)


def forward_kernel(k):
    width = k.h1.shape[1]
    ffn = k.w_in.shape[0]
    sec, _ = where_am_i()
    get_lens = load(k.lengths, k.lens, k.sems.at[7])
    get_in = load(k.mats.at[: 3 * width], k.raw_attn, k.sems.at[0])
    get_x = load(k.x, k.x_here, k.sems.at[1])
    get_vecs = load(k.vectors, k.raw_vecs, k.sems.at[2])
    get_attn_out = load(k.mats.at[3 * width : 4 * width], k.w_attn_out, k.sems.at[3])
    get_ffn = load(k.mats.at[6 * width : 6 * width + ffn], k.raw_ffn, k.sems.at[4])
    get_out = load(k.mats.at[6 * width + ffn :], k.w_out, k.sems.at[5])
    get_cross = pltpu.make_async_copy(k.mats.at[4 * width : 6 * width], k.raw_cross, k.sems.at[6])

    @pl.when(sec == 1)
    def _():
        get_cross.start()

    get_lens.wait()
    fill_mask(k.mask, k.lens, sec, sec, sec == 1)
    k.go.mask.start()
    get_in.wait()
    split_rows(k.raw_attn, k.wide, 3, k.w_attn, 0)
    k.go.w_attn.start()
    get_x.wait()
    for j in range(3):
        part = dot(k.x_here[...], k.w_attn[j * width : (j + 1) * width])
        k.qkv[:, j * width : (j + 1) * width] = part.astype(BF16)
    k.go.qkv.start()
    attend_forward((k.qkv, 0), (k.qkv, width), (k.qkv, 2 * width), k.mask, k.mixed, k.lse)
    k.go.mixed.start()
    k.go.lse.start()
    get_vecs.wait()
    k.vecs[...] = k.raw_vecs[...].astype(F32)
    vecs = k.vecs
    get_attn_out.wait()
    k.go.w_attn_out.start()
    hidden = k.x_here[...].astype(F32) + dot(k.mixed[...], k.w_attn_out[...])
    normal, rstd = norm_parts(hidden)
    k.normal1[...], k.rstd1[...] = normal, jnp.broadcast_to(rstd, (rstd.shape[0], LANES))
    k.go.normal1.start()
    k.go.rstd1.start()
    k.h1[...] = normal * small(vecs, GAIN1, width) + small(vecs, SHIFT1, width)
    get_ffn.wait()
    split_rows(k.raw_ffn, k.wide, ffn // width, k.w_in, 0)
    get_out.wait()

    @pl.when(sec == 0)
    def _():
        memory_of(k, slice(0, k.memory.shape[0]))
        k.low[: k.memory.shape[0]] = k.memory[...]
        k.go.low.start()

    @pl.when(sec == 1)
    def _():
        k.low[...] = k.h1[...].astype(BF16)
        k.go.low.start()
        get_cross.wait()
        split_rows(k.raw_cross, k.wide, 2, k.w_cross, 0)
        k.qc[...] = dot(k.low[...], k.w_cross[:width]).astype(BF16)

    k.go.mask.wait()
    k.go.w_attn.wait()
    k.go.qkv.wait()
    k.go.mixed.wait()
    k.go.lse.wait()
    k.go.w_attn_out.wait()
    k.go.normal1.wait()
    k.go.rstd1.wait()
    k.go.low.wait()


def forward_rest_kernel(k):
    sec, _ = where_am_i()

    @pl.when(sec == 0)
    def _():
        half = k.memory.shape[0]
        memory_of(k, slice(half, 2 * half))
        k.low_rest[...] = k.memory[...]
        k.go.low_rest.start()
        k.go.low_rest.wait()


def prepare_kernel(k):
    width = k.raw.shape[1]
    seq_len = k.mask.shape[1]
    sec, core = where_am_i()

    @pl.when(sec == 1)
    def _():
        get_cot = load(k.cot_all, k.raw_cot, k.sems.at[0])
        get_lens = load(k.lengths, k.lens, k.sems.at[1])
        k.raw[pl.ds(pl.multiple_of(core * width, width), width)] = k.cross_mine[...]
        k.raw[pl.ds(pl.multiple_of((1 - core) * width, width), width)] = k.cross_other[...]
        split_rows(k.raw, k.wide, 2, k.w_pairs, 0)
        get_lens.wait()
        fill_mask(k.mask, k.lens, 1, 0, None)
        get_cot.wait()
        position = lax.broadcasted_iota(jnp.int32, (seq_len, 1), 0)
        for r in range(k.lens.shape[1]):
            used = sentence_ends(k.lens, 1, r)[-1]
            rows = slice(r * seq_len, (r + 1) * seq_len)
            k.cot[rows] = jnp.where(position < used, k.raw_cot[rows].astype(F32), 0.0).astype(BF16)


def decoder_kernel(k, part):
    half, width = k.memory.shape
    rows = slice(part * half, (part + 1) * half)
    vecs = k.vecs
    sec, _ = where_am_i()
    top = k.layer_out.at[rows] if part == 1 else k.top
    grad_keys = (k.back, width) if part == 0 else (k.rest, width)
    grad_values = (k.grad_values, 0) if part == 0 else (k.rest, 2 * width)
    if part == 1:
        k.layer_out[:half] = k.top_before[...]

    @pl.when(sec == 0)
    def _():
        top[...] = k.near_memory[...]

    @pl.when(sec == 1)
    def _():
        mask, qc, act, side = k.mask.at[rows], k.qc.at[rows], k.act.at[rows], k.side.at[rows]
        for j in range(2):
            pair = dot(k.memory[...], k.w_pairs[j * width : (j + 1) * width])
            k.pairs[:, j * width : (j + 1) * width] = pair.astype(BF16)
        attend_forward((qc, 0), (k.pairs, 0), (k.pairs, width), mask, k.mixed, k.lse)
        k.go.mixed.start()
        hidden2 = k.h1[rows] + dot(k.mixed[...], k.w_cross[width:])
        gain2, shift2 = small(vecs, GAIN2, width), small(vecs, SHIFT2, width)
        normal2, rstd2 = norm_parts(hidden2)
        k.normal2[...], k.rstd2[...] = normal2, jnp.broadcast_to(rstd2, (half, LANES))
        normed2 = normal2 * gain2 + shift2
        k.low2[rows] = normed2.astype(BF16)
        ffn_forward(normed2, k.w_in, k.w_out, vecs, act, k.slope, k.total)
        normal3, rstd3 = norm_parts(k.total[...])
        gain3, shift3 = small(vecs, GAIN3, width), small(vecs, SHIFT3, width)
        top[...] = (normal3 * gain3 + shift3).astype(BF16)
        grad_sum3, d_gain, d_shift = norm_backward(
            normal3, rstd3, gain3, k.cot[rows].astype(F32)
        )
        set_small(k.vec_grads, GAIN3, width, d_gain)
        set_small(k.vec_grads, SHIFT3, width, d_shift)
        grad_low = grad_sum3.astype(BF16)
        k.grad_ffn[rows] = grad_low
        set_small(
            k.vec_grads, BIAS_OUT, width, jnp.sum(grad_low.astype(F32), axis=0, keepdims=True)
        )
        k.total[...] = grad_sum3
        ffn_backward(grad_low, k.w_in, k.w_out, k.slope, side, k.vec_grads, k.total)
        grad_hidden2, d_gain, d_shift = norm_backward(
            k.normal2[...], k.rstd2[:, :1], gain2, k.total[...]
        )
        set_small(k.vec_grads, GAIN2, width, d_gain)
        set_small(k.vec_grads, SHIFT2, width, d_shift)
        k.grad_sum2[rows] = grad_hidden2
        low = grad_hidden2.astype(BF16)
        k.right[:, width:] = low
        k.grad_mixed[...] = dot_nt(low, k.w_cross[width:]).astype(BF16)
        attend_backward(
            (qc, 0), (k.pairs, 0), (k.pairs, width), mask, k.lse, k.grad_mixed,
            (k.right, 0), grad_keys, grad_values,
        )
        k.go.right.start()
        k.grad_qc[rows] = k.right[:, :width]
        back = jnp.zeros((half, width), F32)
        for j, (ref, at) in enumerate((grad_keys, grad_values)):
            back = back + dot_nt(ref[:, at : at + width], k.w_pairs[j * width : (j + 1) * width])
        if part == 0:
            k.back[:, :width] = back.astype(BF16)
        else:
            k.grad_memory[...] = back.astype(BF16)
            k.rest[:, :width] = k.values_before[...]
        if part == 1:
            k.vec_grads[...] += k.vec_before[...]
        k.go.mixed.wait()
        k.go.right.wait()

    if part == 1:
        k.go.layer_out.start()
        k.go.layer_out.wait()


def ffn_weight_grads(k, act, low, grad_pre, grad_ffn):
    width = k.h1.shape[1]
    ffn = k.w_in.shape[0]
    chunks = ffn // width

    def step(j, cut):
        put_part(k.wide, j, chunks, dot_tn(low[...], grad_pre[:, cut]))
        there = pl.ds(pl.multiple_of(ffn + j * width, width), width)
        k.flat[there] = dot_tn(act[:, cut], grad_ffn[...]).astype(BF16)

    for_chunks(chunks, width, step)


def put_sides(k, first, vec_grads, first_owner, core):
    width = k.flat.shape[1]
    if len(k.keep.shape) == 2:
        k.keep[...] = k.flat[first : first + k.keep.shape[0]]
        return
    count, rows, _ = k.keep.shape
    rows -= TAIL
    share = vec_grads.shape[1] // (4 * count)

    def tail(at):
        owner = first_owner + at
        row = vec_grads[:, owner * share : (owner + 1) * share]
        row = jnp.concatenate([row, jnp.zeros((1, width - share), F32)], axis=1)
        return jnp.broadcast_to(row, (TAIL, width)).astype(BF16)

    for at in range(count):
        mine = first + (2 * at + core) * rows
        other = first + (2 * at + 1 - core) * rows
        k.keep[at, :rows] = k.flat[pl.ds(pl.multiple_of(mine, TAIL), rows)]
        k.give[at, :rows] = k.flat[pl.ds(pl.multiple_of(other, TAIL), rows)]

        @pl.when(core == 0)
        def _(at=at):
            k.keep[at, rows:] = tail(2 * at)
            k.give[at, rows:] = tail(2 * at + 1)

        @pl.when(core == 1)
        def _(at=at):
            k.keep[at, rows:] = tail(2 * at + 1)
            k.give[at, rows:] = tail(2 * at)


def backward_kernel(k):
    width = k.h1.shape[1]
    ffn = k.w_in.shape[0]
    vecs = k.vecs
    sec, core = where_am_i()
    half = k.back.shape[0]
    first, rest = slice(0, half), slice(half, 2 * half)
    wanted = ("normal1", "rstd1", "w_attn_out", "mask", "lse", "qkv", "w_attn", "x", "mixed")
    arriving = [(getattr(k, "far_" + name), getattr(k, name)) for name in wanted]
    arriving += [
        (k.far_low.at[first], k.low.at[first]),
        (k.far_right0, k.right.at[first]),
        (k.far_right1, k.right.at[rest]),
        (k.far_cross_mixed0, k.cross_mixed.at[first]),
        (k.far_cross_mixed1, k.cross_mixed.at[rest]),
    ]
    coming = [load(*ends, k.sems.at[at]) for at, ends in enumerate(arriving)]
    last_sem = k.sems.at[len(coming)]

    @pl.when(sec == 0)
    def _():
        load(k.far_low_rest, k.low.at[rest], last_sem)

    @pl.when(sec == 1)
    def _():
        load(k.far_low.at[rest], k.low.at[rest], last_sem)

    coming.append(pltpu.make_async_copy(k.far_low_rest, k.low.at[rest], last_sem))

    @pl.when(sec == 0)
    def _():
        grad_memory = jnp.concatenate([k.back[:, :width], k.grad_memory[...]], axis=0)
        grad, d_gain, d_shift = norm_backward(
            k.normal3[...], k.rstd3[:, :1], small(vecs, GAIN3, width), grad_memory.astype(F32)
        )
        set_small(k.vec_grads, GAIN3, width, d_gain)
        set_small(k.vec_grads, SHIFT3, width, d_shift)
        total, d_gain, d_shift = norm_backward(
            k.normal2[...], k.rstd2[:, :1], small(vecs, GAIN2, width), grad
        )
        set_small(k.vec_grads, GAIN2, width, d_gain)
        set_small(k.vec_grads, SHIFT2, width, d_shift)
        grad_low = total.astype(BF16)
        k.grad_ffn[...] = grad_low
        set_small(
            k.vec_grads, BIAS_OUT, width, jnp.sum(grad_low.astype(F32), axis=0, keepdims=True)
        )
        k.low1[...] = k.h1[...].astype(BF16)
        k.grad_h1[...] = total
        ffn_backward(grad_low, k.w_in, k.w_out, k.side, k.grad_pre, k.vec_grads, k.grad_h1)
        ffn_weight_grads(k, k.act, k.low1, k.grad_pre, k.grad_ffn)

    @pl.when(sec == 1)
    def _():
        k.vec_grads[...] = k.dec_vec_grads[...]
        k.grad_h1[...] = k.grad_sum2[...] + dot_nt(k.grad_qc[...], k.w_cross[:width])
        ffn_weight_grads(k, k.act, k.low2, k.side, k.dec_grad_ffn)

    take_parts(k.wide, ffn, k.flat, 0)
    early = k.early.shape[0]
    k.early[...] = k.flat[:early]
    for copy in coming:
        copy.wait()
    grad, d_gain, d_shift = norm_backward(
        k.normal1[...], k.rstd1[:, :1], small(vecs, GAIN1, width), k.grad_h1[...]
    )
    set_small(k.vec_grads, GAIN1, width, d_gain)
    set_small(k.vec_grads, SHIFT1, width, d_shift)
    put_sides(k, early, k.vec_grads, 2 * k.keep.shape[0], core)
    low = grad.astype(BF16)
    k.grad_attn[...] = low
    k.grad_mixed[...] = dot_nt(low, k.w_attn_out[...]).astype(BF16)
    attend_backward(
        (k.qkv, 0), (k.qkv, width), (k.qkv, 2 * width), k.mask, k.lse, k.grad_mixed,
        (k.grad_qkv, 0), (k.grad_qkv, width), (k.grad_qkv, 2 * width),
    )
    for j in range(3):
        cut = slice(j * width, (j + 1) * width)
        grad = grad + dot_nt(k.grad_qkv[:, cut], k.w_attn[cut])
    k.grad_x[...] = grad
    k.go.grad_x.start()
    k.go.grad_x.wait()


def attn_grad_kernel(k):
    width = k.x.shape[1]
    half = k.rest.shape[0]
    sec, core = where_am_i()

    def step(j, cut):
        put_part(k.wide, j, 3, dot_tn(k.x[...], k.grad_qkv[:, cut]))

    for_chunks(3, width, step)
    take_parts(k.wide, 3 * width, k.flat, 0)
    k.flat[3 * width : 4 * width] = dot_tn(k.mixed[...], k.grad_attn[...]).astype(BF16)

    @pl.when(sec == 0)
    def _():
        for j in range(2):
            first = k.back[:, width:] if j == 0 else k.rest[:, :width]
            second = k.rest[:, (j + 1) * width : (j + 2) * width]
            put_part(k.wide, j, 2, dot_tn(k.low[:half], first) + dot_tn(k.low[half:], second))

    @pl.when(sec == 1)
    def _():
        put_part(k.wide, 0, 2, dot_tn(k.low[...], k.right[:, :width]))
        put_part(k.wide, 1, 2, dot_tn(k.cross_mixed[...], k.right[:, width:]))

    take_parts(k.wide, 2 * width, k.flat, 4 * width)
    k.flat[6 * width :] = k.early[...]
    put_sides(k, 0, k.vec_grads, 0, core)


class Refs(types.SimpleNamespace):
    pass


def run_kernel(kernel, name, hbm, vmem, outs, far_outs, scratch, loads, spare, reuse=(), work=10**10, smem=None):
    smem = smem or {}
    ins = {**smem, **hbm, **vmem}
    near = {n: pltpu.VMEM(*spec) for n, spec in far_outs.items()}
    near.update({n: pltpu.VMEM(*spec) if isinstance(spec, tuple) else spec for n, spec in scratch.items()})
    names = [*ins, *outs, *far_outs, *near, "sems", "leave_sems"]

    def run(*refs):
        k = Refs(**dict(zip(names, refs)))
        first = len(ins) + len(outs)
        k.go = Refs()
        for at, n in enumerate(far_outs):
            copy = pltpu.make_async_copy(getattr(k, n), refs[first + at], k.leave_sems.at[at])
            setattr(k.go, n, copy)
        kernel(k)

    results = pl.pallas_call(
        run,
        name=name,
        in_specs=[SMEM] * len(smem) + [HBM] * len(hbm) + [VMEM] * len(vmem),
        out_specs=[VMEM] * len(outs) + [HBM] * len(far_outs),
        out_shape=[pltpu.VMEM(*spec) for spec in outs.values()]
        + [pltpu.HBM(*spec) for spec in far_outs.values()],
        scratch_shapes=[
            *near.values(),
            pltpu.SemaphoreType.DMA((max(loads, 1),)),
            pltpu.SemaphoreType.DMA((max(len(far_outs), 1),)),
        ],
        compiler_params=pltpu.CompilerParams(
            vmem_limit_bytes=int(spare * 2**20)
            + sum(math.prod(b.shape) * jnp.dtype(b.dtype).itemsize for b in near.values())
        ),
        input_output_aliases={[*ins].index(old): [*outs].index(new) for old, new in reuse},
        cost_estimate=pl.CostEstimate(flops=work, bytes_accessed=1, transcendentals=0),
    )(
        *smem.values(),
        *[pltpu.with_memory_space_constraint(array, pltpu.HBM) for array in hbm.values()],
        *[pltpu.with_memory_space_constraint(array, pltpu.VMEM) for array in vmem.values()],
    )
    return Refs(**dict(zip([*outs, *far_outs], results)))


SMEM = pl.BlockSpec(memory_space=pltpu.SMEM)
HBM = pl.BlockSpec(memory_space=pltpu.HBM)
VMEM = pl.BlockSpec(memory_space=pltpu.VMEM)
ANY = pl.BlockSpec(memory_space=pl.ANY)


def swapped(array, axis, bit):
    devices = lax.axis_size(axis)
    return lax.ppermute(array, axis, [(i, i ^ bit) for i in range(devices)])


def held_until(array, *others):
    return lax.optimization_barrier((array, *others))[0]


def own_bit(bit):
    return (lax.axis_index("dp") >> bit) & 1


def swapped_middle(array):
    ranks = lax.axis_size("dp")
    quarter = ranks // 4
    pairs = [(i, i + quarter) for i in range(quarter, 2 * quarter)]
    pairs += [(j, i) for i, j in pairs]
    outer = [*range(quarter), *range(ranks - quarter, ranks)]
    return lax.ppermute(array, "dp", pairs + [(i, i ^ 1) for i in outer])


def at_middle():
    return own_bit(2) != own_bit(3)


def quick_kernel(kernel, name, ins, outs):
    return run_kernel(kernel, name, {}, ins, outs, {}, {}, 0, 4, work=10**8)


def sum_of_cores(far, cut, low, core_low, high, core_high):
    shape = (cut.stop - cut.start, low.shape[2])

    def kernel(k):
        y, z = own_bit(1), own_bit(2)

        def fill(keep, core, at, give, mine):
            here, there = 2 * at + y, 2 * at + 1 - y
            give[...] = (keep[there, cut].astype(F32) + core[there, cut].astype(F32)).astype(BF16)
            mine[...] = keep[here, cut].astype(F32) + core[here, cut].astype(F32)

        @pl.when(own_bit(3) == 0)
        def _():
            side = (k.high, k.core_high) if far else (k.low, k.core_low)
            fill(*side, 1 if far else 1 - z, k.give0, k.mine0)
            fill(*side, 0 if far else z, k.give1, k.mine1)

        @pl.when(own_bit(3) == 1)
        def _():
            side = (k.low, k.core_low) if far else (k.high, k.core_high)
            fill(*side, 0 if far else 1 - z, k.give0, k.mine0)
            fill(*side, 1 if far else z, k.give1, k.mine1)

    ins = dict(low=low, core_low=core_low, high=high, core_high=core_high)
    outs = dict(give0=(shape, BF16), mine0=(shape, F32), give1=(shape, BF16), mine1=(shape, F32))
    return quick_kernel(kernel, "sum_of_cores", ins, outs)


def added(wide, part, middle=None, full=False):
    def kernel(k):
        total = k.wide[...] + k.part[...].astype(F32)
        if middle is not None:
            total = total + jnp.where(at_middle(), k.middle[...].astype(F32), 0.0)
        k.low[...] = total.astype(BF16)
        if full:
            k.full[...] = total

    ins = dict(wide=wide, part=part)
    if middle is not None:
        ins = dict(wide=wide, part=part, middle=middle)
    outs = dict(low=(wide.shape, BF16))
    if full:
        outs = dict(low=(wide.shape, BF16), full=(wide.shape, F32))
    return quick_kernel(kernel, "added", ins, outs)


def sum_over_dp(cut, low, core_low, high, core_high):
    far = sum_of_cores(True, cut, low, core_low, high, core_high)
    near = sum_of_cores(False, cut, low, core_low, high, core_high)
    from_y3, from_y2 = swapped(far.give0, "dp", 2), swapped(far.give1, "dp", 2)
    from_y1, from_y0 = swapped(near.give0, "dp", 2), swapped(near.give1, "dp", 2)
    third = added(far.mine0, from_y3, full=True)
    from_end3 = swapped(third.low, "dp", 4)
    second = added(far.mine1, from_y2, full=True)
    from_end2 = swapped(second.low, "dp", 4)
    from_middle3 = swapped_middle(added(third.full, from_end3).low)
    from_middle2 = swapped_middle(added(second.full, from_end2).low)
    from_end1 = swapped(added(near.mine0, from_y1, from_middle3).low, "dp", 4)
    return dict(zip(SUMMANDS, (near.mine1, from_y0, from_end1, from_middle2)))


def adam_of(grad, master, mean_old, square_old, step):
    mean_new = 0.9 * mean_old + 0.1 * grad
    square_new = 0.98 * square_old + 0.02 * grad * grad
    rate = step.shape[1] ** (-0.5) * jnp.minimum(lax.rsqrt(step), step * WARMUP_STEPS ** (-1.5))
    mean_share = 1.0 - jnp.exp(step * math.log(0.9))
    square_share = 1.0 - jnp.exp(step * math.log(0.98))
    fixed_mean = mean_new * (1.0 / mean_share)
    fixed_square = square_new * (1.0 / square_share)
    change = -rate * fixed_mean / (jnp.sqrt(fixed_square) + ADAM_EPS)
    return change, mean_new, square_new, master + change


def adam_kernel(k, full):
    width = k.master.shape[1]
    share = k.vec_master.shape[1]
    step = jnp.full((1, width), k.step[0], jnp.int32).astype(F32)
    rows = k.master.shape[0]
    middle = at_middle()
    totals = []
    for at in range(len([name for name in vars(k) if name.startswith("mine")])):
        mine, *low = [getattr(k, f"{name}{at}")[...].astype(F32) for name in SUMMANDS]
        from_y, from_end, from_middle = low
        totals.append(mine + from_y + from_end + jnp.where(middle, from_middle, 0.0))
    total = jnp.concatenate(totals, axis=0)
    grad, vec_grad = total[:rows], total[rows : rows + 1]
    parts = adam_of(grad, k.master[...], k.mean[...], k.square[...], step)
    if full:
        k.grad[...] = grad
        k.change[...], k.mean_new[...], k.square_new[...] = parts[:3]
    else:
        k.own[:rows] = parts[3].astype(BF16)
    pad = jnp.zeros((1, width - share), F32)

    def padded(ref):
        return jnp.concatenate([ref[...], pad], axis=1)

    parts = adam_of(
        vec_grad, padded(k.vec_master), padded(k.vec_mean), padded(k.vec_square), step
    )
    if full:
        k.vec_grad[...] = vec_grad[:, :share]
        k.vec_change[...] = parts[0][:, :share]
        k.vec_mean_new[...] = parts[1][:, :share]
        k.vec_square_new[...] = parts[2][:, :share]
        for copy in vars(k.go).values():
            copy.start()
        for copy in vars(k.go).values():
            copy.wait()
    else:
        k.own[rows:] = jnp.broadcast_to(parts[3], (TAIL, width)).astype(BF16)


def adam(summands, state, step, full):
    shape, vec_shape = state.master.shape, state.vec_master.shape
    outs, far = {}, {}
    if full:
        far = dict.fromkeys(("grad", "change", "mean_new", "square_new"), (shape, F32))
        far.update({"vec_" + name: (vec_shape, F32) for name in far})
    else:
        outs = {"own": ((shape[0] + TAIL, shape[1]), BF16)}
    return run_kernel(
        lambda k: adam_kernel(k, full), "adam_outputs" if full else "adam", {},
        {**summands, **vars(state)}, outs, far, {}, 0, 6, work=10**9, smem={"step": step},
    )


def place_blocks(pieces, share, rows_all, before=None):
    arrays = [piece[-1] for piece in pieces]
    width = arrays[0].shape[1]
    extra = [] if before is None else [*before]

    def kernel(*refs):
        ins, (target, tails, sems) = refs[: len(arrays)], refs[-3:]
        me = lax.axis_index("dp")
        owners = [z(me >> 2) * 4 + ((me & 3) ^ (2 * y + core)) for z, y, core, _ in pieces]
        copies = []
        for at, (owner, ref) in enumerate(zip(owners, ins)):
            there = pl.ds(pl.multiple_of(owner * share, share), share)
            copies.append(load(ref.at[:share], target.at[there], sems.at[at]))
        if extra:
            tails[...] = refs[len(arrays) + 1][...]
        for owner, ref in zip(owners, ins):
            tails[owner] = ref[share:]
        for copy in copies:
            copy.wait()

    return pl.pallas_call(
        kernel,
        name="place_blocks",
        in_specs=[VMEM] * len(arrays) + [HBM, VMEM][: len(extra)],
        out_specs=[HBM, VMEM],
        out_shape=[
            pltpu.HBM((rows_all, width), BF16),
            pltpu.VMEM((rows_all // share, TAIL, width), BF16),
        ],
        scratch_shapes=[pltpu.SemaphoreType.DMA((len(arrays),))],
        input_output_aliases={len(arrays): 0} if extra else {},
        compiler_params=pltpu.CompilerParams(vmem_limit_bytes=4 * 2**20),
        cost_estimate=pl.CostEstimate(flops=10**9, bytes_accessed=1, transcendentals=0),
    )(*[pltpu.with_memory_space_constraint(array, pltpu.VMEM) for array in arrays], *extra)


def either(middle, end):
    def kernel(k):
        @pl.when(at_middle())
        def _():
            k.out[...] = k.middle[...]

        @pl.when(jnp.logical_not(at_middle()))
        def _():
            k.out[...] = k.end[...]

    outs = dict(out=(end.shape, BF16))
    return quick_kernel(kernel, "either", dict(middle=middle, end=end), outs).out


def gather_blocks(own, share, rows_all, meanwhile):
    end1, middle1 = swapped(own, "dp", 4), swapped_middle(own)
    end1, from_y0 = lax.optimization_barrier((end1, swapped(own, "dp", 2)))
    end2, middle2 = swapped(middle1, "dp", 4), swapped_middle(end1)
    from_y1 = swapped(end1, "dp", 2)
    end3 = swapped(middle2, "dp", 4)
    second = either(middle1, end2)
    from_y2 = swapped(second, "dp", 2)
    third = either(middle2, end3)
    from_y3 = swapped(third, "dp", 2)

    def both(z, y, array):
        return [(z, y, 0, array), (z, y, 1, swapped(array, "dp", 1))]

    def same(z):
        return z

    def next_to(z):
        return z ^ 1

    def nearer(z):
        return 2 - (z >> 1)

    def farther(z):
        return 3 - 3 * (z >> 1)

    early = both(same, 0, own) + both(same, 1, from_y0) + both(next_to, 0, end1)
    early += both(next_to, 1, from_y1) + both(nearer, 0, second)
    first = place_blocks(early, share, rows_all)
    from_y3 = held_until(from_y3, *first, meanwhile)
    late = both(nearer, 1, from_y2) + both(farther, 0, third) + both(farther, 1, from_y3)
    return place_blocks(late, share, rows_all, first)


def body(
    inputs,
    lengths,
    cotangent,
    matrices,
    vectors,
    master_matrices,
    master_vectors,
    matrix_mean,
    matrix_square,
    vector_mean,
    vector_square,
    adam_step,
):
    row_count, seq_len, width = inputs.shape[1:]
    tokens = row_count * seq_len
    rows_all, vec_all = matrices.shape[1], vectors.shape[1]
    ffn = (rows_all - 6 * width) // 2
    half = rows_all // 2
    ranks = lax.axis_size("dp")
    share, vec_share = rows_all // ranks, vec_all // ranks
    by_swaps = ranks == 16 and share % 32 == 0
    block = (ranks // 4, share + TAIL, width) if by_swaps else (half, width)
    me = lax.axis_index("dp")

    x = inputs.reshape(tokens, width)
    cot = cotangent.reshape(tokens, width)
    mats = matrices.reshape(rows_all, width)
    lens_here = pltpu.SMEM(lengths.shape, jnp.int32)

    def spec(columns, dtype):
        return ((tokens, columns), dtype)

    full, low, deep = spec(width, F32), spec(width, BF16), spec(ffn, BF16)
    square, mask = ((width, width), BF16), spec(seq_len, F32)
    double, w_ffn = ((2 * width, width), BF16), ((ffn, width), BF16)
    lse = ((row_count, HEADS, seq_len), F32)
    norms = dict(normal2=full, rstd2=spec(LANES, F32), normal3=full, rstd3=spec(LANES, F32))
    half_tokens = tokens // 2
    half_low, half_full = ((half_tokens, width), BF16), ((half_tokens, width), F32)
    half_double, half_triple = ((half_tokens, 2 * width), BF16), ((half_tokens, 3 * width), BF16)
    all_vecs, triple = ((1, vec_all), F32), spec(3 * width, BF16)
    sided = dict(keep=(block, BF16))
    if by_swaps:
        sided["give"] = (block, BF16)
    early = ((half - 6 * width, width), BF16)

    def wide(rows):
        return ((width // LANES, rows, LANES), F32)

    cross_half = lax.dynamic_slice(mats, ((4 + (me & 1)) * width, 0), (width, width), allow_negative_indices=False)
    cross_mine = swapped(cross_half, "section", 1)
    f = run_kernel(
        forward_kernel, "forward", dict(mats=mats, x=x, vectors=vectors, lengths=lengths), {},
        dict(
            h1=full, w_in=w_ffn, act=deep, slope=deep, **norms,
            memory=half_low, w_cross=double, qc=low, w_out=w_ffn, vecs=all_vecs,
        ),
        dict(
            qkv=triple, lse=lse, mixed=low, normal1=full, rstd1=spec(LANES, F32), mask=mask, w_attn_out=square,
            w_attn=((3 * width, width), BF16), low=low,
        ),
        dict(
            raw_attn=((3 * width, width), BF16), raw_cross=double, raw_ffn=w_ffn,
            x_here=low, total=half_full, wide=wide(ffn), raw_vecs=((1, vec_all), BF16), lens=lens_here,
        ),
        8, 10,
    )
    memory_far0 = swapped(f.memory, "section", 1)
    r = run_kernel(
        forward_rest_kernel, "forward_rest", {},
        dict(
            h1=f.h1, w_in=f.w_in, w_out=f.w_out, vecs=f.vecs, old_act=f.act, old_slope=f.slope,
            **{"old_" + name: getattr(f, name) for name in norms},
        ),
        dict(act=deep, slope=deep, **norms, memory=half_low), dict(low_rest=half_low),
        dict(total=half_full), 0, 6,
        [("old_" + name, name) for name in ("act", "slope", *norms)],
        work=WORK_REST,
    )
    memory_far1 = swapped(r.memory, "section", 1)
    cross_mine = held_until(cross_mine, f.memory)
    cross_other = swapped(cross_mine, "dp", 1)
    p = run_kernel(
        prepare_kernel, "prepare", dict(cot_all=cot, lengths=lengths),
        dict(cross_mine=cross_mine, cross_other=cross_other),
        dict(w_pairs=double, mask=mask, cot=low), {},
        dict(raw=double, wide=wide(2 * width), raw_cot=low, lens=lens_here),
        2, 4,
    )
    shared = dict(
        **vars(p), w_cross=f.w_cross, qc=f.qc, h1=f.h1, w_in=f.w_in, w_out=f.w_out, vecs=f.vecs,
    )
    for_tokens = dict(act=deep, side=deep, grad_ffn=low, low2=low, grad_qc=low, grad_sum2=full)
    far_half = dict(mixed=half_low, right=half_double)
    held = dict(
        pairs=half_double, slope=((half_tokens, ffn), F32), lse=((row_count // 2, HEADS, seq_len), F32),
        grad_mixed=half_low, total=half_full, normal2=half_full, rstd2=((half_tokens, LANES), F32),
    )
    d = run_kernel(
        lambda k: decoder_kernel(k, 0), "decoder", {},
        dict(memory=memory_far0, near_memory=f.memory, **shared, enc_act=r.act, enc_slope=r.slope),
        dict(
            back=half_double, grad_values=half_low, vec_grads=all_vecs, **for_tokens, top=half_low,
        ),
        far_half, held,
        0, SPARE_D, (("enc_act", "act"), ("enc_slope", "side")), work=WORK_D,
    )
    back_far = swapped(d.back, "section", 1)
    before = {"old_" + name: getattr(d, name) for name in for_tokens}
    e = run_kernel(
        lambda k: decoder_kernel(k, 1), "decoder_rest", {},
        dict(
            memory=memory_far1, near_memory=r.memory, **shared, **before, vec_before=d.vec_grads,
            top_before=d.top, values_before=d.grad_values,
        ),
        dict(grad_memory=half_low, rest=half_triple, vec_grads=all_vecs, **for_tokens),
        dict(layer_out=low, **far_half), held,
        0, SPARE_D, [("old_" + name, name) for name in for_tokens], work=WORK_D,
    )
    grad_memory_far = swapped(e.grad_memory, "section", 1)
    rest_far = swapped(e.rest, "section", 1)
    ahead = dict(
        normal1=full, rstd1=spec(LANES, F32), w_attn_out=square, mask=mask, lse=lse, qkv=triple,
        w_attn=((3 * width, width), BF16),
    )
    s = run_kernel(
        backward_kernel, "backward",
        dict(
            **{"far_" + name: getattr(f, name) for name in ahead},
            far_x=x, far_mixed=f.mixed, far_low=f.low, far_low_rest=r.low_rest,
            far_right0=d.right, far_right1=e.right, far_cross_mixed0=d.mixed, far_cross_mixed1=e.mixed,
        ),
        dict(
            dec_grad_ffn=e.grad_ffn, dec_vec_grads=e.vec_grads,
            back=back_far, grad_memory=grad_memory_far, act=e.act, side=e.side,
            low2=e.low2, grad_qc=e.grad_qc, grad_sum2=e.grad_sum2, **{name: getattr(r, name) for name in norms}, h1=f.h1, w_in=f.w_in, w_out=f.w_out, w_cross=f.w_cross, vecs=f.vecs,
        ),
        dict(
            vec_grads=all_vecs, early=early, **sided, grad_attn=low, grad_qkv=triple,
            x=low, mixed=low, low=low, right=spec(2 * width, BF16), cross_mixed=low,
        ),
        dict(grad_x=full),
        dict(
            grad_pre=deep, grad_ffn=low, low1=low, wide=wide(ffn), grad_h1=full,
            flat=((2 * ffn, width), BF16), grad_mixed=low, **ahead,
        ),
        15, 9, work=4 * 10**10,
    )
    if by_swaps:
        core_high = swapped(s.give, "dp", 1)
    a = run_kernel(
        attn_grad_kernel, "attn_grad", {},
        dict(
            grad_qkv=s.grad_qkv, vec_grads=s.vec_grads, early=s.early, back=back_far, rest=rest_far,
            x=s.x, grad_attn=s.grad_attn, mixed=s.mixed, low=s.low, right=s.right, cross_mixed=s.cross_mixed,
        ),
        sided, {}, dict(wide=wide(3 * width), flat=((half, width), BF16)), 0, 4,
    )

    state = Refs(master=master_matrices[0], mean=matrix_mean[0], square=matrix_square[0])
    state = Refs(**vars(state), vec_master=master_vectors, vec_mean=vector_mean, vec_square=vector_square)
    if by_swaps:
        core_low = swapped(a.give, "dp", 1)
        first_rows = (share + TAIL) // 2 // 16 * 16
        summands = {}
        for at, cut in enumerate((slice(0, first_rows), slice(first_rows, share + TAIL))):
            parts = sum_over_dp(cut, a.keep, core_low, s.keep, core_high)
            summands.update({f"{name}{at}": part for name, part in parts.items()})
        own = adam(summands, state, adam_step, False).own
        result = adam(summands, state, adam_step, True)
        new_mat, tails = gather_blocks(own, share, rows_all, result.change)
        new_vec = tails[:, 0, :vec_share].reshape(1, vec_all)
    else:
        whole = jnp.concatenate([a.keep, s.keep], axis=0)
        grad = lax.psum_scatter(whole, "dp", scatter_dimension=0, tiled=True).astype(F32)
        vec_grad = lax.dynamic_slice(
            lax.psum(s.vec_grads, "dp"), (0, me * vec_share), (1, vec_share)
        )
        step = jnp.full((1, width), adam_step[0].astype(F32))
        parts = adam_of(grad, state.master, state.mean, state.square, step)
        vec_step = jnp.full((1, width), adam_step[0].astype(F32))
        pad = ((0, 0), (0, width - vec_share))
        vec_parts = [
            part[:, :vec_share]
            for part in adam_of(
                *[jnp.pad(v, pad) for v in (vec_grad, master_vectors, vector_mean, vector_square)],
                vec_step,
            )
        ]
        names = ("change", "mean_new", "square_new")
        result = dict(grad=grad, vec_grad=vec_grad, **dict(zip(names, parts)))
        result.update({"vec_" + name: part for name, part in zip(names, vec_parts)})
        result = Refs(**result)
        new_mat = lax.all_gather(parts[3].astype(BF16), "dp", axis=0, tiled=True)
        new_vec = lax.all_gather(vec_parts[3].astype(BF16), "dp", axis=1, tiled=True)
    return (
        e.layer_out.reshape(1, row_count, seq_len, width),
        s.grad_x.reshape(1, row_count, seq_len, width),
        result.grad[None],
        result.vec_grad,
        result.change[None],
        result.vec_change,
        result.mean_new[None],
        result.square_new[None],
        result.vec_mean_new,
        result.vec_square_new,
        new_mat[None],
        new_vec,
    )


def solution(mesh):
    return jax.shard_map(
        body,
        mesh=mesh,
        in_specs=(
            P("section", "dp", None, None),
            P(None, "dp", None),
            P("dp", None, None),
            P("section", None, None),
            P("section", None),
            P("section", "dp", None),
            P("section", "dp"),
            P("section", "dp", None),
            P("section", "dp", None),
            P("section", "dp"),
            P("section", "dp"),
            P(),
        ),
        out_specs=(
            P("section", "dp", None, None),
            P("section", "dp", None, None),
            P("section", "dp", None),
            P("section", "dp"),
            P("section", "dp", None),
            P("section", "dp"),
            P("section", "dp", None),
            P("section", "dp", None),
            P("section", "dp"),
            P("section", "dp"),
            P("section", None, None),
            P("section", None),
        ),
        check_vma=False,
    )
```

```python
import math
import types

import jax
import jax.numpy as jnp
from jax import lax
from jax.experimental import pallas as pl
from jax.experimental.pallas import tpu as pltpu
from jax.sharding import PartitionSpec as P

HEADS = 8
HEAD_DIM = 64
PAIR = 2 * HEAD_DIM
LANES = 128
TAIL = 16
EARLY_LANES = 256
SUMMANDS = ("mine", "from_y", "from_end", "from_middle")
UNROLL_CHUNKS = True
WORK_REST = 10**10
WORK_D = 4 * 10**10
SPARE_D = 8

MASK_FILL = -1e30
NORM_EPS = 1e-05
ADAM_EPS = 1e-09
WARMUP_STEPS = 4000.0

F32 = jnp.float32
BF16 = jnp.bfloat16

BIAS_OUT, GAIN1, SHIFT1, GAIN2, SHIFT2, GAIN3, SHIFT3 = range(-7, 0)


def dot(left, right):
    return jnp.dot(left, right, preferred_element_type=F32)


def dot_nt(left, right):
    return lax.dot_general(left, right, (((1,), (1,)), ((), ())), preferred_element_type=F32)


def dot_tn(left, right):
    return lax.dot_general(left, right, (((0,), (0,)), ((), ())), preferred_element_type=F32)


def norm_parts(hidden):
    centre = hidden - jnp.mean(hidden, axis=-1, keepdims=True)
    rstd = lax.rsqrt(jnp.mean(centre * centre, axis=-1, keepdims=True) + NORM_EPS)
    return centre * rstd, rstd


def norm_backward(normal, rstd, gain, grad):
    scaled = grad * gain
    inner = jnp.mean(scaled * normal, axis=-1, keepdims=True)
    grad_in = rstd * (scaled - jnp.mean(scaled, axis=-1, keepdims=True) - normal * inner)
    grad_gain = jnp.sum(grad * normal, axis=0, keepdims=True)
    grad_shift = jnp.sum(grad, axis=0, keepdims=True)
    return grad_in, grad_gain, grad_shift


def act_parts(pre):
    cdf = 0.5 * (1.0 + lax.erf(pre * (0.5**0.5)))
    pdf = jnp.exp(-0.5 * pre * pre) * 0.3989422804014327
    return pre * cdf, cdf + pre * pdf


def split_rows(raw, wide, parts, out, base):
    width = raw.shape[1]
    for c in range(width // LANES):
        cut = slice(c * LANES, (c + 1) * LANES)
        wide[c, : parts * width] = raw[: parts * width, cut].astype(F32)
        for j in range(parts):
            out[(base + j) * width : (base + j + 1) * width, cut] = wide[
                c, pl.ds(j, width, stride=parts), :
            ].astype(BF16)


def put_part(wide, j, parts, values):
    rows, width = values.shape
    for c in range(width // LANES):
        wide[c, pl.ds(j, rows, stride=parts), :] = values[:, c * LANES : (c + 1) * LANES]


def take_parts(wide, rows, out, first):
    for c in range(wide.shape[0]):
        out[first : first + rows, c * LANES : (c + 1) * LANES] = wide[c, :rows].astype(BF16)


def sentence_ends(lens, side, row):
    ends, total = [], 0
    for j in range(lens.shape[2]):
        total = total + lens[side, row, j]
        ends.append(total)
    return ends


def sentence_of(ends, position):
    found = jnp.zeros(position.shape, jnp.int32)
    for end in ends:
        found = found + (position >= end).astype(jnp.int32)
    return found


def fill_mask(mask, lens, query_side, key_side, causal):
    seq_len = mask.shape[1]
    row_count, sents = lens.shape[1:]
    q_pos = lax.broadcasted_iota(jnp.int32, (seq_len, seq_len), 1)
    k_pos = lax.broadcasted_iota(jnp.int32, (seq_len, seq_len), 0)
    for r in range(row_count):
        q_ids = sentence_of(sentence_ends(lens, query_side, r), q_pos)
        k_ids = sentence_of(sentence_ends(lens, key_side, r), k_pos)
        same = jnp.where(q_ids == k_ids, 1, 0)
        if causal is not None:
            same = jnp.where(q_pos >= k_pos, same, jnp.where(causal, 0, same))
        allowed = jnp.where(q_ids == sents, 1, same)
        mask[r * seq_len : (r + 1) * seq_len] = allowed.astype(F32)


def both_heads(block, lane):
    even = (lane < HEAD_DIM).astype(BF16)
    return jnp.concatenate([block * even, block * (1 - even)], axis=0)


def both_heads_across(block):
    turned = block.T
    even = (lax.broadcasted_iota(jnp.int32, (PAIR, 1), 0) < HEAD_DIM).astype(BF16)
    return jnp.concatenate([turned * even, turned * (1 - even)], axis=1)


def one_of(stacked, lane):
    keys = stacked.shape[0] // 2
    return jnp.where(lane < HEAD_DIM, stacked[:keys], stacked[keys:])


def for_rows(mask, step):
    seq_len = mask.shape[1]

    def turn(row, carried):
        step(row, pl.ds(pl.multiple_of(row * seq_len, seq_len), seq_len), range(HEADS // 2))
        return carried

    lax.fori_loop(0, mask.shape[0] // seq_len, turn, 0)


def pair_lanes(first, p):
    return slice(first + p * PAIR, first + (p + 1) * PAIR)


def attend_forward(query, keys, values, mask, out, lse):
    seq_len = mask.shape[1]
    lane = lax.broadcasted_iota(jnp.int32, (1, PAIR), 1)
    (q_ref, q_at), (k_ref, k_at), (v_ref, v_at) = query, keys, values

    def step(row, rows, pairs):
        scores = [
            dot_nt(both_heads(k_ref[rows, pair_lanes(k_at, p)], lane), q_ref[rows, pair_lanes(q_at, p)])
            for p in pairs
        ]
        mixed = []
        for p in pairs:
            probs = []
            for half in range(2):
                part = scores[p][half * seq_len : (half + 1) * seq_len] * HEAD_DIM ** (-0.5)
                part = jnp.where(mask[rows] > 0.0, part, MASK_FILL)
                top = jnp.max(part, axis=0, keepdims=True)
                raised = jnp.exp(part - top)
                total = jnp.sum(raised, axis=0, keepdims=True)
                probs.append((raised * (1.0 / total)).astype(BF16))
                lse[row, 2 * p + half : 2 * p + half + 1] = top + jnp.log(total)
            values = both_heads_across(v_ref[rows, pair_lanes(v_at, p)])
            mixed.append(dot(values, jnp.concatenate(probs, axis=0)))
        for p in pairs:
            out[rows, pair_lanes(0, p)] = mixed[p].T.astype(BF16)

    for_rows(mask, step)


def attend_backward(query, keys, values, mask, lse, grad_out, grad_q, grad_k, grad_v):
    seq_len = mask.shape[1]
    lane = lax.broadcasted_iota(jnp.int32, (1, PAIR), 1)
    scale = HEAD_DIM ** (-0.5)
    (q_ref, q_at), (k_ref, k_at), (v_ref, v_at) = query, keys, values
    (gq_ref, gq_at), (gk_ref, gk_at), (gv_ref, gv_at) = grad_q, grad_k, grad_v

    def step(row, rows, pairs):
        qs = [q_ref[rows, pair_lanes(q_at, p)] for p in pairs]
        ks = [k_ref[rows, pair_lanes(k_at, p)] for p in pairs]
        gos = [grad_out[rows, pair_lanes(0, p)] for p in pairs]
        scores = [dot_nt(both_heads(ks[p], lane), qs[p]) for p in pairs]
        grad_probs = [
            dot_nt(both_heads(v_ref[rows, pair_lanes(v_at, p)], lane), gos[p]) for p in pairs
        ]
        probs, grad_scores = [], []
        for p in pairs:
            prob_parts, score_parts = [], []
            for half in range(2):
                cut = slice(half * seq_len, (half + 1) * seq_len)
                part = jnp.where(mask[rows] > 0.0, scores[p][cut] * scale, MASK_FILL)
                prob = jnp.exp(part - lse[row, 2 * p + half : 2 * p + half + 1])
                gp = grad_probs[p][cut]
                inner = jnp.sum(prob * gp, axis=0, keepdims=True)
                prob_parts.append(prob.astype(BF16))
                score_parts.append((prob * (gp - inner)).astype(BF16))
            probs.append(jnp.concatenate(prob_parts, axis=0))
            grad_scores.append(jnp.concatenate(score_parts, axis=0))
        grad_vs = [dot(probs[p], gos[p]) for p in pairs]
        grad_ks = [dot(grad_scores[p], qs[p]) for p in pairs]
        grad_qs = [dot(both_heads_across(ks[p]), grad_scores[p]) for p in pairs]
        for p in pairs:
            gv_ref[rows, pair_lanes(gv_at, p)] = one_of(grad_vs[p], lane).astype(BF16)
            gk_ref[rows, pair_lanes(gk_at, p)] = (one_of(grad_ks[p], lane) * scale).astype(BF16)
            gq_ref[rows, pair_lanes(gq_at, p)] = (grad_qs[p].T * scale).astype(BF16)

    for_rows(mask, step)


def small(vecs, which, width):
    pieces = vecs.shape[1] // width
    at = (which if which >= 0 else pieces + which) * width
    return vecs[:, at : at + width].astype(F32)


def set_small(vecs, which, width, value):
    pieces = vecs.shape[1] // width
    at = (which if which >= 0 else pieces + which) * width
    vecs[:, at : at + width] = value


def where_am_i():
    return lax.axis_index("section"), lax.rem(lax.axis_index("dp"), 2)


def for_chunks(count, width, step):
    def turn(j, carried):
        step(j, pl.ds(pl.multiple_of(j * width, width), width))
        return carried

    lax.fori_loop(0, count, turn, 0, unroll=UNROLL_CHUNKS)


def ffn_forward(normed, w_in, w_out, vecs, act, slope, total):
    width = normed.shape[1]
    low = normed.astype(BF16)
    total[...] = normed + small(vecs, BIAS_OUT, width)

    def step(j, cut):
        pre = dot(low, w_in[cut]) + vecs[:, cut]
        value, derivative = act_parts(pre)
        value = value.astype(BF16)
        act[:, cut] = value
        slope[:, cut] = derivative.astype(slope.dtype)
        total[...] += dot(value, w_out[cut])

    for_chunks(w_in.shape[0] // width, width, step)


def ffn_backward(grad_low, w_in, w_out, slope, grad_pre, vec_grads, total):
    width = grad_low.shape[1]

    def step(j, cut):
        grad = (dot_nt(grad_low, w_out[cut]) * slope[:, cut].astype(F32)).astype(BF16)
        grad_pre[:, cut] = grad
        vec_grads[:, cut] = jnp.sum(grad.astype(F32), axis=0, keepdims=True)
        total[...] += dot_nt(grad, w_in[cut])

    for_chunks(w_in.shape[0] // width, width, step)


def load(source, target, sem):
    copy = pltpu.make_async_copy(source, target, sem)
    copy.start()
    return copy


def memory_of(k, rows):
    width = k.h1.shape[1]
    vecs = k.vecs
    ffn_forward(k.h1[rows], k.w_in, k.w_out, vecs, k.act.at[rows], k.slope.at[rows], k.total)
    normal, rstd = norm_parts(k.total[...])
    k.normal2[rows], k.rstd2[rows] = normal, jnp.broadcast_to(rstd, (rstd.shape[0], LANES))
    normal, rstd = norm_parts(normal * small(vecs, GAIN2, width) + small(vecs, SHIFT2, width))
    k.normal3[rows], k.rstd3[rows] = normal, jnp.broadcast_to(rstd, (rstd.shape[0], LANES))
    third = normal * small(vecs, GAIN3, width) + small(vecs, SHIFT3, width)
    k.memory[...] = third.astype(BF16)


def forward_kernel(k):
    width = k.h1.shape[1]
    ffn = k.w_in.shape[0]
    sec, _ = where_am_i()
    get_lens = load(k.lengths, k.lens, k.sems.at[7])
    get_in = load(k.mats.at[: 3 * width], k.raw_attn, k.sems.at[0])
    get_x = load(k.x, k.x_here, k.sems.at[1])
    get_vecs = load(k.vectors, k.raw_vecs, k.sems.at[2])
    get_attn_out = load(k.mats.at[3 * width : 4 * width], k.w_attn_out, k.sems.at[3])
    get_ffn = load(k.mats.at[6 * width : 6 * width + ffn], k.raw_ffn, k.sems.at[4])
    get_out = load(k.mats.at[6 * width + ffn :], k.w_out, k.sems.at[5])
    get_cross = pltpu.make_async_copy(k.mats.at[4 * width : 6 * width], k.raw_cross, k.sems.at[6])

    @pl.when(sec == 1)
    def _():
        get_cross.start()

    get_lens.wait()
    fill_mask(k.mask, k.lens, sec, sec, sec == 1)
    k.go.mask.start()
    get_in.wait()
    split_rows(k.raw_attn, k.wide, 3, k.w_attn, 0)
    k.go.w_attn.start()
    get_x.wait()
    for j in range(3):
        part = dot(k.x_here[...], k.w_attn[j * width : (j + 1) * width])
        k.qkv[:, j * width : (j + 1) * width] = part.astype(BF16)
    k.go.qkv.start()
    attend_forward((k.qkv, 0), (k.qkv, width), (k.qkv, 2 * width), k.mask, k.mixed, k.lse)
    k.go.mixed.start()
    k.go.lse.start()
    get_vecs.wait()
    k.vecs[...] = k.raw_vecs[...].astype(F32)
    vecs = k.vecs
    get_attn_out.wait()
    k.go.w_attn_out.start()
    hidden = k.x_here[...].astype(F32) + dot(k.mixed[...], k.w_attn_out[...])
    normal, rstd = norm_parts(hidden)
    k.normal1[...], k.rstd1[...] = normal, jnp.broadcast_to(rstd, (rstd.shape[0], LANES))
    k.go.normal1.start()
    k.go.rstd1.start()
    k.h1[...] = normal * small(vecs, GAIN1, width) + small(vecs, SHIFT1, width)
    get_ffn.wait()
    split_rows(k.raw_ffn, k.wide, ffn // width, k.w_in, 0)
    get_out.wait()

    @pl.when(sec == 0)
    def _():
        memory_of(k, slice(0, k.memory.shape[0]))
        k.low[: k.memory.shape[0]] = k.memory[...]
        k.go.low.start()

    @pl.when(sec == 1)
    def _():
        k.low[...] = k.h1[...].astype(BF16)
        k.go.low.start()
        get_cross.wait()
        split_rows(k.raw_cross, k.wide, 2, k.w_cross, 0)
        k.qc[...] = dot(k.low[...], k.w_cross[:width]).astype(BF16)

    k.go.mask.wait()
    k.go.w_attn.wait()
    k.go.qkv.wait()
    k.go.mixed.wait()
    k.go.lse.wait()
    k.go.w_attn_out.wait()
    k.go.normal1.wait()
    k.go.rstd1.wait()
    k.go.low.wait()


def forward_rest_kernel(k):
    sec, _ = where_am_i()

    @pl.when(sec == 0)
    def _():
        half = k.memory.shape[0]
        memory_of(k, slice(half, 2 * half))
        k.low_rest[...] = k.memory[...]
        k.go.low_rest.start()
        k.go.low_rest.wait()


def prepare_kernel(k):
    width = k.raw.shape[1]
    seq_len = k.mask.shape[1]
    sec, core = where_am_i()

    @pl.when(sec == 1)
    def _():
        get_cot = load(k.cot_all, k.raw_cot, k.sems.at[0])
        get_lens = load(k.lengths, k.lens, k.sems.at[1])
        k.raw[pl.ds(pl.multiple_of(core * width, width), width)] = k.cross_mine[...]
        k.raw[pl.ds(pl.multiple_of((1 - core) * width, width), width)] = k.cross_other[...]
        split_rows(k.raw, k.wide, 2, k.w_pairs, 0)
        get_lens.wait()
        fill_mask(k.mask, k.lens, 1, 0, None)
        get_cot.wait()
        position = lax.broadcasted_iota(jnp.int32, (seq_len, 1), 0)
        for r in range(k.lens.shape[1]):
            used = sentence_ends(k.lens, 1, r)[-1]
            rows = slice(r * seq_len, (r + 1) * seq_len)
            k.cot[rows] = jnp.where(position < used, k.raw_cot[rows].astype(F32), 0.0).astype(BF16)


def decoder_kernel(k, part):
    half, width = k.memory.shape
    rows = slice(part * half, (part + 1) * half)
    vecs = k.vecs
    sec, _ = where_am_i()
    top = k.layer_out.at[rows] if part == 1 else k.top
    pairs_at = 0 if part == 0 else 2 * width - EARLY_LANES
    grad_pairs = k.grad_pairs if part == 0 else k.rest
    grad_keys, grad_values = (grad_pairs, pairs_at), (grad_pairs, pairs_at + width)
    if part == 1:
        k.layer_out[:half] = k.top_before[...]

    @pl.when(sec == 0)
    def _():
        top[...] = k.near_memory[...]

    @pl.when(sec == 1)
    def _():
        mask, qc, act, side = k.mask.at[rows], k.qc.at[rows], k.act.at[rows], k.side.at[rows]
        for j in range(2):
            pair = dot(k.memory[...], k.w_pairs[j * width : (j + 1) * width])
            k.pairs[:, j * width : (j + 1) * width] = pair.astype(BF16)
        attend_forward((qc, 0), (k.pairs, 0), (k.pairs, width), mask, k.mixed, k.lse)
        k.go.mixed.start()
        hidden2 = k.h1[rows] + dot(k.mixed[...], k.w_cross[width:])
        gain2, shift2 = small(vecs, GAIN2, width), small(vecs, SHIFT2, width)
        normal2, rstd2 = norm_parts(hidden2)
        k.normal2[...], k.rstd2[...] = normal2, jnp.broadcast_to(rstd2, (half, LANES))
        normed2 = normal2 * gain2 + shift2
        k.low2[rows] = normed2.astype(BF16)
        ffn_forward(normed2, k.w_in, k.w_out, vecs, act, k.slope, k.total)
        normal3, rstd3 = norm_parts(k.total[...])
        gain3, shift3 = small(vecs, GAIN3, width), small(vecs, SHIFT3, width)
        top[...] = (normal3 * gain3 + shift3).astype(BF16)
        grad_sum3, d_gain, d_shift = norm_backward(
            normal3, rstd3, gain3, k.cot[rows].astype(F32)
        )
        set_small(k.vec_grads, GAIN3, width, d_gain)
        set_small(k.vec_grads, SHIFT3, width, d_shift)
        grad_low = grad_sum3.astype(BF16)
        k.grad_ffn[rows] = grad_low
        set_small(
            k.vec_grads, BIAS_OUT, width, jnp.sum(grad_low.astype(F32), axis=0, keepdims=True)
        )
        k.total[...] = grad_sum3
        ffn_backward(grad_low, k.w_in, k.w_out, k.slope, side, k.vec_grads, k.total)
        grad_hidden2, d_gain, d_shift = norm_backward(
            k.normal2[...], k.rstd2[:, :1], gain2, k.total[...]
        )
        set_small(k.vec_grads, GAIN2, width, d_gain)
        set_small(k.vec_grads, SHIFT2, width, d_shift)
        k.grad_sum2[rows] = grad_hidden2
        low = grad_hidden2.astype(BF16)
        k.right[:, width:] = low
        k.grad_mixed[...] = dot_nt(low, k.w_cross[width:]).astype(BF16)
        attend_backward(
            (qc, 0), (k.pairs, 0), (k.pairs, width), mask, k.lse, k.grad_mixed,
            (k.right, 0), grad_keys, grad_values,
        )
        k.go.right.start()
        k.grad_qc[rows] = k.right[:, :width]
        back = jnp.zeros((half, width), F32)
        for j, (ref, at) in enumerate((grad_keys, grad_values)):
            back = back + dot_nt(ref[:, at : at + width], k.w_pairs[j * width : (j + 1) * width])
        if part == 0:
            k.back[:, :width] = back.astype(BF16)
            k.back[:, width:] = k.grad_pairs[:, :EARLY_LANES]
        else:
            k.grad_memory[...] = back.astype(BF16)
            k.rest[:, :pairs_at] = k.pairs_before[:, EARLY_LANES:]
        if part == 1:
            k.vec_grads[...] += k.vec_before[...]
        k.go.mixed.wait()
        k.go.right.wait()

    if part == 1:
        k.go.layer_out.start()
        k.go.layer_out.wait()


def ffn_weight_grads(k, act, low, grad_pre, grad_ffn):
    width = k.h1.shape[1]
    ffn = k.w_in.shape[0]
    chunks = ffn // width

    def step(j, cut):
        put_part(k.wide, j, chunks, dot_tn(low[...], grad_pre[:, cut]))
        there = pl.ds(pl.multiple_of(ffn + j * width, width), width)
        k.flat[there] = dot_tn(act[:, cut], grad_ffn[...]).astype(BF16)

    for_chunks(chunks, width, step)


def put_sides(k, first, z, vec_grads, core):
    width = k.flat.shape[1]
    keep = getattr(k, f"keep{z}")
    if len(keep.shape) == 2:
        keep[...] = k.flat[first : first + keep.shape[0]]
        return
    give = getattr(k, f"give{z}")
    count, rows, _ = keep.shape
    rows -= TAIL
    share = vec_grads.shape[1] // (8 * count)

    def tail(at):
        owner = 2 * count * z + at
        row = vec_grads[:, owner * share : (owner + 1) * share]
        row = jnp.concatenate([row, jnp.zeros((1, width - share), F32)], axis=1)
        return jnp.broadcast_to(row, (TAIL, width)).astype(BF16)

    for at in range(count):
        mine = first + (2 * at + core) * rows
        other = first + (2 * at + 1 - core) * rows
        keep[at, :rows] = k.flat[pl.ds(pl.multiple_of(mine, TAIL), rows)]
        give[at, :rows] = k.flat[pl.ds(pl.multiple_of(other, TAIL), rows)]

        @pl.when(core == 0)
        def _(at=at):
            keep[at, rows:] = tail(2 * at)
            give[at, rows:] = tail(2 * at + 1)

        @pl.when(core == 1)
        def _(at=at):
            keep[at, rows:] = tail(2 * at + 1)
            give[at, rows:] = tail(2 * at)


def backward_kernel(k):
    width = k.h1.shape[1]
    ffn = k.w_in.shape[0]
    vecs = k.vecs
    sec, core = where_am_i()
    half = k.back.shape[0]
    first, rest = slice(0, half), slice(half, 2 * half)
    wanted = ("normal1", "rstd1", "w_attn_out", "mask", "lse", "qkv", "w_attn", "x", "mixed")
    arriving = [(getattr(k, "far_" + name), getattr(k, name)) for name in wanted]
    arriving += [
        (k.far_low.at[first], k.low.at[first]),
        (k.far_right0, k.right.at[first]),
        (k.far_right1, k.right.at[rest]),
        (k.far_cross_mixed0, k.cross_mixed.at[first]),
        (k.far_cross_mixed1, k.cross_mixed.at[rest]),
    ]
    coming = [load(*ends, k.sems.at[at]) for at, ends in enumerate(arriving)]
    last_sem = k.sems.at[len(coming)]

    @pl.when(sec == 0)
    def _():
        load(k.far_low_rest, k.low.at[rest], last_sem)

    @pl.when(sec == 1)
    def _():
        load(k.far_low.at[rest], k.low.at[rest], last_sem)

    coming.append(pltpu.make_async_copy(k.far_low_rest, k.low.at[rest], last_sem))

    @pl.when(sec == 0)
    def _():
        grad_memory = jnp.concatenate([k.back[:, :width], k.grad_memory[...]], axis=0)
        grad, d_gain, d_shift = norm_backward(
            k.normal3[...], k.rstd3[:, :1], small(vecs, GAIN3, width), grad_memory.astype(F32)
        )
        set_small(k.vec_grads, GAIN3, width, d_gain)
        set_small(k.vec_grads, SHIFT3, width, d_shift)
        total, d_gain, d_shift = norm_backward(
            k.normal2[...], k.rstd2[:, :1], small(vecs, GAIN2, width), grad
        )
        set_small(k.vec_grads, GAIN2, width, d_gain)
        set_small(k.vec_grads, SHIFT2, width, d_shift)
        grad_low = total.astype(BF16)
        k.grad_ffn[...] = grad_low
        set_small(
            k.vec_grads, BIAS_OUT, width, jnp.sum(grad_low.astype(F32), axis=0, keepdims=True)
        )
        k.low1[...] = k.h1[...].astype(BF16)
        k.grad_h1[...] = total
        ffn_backward(grad_low, k.w_in, k.w_out, k.side, k.grad_pre, k.vec_grads, k.grad_h1)
        ffn_weight_grads(k, k.act, k.low1, k.grad_pre, k.grad_ffn)

    @pl.when(sec == 1)
    def _():
        k.vec_grads[...] = k.dec_vec_grads[...]
        k.grad_h1[...] = k.grad_sum2[...] + dot_nt(k.grad_qc[...], k.w_cross[:width])
        ffn_weight_grads(k, k.act, k.low2, k.side, k.dec_grad_ffn)

    take_parts(k.wide, ffn, k.flat, 0)
    early = k.early.shape[0]
    k.early[...] = k.flat[:early]
    for copy in coming:
        copy.wait()
    grad, d_gain, d_shift = norm_backward(
        k.normal1[...], k.rstd1[:, :1], small(vecs, GAIN1, width), k.grad_h1[...]
    )
    set_small(k.vec_grads, GAIN1, width, d_gain)
    set_small(k.vec_grads, SHIFT1, width, d_shift)
    put_sides(k, early, 2, k.vec_grads, core)
    put_sides(k, (k.flat.shape[0] + early) // 2, 3, k.vec_grads, core)
    low = grad.astype(BF16)
    k.grad_attn[...] = low
    k.grad_mixed[...] = dot_nt(low, k.w_attn_out[...]).astype(BF16)
    attend_backward(
        (k.qkv, 0), (k.qkv, width), (k.qkv, 2 * width), k.mask, k.lse, k.grad_mixed,
        (k.grad_qkv, 0), (k.grad_qkv, width), (k.grad_qkv, 2 * width),
    )
    for j in range(3):
        cut = slice(j * width, (j + 1) * width)
        grad = grad + dot_nt(k.grad_qkv[:, cut], k.w_attn[cut])
    k.grad_x[...] = grad
    k.go.grad_x.start()
    k.go.grad_x.wait()


def attn_grad_kernel(k):
    width = k.x.shape[1]
    quarter = k.flat.shape[0]
    _, core = where_am_i()

    def step(j, cut):
        put_part(k.wide, j, 3, dot_tn(k.x[...], k.grad_qkv[:, cut]))

    for_chunks(3, width, step)
    take_parts(k.wide, 3 * width, k.flat, 0)
    grad = dot_tn(k.mixed[...], k.grad_attn[...]).astype(BF16)
    k.flat[3 * width :] = grad[: quarter - 3 * width]
    k.left[...] = grad[quarter - 3 * width :]
    put_sides(k, 0, 0, k.vec_grads, core)


def cross_grad_kernel(k):
    half = k.rest.shape[0]
    first, width = k.left.shape
    sec, core = where_am_i()
    k.flat[:first] = k.left[...]
    k.flat[first + 2 * width :] = k.early[...]

    @pl.when(sec == 0)
    def _():
        rest = k.rest[...]
        at = width - EARLY_LANES
        keys0 = jnp.concatenate([k.back[:, width:], rest[:, :at]], axis=1)
        before = (keys0, rest[:, at : at + width])
        at += width
        after = (rest[:, at : at + width], rest[:, at + width :])
        for j in range(2):
            grad = dot_tn(k.low[:half], before[j]) + dot_tn(k.low[half:], after[j])
            put_part(k.wide, j, 2, grad)

    @pl.when(sec == 1)
    def _():
        put_part(k.wide, 0, 2, dot_tn(k.low[...], k.right[:, :width]))
        put_part(k.wide, 1, 2, dot_tn(k.cross_mixed[...], k.right[:, width:]))

    take_parts(k.wide, 2 * width, k.flat, first)
    put_sides(k, 0, 1, k.vec_grads, core)


class Refs(types.SimpleNamespace):
    pass


def run_kernel(kernel, name, hbm, vmem, outs, far_outs, scratch, loads, spare, reuse=(), work=10**10, smem=None):
    smem = smem or {}
    ins = {**smem, **hbm, **vmem}
    near = {n: pltpu.VMEM(*spec) for n, spec in far_outs.items()}
    near.update({n: pltpu.VMEM(*spec) if isinstance(spec, tuple) else spec for n, spec in scratch.items()})
    names = [*ins, *outs, *far_outs, *near, "sems", "leave_sems"]

    def run(*refs):
        k = Refs(**dict(zip(names, refs)))
        first = len(ins) + len(outs)
        k.go = Refs()
        for at, n in enumerate(far_outs):
            copy = pltpu.make_async_copy(getattr(k, n), refs[first + at], k.leave_sems.at[at])
            setattr(k.go, n, copy)
        kernel(k)

    results = pl.pallas_call(
        run,
        name=name,
        in_specs=[SMEM] * len(smem) + [HBM] * len(hbm) + [VMEM] * len(vmem),
        out_specs=[VMEM] * len(outs) + [HBM] * len(far_outs),
        out_shape=[pltpu.VMEM(*spec) for spec in outs.values()]
        + [pltpu.HBM(*spec) for spec in far_outs.values()],
        scratch_shapes=[
            *near.values(),
            pltpu.SemaphoreType.DMA((max(loads, 1),)),
            pltpu.SemaphoreType.DMA((max(len(far_outs), 1),)),
        ],
        compiler_params=pltpu.CompilerParams(
            vmem_limit_bytes=int(spare * 2**20)
            + sum(math.prod(b.shape) * jnp.dtype(b.dtype).itemsize for b in near.values())
        ),
        input_output_aliases={[*ins].index(old): [*outs].index(new) for old, new in reuse},
        cost_estimate=pl.CostEstimate(flops=work, bytes_accessed=1, transcendentals=0),
    )(
        *smem.values(),
        *[pltpu.with_memory_space_constraint(array, pltpu.HBM) for array in hbm.values()],
        *[pltpu.with_memory_space_constraint(array, pltpu.VMEM) for array in vmem.values()],
    )
    return Refs(**dict(zip([*outs, *far_outs], results)))


SMEM = pl.BlockSpec(memory_space=pltpu.SMEM)
HBM = pl.BlockSpec(memory_space=pltpu.HBM)
VMEM = pl.BlockSpec(memory_space=pltpu.VMEM)
ANY = pl.BlockSpec(memory_space=pl.ANY)


def swapped(array, axis, bit):
    devices = lax.axis_size(axis)
    return lax.ppermute(array, axis, [(i, i ^ bit) for i in range(devices)])


def held_until(array, *others):
    return lax.optimization_barrier((array, *others))[0]


def own_bit(bit):
    return (lax.axis_index("dp") >> bit) & 1


def swapped_middle(array):
    ranks = lax.axis_size("dp")
    quarter = ranks // 4
    pairs = [(i, i + quarter) for i in range(quarter, 2 * quarter)]
    pairs += [(j, i) for i, j in pairs]
    outer = [*range(quarter), *range(ranks - quarter, ranks)]
    return lax.ppermute(array, "dp", pairs + [(i, i ^ 1) for i in outer])


def at_middle():
    return own_bit(2) != own_bit(3)


def quick_kernel(kernel, name, ins, outs):
    return run_kernel(kernel, name, {}, ins, outs, {}, {}, 0, 4, work=10**8)


def sum_of_cores(cut, quarters, ways):
    rows, width = cut.stop - cut.start, quarters[0][0].shape[2]
    used = sorted({way(z) for way in ways for z in range(4)})

    def kernel(k):
        y = own_bit(1)
        here = lax.axis_index("dp") >> 2
        for z in range(4):

            @pl.when(here == z)
            def _(z=z):
                for at, way in enumerate(ways):
                    keep, core = getattr(k, f"keep{way(z)}"), getattr(k, f"core{way(z)}")
                    total = keep[1 - y, cut].astype(F32) + core[1 - y, cut].astype(F32)
                    getattr(k, f"give{at}")[...] = total.astype(BF16)
                    total = keep[y, cut].astype(F32) + core[y, cut].astype(F32)
                    getattr(k, f"mine{at}")[...] = total

    ins = {f"keep{z}": quarters[z][0] for z in used}
    ins.update({f"core{z}": quarters[z][1] for z in used})
    outs = {f"give{at}": ((rows, width), BF16) for at in range(len(ways))}
    outs.update({f"mine{at}": ((rows, width), F32) for at in range(len(ways))})
    return quick_kernel(kernel, "sum_of_cores", ins, outs)


def same(z):
    return z


def next_to(z):
    return z ^ 1


def nearer(z):
    return 2 - (z >> 1)


def farther(z):
    return 3 - 3 * (z >> 1)


def added(wide, part, middle=None, full=False):
    def kernel(k):
        total = k.wide[...] + k.part[...].astype(F32)
        if middle is not None:
            total = total + jnp.where(at_middle(), k.middle[...].astype(F32), 0.0)
        k.low[...] = total.astype(BF16)
        if full:
            k.full[...] = total

    ins = dict(wide=wide, part=part)
    if middle is not None:
        ins = dict(wide=wide, part=part, middle=middle)
    outs = dict(low=(wide.shape, BF16))
    if full:
        outs = dict(low=(wide.shape, BF16), full=(wide.shape, F32))
    return quick_kernel(kernel, "added", ins, outs)


def sum_over_dp(cut, quarters, farthest):
    middle = sum_of_cores(cut, quarters, (nearer,))
    near = sum_of_cores(cut, quarters, (next_to, same))
    from_y3, from_y2 = swapped(farthest.give0, "dp", 2), swapped(middle.give0, "dp", 2)
    from_y1, from_y0 = swapped(near.give0, "dp", 2), swapped(near.give1, "dp", 2)
    third = added(farthest.mine0, from_y3, full=True)
    from_end3 = swapped(third.low, "dp", 4)
    second = added(middle.mine0, from_y2, full=True)
    from_end2 = swapped(second.low, "dp", 4)
    from_middle3 = swapped_middle(added(third.full, from_end3).low)
    from_middle2 = swapped_middle(added(second.full, from_end2).low)
    from_end1 = swapped(added(near.mine0, from_y1, from_middle3).low, "dp", 4)
    return dict(zip(SUMMANDS, (near.mine1, from_y0, from_end1, from_middle2)))


def adam_of(grad, master, mean_old, square_old, step):
    mean_new = 0.9 * mean_old + 0.1 * grad
    square_new = 0.98 * square_old + 0.02 * grad * grad
    rate = step.shape[1] ** (-0.5) * jnp.minimum(lax.rsqrt(step), step * WARMUP_STEPS ** (-1.5))
    mean_share = 1.0 - jnp.exp(step * math.log(0.9))
    square_share = 1.0 - jnp.exp(step * math.log(0.98))
    fixed_mean = mean_new * (1.0 / mean_share)
    fixed_square = square_new * (1.0 / square_share)
    change = -rate * fixed_mean / (jnp.sqrt(fixed_square) + ADAM_EPS)
    return change, mean_new, square_new, master + change


def adam_kernel(k, full):
    width = k.master.shape[1]
    share = k.vec_master.shape[1]
    step = jnp.full((1, width), k.step[0], jnp.int32).astype(F32)
    rows = k.master.shape[0]
    middle = at_middle()
    totals = []
    for at in range(len([name for name in vars(k) if name.startswith("mine")])):
        mine, *low = [getattr(k, f"{name}{at}")[...].astype(F32) for name in SUMMANDS]
        from_y, from_end, from_middle = low
        totals.append(mine + from_y + from_end + jnp.where(middle, from_middle, 0.0))
    total = jnp.concatenate(totals, axis=0)
    grad, vec_grad = total[:rows], total[rows : rows + 1]
    parts = adam_of(grad, k.master[...], k.mean[...], k.square[...], step)
    if full:
        k.grad[...] = grad
        k.change[...], k.mean_new[...], k.square_new[...] = parts[:3]
    else:
        k.own[:rows] = parts[3].astype(BF16)
    pad = jnp.zeros((1, width - share), F32)

    def padded(ref):
        return jnp.concatenate([ref[...], pad], axis=1)

    parts = adam_of(
        vec_grad, padded(k.vec_master), padded(k.vec_mean), padded(k.vec_square), step
    )
    if full:
        k.vec_grad[...] = vec_grad[:, :share]
        k.vec_change[...] = parts[0][:, :share]
        k.vec_mean_new[...] = parts[1][:, :share]
        k.vec_square_new[...] = parts[2][:, :share]
        for copy in vars(k.go).values():
            copy.start()
        for copy in vars(k.go).values():
            copy.wait()
    else:
        k.own[rows:] = jnp.broadcast_to(parts[3], (TAIL, width)).astype(BF16)


def adam(summands, state, step, full):
    shape, vec_shape = state.master.shape, state.vec_master.shape
    outs, far = {}, {}
    if full:
        far = dict.fromkeys(("grad", "change", "mean_new", "square_new"), (shape, F32))
        far.update({"vec_" + name: (vec_shape, F32) for name in far})
    else:
        outs = {"own": ((shape[0] + TAIL, shape[1]), BF16)}
    return run_kernel(
        lambda k: adam_kernel(k, full), "adam_outputs" if full else "adam", {},
        {**summands, **vars(state)}, outs, far, {}, 0, 6, work=10**9, smem={"step": step},
    )


def place_blocks(pieces, share, rows_all, before=None):
    arrays = [piece[-1] for piece in pieces]
    width = arrays[0].shape[1]
    extra = [] if before is None else [*before]

    def kernel(*refs):
        ins, (target, tails, sems) = refs[: len(arrays)], refs[-3:]
        me = lax.axis_index("dp")
        owners = [z(me >> 2) * 4 + ((me & 3) ^ (2 * y + core)) for z, y, core, _ in pieces]
        copies = []
        for at, (owner, ref) in enumerate(zip(owners, ins)):
            there = pl.ds(pl.multiple_of(owner * share, share), share)
            copies.append(load(ref.at[:share], target.at[there], sems.at[at]))
        if extra:
            tails[...] = refs[len(arrays) + 1][...]
        for owner, ref in zip(owners, ins):
            tails[owner] = ref[share:]
        for copy in copies:
            copy.wait()

    return pl.pallas_call(
        kernel,
        name="place_blocks",
        in_specs=[VMEM] * len(arrays) + [HBM, VMEM][: len(extra)],
        out_specs=[HBM, VMEM],
        out_shape=[
            pltpu.HBM((rows_all, width), BF16),
            pltpu.VMEM((rows_all // share, TAIL, width), BF16),
        ],
        scratch_shapes=[pltpu.SemaphoreType.DMA((len(arrays),))],
        input_output_aliases={len(arrays): 0} if extra else {},
        compiler_params=pltpu.CompilerParams(vmem_limit_bytes=4 * 2**20),
        cost_estimate=pl.CostEstimate(flops=10**9, bytes_accessed=1, transcendentals=0),
    )(*[pltpu.with_memory_space_constraint(array, pltpu.VMEM) for array in arrays], *extra)


def either(middle, end):
    def kernel(k):
        @pl.when(at_middle())
        def _():
            k.out[...] = k.middle[...]

        @pl.when(jnp.logical_not(at_middle()))
        def _():
            k.out[...] = k.end[...]

    outs = dict(out=(end.shape, BF16))
    return quick_kernel(kernel, "either", dict(middle=middle, end=end), outs).out


def gather_blocks(own, share, rows_all, meanwhile):
    end1, middle1 = swapped(own, "dp", 4), swapped_middle(own)
    end1, from_y0 = lax.optimization_barrier((end1, swapped(own, "dp", 2)))
    end2, middle2 = swapped(middle1, "dp", 4), swapped_middle(end1)
    from_y1 = swapped(end1, "dp", 2)
    end3 = swapped(middle2, "dp", 4)
    second = either(middle1, end2)
    from_y2 = swapped(second, "dp", 2)
    third = either(middle2, end3)
    from_y3 = swapped(third, "dp", 2)

    def both(z, y, array):
        return [(z, y, 0, array), (z, y, 1, swapped(array, "dp", 1))]

    early = both(same, 0, own) + both(same, 1, from_y0) + both(next_to, 0, end1)
    early += both(next_to, 1, from_y1) + both(nearer, 0, second)
    first = place_blocks(early, share, rows_all)
    from_y3 = held_until(from_y3, *first, meanwhile)
    late = both(nearer, 1, from_y2) + both(farther, 0, third) + both(farther, 1, from_y3)
    return place_blocks(late, share, rows_all, first)


def body(
    inputs,
    lengths,
    cotangent,
    matrices,
    vectors,
    master_matrices,
    master_vectors,
    matrix_mean,
    matrix_square,
    vector_mean,
    vector_square,
    adam_step,
):
    row_count, seq_len, width = inputs.shape[1:]
    tokens = row_count * seq_len
    rows_all, vec_all = matrices.shape[1], vectors.shape[1]
    ffn = (rows_all - 6 * width) // 2
    half = rows_all // 2
    ranks = lax.axis_size("dp")
    share, vec_share = rows_all // ranks, vec_all // ranks
    by_swaps = ranks == 16 and share % 32 == 0
    me = lax.axis_index("dp")

    x = inputs.reshape(tokens, width)
    cot = cotangent.reshape(tokens, width)
    mats = matrices.reshape(rows_all, width)
    lens_here = pltpu.SMEM(lengths.shape, jnp.int32)

    def spec(columns, dtype):
        return ((tokens, columns), dtype)

    full, low, deep = spec(width, F32), spec(width, BF16), spec(ffn, BF16)
    square, mask = ((width, width), BF16), spec(seq_len, F32)
    double, w_ffn = ((2 * width, width), BF16), ((ffn, width), BF16)
    lse = ((row_count, HEADS, seq_len), F32)
    norms = dict(normal2=full, rstd2=spec(LANES, F32), normal3=full, rstd3=spec(LANES, F32))
    half_tokens = tokens // 2
    half_low, half_full = ((half_tokens, width), BF16), ((half_tokens, width), F32)
    half_double, half_back = ((half_tokens, 2 * width), BF16), ((half_tokens, width + EARLY_LANES), BF16)
    half_rest = ((half_tokens, 4 * width - EARLY_LANES), BF16)
    all_vecs, triple = ((1, vec_all), F32), spec(3 * width, BF16)
    block = (ranks // 8, share + TAIL, width) if by_swaps else (half // 2, width)

    def sides(*zs):
        kinds = ("keep", "give") if by_swaps else ("keep",)
        return {f"{kind}{z}": (block, BF16) for z in zs for kind in kinds}

    early = ((half - 6 * width, width), BF16)

    def wide(rows):
        return ((width // LANES, rows, LANES), F32)

    cross_half = lax.dynamic_slice(mats, ((4 + (me & 1)) * width, 0), (width, width), allow_negative_indices=False)
    cross_mine = swapped(cross_half, "section", 1)
    f = run_kernel(
        forward_kernel, "forward", dict(mats=mats, x=x, vectors=vectors, lengths=lengths), {},
        dict(
            h1=full, w_in=w_ffn, act=deep, slope=deep, **norms,
            memory=half_low, w_cross=double, qc=low, w_out=w_ffn, vecs=all_vecs,
        ),
        dict(
            qkv=triple, lse=lse, mixed=low, normal1=full, rstd1=spec(LANES, F32), mask=mask, w_attn_out=square,
            w_attn=((3 * width, width), BF16), low=low,
        ),
        dict(
            raw_attn=((3 * width, width), BF16), raw_cross=double, raw_ffn=w_ffn,
            x_here=low, total=half_full, wide=wide(ffn), raw_vecs=((1, vec_all), BF16), lens=lens_here,
        ),
        8, 10,
    )
    memory_far0 = swapped(f.memory, "section", 1)
    r = run_kernel(
        forward_rest_kernel, "forward_rest", {},
        dict(
            h1=f.h1, w_in=f.w_in, w_out=f.w_out, vecs=f.vecs, old_act=f.act, old_slope=f.slope,
            **{"old_" + name: getattr(f, name) for name in norms},
        ),
        dict(act=deep, slope=deep, **norms, memory=half_low), dict(low_rest=half_low),
        dict(total=half_full), 0, 6,
        [("old_" + name, name) for name in ("act", "slope", *norms)],
        work=WORK_REST,
    )
    memory_far1 = swapped(r.memory, "section", 1)
    cross_mine = held_until(cross_mine, f.memory)
    cross_other = swapped(cross_mine, "dp", 1)
    p = run_kernel(
        prepare_kernel, "prepare", dict(cot_all=cot, lengths=lengths),
        dict(cross_mine=cross_mine, cross_other=cross_other),
        dict(w_pairs=double, mask=mask, cot=low), {},
        dict(raw=double, wide=wide(2 * width), raw_cot=low, lens=lens_here),
        2, 4,
    )
    shared = dict(
        **vars(p), w_cross=f.w_cross, qc=f.qc, h1=f.h1, w_in=f.w_in, w_out=f.w_out, vecs=f.vecs,
    )
    for_tokens = dict(act=deep, side=deep, grad_ffn=low, low2=low, grad_qc=low, grad_sum2=full)
    far_half = dict(mixed=half_low, right=half_double)
    held = dict(
        pairs=half_double, slope=((half_tokens, ffn), F32), lse=((row_count // 2, HEADS, seq_len), F32),
        grad_mixed=half_low, total=half_full, normal2=half_full, rstd2=((half_tokens, LANES), F32),
    )
    d = run_kernel(
        lambda k: decoder_kernel(k, 0), "decoder", {},
        dict(memory=memory_far0, near_memory=f.memory, **shared, enc_act=r.act, enc_slope=r.slope),
        dict(
            back=half_back, grad_pairs=half_double, vec_grads=all_vecs, **for_tokens, top=half_low,
        ),
        far_half, held,
        0, SPARE_D, (("enc_act", "act"), ("enc_slope", "side")), work=WORK_D,
    )
    back_far = swapped(d.back, "section", 1)
    before = {"old_" + name: getattr(d, name) for name in for_tokens}
    e = run_kernel(
        lambda k: decoder_kernel(k, 1), "decoder_rest", {},
        dict(
            memory=memory_far1, near_memory=r.memory, **shared, **before, vec_before=d.vec_grads,
            top_before=d.top, pairs_before=d.grad_pairs,
        ),
        dict(grad_memory=half_low, rest=half_rest, vec_grads=all_vecs, **for_tokens),
        dict(layer_out=low, **far_half), held,
        0, SPARE_D, [("old_" + name, name) for name in for_tokens], work=WORK_D,
    )
    grad_memory_far = swapped(e.grad_memory, "section", 1)
    rest_far = swapped(e.rest, "section", 1)
    ahead = dict(
        normal1=full, rstd1=spec(LANES, F32), w_attn_out=square, mask=mask, lse=lse, qkv=triple,
        w_attn=((3 * width, width), BF16),
    )
    s = run_kernel(
        backward_kernel, "backward",
        dict(
            **{"far_" + name: getattr(f, name) for name in ahead},
            far_x=x, far_mixed=f.mixed, far_low=f.low, far_low_rest=r.low_rest,
            far_right0=d.right, far_right1=e.right, far_cross_mixed0=d.mixed, far_cross_mixed1=e.mixed,
        ),
        dict(
            dec_grad_ffn=e.grad_ffn, dec_vec_grads=e.vec_grads,
            back=back_far, grad_memory=grad_memory_far, act=e.act, side=e.side,
            low2=e.low2, grad_qc=e.grad_qc, grad_sum2=e.grad_sum2, **{name: getattr(r, name) for name in norms}, h1=f.h1, w_in=f.w_in, w_out=f.w_out, w_cross=f.w_cross, vecs=f.vecs,
        ),
        dict(
            vec_grads=all_vecs, early=early, **sides(2, 3), grad_attn=low, grad_qkv=triple,
            x=low, mixed=low, low=low, right=spec(2 * width, BF16), cross_mixed=low,
        ),
        dict(grad_x=full),
        dict(
            grad_pre=deep, grad_ffn=low, low1=low, wide=wide(ffn), grad_h1=full,
            flat=((2 * ffn, width), BF16), grad_mixed=low, **ahead,
        ),
        15, 9, work=4 * 10**10,
    )
    quarter_flat = ((half // 2, width), BF16)
    a = run_kernel(
        attn_grad_kernel, "attn_grad", {},
        dict(
            grad_qkv=s.grad_qkv, vec_grads=s.vec_grads, x=s.x, grad_attn=s.grad_attn, mixed=s.mixed,
        ),
        dict(left=((4 * width - half // 2, width), BF16), **sides(0)), {},
        dict(wide=wide(3 * width), flat=quarter_flat), 0, 4, work=10**8,
    )
    if by_swaps:
        first, third = (a.keep0, swapped(a.give0, "dp", 1)), (s.keep3, swapped(s.give3, "dp", 1))
        second = (s.keep2, swapped(s.give2, "dp", 1))
        first_rows = (share + TAIL) // 2 // 16 * 16
        cuts = (slice(0, first_rows), slice(first_rows, share + TAIL))
        farthest = [sum_of_cores(cut, (first, None, None, third), (farther,)) for cut in cuts]
    b = run_kernel(
        cross_grad_kernel, "cross_grad", {},
        dict(
            left=a.left, vec_grads=s.vec_grads, early=s.early, back=back_far, rest=rest_far, low=s.low,
            right=s.right, cross_mixed=s.cross_mixed,
        ),
        sides(1), {}, dict(wide=wide(2 * width), flat=quarter_flat), 0, 4, work=10**8,
    )

    state = Refs(master=master_matrices[0], mean=matrix_mean[0], square=matrix_square[0])
    state = Refs(**vars(state), vec_master=master_vectors, vec_mean=vector_mean, vec_square=vector_square)
    if by_swaps:
        quarters = (first, (b.keep1, swapped(b.give1, "dp", 1)), second, third)
        summands = {}
        for at, cut in enumerate(cuts):
            parts = sum_over_dp(cut, quarters, farthest[at])
            summands.update({f"{name}{at}": part for name, part in parts.items()})
        own = adam(summands, state, adam_step, False).own
        result = adam(summands, state, adam_step, True)
        new_mat, tails = gather_blocks(own, share, rows_all, result.change)
        new_vec = tails[:, 0, :vec_share].reshape(1, vec_all)
    else:
        whole = jnp.concatenate([a.keep0, b.keep1, s.keep2, s.keep3], axis=0)
        grad = lax.psum_scatter(whole, "dp", scatter_dimension=0, tiled=True).astype(F32)
        vec_grad = lax.dynamic_slice(
            lax.psum(s.vec_grads, "dp"), (0, me * vec_share), (1, vec_share)
        )
        step = jnp.full((1, width), adam_step[0].astype(F32))
        parts = adam_of(grad, state.master, state.mean, state.square, step)
        vec_step = jnp.full((1, width), adam_step[0].astype(F32))
        pad = ((0, 0), (0, width - vec_share))
        vec_parts = [
            part[:, :vec_share]
            for part in adam_of(
                *[jnp.pad(v, pad) for v in (vec_grad, master_vectors, vector_mean, vector_square)],
                vec_step,
            )
        ]
        names = ("change", "mean_new", "square_new")
        result = dict(grad=grad, vec_grad=vec_grad, **dict(zip(names, parts)))
        result.update({"vec_" + name: part for name, part in zip(names, vec_parts)})
        result = Refs(**result)
        new_mat = lax.all_gather(parts[3].astype(BF16), "dp", axis=0, tiled=True)
        new_vec = lax.all_gather(vec_parts[3].astype(BF16), "dp", axis=1, tiled=True)
    return (
        e.layer_out.reshape(1, row_count, seq_len, width),
        s.grad_x.reshape(1, row_count, seq_len, width),
        result.grad[None],
        result.vec_grad,
        result.change[None],
        result.vec_change,
        result.mean_new[None],
        result.square_new[None],
        result.vec_mean_new,
        result.vec_square_new,
        new_mat[None],
        new_vec,
    )


def solution(mesh):
    return jax.shard_map(
        body,
        mesh=mesh,
        in_specs=(
            P("section", "dp", None, None),
            P(None, "dp", None),
            P("dp", None, None),
            P("section", None, None),
            P("section", None),
            P("section", "dp", None),
            P("section", "dp"),
            P("section", "dp", None),
            P("section", "dp", None),
            P("section", "dp"),
            P("section", "dp"),
            P(),
        ),
        out_specs=(
            P("section", "dp", None, None),
            P("section", "dp", None, None),
            P("section", "dp", None),
            P("section", "dp"),
            P("section", "dp", None),
            P("section", "dp"),
            P("section", "dp", None),
            P("section", "dp", None),
            P("section", "dp"),
            P("section", "dp"),
            P("section", None, None),
            P("section", None),
        ),
        check_vma=False,
    )
```

```python
import math
import types

import jax
import jax.numpy as jnp
from jax import lax
from jax.experimental import pallas as pl
from jax.experimental.pallas import tpu as pltpu
from jax.sharding import PartitionSpec as P

HEADS = 8
HEAD_DIM = 64
PAIR = 2 * HEAD_DIM
LANES = 128
TAIL = 16
EARLY_LANES = 384
SUMMANDS = ("mine", "from_y", "from_end", "from_middle")
UNROLL_CHUNKS = True
WORK_REST = 10**10
WORK_D = 4 * 10**10
SPARE_D = 8

MASK_FILL = -1e30
NORM_EPS = 1e-05
ADAM_EPS = 1e-09
WARMUP_STEPS = 4000.0

F32 = jnp.float32
BF16 = jnp.bfloat16

BIAS_OUT, GAIN1, SHIFT1, GAIN2, SHIFT2, GAIN3, SHIFT3 = range(-7, 0)


def dot(left, right):
    return jnp.dot(left, right, preferred_element_type=F32)


def dot_nt(left, right):
    return lax.dot_general(left, right, (((1,), (1,)), ((), ())), preferred_element_type=F32)


def dot_tn(left, right):
    return lax.dot_general(left, right, (((0,), (0,)), ((), ())), preferred_element_type=F32)


def norm_parts(hidden):
    centre = hidden - jnp.mean(hidden, axis=-1, keepdims=True)
    rstd = lax.rsqrt(jnp.mean(centre * centre, axis=-1, keepdims=True) + NORM_EPS)
    return centre * rstd, rstd


def norm_backward(normal, rstd, gain, grad):
    scaled = grad * gain
    inner = jnp.mean(scaled * normal, axis=-1, keepdims=True)
    grad_in = rstd * (scaled - jnp.mean(scaled, axis=-1, keepdims=True) - normal * inner)
    grad_gain = jnp.sum(grad * normal, axis=0, keepdims=True)
    grad_shift = jnp.sum(grad, axis=0, keepdims=True)
    return grad_in, grad_gain, grad_shift


def act_parts(pre):
    cdf = 0.5 * (1.0 + lax.erf(pre * (0.5**0.5)))
    pdf = jnp.exp(-0.5 * pre * pre) * 0.3989422804014327
    return pre * cdf, cdf + pre * pdf


def split_rows(raw, wide, parts, out, base):
    width = raw.shape[1]
    for c in range(width // LANES):
        cut = slice(c * LANES, (c + 1) * LANES)
        wide[c, : parts * width] = raw[: parts * width, cut].astype(F32)
        for j in range(parts):
            out[(base + j) * width : (base + j + 1) * width, cut] = wide[
                c, pl.ds(j, width, stride=parts), :
            ].astype(BF16)


def put_part(wide, j, parts, values):
    rows, width = values.shape
    for c in range(width // LANES):
        wide[c, pl.ds(j, rows, stride=parts), :] = values[:, c * LANES : (c + 1) * LANES]


def take_parts(wide, rows, out, first):
    for c in range(wide.shape[0]):
        out[first : first + rows, c * LANES : (c + 1) * LANES] = wide[c, :rows].astype(BF16)


def sentence_ends(lens, side, row):
    ends, total = [], 0
    for j in range(lens.shape[2]):
        total = total + lens[side, row, j]
        ends.append(total)
    return ends


def sentence_of(ends, position):
    found = jnp.zeros(position.shape, jnp.int32)
    for end in ends:
        found = found + (position >= end).astype(jnp.int32)
    return found


def fill_mask(mask, lens, query_side, key_side, causal):
    seq_len = mask.shape[1]
    row_count, sents = lens.shape[1:]
    q_pos = lax.broadcasted_iota(jnp.int32, (seq_len, seq_len), 1)
    k_pos = lax.broadcasted_iota(jnp.int32, (seq_len, seq_len), 0)
    for r in range(row_count):
        q_ids = sentence_of(sentence_ends(lens, query_side, r), q_pos)
        k_ids = sentence_of(sentence_ends(lens, key_side, r), k_pos)
        same = jnp.where(q_ids == k_ids, 1, 0)
        if causal is not None:
            same = jnp.where(q_pos >= k_pos, same, jnp.where(causal, 0, same))
        allowed = jnp.where(q_ids == sents, 1, same)
        mask[r * seq_len : (r + 1) * seq_len] = allowed.astype(F32)


def both_heads(block, lane):
    even = (lane < HEAD_DIM).astype(BF16)
    return jnp.concatenate([block * even, block * (1 - even)], axis=0)


def both_heads_across(block):
    turned = block.T
    even = (lax.broadcasted_iota(jnp.int32, (PAIR, 1), 0) < HEAD_DIM).astype(BF16)
    return jnp.concatenate([turned * even, turned * (1 - even)], axis=1)


def one_of(stacked, lane):
    keys = stacked.shape[0] // 2
    return jnp.where(lane < HEAD_DIM, stacked[:keys], stacked[keys:])


def for_rows(mask, step):
    seq_len = mask.shape[1]

    def turn(row, carried):
        step(row, pl.ds(pl.multiple_of(row * seq_len, seq_len), seq_len), range(HEADS // 2))
        return carried

    lax.fori_loop(0, mask.shape[0] // seq_len, turn, 0)


def pair_lanes(first, p):
    return slice(first + p * PAIR, first + (p + 1) * PAIR)


def attend_forward(query, keys, values, mask, out, lse):
    seq_len = mask.shape[1]
    lane = lax.broadcasted_iota(jnp.int32, (1, PAIR), 1)
    (q_ref, q_at), (k_ref, k_at), (v_ref, v_at) = query, keys, values

    def step(row, rows, pairs):
        scores = [
            dot_nt(both_heads(k_ref[rows, pair_lanes(k_at, p)], lane), q_ref[rows, pair_lanes(q_at, p)])
            for p in pairs
        ]
        mixed = []
        for p in pairs:
            probs = []
            for half in range(2):
                part = scores[p][half * seq_len : (half + 1) * seq_len] * HEAD_DIM ** (-0.5)
                part = jnp.where(mask[rows] > 0.0, part, MASK_FILL)
                top = jnp.max(part, axis=0, keepdims=True)
                raised = jnp.exp(part - top)
                total = jnp.sum(raised, axis=0, keepdims=True)
                probs.append((raised * (1.0 / total)).astype(BF16))
                lse[row, 2 * p + half : 2 * p + half + 1] = top + jnp.log(total)
            values = both_heads_across(v_ref[rows, pair_lanes(v_at, p)])
            mixed.append(dot(values, jnp.concatenate(probs, axis=0)))
        for p in pairs:
            out[rows, pair_lanes(0, p)] = mixed[p].T.astype(BF16)

    for_rows(mask, step)


def attend_backward(query, keys, values, mask, lse, grad_out, grad_q, grad_k, grad_v):
    seq_len = mask.shape[1]
    lane = lax.broadcasted_iota(jnp.int32, (1, PAIR), 1)
    scale = HEAD_DIM ** (-0.5)
    (q_ref, q_at), (k_ref, k_at), (v_ref, v_at) = query, keys, values
    (gq_ref, gq_at), (gk_ref, gk_at), (gv_ref, gv_at) = grad_q, grad_k, grad_v

    def step(row, rows, pairs):
        qs = [q_ref[rows, pair_lanes(q_at, p)] for p in pairs]
        ks = [k_ref[rows, pair_lanes(k_at, p)] for p in pairs]
        gos = [grad_out[rows, pair_lanes(0, p)] for p in pairs]
        scores = [dot_nt(both_heads(ks[p], lane), qs[p]) for p in pairs]
        grad_probs = [
            dot_nt(both_heads(v_ref[rows, pair_lanes(v_at, p)], lane), gos[p]) for p in pairs
        ]
        probs, grad_scores = [], []
        for p in pairs:
            prob_parts, score_parts = [], []
            for half in range(2):
                cut = slice(half * seq_len, (half + 1) * seq_len)
                part = jnp.where(mask[rows] > 0.0, scores[p][cut] * scale, MASK_FILL)
                prob = jnp.exp(part - lse[row, 2 * p + half : 2 * p + half + 1])
                gp = grad_probs[p][cut]
                inner = jnp.sum(prob * gp, axis=0, keepdims=True)
                prob_parts.append(prob.astype(BF16))
                score_parts.append((prob * (gp - inner)).astype(BF16))
            probs.append(jnp.concatenate(prob_parts, axis=0))
            grad_scores.append(jnp.concatenate(score_parts, axis=0))
        grad_vs = [dot(probs[p], gos[p]) for p in pairs]
        grad_ks = [dot(grad_scores[p], qs[p]) for p in pairs]
        grad_qs = [dot(both_heads_across(ks[p]), grad_scores[p]) for p in pairs]
        for p in pairs:
            gv_ref[rows, pair_lanes(gv_at, p)] = one_of(grad_vs[p], lane).astype(BF16)
            gk_ref[rows, pair_lanes(gk_at, p)] = (one_of(grad_ks[p], lane) * scale).astype(BF16)
            gq_ref[rows, pair_lanes(gq_at, p)] = (grad_qs[p].T * scale).astype(BF16)

    for_rows(mask, step)


def small(vecs, which, width):
    pieces = vecs.shape[1] // width
    at = (which if which >= 0 else pieces + which) * width
    return vecs[:, at : at + width].astype(F32)


def set_small(vecs, which, width, value):
    pieces = vecs.shape[1] // width
    at = (which if which >= 0 else pieces + which) * width
    vecs[:, at : at + width] = value


def where_am_i():
    return lax.axis_index("section"), lax.rem(lax.axis_index("dp"), 2)


def for_chunks(count, width, step):
    def turn(j, carried):
        step(j, pl.ds(pl.multiple_of(j * width, width), width))
        return carried

    lax.fori_loop(0, count, turn, 0, unroll=UNROLL_CHUNKS)


def ffn_forward(normed, w_in, w_out, vecs, act, slope, total):
    width = normed.shape[1]
    low = normed.astype(BF16)
    total[...] = normed + small(vecs, BIAS_OUT, width)

    def step(j, cut):
        pre = dot(low, w_in[cut]) + vecs[:, cut]
        value, derivative = act_parts(pre)
        value = value.astype(BF16)
        act[:, cut] = value
        slope[:, cut] = derivative.astype(slope.dtype)
        total[...] += dot(value, w_out[cut])

    for_chunks(w_in.shape[0] // width, width, step)


def ffn_backward(grad_low, w_in, w_out, slope, grad_pre, vec_grads, total):
    width = grad_low.shape[1]

    def step(j, cut):
        grad = (dot_nt(grad_low, w_out[cut]) * slope[:, cut].astype(F32)).astype(BF16)
        grad_pre[:, cut] = grad
        vec_grads[:, cut] = jnp.sum(grad.astype(F32), axis=0, keepdims=True)
        total[...] += dot_nt(grad, w_in[cut])

    for_chunks(w_in.shape[0] // width, width, step)


def load(source, target, sem):
    copy = pltpu.make_async_copy(source, target, sem)
    copy.start()
    return copy


def memory_of(k, rows):
    width = k.h1.shape[1]
    vecs = k.vecs
    ffn_forward(k.h1[rows], k.w_in, k.w_out, vecs, k.act.at[rows], k.slope.at[rows], k.total)
    normal, rstd = norm_parts(k.total[...])
    k.normal2[rows], k.rstd2[rows] = normal, jnp.broadcast_to(rstd, (rstd.shape[0], LANES))
    normal, rstd = norm_parts(normal * small(vecs, GAIN2, width) + small(vecs, SHIFT2, width))
    k.normal3[rows], k.rstd3[rows] = normal, jnp.broadcast_to(rstd, (rstd.shape[0], LANES))
    third = normal * small(vecs, GAIN3, width) + small(vecs, SHIFT3, width)
    k.memory[...] = third.astype(BF16)


def forward_kernel(k):
    width = k.h1.shape[1]
    ffn = k.w_in.shape[0]
    sec, _ = where_am_i()
    get_lens = load(k.lengths, k.lens, k.sems.at[7])
    get_in = load(k.mats.at[: 3 * width], k.raw_attn, k.sems.at[0])
    get_x = load(k.x, k.x_here, k.sems.at[1])
    get_vecs = load(k.vectors, k.raw_vecs, k.sems.at[2])
    get_attn_out = load(k.mats.at[3 * width : 4 * width], k.w_attn_out, k.sems.at[3])
    get_ffn = load(k.mats.at[6 * width : 6 * width + ffn], k.raw_ffn, k.sems.at[4])
    get_out = load(k.mats.at[6 * width + ffn :], k.w_out, k.sems.at[5])
    get_cross = pltpu.make_async_copy(k.mats.at[4 * width : 6 * width], k.raw_cross, k.sems.at[6])

    @pl.when(sec == 1)
    def _():
        get_cross.start()

    get_lens.wait()
    fill_mask(k.mask, k.lens, sec, sec, sec == 1)
    k.go.mask.start()
    get_in.wait()
    split_rows(k.raw_attn, k.wide, 3, k.w_attn, 0)
    k.go.w_attn.start()
    get_x.wait()
    for j in range(3):
        part = dot(k.x_here[...], k.w_attn[j * width : (j + 1) * width])
        k.qkv[:, j * width : (j + 1) * width] = part.astype(BF16)
    k.go.qkv.start()
    attend_forward((k.qkv, 0), (k.qkv, width), (k.qkv, 2 * width), k.mask, k.mixed, k.lse)
    k.go.mixed.start()
    k.go.lse.start()
    get_vecs.wait()
    k.vecs[...] = k.raw_vecs[...].astype(F32)
    vecs = k.vecs
    get_attn_out.wait()
    k.go.w_attn_out.start()
    hidden = k.x_here[...].astype(F32) + dot(k.mixed[...], k.w_attn_out[...])
    normal, rstd = norm_parts(hidden)
    k.normal1[...], k.rstd1[...] = normal, jnp.broadcast_to(rstd, (rstd.shape[0], LANES))
    k.go.normal1.start()
    k.go.rstd1.start()
    k.h1[...] = normal * small(vecs, GAIN1, width) + small(vecs, SHIFT1, width)
    get_ffn.wait()
    split_rows(k.raw_ffn, k.wide, ffn // width, k.w_in, 0)
    get_out.wait()

    @pl.when(sec == 0)
    def _():
        memory_of(k, slice(0, k.memory.shape[0]))
        k.low[: k.memory.shape[0]] = k.memory[...]
        k.go.low.start()

    @pl.when(sec == 1)
    def _():
        k.low[...] = k.h1[...].astype(BF16)
        k.go.low.start()
        get_cross.wait()
        split_rows(k.raw_cross, k.wide, 2, k.w_cross, 0)
        k.qc[...] = dot(k.low[...], k.w_cross[:width]).astype(BF16)

    k.go.mask.wait()
    k.go.w_attn.wait()
    k.go.qkv.wait()
    k.go.mixed.wait()
    k.go.lse.wait()
    k.go.w_attn_out.wait()
    k.go.normal1.wait()
    k.go.rstd1.wait()
    k.go.low.wait()


def forward_rest_kernel(k):
    sec, _ = where_am_i()

    @pl.when(sec == 0)
    def _():
        half = k.memory.shape[0]
        memory_of(k, slice(half, 2 * half))
        k.low_rest[...] = k.memory[...]
        k.go.low_rest.start()
        k.go.low_rest.wait()


def prepare_kernel(k):
    width = k.raw.shape[1]
    seq_len = k.mask.shape[1]
    sec, core = where_am_i()

    @pl.when(sec == 1)
    def _():
        get_cot = load(k.cot_all, k.raw_cot, k.sems.at[0])
        get_lens = load(k.lengths, k.lens, k.sems.at[1])
        k.raw[pl.ds(pl.multiple_of(core * width, width), width)] = k.cross_mine[...]
        k.raw[pl.ds(pl.multiple_of((1 - core) * width, width), width)] = k.cross_other[...]
        split_rows(k.raw, k.wide, 2, k.w_pairs, 0)
        get_lens.wait()
        fill_mask(k.mask, k.lens, 1, 0, None)
        get_cot.wait()
        position = lax.broadcasted_iota(jnp.int32, (seq_len, 1), 0)
        for r in range(k.lens.shape[1]):
            used = sentence_ends(k.lens, 1, r)[-1]
            rows = slice(r * seq_len, (r + 1) * seq_len)
            k.cot[rows] = jnp.where(position < used, k.raw_cot[rows].astype(F32), 0.0).astype(BF16)


def decoder_kernel(k, part):
    half, width = k.memory.shape
    rows = slice(part * half, (part + 1) * half)
    vecs = k.vecs
    sec, _ = where_am_i()
    top = k.layer_out.at[rows] if part == 1 else k.top
    pairs_at = 0 if part == 0 else 2 * width - EARLY_LANES
    grad_pairs = k.grad_pairs if part == 0 else k.rest
    grad_keys, grad_values = (grad_pairs, pairs_at), (grad_pairs, pairs_at + width)
    if part == 1:
        k.layer_out[:half] = k.top_before[...]

    @pl.when(sec == 0)
    def _():
        top[...] = k.near_memory[...]

    @pl.when(sec == 1)
    def _():
        mask, qc, act, side = k.mask.at[rows], k.qc.at[rows], k.act.at[rows], k.side.at[rows]
        for j in range(2):
            pair = dot(k.memory[...], k.w_pairs[j * width : (j + 1) * width])
            k.pairs[:, j * width : (j + 1) * width] = pair.astype(BF16)
        attend_forward((qc, 0), (k.pairs, 0), (k.pairs, width), mask, k.mixed, k.lse)
        k.go.mixed.start()
        hidden2 = k.h1[rows] + dot(k.mixed[...], k.w_cross[width:])
        gain2, shift2 = small(vecs, GAIN2, width), small(vecs, SHIFT2, width)
        normal2, rstd2 = norm_parts(hidden2)
        k.normal2[...], k.rstd2[...] = normal2, jnp.broadcast_to(rstd2, (half, LANES))
        normed2 = normal2 * gain2 + shift2
        k.low2[rows] = normed2.astype(BF16)
        ffn_forward(normed2, k.w_in, k.w_out, vecs, act, k.slope, k.total)
        normal3, rstd3 = norm_parts(k.total[...])
        gain3, shift3 = small(vecs, GAIN3, width), small(vecs, SHIFT3, width)
        top[...] = (normal3 * gain3 + shift3).astype(BF16)
        grad_sum3, d_gain, d_shift = norm_backward(
            normal3, rstd3, gain3, k.cot[rows].astype(F32)
        )
        set_small(k.vec_grads, GAIN3, width, d_gain)
        set_small(k.vec_grads, SHIFT3, width, d_shift)
        grad_low = grad_sum3.astype(BF16)
        k.grad_ffn[rows] = grad_low
        set_small(
            k.vec_grads, BIAS_OUT, width, jnp.sum(grad_low.astype(F32), axis=0, keepdims=True)
        )
        k.total[...] = grad_sum3
        ffn_backward(grad_low, k.w_in, k.w_out, k.slope, side, k.vec_grads, k.total)
        grad_hidden2, d_gain, d_shift = norm_backward(
            k.normal2[...], k.rstd2[:, :1], gain2, k.total[...]
        )
        set_small(k.vec_grads, GAIN2, width, d_gain)
        set_small(k.vec_grads, SHIFT2, width, d_shift)
        k.grad_sum2[rows] = grad_hidden2
        low = grad_hidden2.astype(BF16)
        k.right[:, width:] = low
        k.grad_mixed[...] = dot_nt(low, k.w_cross[width:]).astype(BF16)
        attend_backward(
            (qc, 0), (k.pairs, 0), (k.pairs, width), mask, k.lse, k.grad_mixed,
            (k.right, 0), grad_keys, grad_values,
        )
        k.go.right.start()
        k.grad_sum2[rows] += dot_nt(k.right[:, :width], k.w_cross[:width])
        back = jnp.zeros((half, width), F32)
        for j, (ref, at) in enumerate((grad_keys, grad_values)):
            back = back + dot_nt(ref[:, at : at + width], k.w_pairs[j * width : (j + 1) * width])
        if part == 0:
            k.back[:, :width] = back.astype(BF16)
            k.back[:, width:] = k.grad_pairs[:, :EARLY_LANES]
        else:
            k.grad_memory[...] = back.astype(BF16)
            k.rest[:, :pairs_at] = k.pairs_before[:, EARLY_LANES:]
        if part == 1:
            k.vec_grads[...] += k.vec_before[...]
        k.go.mixed.wait()
        k.go.right.wait()

    if part == 1:
        k.go.layer_out.start()
        k.go.layer_out.wait()


def ffn_weight_grads(k, act, low, grad_pre, grad_ffn):
    width = k.h1.shape[1]
    ffn = k.w_in.shape[0]
    chunks = ffn // width

    def step(j, cut):
        put_part(k.wide, j, chunks, dot_tn(low[...], grad_pre[:, cut]))
        there = pl.ds(pl.multiple_of(ffn + j * width, width), width)
        k.flat[there] = dot_tn(act[:, cut], grad_ffn[...]).astype(BF16)

    for_chunks(chunks, width, step)


def put_sides(k, first, z, vec_grads, core):
    width = k.flat.shape[1]
    keep = getattr(k, f"keep{z}")
    if len(keep.shape) == 2:
        keep[...] = k.flat[first : first + keep.shape[0]]
        return
    gives = [getattr(k, f"give{z}{at}") for at in range(2)]
    count, rows, _ = keep.shape
    rows -= TAIL
    split = gives[0].shape[1]
    share = vec_grads.shape[1] // (8 * count)

    def tail(at):
        owner = 2 * count * z + at
        row = vec_grads[:, owner * share : (owner + 1) * share]
        row = jnp.concatenate([row, jnp.zeros((1, width - share), F32)], axis=1)
        return jnp.broadcast_to(row, (TAIL, width)).astype(BF16)

    for at in range(count):
        mine = first + (2 * at + core) * rows
        other = first + (2 * at + 1 - core) * rows
        keep[at, :rows] = k.flat[pl.ds(pl.multiple_of(mine, TAIL), rows)]
        gives[0][at] = k.flat[pl.ds(pl.multiple_of(other, TAIL), split)]
        gives[1][at, : rows - split] = k.flat[pl.ds(pl.multiple_of(other + split, TAIL), rows - split)]

        @pl.when(core == 0)
        def _(at=at):
            keep[at, rows:] = tail(2 * at)
            gives[1][at, rows - split :] = tail(2 * at + 1)

        @pl.when(core == 1)
        def _(at=at):
            keep[at, rows:] = tail(2 * at + 1)
            gives[1][at, rows - split :] = tail(2 * at)


def backward_kernel(k):
    width = k.h1.shape[1]
    ffn = k.w_in.shape[0]
    vecs = k.vecs
    sec, core = where_am_i()
    half = k.back.shape[0]
    first, rest = slice(0, half), slice(half, 2 * half)
    wanted = ("normal1", "rstd1", "w_attn_out", "mask", "lse", "qkv", "w_attn", "x", "mixed")
    arriving = [(getattr(k, "far_" + name), getattr(k, name)) for name in wanted]
    arriving += [
        (k.far_low.at[first], k.low.at[first]),
        (k.far_right0, k.right.at[first]),
        (k.far_right1, k.right.at[rest]),
        (k.far_cross_mixed0, k.cross_mixed.at[first]),
        (k.far_cross_mixed1, k.cross_mixed.at[rest]),
    ]
    coming = [load(*ends, k.sems.at[at]) for at, ends in enumerate(arriving)]
    last_sem = k.sems.at[len(coming)]

    @pl.when(sec == 0)
    def _():
        load(k.far_low_rest, k.low.at[rest], last_sem)

    @pl.when(sec == 1)
    def _():
        load(k.far_low.at[rest], k.low.at[rest], last_sem)

    coming.append(pltpu.make_async_copy(k.far_low_rest, k.low.at[rest], last_sem))

    @pl.when(sec == 0)
    def _():
        grad_memory = jnp.concatenate([k.back[:, :width], k.grad_memory[...]], axis=0)
        grad, d_gain, d_shift = norm_backward(
            k.normal3[...], k.rstd3[:, :1], small(vecs, GAIN3, width), grad_memory.astype(F32)
        )
        set_small(k.vec_grads, GAIN3, width, d_gain)
        set_small(k.vec_grads, SHIFT3, width, d_shift)
        total, d_gain, d_shift = norm_backward(
            k.normal2[...], k.rstd2[:, :1], small(vecs, GAIN2, width), grad
        )
        set_small(k.vec_grads, GAIN2, width, d_gain)
        set_small(k.vec_grads, SHIFT2, width, d_shift)
        grad_low = total.astype(BF16)
        k.grad_ffn[...] = grad_low
        set_small(
            k.vec_grads, BIAS_OUT, width, jnp.sum(grad_low.astype(F32), axis=0, keepdims=True)
        )
        k.low1[...] = k.h1[...].astype(BF16)
        k.grad_h1[...] = total
        ffn_backward(grad_low, k.w_in, k.w_out, k.side, k.grad_pre, k.vec_grads, k.grad_h1)
        ffn_weight_grads(k, k.act, k.low1, k.grad_pre, k.grad_ffn)

    @pl.when(sec == 1)
    def _():
        k.vec_grads[...] = k.dec_vec_grads[...]
        k.grad_h1[...] = k.grad_sum2[...]
        ffn_weight_grads(k, k.act, k.low2, k.side, k.dec_grad_ffn)

    take_parts(k.wide, ffn, k.flat, 0)
    early = k.early.shape[0]
    k.early[...] = k.flat[:early]
    for copy in coming:
        copy.wait()
    grad, d_gain, d_shift = norm_backward(
        k.normal1[...], k.rstd1[:, :1], small(vecs, GAIN1, width), k.grad_h1[...]
    )
    set_small(k.vec_grads, GAIN1, width, d_gain)
    set_small(k.vec_grads, SHIFT1, width, d_shift)
    put_sides(k, early, 2, k.vec_grads, core)
    put_sides(k, (k.flat.shape[0] + early) // 2, 3, k.vec_grads, core)
    low = grad.astype(BF16)
    k.grad_attn[...] = low
    k.grad_mixed[...] = dot_nt(low, k.w_attn_out[...]).astype(BF16)
    attend_backward(
        (k.qkv, 0), (k.qkv, width), (k.qkv, 2 * width), k.mask, k.lse, k.grad_mixed,
        (k.grad_qkv, 0), (k.grad_qkv, width), (k.grad_qkv, 2 * width),
    )
    for j in range(3):
        cut = slice(j * width, (j + 1) * width)
        grad = grad + dot_nt(k.grad_qkv[:, cut], k.w_attn[cut])
    k.grad_x[...] = grad
    k.go.grad_x.start()
    k.go.grad_x.wait()


def attn_grad_kernel(k):
    width = k.x.shape[1]
    quarter = k.flat.shape[0]
    _, core = where_am_i()

    def step(j, cut):
        put_part(k.wide, j, 3, dot_tn(k.x[...], k.grad_qkv[:, cut]))

    for_chunks(3, width, step)
    take_parts(k.wide, 3 * width, k.flat, 0)
    grad = dot_tn(k.mixed[...], k.grad_attn[...]).astype(BF16)
    k.flat[3 * width :] = grad[: quarter - 3 * width]
    k.left[...] = grad[quarter - 3 * width :]
    put_sides(k, 0, 0, k.vec_grads, core)


def cross_grad_kernel(k):
    half = k.rest.shape[0]
    first, width = k.left.shape
    sec, core = where_am_i()
    k.flat[:first] = k.left[...]
    k.flat[first + 2 * width :] = k.early[...]

    @pl.when(sec == 0)
    def _():
        rest = k.rest[...]
        at = width - EARLY_LANES
        keys0 = jnp.concatenate([k.back[:, width:], rest[:, :at]], axis=1)
        before = (keys0, rest[:, at : at + width])
        at += width
        after = (rest[:, at : at + width], rest[:, at + width :])
        for j in range(2):
            grad = dot_tn(k.low[:half], before[j]) + dot_tn(k.low[half:], after[j])
            put_part(k.wide, j, 2, grad)

    @pl.when(sec == 1)
    def _():
        put_part(k.wide, 0, 2, dot_tn(k.low[...], k.right[:, :width]))
        put_part(k.wide, 1, 2, dot_tn(k.cross_mixed[...], k.right[:, width:]))

    take_parts(k.wide, 2 * width, k.flat, first)
    put_sides(k, 0, 1, k.vec_grads, core)


class Refs(types.SimpleNamespace):
    pass


def run_kernel(kernel, name, hbm, vmem, outs, far_outs, scratch, loads, spare, reuse=(), work=10**10, smem=None):
    smem = smem or {}
    ins = {**smem, **hbm, **vmem}
    near = {n: pltpu.VMEM(*spec) for n, spec in far_outs.items()}
    near.update({n: pltpu.VMEM(*spec) if isinstance(spec, tuple) else spec for n, spec in scratch.items()})
    names = [*ins, *outs, *far_outs, *near, "sems", "leave_sems"]

    def run(*refs):
        k = Refs(**dict(zip(names, refs)))
        first = len(ins) + len(outs)
        k.go = Refs()
        for at, n in enumerate(far_outs):
            copy = pltpu.make_async_copy(getattr(k, n), refs[first + at], k.leave_sems.at[at])
            setattr(k.go, n, copy)
        kernel(k)

    results = pl.pallas_call(
        run,
        name=name,
        in_specs=[SMEM] * len(smem) + [HBM] * len(hbm) + [VMEM] * len(vmem),
        out_specs=[VMEM] * len(outs) + [HBM] * len(far_outs),
        out_shape=[pltpu.VMEM(*spec) for spec in outs.values()]
        + [pltpu.HBM(*spec) for spec in far_outs.values()],
        scratch_shapes=[
            *near.values(),
            pltpu.SemaphoreType.DMA((max(loads, 1),)),
            pltpu.SemaphoreType.DMA((max(len(far_outs), 1),)),
        ],
        compiler_params=pltpu.CompilerParams(
            vmem_limit_bytes=int(spare * 2**20)
            + sum(math.prod(b.shape) * jnp.dtype(b.dtype).itemsize for b in near.values())
        ),
        input_output_aliases={[*ins].index(old): [*outs].index(new) for old, new in reuse},
        cost_estimate=pl.CostEstimate(flops=work, bytes_accessed=1, transcendentals=0),
    )(
        *smem.values(),
        *[pltpu.with_memory_space_constraint(array, pltpu.HBM) for array in hbm.values()],
        *[pltpu.with_memory_space_constraint(array, pltpu.VMEM) for array in vmem.values()],
    )
    return Refs(**dict(zip([*outs, *far_outs], results)))


SMEM = pl.BlockSpec(memory_space=pltpu.SMEM)
HBM = pl.BlockSpec(memory_space=pltpu.HBM)
VMEM = pl.BlockSpec(memory_space=pltpu.VMEM)
ANY = pl.BlockSpec(memory_space=pl.ANY)


def swapped(array, axis, bit):
    devices = lax.axis_size(axis)
    return lax.ppermute(array, axis, [(i, i ^ bit) for i in range(devices)])


def held_until(array, *others):
    return lax.optimization_barrier((array, *others))[0]


def own_bit(bit):
    return (lax.axis_index("dp") >> bit) & 1


def swapped_middle(array):
    ranks = lax.axis_size("dp")
    quarter = ranks // 4
    pairs = [(i, i + quarter) for i in range(quarter, 2 * quarter)]
    pairs += [(j, i) for i, j in pairs]
    outer = [*range(quarter), *range(ranks - quarter, ranks)]
    return lax.ppermute(array, "dp", pairs + [(i, i ^ 1) for i in outer])


def at_middle():
    return own_bit(2) != own_bit(3)


def quick_kernel(kernel, name, ins, outs):
    return run_kernel(kernel, name, {}, ins, outs, {}, {}, 0, 4, work=10**8)


def sum_of_cores(cut, quarters, ways):
    rows, width = cut.stop - cut.start, quarters[0][0].shape[2]
    used = sorted({way(z) for way in ways for z in range(4)})

    def kernel(k):
        y = own_bit(1)
        here = lax.axis_index("dp") >> 2
        for z in range(4):

            @pl.when(here == z)
            def _(z=z):
                for at, way in enumerate(ways):
                    keep, core = getattr(k, f"keep{way(z)}"), getattr(k, f"core{way(z)}")
                    total = keep[1 - y, cut].astype(F32) + core[1 - y].astype(F32)
                    getattr(k, f"give{at}")[...] = total.astype(BF16)
                    total = keep[y, cut].astype(F32) + core[y].astype(F32)
                    getattr(k, f"mine{at}")[...] = total

    ins = {f"keep{z}": quarters[z][0] for z in used}
    ins.update({f"core{z}": quarters[z][1] for z in used})
    outs = {f"give{at}": ((rows, width), BF16) for at in range(len(ways))}
    outs.update({f"mine{at}": ((rows, width), F32) for at in range(len(ways))})
    return quick_kernel(kernel, "sum_of_cores", ins, outs)


def same(z):
    return z


def next_to(z):
    return z ^ 1


def nearer(z):
    return 2 - (z >> 1)


def farther(z):
    return 3 - 3 * (z >> 1)


def added(wide, part, middle=None, full=False):
    def kernel(k):
        total = k.wide[...] + k.part[...].astype(F32)
        if middle is not None:
            total = total + jnp.where(at_middle(), k.middle[...].astype(F32), 0.0)
        k.low[...] = total.astype(BF16)
        if full:
            k.full[...] = total

    ins = dict(wide=wide, part=part)
    if middle is not None:
        ins = dict(wide=wide, part=part, middle=middle)
    outs = dict(low=(wide.shape, BF16))
    if full:
        outs = dict(low=(wide.shape, BF16), full=(wide.shape, F32))
    return quick_kernel(kernel, "added", ins, outs)


def sum_over_dp(cut, quarters, farthest):
    middle = sum_of_cores(cut, quarters, (nearer,))
    near = sum_of_cores(cut, quarters, (next_to, same))
    from_y3, from_y2 = swapped(farthest.give0, "dp", 2), swapped(middle.give0, "dp", 2)
    from_y1, from_y0 = swapped(near.give0, "dp", 2), swapped(near.give1, "dp", 2)
    third = added(farthest.mine0, from_y3, full=True)
    from_end3 = swapped(third.low, "dp", 4)
    second = added(middle.mine0, from_y2, full=True)
    from_end2 = swapped(second.low, "dp", 4)
    from_middle3 = swapped_middle(added(third.full, from_end3).low)
    from_middle2 = swapped_middle(added(second.full, from_end2).low)
    from_end1 = swapped(added(near.mine0, from_y1, from_middle3).low, "dp", 4)
    return dict(zip(SUMMANDS, (near.mine1, from_y0, from_end1, from_middle2)))


def adam_of(grad, master, mean_old, square_old, step):
    mean_new = 0.9 * mean_old + 0.1 * grad
    square_new = 0.98 * square_old + 0.02 * grad * grad
    rate = step.shape[1] ** (-0.5) * jnp.minimum(lax.rsqrt(step), step * WARMUP_STEPS ** (-1.5))
    mean_share = 1.0 - jnp.exp(step * math.log(0.9))
    square_share = 1.0 - jnp.exp(step * math.log(0.98))
    fixed_mean = mean_new * (1.0 / mean_share)
    fixed_square = square_new * (1.0 / square_share)
    change = -rate * fixed_mean / (jnp.sqrt(fixed_square) + ADAM_EPS)
    return change, mean_new, square_new, master + change


def adam_kernel(k, full):
    width = k.master.shape[1]
    share = k.vec_master.shape[1]
    step = jnp.full((1, width), k.step[0], jnp.int32).astype(F32)
    rows = k.master.shape[0]
    middle = at_middle()
    totals = []
    for at in range(len([name for name in vars(k) if name.startswith("mine")])):
        mine, *low = [getattr(k, f"{name}{at}")[...].astype(F32) for name in SUMMANDS]
        from_y, from_end, from_middle = low
        totals.append(mine + from_y + from_end + jnp.where(middle, from_middle, 0.0))
    total = jnp.concatenate(totals, axis=0)
    grad, vec_grad = total[:rows], total[rows : rows + 1]
    parts = adam_of(grad, k.master[...], k.mean[...], k.square[...], step)
    if full:
        k.grad[...] = grad
        k.change[...], k.mean_new[...], k.square_new[...] = parts[:3]
    else:
        k.own[:rows] = parts[3].astype(BF16)
    pad = jnp.zeros((1, width - share), F32)

    def padded(ref):
        return jnp.concatenate([ref[...], pad], axis=1)

    parts = adam_of(
        vec_grad, padded(k.vec_master), padded(k.vec_mean), padded(k.vec_square), step
    )
    if full:
        k.vec_grad[...] = vec_grad[:, :share]
        k.vec_change[...] = parts[0][:, :share]
        k.vec_mean_new[...] = parts[1][:, :share]
        k.vec_square_new[...] = parts[2][:, :share]
        for copy in vars(k.go).values():
            copy.start()
        for copy in vars(k.go).values():
            copy.wait()
    else:
        k.own[rows:] = jnp.broadcast_to(parts[3], (TAIL, width)).astype(BF16)


def adam(summands, state, step, full):
    shape, vec_shape = state.master.shape, state.vec_master.shape
    outs, far = {}, {}
    if full:
        far = dict.fromkeys(("grad", "change", "mean_new", "square_new"), (shape, F32))
        far.update({"vec_" + name: (vec_shape, F32) for name in far})
    else:
        outs = {"own": ((shape[0] + TAIL, shape[1]), BF16)}
    return run_kernel(
        lambda k: adam_kernel(k, full), "adam_outputs" if full else "adam", {},
        {**summands, **vars(state)}, outs, far, {}, 0, 6, work=10**9, smem={"step": step},
    )


def place_blocks(pieces, share, rows_all, before=None):
    arrays = [piece[-1] for piece in pieces]
    width = arrays[0].shape[1]
    extra = [] if before is None else [*before]

    def kernel(*refs):
        ins, (target, tails, sems) = refs[: len(arrays)], refs[-3:]
        me = lax.axis_index("dp")
        owners = [z(me >> 2) * 4 + ((me & 3) ^ (2 * y + core)) for z, y, core, _ in pieces]
        copies = []
        for at, (owner, ref) in enumerate(zip(owners, ins)):
            there = pl.ds(pl.multiple_of(owner * share, share), share)
            copies.append(load(ref.at[:share], target.at[there], sems.at[at]))
        if extra:
            tails[...] = refs[len(arrays) + 1][...]
        for owner, ref in zip(owners, ins):
            tails[owner] = ref[share:]
        for copy in copies:
            copy.wait()

    return pl.pallas_call(
        kernel,
        name="place_blocks",
        in_specs=[VMEM] * len(arrays) + [HBM, VMEM][: len(extra)],
        out_specs=[HBM, VMEM],
        out_shape=[
            pltpu.HBM((rows_all, width), BF16),
            pltpu.VMEM((rows_all // share, TAIL, width), BF16),
        ],
        scratch_shapes=[pltpu.SemaphoreType.DMA((len(arrays),))],
        input_output_aliases={len(arrays): 0} if extra else {},
        compiler_params=pltpu.CompilerParams(vmem_limit_bytes=4 * 2**20),
        cost_estimate=pl.CostEstimate(flops=10**9, bytes_accessed=1, transcendentals=0),
    )(*[pltpu.with_memory_space_constraint(array, pltpu.VMEM) for array in arrays], *extra)


def either(middle, end):
    def kernel(k):
        @pl.when(at_middle())
        def _():
            k.out[...] = k.middle[...]

        @pl.when(jnp.logical_not(at_middle()))
        def _():
            k.out[...] = k.end[...]

    outs = dict(out=(end.shape, BF16))
    return quick_kernel(kernel, "either", dict(middle=middle, end=end), outs).out


def gather_blocks(own, share, rows_all, meanwhile):
    end1, middle1 = swapped(own, "dp", 4), swapped_middle(own)
    end1, from_y0 = lax.optimization_barrier((end1, swapped(own, "dp", 2)))
    end2, middle2 = swapped(middle1, "dp", 4), swapped_middle(end1)
    from_y1 = swapped(end1, "dp", 2)
    end3 = swapped(middle2, "dp", 4)
    second = either(middle1, end2)
    from_y2 = swapped(second, "dp", 2)
    third = either(middle2, end3)
    from_y3 = swapped(third, "dp", 2)

    def both(z, y, array):
        return [(z, y, 0, array), (z, y, 1, swapped(array, "dp", 1))]

    early = both(same, 0, own) + both(same, 1, from_y0) + both(next_to, 0, end1)
    early += both(next_to, 1, from_y1) + both(nearer, 0, second)
    first = place_blocks(early, share, rows_all)
    from_y3 = held_until(from_y3, *first, meanwhile)
    late = both(nearer, 1, from_y2) + both(farther, 0, third) + both(farther, 1, from_y3)
    return place_blocks(late, share, rows_all, first)


def body(
    inputs,
    lengths,
    cotangent,
    matrices,
    vectors,
    master_matrices,
    master_vectors,
    matrix_mean,
    matrix_square,
    vector_mean,
    vector_square,
    adam_step,
):
    row_count, seq_len, width = inputs.shape[1:]
    tokens = row_count * seq_len
    rows_all, vec_all = matrices.shape[1], vectors.shape[1]
    ffn = (rows_all - 6 * width) // 2
    half = rows_all // 2
    ranks = lax.axis_size("dp")
    share, vec_share = rows_all // ranks, vec_all // ranks
    by_swaps = ranks == 16 and share % 32 == 0
    me = lax.axis_index("dp")

    x = inputs.reshape(tokens, width)
    cot = cotangent.reshape(tokens, width)
    mats = matrices.reshape(rows_all, width)
    lens_here = pltpu.SMEM(lengths.shape, jnp.int32)

    def spec(columns, dtype):
        return ((tokens, columns), dtype)

    full, low, deep = spec(width, F32), spec(width, BF16), spec(ffn, BF16)
    square, mask = ((width, width), BF16), spec(seq_len, F32)
    double, w_ffn = ((2 * width, width), BF16), ((ffn, width), BF16)
    lse = ((row_count, HEADS, seq_len), F32)
    norms = dict(normal2=full, rstd2=spec(LANES, F32), normal3=full, rstd3=spec(LANES, F32))
    half_tokens = tokens // 2
    half_low, half_full = ((half_tokens, width), BF16), ((half_tokens, width), F32)
    half_double, half_back = ((half_tokens, 2 * width), BF16), ((half_tokens, width + EARLY_LANES), BF16)
    half_rest = ((half_tokens, 4 * width - EARLY_LANES), BF16)
    all_vecs, triple = ((1, vec_all), F32), spec(3 * width, BF16)
    block = (ranks // 8, share + TAIL, width) if by_swaps else (half // 2, width)

    first_rows = (share + TAIL) // 2 // 16 * 16
    cuts = (slice(0, first_rows), slice(first_rows, share + TAIL))

    def sides(*zs):
        result = {f"keep{z}": (block, BF16) for z in zs}
        if by_swaps:
            for at, cut in enumerate(cuts):
                rows = cut.stop - cut.start
                result.update({f"give{z}{at}": ((block[0], rows, width), BF16) for z in zs})
        return result

    def quarter(kernel, z, at):
        return getattr(kernel, f"keep{z}"), swapped(getattr(kernel, f"give{z}{at}"), "dp", 1)

    early = ((half - 6 * width, width), BF16)

    def wide(rows):
        return ((width // LANES, rows, LANES), F32)

    cross_half = lax.dynamic_slice(mats, ((4 + (me & 1)) * width, 0), (width, width), allow_negative_indices=False)
    cross_mine = swapped(cross_half, "section", 1)
    f = run_kernel(
        forward_kernel, "forward", dict(mats=mats, x=x, vectors=vectors, lengths=lengths), {},
        dict(
            h1=full, w_in=w_ffn, act=deep, slope=deep, **norms,
            memory=half_low, w_cross=double, qc=low, w_out=w_ffn, vecs=all_vecs,
        ),
        dict(
            qkv=triple, lse=lse, mixed=low, normal1=full, rstd1=spec(LANES, F32), mask=mask, w_attn_out=square,
            w_attn=((3 * width, width), BF16), low=low,
        ),
        dict(
            raw_attn=((3 * width, width), BF16), raw_cross=double, raw_ffn=w_ffn,
            x_here=low, total=half_full, wide=wide(ffn), raw_vecs=((1, vec_all), BF16), lens=lens_here,
        ),
        8, 10,
    )
    memory_far0 = swapped(f.memory, "section", 1)
    r = run_kernel(
        forward_rest_kernel, "forward_rest", {},
        dict(
            h1=f.h1, w_in=f.w_in, w_out=f.w_out, vecs=f.vecs, old_act=f.act, old_slope=f.slope,
            **{"old_" + name: getattr(f, name) for name in norms},
        ),
        dict(act=deep, slope=deep, **norms, memory=half_low), dict(low_rest=half_low),
        dict(total=half_full), 0, 6,
        [("old_" + name, name) for name in ("act", "slope", *norms)],
        work=WORK_REST,
    )
    memory_far1 = swapped(r.memory, "section", 1)
    cross_mine = held_until(cross_mine, f.memory)
    cross_other = swapped(cross_mine, "dp", 1)
    p = run_kernel(
        prepare_kernel, "prepare", dict(cot_all=cot, lengths=lengths),
        dict(cross_mine=cross_mine, cross_other=cross_other),
        dict(w_pairs=double, mask=mask, cot=low), {},
        dict(raw=double, wide=wide(2 * width), raw_cot=low, lens=lens_here),
        2, 4,
    )
    shared = dict(
        **vars(p), w_cross=f.w_cross, qc=f.qc, h1=f.h1, w_in=f.w_in, w_out=f.w_out, vecs=f.vecs,
    )
    for_tokens = dict(act=deep, side=deep, grad_ffn=low, low2=low, grad_sum2=full)
    far_half = dict(mixed=half_low, right=half_double)
    held = dict(
        pairs=half_double, slope=((half_tokens, ffn), F32), lse=((row_count // 2, HEADS, seq_len), F32),
        grad_mixed=half_low, total=half_full, normal2=half_full, rstd2=((half_tokens, LANES), F32),
    )
    d = run_kernel(
        lambda k: decoder_kernel(k, 0), "decoder", {},
        dict(memory=memory_far0, near_memory=f.memory, **shared, enc_act=r.act, enc_slope=r.slope),
        dict(
            back=half_back, grad_pairs=half_double, vec_grads=all_vecs, **for_tokens, top=half_low,
        ),
        far_half, held,
        0, SPARE_D, (("enc_act", "act"), ("enc_slope", "side")), work=WORK_D,
    )
    back_far = swapped(d.back, "section", 1)
    before = {"old_" + name: getattr(d, name) for name in for_tokens}
    e = run_kernel(
        lambda k: decoder_kernel(k, 1), "decoder_rest", {},
        dict(
            memory=memory_far1, near_memory=r.memory, **shared, **before, vec_before=d.vec_grads,
            top_before=d.top, pairs_before=d.grad_pairs,
        ),
        dict(grad_memory=half_low, rest=half_rest, vec_grads=all_vecs, **for_tokens),
        dict(layer_out=low, **far_half), held,
        0, SPARE_D, [("old_" + name, name) for name in for_tokens], work=WORK_D,
    )
    grad_memory_far = swapped(e.grad_memory, "section", 1)
    rest_far = swapped(e.rest, "section", 1)
    ahead = dict(
        normal1=full, rstd1=spec(LANES, F32), w_attn_out=square, mask=mask, lse=lse, qkv=triple,
        w_attn=((3 * width, width), BF16),
    )
    s = run_kernel(
        backward_kernel, "backward",
        dict(
            **{"far_" + name: getattr(f, name) for name in ahead},
            far_x=x, far_mixed=f.mixed, far_low=f.low, far_low_rest=r.low_rest,
            far_right0=d.right, far_right1=e.right, far_cross_mixed0=d.mixed, far_cross_mixed1=e.mixed,
        ),
        dict(
            dec_grad_ffn=e.grad_ffn, dec_vec_grads=e.vec_grads,
            back=back_far, grad_memory=grad_memory_far, act=e.act, side=e.side,
            low2=e.low2, grad_sum2=e.grad_sum2, **{name: getattr(r, name) for name in norms}, h1=f.h1, w_in=f.w_in, w_out=f.w_out, vecs=f.vecs,
        ),
        dict(
            vec_grads=all_vecs, early=early, **sides(2, 3), grad_attn=low, grad_qkv=triple,
            x=low, mixed=low, low=low, right=spec(2 * width, BF16), cross_mixed=low,
        ),
        dict(grad_x=full),
        dict(
            grad_pre=deep, grad_ffn=low, low1=low, wide=wide(ffn), grad_h1=full,
            flat=((2 * ffn, width), BF16), grad_mixed=low, **ahead,
        ),
        15, 9, work=4 * 10**10,
    )
    quarter_flat = ((half // 2, width), BF16)
    a = run_kernel(
        attn_grad_kernel, "attn_grad", {},
        dict(
            grad_qkv=s.grad_qkv, vec_grads=s.vec_grads, x=s.x, grad_attn=s.grad_attn, mixed=s.mixed,
        ),
        dict(left=((4 * width - half // 2, width), BF16), **sides(0)), {},
        dict(wide=wide(3 * width), flat=quarter_flat), 0, 4, work=10**8,
    )
    if by_swaps:
        ends = [(quarter(a, 0, at), quarter(s, 3, at)) for at in range(2)]
        farthest = [
            sum_of_cores(cut, (first, None, None, third), (farther,))
            for cut, (first, third) in zip(cuts, ends)
        ]
        left = held_until(a.left, farthest[0].give0)
    else:
        left = a.left
    b = run_kernel(
        cross_grad_kernel, "cross_grad", {},
        dict(
            left=left, vec_grads=s.vec_grads, early=s.early, back=back_far, rest=rest_far, low=s.low,
            right=s.right, cross_mixed=s.cross_mixed,
        ),
        sides(1), {}, dict(wide=wide(2 * width), flat=quarter_flat), 0, 4, work=10**8,
    )

    state = Refs(master=master_matrices[0], mean=matrix_mean[0], square=matrix_square[0])
    state = Refs(**vars(state), vec_master=master_vectors, vec_mean=vector_mean, vec_square=vector_square)
    if by_swaps:
        summands = {}
        for at, cut in enumerate(cuts):
            first, third = ends[at]
            quarters = (first, quarter(b, 1, at), quarter(s, 2, at), third)
            parts = sum_over_dp(cut, quarters, farthest[at])
            summands.update({f"{name}{at}": part for name, part in parts.items()})
        own = adam(summands, state, adam_step, False).own
        result = adam(summands, state, adam_step, True)
        new_mat, tails = gather_blocks(own, share, rows_all, result.change)
        new_vec = tails[:, 0, :vec_share].reshape(1, vec_all)
    else:
        whole = jnp.concatenate([a.keep0, b.keep1, s.keep2, s.keep3], axis=0)
        grad = lax.psum_scatter(whole, "dp", scatter_dimension=0, tiled=True).astype(F32)
        vec_grad = lax.dynamic_slice(
            lax.psum(s.vec_grads, "dp"), (0, me * vec_share), (1, vec_share)
        )
        step = jnp.full((1, width), adam_step[0].astype(F32))
        parts = adam_of(grad, state.master, state.mean, state.square, step)
        vec_step = jnp.full((1, width), adam_step[0].astype(F32))
        pad = ((0, 0), (0, width - vec_share))
        vec_parts = [
            part[:, :vec_share]
            for part in adam_of(
                *[jnp.pad(v, pad) for v in (vec_grad, master_vectors, vector_mean, vector_square)],
                vec_step,
            )
        ]
        names = ("change", "mean_new", "square_new")
        result = dict(grad=grad, vec_grad=vec_grad, **dict(zip(names, parts)))
        result.update({"vec_" + name: part for name, part in zip(names, vec_parts)})
        result = Refs(**result)
        new_mat = lax.all_gather(parts[3].astype(BF16), "dp", axis=0, tiled=True)
        new_vec = lax.all_gather(vec_parts[3].astype(BF16), "dp", axis=1, tiled=True)
    return (
        e.layer_out.reshape(1, row_count, seq_len, width),
        s.grad_x.reshape(1, row_count, seq_len, width),
        result.grad[None],
        result.vec_grad,
        result.change[None],
        result.vec_change,
        result.mean_new[None],
        result.square_new[None],
        result.vec_mean_new,
        result.vec_square_new,
        new_mat[None],
        new_vec,
    )


def solution(mesh):
    return jax.shard_map(
        body,
        mesh=mesh,
        in_specs=(
            P("section", "dp", None, None),
            P(None, "dp", None),
            P("dp", None, None),
            P("section", None, None),
            P("section", None),
            P("section", "dp", None),
            P("section", "dp"),
            P("section", "dp", None),
            P("section", "dp", None),
            P("section", "dp"),
            P("section", "dp"),
            P(),
        ),
        out_specs=(
            P("section", "dp", None, None),
            P("section", "dp", None, None),
            P("section", "dp", None),
            P("section", "dp"),
            P("section", "dp", None),
            P("section", "dp"),
            P("section", "dp", None),
            P("section", "dp", None),
            P("section", "dp"),
            P("section", "dp"),
            P("section", None, None),
            P("section", None),
        ),
        check_vma=False,
    )
```

```python
import math
import types

import jax
import jax.numpy as jnp
from jax import lax
from jax.experimental import pallas as pl
from jax.experimental.pallas import tpu as pltpu
from jax.sharding import PartitionSpec as P

HEADS = 8
HEAD_DIM = 64
PAIR = 2 * HEAD_DIM
LANES = 128
TAIL = 16
EARLY_LANES = 384
SUMMANDS = ("mine", "from_y", "from_end", "from_middle")
UNROLL_CHUNKS = True
WORK_REST = 10**10
WORK_D = 4 * 10**10
SPARE_D = 8

MASK_FILL = -1e30
NORM_EPS = 1e-05
ADAM_EPS = 1e-09
WARMUP_STEPS = 4000.0

F32 = jnp.float32
BF16 = jnp.bfloat16

BIAS_OUT, GAIN1, SHIFT1, GAIN2, SHIFT2, GAIN3, SHIFT3 = range(-7, 0)


def dot(left, right):
    return jnp.dot(left, right, preferred_element_type=F32)


def dot_nt(left, right):
    return lax.dot_general(left, right, (((1,), (1,)), ((), ())), preferred_element_type=F32)


def dot_tn(left, right):
    return lax.dot_general(left, right, (((0,), (0,)), ((), ())), preferred_element_type=F32)


def norm_parts(hidden):
    centre = hidden - jnp.mean(hidden, axis=-1, keepdims=True)
    rstd = lax.rsqrt(jnp.mean(centre * centre, axis=-1, keepdims=True) + NORM_EPS)
    return centre * rstd, rstd


def norm_backward(normal, rstd, gain, grad):
    scaled = grad * gain
    inner = jnp.mean(scaled * normal, axis=-1, keepdims=True)
    grad_in = rstd * (scaled - jnp.mean(scaled, axis=-1, keepdims=True) - normal * inner)
    grad_gain = jnp.sum(grad * normal, axis=0, keepdims=True)
    grad_shift = jnp.sum(grad, axis=0, keepdims=True)
    return grad_in, grad_gain, grad_shift


def act_parts(pre):
    cdf = 0.5 * (1.0 + lax.erf(pre * (0.5**0.5)))
    pdf = jnp.exp(-0.5 * pre * pre) * 0.3989422804014327
    return pre * cdf, cdf + pre * pdf


def split_rows(raw, wide, parts, out, base):
    width = raw.shape[1]
    for c in range(width // LANES):
        cut = slice(c * LANES, (c + 1) * LANES)
        wide[c, : parts * width] = raw[: parts * width, cut].astype(F32)
        for j in range(parts):
            out[(base + j) * width : (base + j + 1) * width, cut] = wide[
                c, pl.ds(j, width, stride=parts), :
            ].astype(BF16)


def put_part(wide, j, parts, values):
    rows, width = values.shape
    for c in range(width // LANES):
        wide[c, pl.ds(j, rows, stride=parts), :] = values[:, c * LANES : (c + 1) * LANES]


def take_parts(wide, rows, out, first):
    for c in range(wide.shape[0]):
        out[first : first + rows, c * LANES : (c + 1) * LANES] = wide[c, :rows].astype(BF16)


def sentence_ends(lens, side, row):
    ends, total = [], 0
    for j in range(lens.shape[2]):
        total = total + lens[side, row, j]
        ends.append(total)
    return ends


def sentence_of(ends, position):
    found = jnp.zeros(position.shape, jnp.int32)
    for end in ends:
        found = found + (position >= end).astype(jnp.int32)
    return found


def fill_mask(mask, lens, query_side, key_side, causal):
    seq_len = mask.shape[1]
    row_count, sents = lens.shape[1:]
    q_pos = lax.broadcasted_iota(jnp.int32, (seq_len, seq_len), 1)
    k_pos = lax.broadcasted_iota(jnp.int32, (seq_len, seq_len), 0)
    for r in range(row_count):
        q_ids = sentence_of(sentence_ends(lens, query_side, r), q_pos)
        k_ids = sentence_of(sentence_ends(lens, key_side, r), k_pos)
        same = jnp.where(q_ids == k_ids, 1, 0)
        if causal is not None:
            same = jnp.where(q_pos >= k_pos, same, jnp.where(causal, 0, same))
        allowed = jnp.where(q_ids == sents, 1, same)
        mask[r * seq_len : (r + 1) * seq_len] = allowed.astype(F32)


def both_heads(block, lane):
    even = (lane < HEAD_DIM).astype(BF16)
    return jnp.concatenate([block * even, block * (1 - even)], axis=0)


def both_heads_across(block):
    turned = block.T
    even = (lax.broadcasted_iota(jnp.int32, (PAIR, 1), 0) < HEAD_DIM).astype(BF16)
    return jnp.concatenate([turned * even, turned * (1 - even)], axis=1)


def one_of(stacked, lane):
    keys = stacked.shape[0] // 2
    return jnp.where(lane < HEAD_DIM, stacked[:keys], stacked[keys:])


def for_rows(mask, step):
    seq_len = mask.shape[1]

    def turn(row, carried):
        step(row, pl.ds(pl.multiple_of(row * seq_len, seq_len), seq_len), range(HEADS // 2))
        return carried

    lax.fori_loop(0, mask.shape[0] // seq_len, turn, 0)


def pair_lanes(first, p):
    return slice(first + p * PAIR, first + (p + 1) * PAIR)


def attend_forward(query, keys, values, mask, out, lse):
    seq_len = mask.shape[1]
    lane = lax.broadcasted_iota(jnp.int32, (1, PAIR), 1)
    (q_ref, q_at), (k_ref, k_at), (v_ref, v_at) = query, keys, values

    def step(row, rows, pairs):
        scores = [
            dot_nt(both_heads(k_ref[rows, pair_lanes(k_at, p)], lane), q_ref[rows, pair_lanes(q_at, p)])
            for p in pairs
        ]
        mixed = []
        for p in pairs:
            probs = []
            for half in range(2):
                part = scores[p][half * seq_len : (half + 1) * seq_len] * HEAD_DIM ** (-0.5)
                part = jnp.where(mask[rows] > 0.0, part, MASK_FILL)
                top = jnp.max(part, axis=0, keepdims=True)
                raised = jnp.exp(part - top)
                total = jnp.sum(raised, axis=0, keepdims=True)
                probs.append((raised * (1.0 / total)).astype(BF16))
                lse[row, 2 * p + half : 2 * p + half + 1] = top + jnp.log(total)
            values = both_heads_across(v_ref[rows, pair_lanes(v_at, p)])
            mixed.append(dot(values, jnp.concatenate(probs, axis=0)))
        for p in pairs:
            out[rows, pair_lanes(0, p)] = mixed[p].T.astype(BF16)

    for_rows(mask, step)


def attend_backward(query, keys, values, mask, lse, grad_out, grad_q, grad_k, grad_v):
    seq_len = mask.shape[1]
    lane = lax.broadcasted_iota(jnp.int32, (1, PAIR), 1)
    scale = HEAD_DIM ** (-0.5)
    (q_ref, q_at), (k_ref, k_at), (v_ref, v_at) = query, keys, values
    (gq_ref, gq_at), (gk_ref, gk_at), (gv_ref, gv_at) = grad_q, grad_k, grad_v

    def step(row, rows, pairs):
        qs = [q_ref[rows, pair_lanes(q_at, p)] for p in pairs]
        ks = [k_ref[rows, pair_lanes(k_at, p)] for p in pairs]
        gos = [grad_out[rows, pair_lanes(0, p)] for p in pairs]
        scores = [dot_nt(both_heads(ks[p], lane), qs[p]) for p in pairs]
        grad_probs = [
            dot_nt(both_heads(v_ref[rows, pair_lanes(v_at, p)], lane), gos[p]) for p in pairs
        ]
        probs, grad_scores = [], []
        for p in pairs:
            prob_parts, score_parts = [], []
            for half in range(2):
                cut = slice(half * seq_len, (half + 1) * seq_len)
                part = jnp.where(mask[rows] > 0.0, scores[p][cut] * scale, MASK_FILL)
                prob = jnp.exp(part - lse[row, 2 * p + half : 2 * p + half + 1])
                gp = grad_probs[p][cut]
                inner = jnp.sum(prob * gp, axis=0, keepdims=True)
                prob_parts.append(prob.astype(BF16))
                score_parts.append((prob * (gp - inner)).astype(BF16))
            probs.append(jnp.concatenate(prob_parts, axis=0))
            grad_scores.append(jnp.concatenate(score_parts, axis=0))
        grad_vs = [dot(probs[p], gos[p]) for p in pairs]
        grad_ks = [dot(grad_scores[p], qs[p]) for p in pairs]
        grad_qs = [dot(both_heads_across(ks[p]), grad_scores[p]) for p in pairs]
        for p in pairs:
            gv_ref[rows, pair_lanes(gv_at, p)] = one_of(grad_vs[p], lane).astype(BF16)
            gk_ref[rows, pair_lanes(gk_at, p)] = (one_of(grad_ks[p], lane) * scale).astype(BF16)
            gq_ref[rows, pair_lanes(gq_at, p)] = (grad_qs[p].T * scale).astype(BF16)

    for_rows(mask, step)


def small(vecs, which, width):
    pieces = vecs.shape[1] // width
    at = (which if which >= 0 else pieces + which) * width
    return vecs[:, at : at + width].astype(F32)


def set_small(vecs, which, width, value):
    pieces = vecs.shape[1] // width
    at = (which if which >= 0 else pieces + which) * width
    vecs[:, at : at + width] = value


def where_am_i():
    return lax.axis_index("section"), lax.rem(lax.axis_index("dp"), 2)


def for_chunks(count, width, step):
    def turn(j, carried):
        step(j, pl.ds(pl.multiple_of(j * width, width), width))
        return carried

    lax.fori_loop(0, count, turn, 0, unroll=UNROLL_CHUNKS)


def ffn_forward(normed, w_in, w_out, vecs, act, slope, total):
    width = normed.shape[1]
    low = normed.astype(BF16)
    total[...] = normed + small(vecs, BIAS_OUT, width)

    def step(j, cut):
        pre = dot(low, w_in[cut]) + vecs[:, cut]
        value, derivative = act_parts(pre)
        value = value.astype(BF16)
        act[:, cut] = value
        slope[:, cut] = derivative.astype(slope.dtype)
        total[...] += dot(value, w_out[cut])

    for_chunks(w_in.shape[0] // width, width, step)


def ffn_backward(grad_low, w_in, w_out, slope, grad_pre, vec_grads, total):
    width = grad_low.shape[1]

    def step(j, cut):
        grad = (dot_nt(grad_low, w_out[cut]) * slope[:, cut].astype(F32)).astype(BF16)
        grad_pre[:, cut] = grad
        vec_grads[:, cut] = jnp.sum(grad.astype(F32), axis=0, keepdims=True)
        total[...] += dot_nt(grad, w_in[cut])

    for_chunks(w_in.shape[0] // width, width, step)


def load(source, target, sem):
    copy = pltpu.make_async_copy(source, target, sem)
    copy.start()
    return copy


def memory_of(k, rows):
    width = k.h1.shape[1]
    vecs = k.vecs
    ffn_forward(k.h1[rows], k.w_in, k.w_out, vecs, k.act.at[rows], k.slope.at[rows], k.total)
    normal, rstd = norm_parts(k.total[...])
    k.normal2[rows], k.rstd2[rows] = normal, jnp.broadcast_to(rstd, (rstd.shape[0], LANES))
    normal, rstd = norm_parts(normal * small(vecs, GAIN2, width) + small(vecs, SHIFT2, width))
    k.normal3[rows], k.rstd3[rows] = normal, jnp.broadcast_to(rstd, (rstd.shape[0], LANES))
    third = normal * small(vecs, GAIN3, width) + small(vecs, SHIFT3, width)
    k.memory[...] = third.astype(BF16)


def forward_kernel(k):
    width = k.h1.shape[1]
    ffn = k.w_in.shape[0]
    sec, _ = where_am_i()
    get_lens = load(k.lengths, k.lens, k.sems.at[7])
    get_in = load(k.mats.at[: 3 * width], k.raw_attn, k.sems.at[0])
    get_x = load(k.x, k.x_here, k.sems.at[1])
    get_vecs = load(k.vectors, k.raw_vecs, k.sems.at[2])
    get_attn_out = load(k.mats.at[3 * width : 4 * width], k.w_attn_out, k.sems.at[3])
    get_ffn = load(k.mats.at[6 * width : 6 * width + ffn], k.raw_ffn, k.sems.at[4])
    get_out = load(k.mats.at[6 * width + ffn :], k.w_out, k.sems.at[5])
    get_cross = pltpu.make_async_copy(k.mats.at[4 * width : 6 * width], k.raw_cross, k.sems.at[6])

    @pl.when(sec == 1)
    def _():
        get_cross.start()

    get_lens.wait()
    fill_mask(k.mask, k.lens, sec, sec, sec == 1)
    k.go.mask.start()
    get_in.wait()
    split_rows(k.raw_attn, k.wide, 3, k.w_attn, 0)
    k.go.w_attn.start()
    get_x.wait()
    for j in range(3):
        part = dot(k.x_here[...], k.w_attn[j * width : (j + 1) * width])
        k.qkv[:, j * width : (j + 1) * width] = part.astype(BF16)
    k.go.qkv.start()
    attend_forward((k.qkv, 0), (k.qkv, width), (k.qkv, 2 * width), k.mask, k.mixed, k.lse)
    k.go.mixed.start()
    k.go.lse.start()
    get_vecs.wait()
    k.vecs[...] = k.raw_vecs[...].astype(F32)
    vecs = k.vecs
    get_attn_out.wait()
    k.go.w_attn_out.start()
    hidden = k.x_here[...].astype(F32) + dot(k.mixed[...], k.w_attn_out[...])
    normal, rstd = norm_parts(hidden)
    k.normal1[...], k.rstd1[...] = normal, jnp.broadcast_to(rstd, (rstd.shape[0], LANES))
    k.go.normal1.start()
    k.go.rstd1.start()
    k.h1[...] = normal * small(vecs, GAIN1, width) + small(vecs, SHIFT1, width)
    get_ffn.wait()
    split_rows(k.raw_ffn, k.wide, ffn // width, k.w_in, 0)
    get_out.wait()

    @pl.when(sec == 0)
    def _():
        memory_of(k, slice(0, k.memory.shape[0]))
        k.low[: k.memory.shape[0]] = k.memory[...]
        k.go.low.start()

    @pl.when(sec == 1)
    def _():
        k.low[...] = k.h1[...].astype(BF16)
        k.go.low.start()
        get_cross.wait()
        split_rows(k.raw_cross, k.wide, 2, k.w_cross, 0)
        k.qc[...] = dot(k.low[...], k.w_cross[:width]).astype(BF16)

    k.go.mask.wait()
    k.go.w_attn.wait()
    k.go.qkv.wait()
    k.go.mixed.wait()
    k.go.lse.wait()
    k.go.w_attn_out.wait()
    k.go.normal1.wait()
    k.go.rstd1.wait()
    k.go.low.wait()


def forward_rest_kernel(k):
    sec, _ = where_am_i()

    @pl.when(sec == 0)
    def _():
        half = k.memory.shape[0]
        memory_of(k, slice(half, 2 * half))
        k.low_rest[...] = k.memory[...]
        k.go.low_rest.start()
        k.go.low_rest.wait()


def prepare_kernel(k):
    width = k.raw.shape[1]
    seq_len = k.mask.shape[1]
    sec, core = where_am_i()

    @pl.when(sec == 1)
    def _():
        get_cot = load(k.cot_all, k.raw_cot, k.sems.at[0])
        get_lens = load(k.lengths, k.lens, k.sems.at[1])
        k.raw[pl.ds(pl.multiple_of(core * width, width), width)] = k.cross_mine[...]
        k.raw[pl.ds(pl.multiple_of((1 - core) * width, width), width)] = k.cross_other[...]
        split_rows(k.raw, k.wide, 2, k.w_pairs, 0)
        get_lens.wait()
        fill_mask(k.mask, k.lens, 1, 0, None)
        get_cot.wait()
        position = lax.broadcasted_iota(jnp.int32, (seq_len, 1), 0)
        for r in range(k.lens.shape[1]):
            used = sentence_ends(k.lens, 1, r)[-1]
            rows = slice(r * seq_len, (r + 1) * seq_len)
            k.cot[rows] = jnp.where(position < used, k.raw_cot[rows].astype(F32), 0.0).astype(BF16)


def decoder_kernel(k, part):
    half, width = k.memory.shape
    rows = slice(part * half, (part + 1) * half)
    vecs = k.vecs
    sec, _ = where_am_i()
    top = k.layer_out.at[rows] if part == 1 else k.top
    pairs_at = 0 if part == 0 else 2 * width - EARLY_LANES
    grad_pairs = k.grad_pairs if part == 0 else k.rest
    grad_keys, grad_values = (grad_pairs, pairs_at), (grad_pairs, pairs_at + width)
    if part == 1:
        k.layer_out[:half] = k.top_before[...]

    @pl.when(sec == 0)
    def _():
        top[...] = k.near_memory[...]

    @pl.when(sec == 1)
    def _():
        mask, qc, act, side = k.mask.at[rows], k.qc.at[rows], k.act.at[rows], k.side.at[rows]
        for j in range(2):
            pair = dot(k.memory[...], k.w_pairs[j * width : (j + 1) * width])
            k.pairs[:, j * width : (j + 1) * width] = pair.astype(BF16)
        attend_forward((qc, 0), (k.pairs, 0), (k.pairs, width), mask, k.mixed, k.lse)
        k.go.mixed.start()
        hidden2 = k.h1[rows] + dot(k.mixed[...], k.w_cross[width:])
        gain2, shift2 = small(vecs, GAIN2, width), small(vecs, SHIFT2, width)
        normal2, rstd2 = norm_parts(hidden2)
        k.normal2[...], k.rstd2[...] = normal2, jnp.broadcast_to(rstd2, (half, LANES))
        normed2 = normal2 * gain2 + shift2
        k.low2[rows] = normed2.astype(BF16)
        ffn_forward(normed2, k.w_in, k.w_out, vecs, act, k.slope, k.total)
        normal3, rstd3 = norm_parts(k.total[...])
        gain3, shift3 = small(vecs, GAIN3, width), small(vecs, SHIFT3, width)
        top[...] = (normal3 * gain3 + shift3).astype(BF16)
        grad_sum3, d_gain, d_shift = norm_backward(
            normal3, rstd3, gain3, k.cot[rows].astype(F32)
        )
        set_small(k.vec_grads, GAIN3, width, d_gain)
        set_small(k.vec_grads, SHIFT3, width, d_shift)
        grad_low = grad_sum3.astype(BF16)
        k.grad_ffn[rows] = grad_low
        set_small(
            k.vec_grads, BIAS_OUT, width, jnp.sum(grad_low.astype(F32), axis=0, keepdims=True)
        )
        k.total[...] = grad_sum3
        ffn_backward(grad_low, k.w_in, k.w_out, k.slope, side, k.vec_grads, k.total)
        grad_hidden2, d_gain, d_shift = norm_backward(
            k.normal2[...], k.rstd2[:, :1], gain2, k.total[...]
        )
        set_small(k.vec_grads, GAIN2, width, d_gain)
        set_small(k.vec_grads, SHIFT2, width, d_shift)
        k.grad_sum2[rows] = grad_hidden2
        low = grad_hidden2.astype(BF16)
        k.right[:, width:] = low
        k.grad_mixed[...] = dot_nt(low, k.w_cross[width:]).astype(BF16)
        attend_backward(
            (qc, 0), (k.pairs, 0), (k.pairs, width), mask, k.lse, k.grad_mixed,
            (k.right, 0), grad_keys, grad_values,
        )
        k.go.right.start()
        k.grad_sum2[rows] += dot_nt(k.right[:, :width], k.w_cross[:width])
        back = jnp.zeros((half, width), F32)
        for j, (ref, at) in enumerate((grad_keys, grad_values)):
            back = back + dot_nt(ref[:, at : at + width], k.w_pairs[j * width : (j + 1) * width])
        if part == 0:
            k.back[:, :width] = back.astype(BF16)
            k.back[:, width:] = k.grad_pairs[:, :EARLY_LANES]
        else:
            k.grad_memory[...] = back.astype(BF16)
            k.rest[:, :pairs_at] = k.pairs_before[:, EARLY_LANES:]
        if part == 1:
            k.vec_grads[...] += k.vec_before[...]
        k.go.mixed.wait()
        k.go.right.wait()

    if part == 1:
        k.go.layer_out.start()
        k.go.layer_out.wait()


def ffn_weight_grads(k, act, low, grad_pre, grad_ffn):
    width = k.h1.shape[1]
    ffn = k.w_in.shape[0]
    chunks = ffn // width

    def step(j, cut):
        put_part(k.wide, j, chunks, dot_tn(low[...], grad_pre[:, cut]))
        there = pl.ds(pl.multiple_of(ffn + j * width, width), width)
        k.flat[there] = dot_tn(act[:, cut], grad_ffn[...]).astype(BF16)

    for_chunks(chunks, width, step)


def put_sides(k, first, z, vec_grads, core):
    width = k.flat.shape[1]
    keep = getattr(k, f"keep{z}")
    if len(keep.shape) == 2:
        keep[...] = k.flat[first : first + keep.shape[0]]
        return
    gives = [getattr(k, f"give{z}{at}") for at in range(2)]
    count, rows, _ = keep.shape
    rows -= TAIL
    split = gives[0].shape[1]
    share = vec_grads.shape[1] // (8 * count)

    def tail(at):
        owner = 2 * count * z + at
        row = vec_grads[:, owner * share : (owner + 1) * share]
        row = jnp.concatenate([row, jnp.zeros((1, width - share), F32)], axis=1)
        return jnp.broadcast_to(row, (TAIL, width)).astype(BF16)

    for at in range(count):
        mine = first + (2 * at + core) * rows
        other = first + (2 * at + 1 - core) * rows
        keep[at, :rows] = k.flat[pl.ds(pl.multiple_of(mine, TAIL), rows)]
        gives[0][at] = k.flat[pl.ds(pl.multiple_of(other, TAIL), split)]
        gives[1][at, : rows - split] = k.flat[pl.ds(pl.multiple_of(other + split, TAIL), rows - split)]

        @pl.when(core == 0)
        def _(at=at):
            keep[at, rows:] = tail(2 * at)
            gives[1][at, rows - split :] = tail(2 * at + 1)

        @pl.when(core == 1)
        def _(at=at):
            keep[at, rows:] = tail(2 * at + 1)
            gives[1][at, rows - split :] = tail(2 * at)


def backward_kernel(k):
    width = k.h1.shape[1]
    ffn = k.w_in.shape[0]
    vecs = k.vecs
    sec, core = where_am_i()
    half = k.back.shape[0]
    first, rest = slice(0, half), slice(half, 2 * half)
    wanted = ("normal1", "rstd1", "w_attn_out", "mask", "lse", "qkv", "w_attn", "x", "mixed")
    arriving = [(getattr(k, "far_" + name), getattr(k, name)) for name in wanted]
    arriving += [
        (k.far_low.at[first], k.low.at[first]),
        (k.far_right0, k.right.at[first]),
        (k.far_right1, k.right.at[rest]),
        (k.far_cross_mixed0, k.cross_mixed.at[first]),
        (k.far_cross_mixed1, k.cross_mixed.at[rest]),
    ]
    coming = [load(*ends, k.sems.at[at]) for at, ends in enumerate(arriving)]
    last_sem = k.sems.at[len(coming)]

    @pl.when(sec == 0)
    def _():
        load(k.far_low_rest, k.low.at[rest], last_sem)

    @pl.when(sec == 1)
    def _():
        load(k.far_low.at[rest], k.low.at[rest], last_sem)

    coming.append(pltpu.make_async_copy(k.far_low_rest, k.low.at[rest], last_sem))

    @pl.when(sec == 0)
    def _():
        grad_memory = jnp.concatenate([k.back[:, :width], k.grad_memory[...]], axis=0)
        grad, d_gain, d_shift = norm_backward(
            k.normal3[...], k.rstd3[:, :1], small(vecs, GAIN3, width), grad_memory.astype(F32)
        )
        set_small(k.vec_grads, GAIN3, width, d_gain)
        set_small(k.vec_grads, SHIFT3, width, d_shift)
        total, d_gain, d_shift = norm_backward(
            k.normal2[...], k.rstd2[:, :1], small(vecs, GAIN2, width), grad
        )
        set_small(k.vec_grads, GAIN2, width, d_gain)
        set_small(k.vec_grads, SHIFT2, width, d_shift)
        grad_low = total.astype(BF16)
        k.grad_ffn[...] = grad_low
        set_small(
            k.vec_grads, BIAS_OUT, width, jnp.sum(grad_low.astype(F32), axis=0, keepdims=True)
        )
        k.low1[...] = k.h1[...].astype(BF16)
        k.grad_h1[...] = total
        ffn_backward(grad_low, k.w_in, k.w_out, k.side, k.grad_pre, k.vec_grads, k.grad_h1)
        ffn_weight_grads(k, k.act, k.low1, k.grad_pre, k.grad_ffn)

    @pl.when(sec == 1)
    def _():
        k.vec_grads[...] = k.dec_vec_grads[...]
        k.grad_h1[...] = k.grad_sum2[...]
        ffn_weight_grads(k, k.act, k.low2, k.side, k.dec_grad_ffn)

    take_parts(k.wide, ffn, k.flat, 0)
    early = k.early.shape[0]
    k.early[...] = k.flat[:early]
    for copy in coming:
        copy.wait()
    grad, d_gain, d_shift = norm_backward(
        k.normal1[...], k.rstd1[:, :1], small(vecs, GAIN1, width), k.grad_h1[...]
    )
    set_small(k.vec_grads, GAIN1, width, d_gain)
    set_small(k.vec_grads, SHIFT1, width, d_shift)
    put_sides(k, early, 2, k.vec_grads, core)
    put_sides(k, (k.flat.shape[0] + early) // 2, 3, k.vec_grads, core)
    low = grad.astype(BF16)
    k.grad_attn[...] = low
    k.grad_mixed[...] = dot_nt(low, k.w_attn_out[...]).astype(BF16)
    attend_backward(
        (k.qkv, 0), (k.qkv, width), (k.qkv, 2 * width), k.mask, k.lse, k.grad_mixed,
        (k.grad_qkv, 0), (k.grad_qkv, width), (k.grad_qkv, 2 * width),
    )
    for j in range(3):
        cut = slice(j * width, (j + 1) * width)
        grad = grad + dot_nt(k.grad_qkv[:, cut], k.w_attn[cut])
    k.grad_x[...] = grad
    k.go.grad_x.start()
    k.go.grad_x.wait()


def attn_grad_kernel(k):
    width = k.x.shape[1]
    quarter = k.flat.shape[0]
    _, core = where_am_i()

    def step(j, cut):
        put_part(k.wide, j, 3, dot_tn(k.x[...], k.grad_qkv[:, cut]))

    for_chunks(3, width, step)
    take_parts(k.wide, 3 * width, k.flat, 0)
    grad = dot_tn(k.mixed[...], k.grad_attn[...]).astype(BF16)
    k.flat[3 * width :] = grad[: quarter - 3 * width]
    k.left[...] = grad[quarter - 3 * width :]
    put_sides(k, 0, 0, k.vec_grads, core)


def cross_grad_kernel(k):
    half = k.rest.shape[0]
    first, width = k.left.shape
    sec, core = where_am_i()
    k.flat[:first] = k.left[...]
    k.flat[first + 2 * width :] = k.early[...]

    @pl.when(sec == 0)
    def _():
        rest = k.rest[...]
        at = width - EARLY_LANES
        keys0 = jnp.concatenate([k.back[:, width:], rest[:, :at]], axis=1)
        before = (keys0, rest[:, at : at + width])
        at += width
        after = (rest[:, at : at + width], rest[:, at + width :])
        for j in range(2):
            grad = dot_tn(k.low[:half], before[j]) + dot_tn(k.low[half:], after[j])
            put_part(k.wide, j, 2, grad)

    @pl.when(sec == 1)
    def _():
        put_part(k.wide, 0, 2, dot_tn(k.low[...], k.right[:, :width]))
        put_part(k.wide, 1, 2, dot_tn(k.cross_mixed[...], k.right[:, width:]))

    take_parts(k.wide, 2 * width, k.flat, first)
    put_sides(k, 0, 1, k.vec_grads, core)


class Refs(types.SimpleNamespace):
    pass


def run_kernel(kernel, name, hbm, vmem, outs, far_outs, scratch, loads, spare, reuse=(), work=10**10, smem=None):
    smem = smem or {}
    ins = {**smem, **hbm, **vmem}
    near = {n: pltpu.VMEM(*spec) for n, spec in far_outs.items()}
    near.update({n: pltpu.VMEM(*spec) if isinstance(spec, tuple) else spec for n, spec in scratch.items()})
    names = [*ins, *outs, *far_outs, *near, "sems", "leave_sems"]

    def run(*refs):
        k = Refs(**dict(zip(names, refs)))
        first = len(ins) + len(outs)
        k.go = Refs()
        for at, n in enumerate(far_outs):
            copy = pltpu.make_async_copy(getattr(k, n), refs[first + at], k.leave_sems.at[at])
            setattr(k.go, n, copy)
        kernel(k)

    results = pl.pallas_call(
        run,
        name=name,
        in_specs=[SMEM] * len(smem) + [HBM] * len(hbm) + [VMEM] * len(vmem),
        out_specs=[VMEM] * len(outs) + [HBM] * len(far_outs),
        out_shape=[pltpu.VMEM(*spec) for spec in outs.values()]
        + [pltpu.HBM(*spec) for spec in far_outs.values()],
        scratch_shapes=[
            *near.values(),
            pltpu.SemaphoreType.DMA((max(loads, 1),)),
            pltpu.SemaphoreType.DMA((max(len(far_outs), 1),)),
        ],
        compiler_params=pltpu.CompilerParams(
            vmem_limit_bytes=int(spare * 2**20)
            + sum(math.prod(b.shape) * jnp.dtype(b.dtype).itemsize for b in near.values())
        ),
        input_output_aliases={[*ins].index(old): [*outs].index(new) for old, new in reuse},
        cost_estimate=pl.CostEstimate(flops=work, bytes_accessed=1, transcendentals=0),
    )(
        *smem.values(),
        *[pltpu.with_memory_space_constraint(array, pltpu.HBM) for array in hbm.values()],
        *[pltpu.with_memory_space_constraint(array, pltpu.VMEM) for array in vmem.values()],
    )
    return Refs(**dict(zip([*outs, *far_outs], results)))


SMEM = pl.BlockSpec(memory_space=pltpu.SMEM)
HBM = pl.BlockSpec(memory_space=pltpu.HBM)
VMEM = pl.BlockSpec(memory_space=pltpu.VMEM)
ANY = pl.BlockSpec(memory_space=pl.ANY)


def swapped(array, axis, bit):
    devices = lax.axis_size(axis)
    return lax.ppermute(array, axis, [(i, i ^ bit) for i in range(devices)])


def held_until(array, *others):
    return lax.optimization_barrier((array, *others))[0]


def own_bit(bit):
    return (lax.axis_index("dp") >> bit) & 1


def swapped_middle(array):
    ranks = lax.axis_size("dp")
    quarter = ranks // 4
    pairs = [(i, i + quarter) for i in range(quarter, 2 * quarter)]
    pairs += [(j, i) for i, j in pairs]
    outer = [*range(quarter), *range(ranks - quarter, ranks)]
    return lax.ppermute(array, "dp", pairs + [(i, i ^ 1) for i in outer])


def at_middle():
    return own_bit(2) != own_bit(3)


def quick_kernel(kernel, name, ins, outs):
    return run_kernel(kernel, name, {}, ins, outs, {}, {}, 0, 4, work=10**8)


def sum_of_cores(cut, quarters, ways):
    rows, width = cut.stop - cut.start, quarters[0][0].shape[2]
    used = sorted({way(z) for way in ways for z in range(4)})

    def kernel(k):
        y = own_bit(1)
        here = lax.axis_index("dp") >> 2
        for z in range(4):

            @pl.when(here == z)
            def _(z=z):
                for at, way in enumerate(ways):
                    keep, core = getattr(k, f"keep{way(z)}"), getattr(k, f"core{way(z)}")
                    total = keep[1 - y, cut].astype(F32) + core[1 - y].astype(F32)
                    getattr(k, f"give{at}")[...] = total.astype(BF16)
                    total = keep[y, cut].astype(F32) + core[y].astype(F32)
                    getattr(k, f"mine{at}")[...] = total

    ins = {f"keep{z}": quarters[z][0] for z in used}
    ins.update({f"core{z}": quarters[z][1] for z in used})
    outs = {f"give{at}": ((rows, width), BF16) for at in range(len(ways))}
    outs.update({f"mine{at}": ((rows, width), F32) for at in range(len(ways))})
    return quick_kernel(kernel, "sum_of_cores", ins, outs)


def same(z):
    return z


def next_to(z):
    return z ^ 1


def nearer(z):
    return 2 - (z >> 1)


def farther(z):
    return 3 - 3 * (z >> 1)


def added(wide, part, middle=None, full=False):
    def kernel(k):
        total = k.wide[...] + k.part[...].astype(F32)
        if middle is not None:
            total = total + jnp.where(at_middle(), k.middle[...].astype(F32), 0.0)
        k.low[...] = total.astype(BF16)
        if full:
            k.full[...] = total

    ins = dict(wide=wide, part=part)
    if middle is not None:
        ins = dict(wide=wide, part=part, middle=middle)
    outs = dict(low=(wide.shape, BF16))
    if full:
        outs = dict(low=(wide.shape, BF16), full=(wide.shape, F32))
    return quick_kernel(kernel, "added", ins, outs)


def sum_over_dp(cut, quarters, farthest):
    middle = sum_of_cores(cut, quarters, (nearer,))
    near = sum_of_cores(cut, quarters, (next_to, same))
    from_y3, from_y2 = swapped(farthest.give0, "dp", 2), swapped(middle.give0, "dp", 2)
    from_y1, from_y0 = swapped(near.give0, "dp", 2), swapped(near.give1, "dp", 2)
    third = added(farthest.mine0, from_y3, full=True)
    from_end3 = swapped(third.low, "dp", 4)
    second = added(middle.mine0, from_y2, full=True)
    from_end2 = swapped(second.low, "dp", 4)
    from_middle3 = swapped_middle(added(third.full, from_end3).low)
    from_middle2 = swapped_middle(added(second.full, from_end2).low)
    from_end1 = swapped(added(near.mine0, from_y1, from_middle3).low, "dp", 4)
    return dict(zip(SUMMANDS, (near.mine1, from_y0, from_end1, from_middle2)))


def adam_of(grad, master, mean_old, square_old, step):
    mean_new = 0.9 * mean_old + 0.1 * grad
    square_new = 0.98 * square_old + 0.02 * grad * grad
    rate = step.shape[1] ** (-0.5) * jnp.minimum(lax.rsqrt(step), step * WARMUP_STEPS ** (-1.5))
    mean_share = 1.0 - jnp.exp(step * math.log(0.9))
    square_share = 1.0 - jnp.exp(step * math.log(0.98))
    fixed_mean = mean_new * (1.0 / mean_share)
    fixed_square = square_new * (1.0 / square_share)
    change = -rate * fixed_mean / (jnp.sqrt(fixed_square) + ADAM_EPS)
    return change, mean_new, square_new, master + change


def adam_kernel(k, full):
    width = k.master.shape[1]
    share = k.vec_master.shape[1]
    step = jnp.full((1, width), k.step[0], jnp.int32).astype(F32)
    rows = k.master.shape[0]
    middle = at_middle()
    totals = []
    for at in range(len([name for name in vars(k) if name.startswith("mine")])):
        mine, *low = [getattr(k, f"{name}{at}")[...].astype(F32) for name in SUMMANDS]
        from_y, from_end, from_middle = low
        totals.append(mine + from_y + from_end + jnp.where(middle, from_middle, 0.0))
    total = jnp.concatenate(totals, axis=0)
    grad, vec_grad = total[:rows], total[rows : rows + 1]
    parts = adam_of(grad, k.master[...], k.mean[...], k.square[...], step)
    if full:
        k.grad[...] = grad
        k.change[...], k.mean_new[...], k.square_new[...] = parts[:3]
    else:
        k.own[:rows] = parts[3].astype(BF16)
    pad = jnp.zeros((1, width - share), F32)

    def padded(ref):
        return jnp.concatenate([ref[...], pad], axis=1)

    parts = adam_of(
        vec_grad, padded(k.vec_master), padded(k.vec_mean), padded(k.vec_square), step
    )
    if full:
        k.vec_grad[...] = vec_grad[:, :share]
        k.vec_change[...] = parts[0][:, :share]
        k.vec_mean_new[...] = parts[1][:, :share]
        k.vec_square_new[...] = parts[2][:, :share]
        for copy in vars(k.go).values():
            copy.start()
        for copy in vars(k.go).values():
            copy.wait()
    else:
        k.own[rows:] = jnp.broadcast_to(parts[3], (TAIL, width)).astype(BF16)


def adam(summands, state, step, full):
    shape, vec_shape = state.master.shape, state.vec_master.shape
    outs, far = {}, {}
    if full:
        far = dict.fromkeys(("grad", "change", "mean_new", "square_new"), (shape, F32))
        far.update({"vec_" + name: (vec_shape, F32) for name in far})
    else:
        outs = {"own": ((shape[0] + TAIL, shape[1]), BF16)}
    return run_kernel(
        lambda k: adam_kernel(k, full), "adam_outputs" if full else "adam", {},
        {**summands, **vars(state)}, outs, far, {}, 0, 6, work=10**9, smem={"step": step},
    )


def place_blocks(pieces, share, rows_all, before=None):
    arrays = [piece[-1] for piece in pieces]
    width = arrays[0].shape[1]
    extra = [] if before is None else [*before]

    def kernel(*refs):
        ins, (target, tails, sems) = refs[: len(arrays)], refs[-3:]
        me = lax.axis_index("dp")
        owners = [z(me >> 2) * 4 + ((me & 3) ^ (2 * y + core)) for z, y, core, _ in pieces]
        copies = []
        for at, (owner, ref) in enumerate(zip(owners, ins)):
            there = pl.ds(pl.multiple_of(owner * share, share), share)
            copies.append(load(ref.at[:share], target.at[there], sems.at[at]))
        if extra:
            tails[...] = refs[len(arrays) + 1][...]
        for owner, ref in zip(owners, ins):
            tails[owner] = ref[share:]
        for copy in copies:
            copy.wait()

    return pl.pallas_call(
        kernel,
        name="place_blocks",
        in_specs=[VMEM] * len(arrays) + [HBM, VMEM][: len(extra)],
        out_specs=[HBM, VMEM],
        out_shape=[
            pltpu.HBM((rows_all, width), BF16),
            pltpu.VMEM((rows_all // share, TAIL, width), BF16),
        ],
        scratch_shapes=[pltpu.SemaphoreType.DMA((len(arrays),))],
        input_output_aliases={len(arrays): 0} if extra else {},
        compiler_params=pltpu.CompilerParams(vmem_limit_bytes=4 * 2**20),
        cost_estimate=pl.CostEstimate(flops=10**9, bytes_accessed=1, transcendentals=0),
    )(*[pltpu.with_memory_space_constraint(array, pltpu.VMEM) for array in arrays], *extra)


def either(middle, end):
    def kernel(k):
        @pl.when(at_middle())
        def _():
            k.out[...] = k.middle[...]

        @pl.when(jnp.logical_not(at_middle()))
        def _():
            k.out[...] = k.end[...]

    outs = dict(out=(end.shape, BF16))
    return quick_kernel(kernel, "either", dict(middle=middle, end=end), outs).out


def gather_blocks(own, share, rows_all, meanwhile):
    end1, middle1 = swapped(own, "dp", 4), swapped_middle(own)
    end1, from_y0 = lax.optimization_barrier((end1, swapped(own, "dp", 2)))
    end2, middle2 = swapped(middle1, "dp", 4), swapped_middle(end1)
    from_y1 = swapped(end1, "dp", 2)
    end3 = swapped(middle2, "dp", 4)
    second = either(middle1, end2)
    from_y2 = swapped(second, "dp", 2)
    third = either(middle2, end3)
    from_y3 = swapped(third, "dp", 2)

    def both(z, y, array):
        return [(z, y, 0, array), (z, y, 1, swapped(array, "dp", 1))]

    early = both(same, 0, own) + both(same, 1, from_y0) + both(next_to, 0, end1)
    early += both(next_to, 1, from_y1) + both(nearer, 0, second)
    first = place_blocks(early, share, rows_all)
    from_y3 = held_until(from_y3, *first, meanwhile)
    late = both(nearer, 1, from_y2) + both(farther, 0, third) + both(farther, 1, from_y3)
    return place_blocks(late, share, rows_all, first)


def body(
    inputs,
    lengths,
    cotangent,
    matrices,
    vectors,
    master_matrices,
    master_vectors,
    matrix_mean,
    matrix_square,
    vector_mean,
    vector_square,
    adam_step,
):
    row_count, seq_len, width = inputs.shape[1:]
    tokens = row_count * seq_len
    rows_all, vec_all = matrices.shape[1], vectors.shape[1]
    ffn = (rows_all - 6 * width) // 2
    half = rows_all // 2
    ranks = lax.axis_size("dp")
    share, vec_share = rows_all // ranks, vec_all // ranks
    by_swaps = ranks == 16 and share % 32 == 0
    me = lax.axis_index("dp")

    x = inputs.reshape(tokens, width)
    cot = cotangent.reshape(tokens, width)
    mats = matrices.reshape(rows_all, width)
    lens_here = pltpu.SMEM(lengths.shape, jnp.int32)

    def spec(columns, dtype):
        return ((tokens, columns), dtype)

    full, low, deep = spec(width, F32), spec(width, BF16), spec(ffn, BF16)
    square, mask = ((width, width), BF16), spec(seq_len, F32)
    double, w_ffn = ((2 * width, width), BF16), ((ffn, width), BF16)
    lse = ((row_count, HEADS, seq_len), F32)
    norms = dict(normal2=full, rstd2=spec(LANES, F32), normal3=full, rstd3=spec(LANES, F32))
    half_tokens = tokens // 2
    half_low, half_full = ((half_tokens, width), BF16), ((half_tokens, width), F32)
    half_double, half_back = ((half_tokens, 2 * width), BF16), ((half_tokens, width + EARLY_LANES), BF16)
    half_rest = ((half_tokens, 4 * width - EARLY_LANES), BF16)
    all_vecs, triple = ((1, vec_all), F32), spec(3 * width, BF16)
    block = (ranks // 8, share + TAIL, width) if by_swaps else (half // 2, width)

    first_rows = (share + TAIL) // 2 // 16 * 16
    cuts = (slice(0, first_rows), slice(first_rows, share + TAIL))

    def sides(*zs):
        result = {f"keep{z}": (block, BF16) for z in zs}
        if by_swaps:
            for at, cut in enumerate(cuts):
                rows = cut.stop - cut.start
                result.update({f"give{z}{at}": ((block[0], rows, width), BF16) for z in zs})
        return result

    def quarter(kernel, z, at):
        return getattr(kernel, f"keep{z}"), swapped(getattr(kernel, f"give{z}{at}"), "dp", 1)

    early = ((half - 6 * width, width), BF16)

    def wide(rows):
        return ((width // LANES, rows + 8, LANES), F32)

    cross_half = lax.dynamic_slice(mats, ((4 + (me & 1)) * width, 0), (width, width), allow_negative_indices=False)
    cross_mine = swapped(cross_half, "section", 1)
    f = run_kernel(
        forward_kernel, "forward", dict(mats=mats, x=x, vectors=vectors, lengths=lengths), {},
        dict(
            h1=full, w_in=w_ffn, act=deep, slope=deep, **norms,
            memory=half_low, w_cross=double, qc=low, w_out=w_ffn, vecs=all_vecs,
        ),
        dict(
            qkv=triple, lse=lse, mixed=low, normal1=full, rstd1=spec(LANES, F32), mask=mask, w_attn_out=square,
            w_attn=((3 * width, width), BF16), low=low,
        ),
        dict(
            raw_attn=((3 * width, width), BF16), raw_cross=double, raw_ffn=w_ffn,
            x_here=low, total=half_full, wide=wide(ffn), raw_vecs=((1, vec_all), BF16), lens=lens_here,
        ),
        8, 10,
    )
    memory_far0 = swapped(f.memory, "section", 1)
    r = run_kernel(
        forward_rest_kernel, "forward_rest", {},
        dict(
            h1=f.h1, w_in=f.w_in, w_out=f.w_out, vecs=f.vecs, old_act=f.act, old_slope=f.slope,
            **{"old_" + name: getattr(f, name) for name in norms},
        ),
        dict(act=deep, slope=deep, **norms, memory=half_low), dict(low_rest=half_low),
        dict(total=half_full), 0, 6,
        [("old_" + name, name) for name in ("act", "slope", *norms)],
        work=WORK_REST,
    )
    memory_far1 = swapped(r.memory, "section", 1)
    cross_mine = held_until(cross_mine, f.memory)
    cross_other = swapped(cross_mine, "dp", 1)
    p = run_kernel(
        prepare_kernel, "prepare", dict(cot_all=cot, lengths=lengths),
        dict(cross_mine=cross_mine, cross_other=cross_other),
        dict(w_pairs=double, mask=mask, cot=low), {},
        dict(raw=double, wide=wide(2 * width), raw_cot=low, lens=lens_here),
        2, 4,
    )
    shared = dict(
        **vars(p), w_cross=f.w_cross, qc=f.qc, h1=f.h1, w_in=f.w_in, w_out=f.w_out, vecs=f.vecs,
    )
    for_tokens = dict(act=deep, side=deep, grad_ffn=low, low2=low, grad_sum2=full)
    far_half = dict(mixed=half_low, right=half_double)
    held = dict(
        pairs=half_double, slope=((half_tokens, ffn), F32), lse=((row_count // 2, HEADS, seq_len), F32),
        grad_mixed=half_low, total=half_full, normal2=half_full, rstd2=((half_tokens, LANES), F32),
    )
    d = run_kernel(
        lambda k: decoder_kernel(k, 0), "decoder", {},
        dict(memory=memory_far0, near_memory=f.memory, **shared, enc_act=r.act, enc_slope=r.slope),
        dict(
            back=half_back, grad_pairs=half_double, vec_grads=all_vecs, **for_tokens, top=half_low,
        ),
        far_half, held,
        0, SPARE_D, (("enc_act", "act"), ("enc_slope", "side")), work=WORK_D,
    )
    back_far = swapped(d.back, "section", 1)
    before = {"old_" + name: getattr(d, name) for name in for_tokens}
    e = run_kernel(
        lambda k: decoder_kernel(k, 1), "decoder_rest", {},
        dict(
            memory=memory_far1, near_memory=r.memory, **shared, **before, vec_before=d.vec_grads,
            top_before=d.top, pairs_before=d.grad_pairs,
        ),
        dict(grad_memory=half_low, rest=half_rest, vec_grads=all_vecs, **for_tokens),
        dict(layer_out=low, **far_half), held,
        0, SPARE_D, [("old_" + name, name) for name in for_tokens], work=WORK_D,
    )
    grad_memory_far = swapped(e.grad_memory, "section", 1)
    rest_far = swapped(e.rest, "section", 1)
    ahead = dict(
        normal1=full, rstd1=spec(LANES, F32), w_attn_out=square, mask=mask, lse=lse, qkv=triple,
        w_attn=((3 * width, width), BF16),
    )
    s = run_kernel(
        backward_kernel, "backward",
        dict(
            **{"far_" + name: getattr(f, name) for name in ahead},
            far_x=x, far_mixed=f.mixed, far_low=f.low, far_low_rest=r.low_rest,
            far_right0=d.right, far_right1=e.right, far_cross_mixed0=d.mixed, far_cross_mixed1=e.mixed,
        ),
        dict(
            dec_grad_ffn=e.grad_ffn, dec_vec_grads=e.vec_grads,
            back=back_far, grad_memory=grad_memory_far, act=e.act, side=e.side,
            low2=e.low2, grad_sum2=e.grad_sum2, **{name: getattr(r, name) for name in norms}, h1=f.h1, w_in=f.w_in, w_out=f.w_out, vecs=f.vecs,
        ),
        dict(
            vec_grads=all_vecs, early=early, **sides(2, 3), grad_attn=low, grad_qkv=triple,
            x=low, mixed=low, low=low, right=spec(2 * width, BF16), cross_mixed=low,
        ),
        dict(grad_x=full),
        dict(
            grad_pre=deep, grad_ffn=low, low1=low, wide=wide(ffn), grad_h1=full,
            flat=((2 * ffn, width), BF16), grad_mixed=low, **ahead,
        ),
        15, 9, work=4 * 10**10,
    )
    quarter_flat = ((half // 2, width), BF16)
    a = run_kernel(
        attn_grad_kernel, "attn_grad", {},
        dict(
            grad_qkv=s.grad_qkv, vec_grads=s.vec_grads, x=s.x, grad_attn=s.grad_attn, mixed=s.mixed,
        ),
        dict(left=((4 * width - half // 2, width), BF16), **sides(0)), {},
        dict(wide=wide(3 * width), flat=quarter_flat), 0, 4, work=10**8,
    )
    if by_swaps:
        ends = [(quarter(a, 0, at), quarter(s, 3, at)) for at in range(2)]
        farthest = [
            sum_of_cores(cut, (first, None, None, third), (farther,))
            for cut, (first, third) in zip(cuts, ends)
        ]
        left = held_until(a.left, farthest[0].give0)
    else:
        left = a.left
    b = run_kernel(
        cross_grad_kernel, "cross_grad", {},
        dict(
            left=left, vec_grads=s.vec_grads, early=s.early, back=back_far, rest=rest_far, low=s.low,
            right=s.right, cross_mixed=s.cross_mixed,
        ),
        sides(1), {}, dict(wide=wide(2 * width), flat=quarter_flat), 0, 4, work=10**8,
    )

    state = Refs(master=master_matrices[0], mean=matrix_mean[0], square=matrix_square[0])
    state = Refs(**vars(state), vec_master=master_vectors, vec_mean=vector_mean, vec_square=vector_square)
    if by_swaps:
        summands = {}
        for at, cut in enumerate(cuts):
            first, third = ends[at]
            quarters = (first, quarter(b, 1, at), quarter(s, 2, at), third)
            parts = sum_over_dp(cut, quarters, farthest[at])
            summands.update({f"{name}{at}": part for name, part in parts.items()})
        own = adam(summands, state, adam_step, False).own
        result = adam(summands, state, adam_step, True)
        new_mat, tails = gather_blocks(own, share, rows_all, result.change)
        new_vec = tails[:, 0, :vec_share].reshape(1, vec_all)
    else:
        whole = jnp.concatenate([a.keep0, b.keep1, s.keep2, s.keep3], axis=0)
        grad = lax.psum_scatter(whole, "dp", scatter_dimension=0, tiled=True).astype(F32)
        vec_grad = lax.dynamic_slice(
            lax.psum(s.vec_grads, "dp"), (0, me * vec_share), (1, vec_share)
        )
        step = jnp.full((1, width), adam_step[0].astype(F32))
        parts = adam_of(grad, state.master, state.mean, state.square, step)
        vec_step = jnp.full((1, width), adam_step[0].astype(F32))
        pad = ((0, 0), (0, width - vec_share))
        vec_parts = [
            part[:, :vec_share]
            for part in adam_of(
                *[jnp.pad(v, pad) for v in (vec_grad, master_vectors, vector_mean, vector_square)],
                vec_step,
            )
        ]
        names = ("change", "mean_new", "square_new")
        result = dict(grad=grad, vec_grad=vec_grad, **dict(zip(names, parts)))
        result.update({"vec_" + name: part for name, part in zip(names, vec_parts)})
        result = Refs(**result)
        new_mat = lax.all_gather(parts[3].astype(BF16), "dp", axis=0, tiled=True)
        new_vec = lax.all_gather(vec_parts[3].astype(BF16), "dp", axis=1, tiled=True)
    return (
        e.layer_out.reshape(1, row_count, seq_len, width),
        s.grad_x.reshape(1, row_count, seq_len, width),
        result.grad[None],
        result.vec_grad,
        result.change[None],
        result.vec_change,
        result.mean_new[None],
        result.square_new[None],
        result.vec_mean_new,
        result.vec_square_new,
        new_mat[None],
        new_vec,
    )


def solution(mesh):
    return jax.shard_map(
        body,
        mesh=mesh,
        in_specs=(
            P("section", "dp", None, None),
            P(None, "dp", None),
            P("dp", None, None),
            P("section", None, None),
            P("section", None),
            P("section", "dp", None),
            P("section", "dp"),
            P("section", "dp", None),
            P("section", "dp", None),
            P("section", "dp"),
            P("section", "dp"),
            P(),
        ),
        out_specs=(
            P("section", "dp", None, None),
            P("section", "dp", None, None),
            P("section", "dp", None),
            P("section", "dp"),
            P("section", "dp", None),
            P("section", "dp"),
            P("section", "dp", None),
            P("section", "dp", None),
            P("section", "dp"),
            P("section", "dp"),
            P("section", None, None),
            P("section", None),
        ),
        check_vma=False,
    )
```
